32 devices in a mesh: parts: 2 (over x), il: 8 (over z, y), xl: 2 (over core).
Axes of the slice: x: 2, y: 2, z: 4, core: 2. Of those that a mesh axis runs over, the one named last changes fastest.
Arguments:
- volume: bfloat16 [18, 2048, 512], P(None, ('parts', 'il'), 'xl'), parts along dimension 1, may hold values from -8 to 8
Outputs:
- inline_dip: float32 [16, 2048, 512], P(None, ('parts', 'il'), 'xl'), parts along dimension 1
- cross_dip: float32 [16, 2048, 512], P(None, ('parts', 'il'), 'xl'), parts along dimension 1
- planarity: float32 [16, 2048, 512], P(None, ('parts', 'il'), 'xl'), parts along dimension 1
The draws below stay inside these ranges and needn't reach their ends.
There are 2 independent parts, one for each index of `parts`. The reference program is written for one: setup_inputs(seed, part) draws one part's arguments, and reference() takes and returns one part's arrays. A program takes and returns all parts, laid end to end along the dimension named above; each array names one. Nothing has to cross between parts.
All inputs are finite; a program needn't handle non-finite values.
Results may differ from the reference program's by a relative error of at most 0.0021.
Values may be sent and summed in bfloat16 or wider, within the bound.
No kernel may reach another device: no remote copies, remote signals or barrier semaphores. Data moves between devices by JAX's collectives and lax.ppermute only.
A program may use at most 64 MiB of HBM per device.

```python
import math
import jax
import jax.numpy as jnp
from jax import lax

DEPTH = 16
RADIUS = 9
NI = 1024
NX = 512


def fault_blocks(key, count):
    keys = jax.random.split(key, 3)
    positions = jnp.arange(count).astype(jnp.int32)
    breaks = (jax.random.randint(keys[0], (count,), 0, 10) == 0) | (positions == 0)
    block_ids = jnp.cumsum(breaks.astype(jnp.int32)) - 1
    starts = lax.cummax(jnp.where(breaks, positions, 0), axis=0)
    offsets = (positions - starts).astype(jnp.float32)
    slopes = jax.random.uniform(keys[1], (count,), jnp.float32, -0.7, 0.7)
    throws = jax.random.uniform(keys[2], (count,), jnp.float32, -math.pi, math.pi)
    return jnp.take(slopes, block_ids) * offsets + jnp.take(throws, block_ids)


def draw_volume(key, part):
    key = jax.random.fold_in(key, 11)
    keys = jax.random.split(key, 6)
    depth_wave = 0.8 + 0.4 * jax.random.uniform(keys[0], (), jnp.float32)
    inline_phase = fault_blocks(keys[1], NI)[None, :, None]
    cross_phase = fault_blocks(keys[2], NX)[None, None, :]
    inline_gain = jnp.exp(jax.random.uniform(keys[3], (1, NI, 1), jnp.float32, math.log(0.6), math.log(1.6)))
    cross_gain = jnp.exp(jax.random.uniform(keys[4], (1, 1, NX), jnp.float32, math.log(0.6), math.log(1.6)))
    depths = (jnp.arange(DEPTH + 2) - 1).astype(jnp.float32)[:, None, None]
    phase = depth_wave * depths + inline_phase + cross_phase
    shape = (DEPTH + 2, NI, NX)
    noise = 0.3 * jnp.clip(jax.random.normal(keys[5], shape, jnp.float32), -4.0, 4.0)
    values = inline_gain * cross_gain * (jnp.cos(phase) + noise)
    return jnp.clip(values, -8.0, 8.0).astype(jnp.bfloat16)


def setup_inputs(seed: int = 0, part: int = 0) -> dict:
    arg_keys = jax.random.split(jax.random.key(seed), 2)
    part_keys = jax.random.split(jax.random.fold_in(arg_keys[1], part), 2)
    volume = draw_volume(jax.random.fold_in(jax.random.fold_in(arg_keys[1], part), 71), part)
    return dict(volume=volume)


def filter_taps():
    offsets = jnp.arange(2 * RADIUS + 1).astype(jnp.float32)
    sigma = RADIUS / 3.0
    shape = jnp.exp(-0.5 * ((offsets - RADIUS) / sigma) ** 2)
    return (shape / jnp.sum(shape)).astype(jnp.bfloat16)

def smooth_along(values, kernel_shape, padding):
    taps = filter_taps().astype(jnp.float32).reshape(kernel_shape)
    stacked = values.astype(jnp.float32).reshape(6, 1, NI, NX)
    result = lax.conv_general_dilated(stacked, taps, (1, 1), padding, precision=lax.Precision.HIGHEST)
    return result.reshape(6, NI, NX)

def attributes(tensor):
    comp_a, comp_b, comp_c, comp_d, comp_e, comp_f = [tensor[index] for index in range(6)]
    inline_dip = -comp_e / (comp_c + 1e-06)
    cross_dip = -comp_f / (comp_c + 1e-06)
    spread = 0.5 * ((comp_a - comp_b) ** 2 + (comp_b - comp_c) ** 2 + (comp_c - comp_a) ** 2)
    spread = spread + 3.0 * (comp_d * comp_d + comp_e * comp_e + comp_f * comp_f)
    planarity = jnp.sqrt(spread) / (comp_a + comp_b + comp_c + 1e-06)
    return (inline_dip, cross_dip, planarity)

def reference(volume):
    width = 2 * RADIUS + 1

    def one_depth(depth_index):
        slab = lax.dynamic_slice_in_dim(volume, depth_index, 3, 0).astype(jnp.float32)
        centre = jnp.pad(slab[1], ((1, 1), (1, 1)))
        grad_i = 0.5 * (centre[2:, 1:-1] - centre[:-2, 1:-1])
        grad_x = 0.5 * (centre[1:-1, 2:] - centre[1:-1, :-2])
        grad_z = 0.5 * (slab[2] - slab[0])
        moments = jnp.stack([grad_i * grad_i, grad_x * grad_x, grad_z * grad_z, grad_i * grad_x, grad_i * grad_z, grad_x * grad_z]).astype(jnp.bfloat16)
        lined = smooth_along(moments, (1, 1, width, 1), ((RADIUS, RADIUS), (0, 0))).astype(jnp.bfloat16)
        tensor = smooth_along(lined, (1, 1, 1, width), ((0, 0), (RADIUS, RADIUS)))
        return attributes(tensor)
    depth_list = jnp.arange(DEPTH).astype(jnp.int32)
    inline_dip, cross_dip, planarity = lax.map(one_depth, depth_list)
    return (inline_dip, cross_dip, planarity)
```

```python
import jax
import jax.numpy as jnp
import ml_dtypes
import numpy as np
from jax import lax
from jax.experimental import pallas as pl
from jax.experimental.pallas import tpu as pltpu
from jax.sharding import PartitionSpec as P

RADIUS = 9
SIDE = 16
SLOTS = 8
BF16 = ml_dtypes.bfloat16


def filter_taps():
    offsets = np.arange(2 * RADIUS + 1).astype(np.float32)
    sigma = np.float32(RADIUS / 3.0)
    shape = np.exp(np.float32(-0.5) * ((offsets - RADIUS) / sigma) ** 2)
    return (shape / np.sum(shape, dtype=np.float32)).astype(BF16).astype(np.float32)


def band(source, target):
    offset = source[:, None] - target[None, :] + RADIUS
    inside = (offset >= 0) & (offset <= 2 * RADIUS)
    return np.where(inside, filter_taps()[np.clip(offset, 0, 2 * RADIUS)], 0.0)


def difference(source, target):
    offset = source[:, None] - target[None, :]
    return (offset == 1).astype(np.float32) - (offset == -1).astype(np.float32)


class Tables:
    def __init__(self, rows, cols):
        self.rows, self.cols = rows, cols
        self.parts, self.at, self.total = [], {}, 0
        slots = np.arange(128) // SIDE
        place = np.arange(128) % SIDE
        row = np.arange(rows)
        position = np.concatenate([row, rows + np.arange(SIDE), np.arange(SIDE) - SIDE])
        self.add("lines", 0.25 * band(position, row).T)
        self.add("diff_i", difference(position, position).T)
        col = np.arange(cols)
        self.add("diff_x", difference(col, col))
        self.add("smooth_x", band(col, col))
        halo_0, halo_1 = cols + place, place - SIDE
        for x, halo in enumerate((halo_0, halo_1)):
            self.add(f"edge{x}", difference(col, halo))
            self.add(f"diff_h{x}", difference(halo, col))
            self.add(f"smooth_h{x}", band(halo, col))
        plane = np.concatenate(
            [1 + slots, 1 + SLOTS + slots, np.where(slots == 0, 0, np.where(slots == 1, 2 * SLOTS + 1, -99))]
        )
        places = np.concatenate([place, place, place])
        for group in range(2):
            centre = 1 + SLOTS * group + slots
            same = (places[:, None] == place[None, :]).astype(np.float32)
            depth = difference(plane, centre) * same
            level = (plane[:, None] == centre[None, :]).astype(np.float32)
            across = difference(places, place) * level
            self.add(f"halo{group}", np.concatenate([depth, across], axis=1))
        self.table = np.concatenate(self.parts, axis=0)

    def add(self, name, matrix):
        count, width = matrix.shape
        padded = np.zeros((-(-count // 16) * 16, self.cols), np.float32)
        padded[:count, :width] = matrix
        self.at[name] = (self.total, count, width)
        self.parts.append(padded.astype(BF16))
        self.total += padded.shape[0]

    def load(self, ref, name):
        start, count, width = self.at[name]
        return ref[start : start + count, :width]


def dot(left, right):
    return jnp.dot(left, right, preferred_element_type=jnp.float32)


def side_kernel(vol_ref, side_ref, top_ref, bottom_ref, top_corner_ref, bottom_corner_ref):
    depths, rows, cols = vol_ref.shape
    x = lax.axis_index("xl")
    first = jnp.where(x == 0, cols - SIDE, 0)
    lane = lax.broadcasted_iota(jnp.int32, (cols, 128), 0)
    place = lax.broadcasted_iota(jnp.int32, (cols, 128), 1)
    pick = (lane == first + lax.rem(place, SIDE)).astype(jnp.float32).astype(jnp.bfloat16)
    slot = lax.div(lax.broadcasted_iota(jnp.int32, (rows, 128), 1), SIDE)

    def piece(depth, index):
        return jnp.where(slot == index, dot(vol_ref[depth], pick), 0.0)

    for tile in range(3):
        planes = ((0, depths - 1), (0, 1)) if tile == 2 else (range(1 + SLOTS * tile, 1 + SLOTS * (tile + 1)), range(SLOTS))
        total = None
        for depth, index in zip(*planes):
            term = piece(depth, index)
            total = term if total is None else total + term
        packed = total.astype(jnp.bfloat16)
        side_ref[tile] = packed
        top_corner_ref[tile] = packed[:SIDE]
        bottom_corner_ref[tile] = packed[rows - SIDE :]
    top_ref[...] = vol_ref[:, :SIDE, :]
    bottom_ref[...] = vol_ref[:, rows - SIDE :, :]


def moments(grad_i, grad_x, grad_z):
    terms = (
        grad_i * grad_i,
        grad_x * grad_x,
        grad_z * grad_z,
        grad_i * grad_x,
        grad_i * grad_z,
        grad_x * grad_z,
    )
    return [term.astype(jnp.bfloat16) for term in terms]


def main_kernel(
    tables, vol_ref, side_ref, next_ref, last_ref, next_corner_ref, last_corner_ref, table_ref,
    dip_i_ref, dip_x_ref, plan_ref,
    pad_ref, halo_ref, lines_ref, smooth_ref, diff_h_ref, lined_h_ref, lined_a_ref, lined_b_ref,
    out_i_ref, out_x_ref, out_p_ref, sems,
):
    depths, rows, cols = vol_ref.shape
    count = depths - 2
    padded = rows + 2 * SIDE
    x = lax.axis_index("xl")
    il = lax.axis_index("il")
    last = lax.axis_size("il") - 1

    pad_ref[:, :rows, :] = vol_ref[...]
    pad_ref[:, rows : rows + SIDE, :] = next_ref[...]
    pad_ref[:, rows + SIDE :, :] = last_ref[...]
    for tile in range(3):
        lanes = slice(128 * tile, 128 * (tile + 1))
        halo_ref[:rows, lanes] = side_ref[tile]
        halo_ref[rows : rows + SIDE, lanes] = next_corner_ref[tile]
        halo_ref[rows + SIDE :, lanes] = last_corner_ref[tile]

    column = lax.broadcasted_iota(jnp.int32, (rows, padded), 1)
    inside = (column < rows) | ((column < rows + SIDE) & (il < last)) | ((column >= rows + SIDE) & (il > 0))
    lines_ref[...] = jnp.where(inside, tables.load(table_ref, "lines").astype(jnp.float32), 0.0).astype(jnp.bfloat16)

    def by_side(name):
        zero = tables.load(table_ref, name + "0").astype(jnp.float32)
        return jnp.where(x == 0, zero, tables.load(table_ref, name + "1").astype(jnp.float32))

    slot_row = lax.div(lax.broadcasted_iota(jnp.int32, (128, cols), 0), SIDE)
    smooth_h, diff_h = by_side("smooth_h"), by_side("diff_h")
    for index in range(SLOTS):
        smooth_ref[index, :cols, :] = tables.load(table_ref, "smooth_x")
        smooth_ref[index, cols:, :] = jnp.where(slot_row == index, smooth_h, 0.0).astype(jnp.bfloat16)
        diff_h_ref[index] = jnp.where(slot_row == index, diff_h, 0.0).astype(jnp.bfloat16)

    diff_i = tables.load(table_ref, "diff_i")
    diff_x = tables.load(table_ref, "diff_x")
    edge = by_side("edge").astype(jnp.bfloat16)
    slot_lane = lax.div(lax.broadcasted_iota(jnp.int32, (padded, 128), 1), SIDE)
    for group in range(2):
        both = dot(halo_ref[...], tables.load(table_ref, f"halo{group}"))
        grad_z, grad_x = both[:, :128], both[:, 128:]
        for index in range(SLOTS):
            near = dot(pad_ref[SLOTS * group + index + 1], edge)
            grad_x = grad_x + jnp.where(slot_lane == index, near, 0.0)
        grad_i = dot(diff_i, halo_ref[:, 128 * group : 128 * (group + 1)])
        for comp, term in enumerate(moments(grad_i, grad_x, grad_z)):
            lined_h_ref[group, rows * comp : rows * (comp + 1), :] = dot(lines_ref[...], term).astype(jnp.bfloat16)

    def stage_lines(z, lined_ref):
        group, index = lax.div(z, SLOTS), lax.rem(z, SLOTS)
        centre = pad_ref[z + 1]
        grad_i = dot(diff_i, centre)
        grad_x = dot(centre, diff_x) + dot(
            halo_ref[:, pl.ds(pl.multiple_of(128 * group, 128), 128)], diff_h_ref[index]
        )
        grad_z = pad_ref[z + 2].astype(jnp.float32) - pad_ref[z].astype(jnp.float32)
        lined_ref[:, cols:] = lined_h_ref[group]
        for comp, term in enumerate(moments(grad_i, grad_x, grad_z)):
            lined_ref[rows * comp : rows * (comp + 1), :cols] = dot(lines_ref[...], term).astype(jnp.bfloat16)

    def copies(z):
        pairs = ((out_i_ref, dip_i_ref), (out_x_ref, dip_x_ref), (out_p_ref, plan_ref))
        return [pltpu.make_async_copy(src.at[z], dst.at[z], sems.at[z, n]) for n, (src, dst) in enumerate(pairs)]

    def stage_attributes(z, lined_ref):
        weights = smooth_ref[lax.rem(z, SLOTS)]
        a, b, c, d, e, f = [dot(lined_ref[rows * comp : rows * (comp + 1), :], weights) for comp in range(6)]
        low = c + 1e-6
        inverse = -1.0 / low
        out_i_ref[z] = e * inverse
        out_x_ref[z] = f * inverse
        spread = (a - b) * (a - c) + (b - c) * (b - c) + 3.0 * (d * d + e * e + f * f)
        out_p_ref[z] = jnp.sqrt(spread) / (a + b + low)
        for copy in copies(z):
            copy.start()

    stage_lines(0, lined_a_ref)

    def pair(k, carry):
        z = 2 * k
        stage_lines(z + 1, lined_b_ref)
        stage_attributes(z, lined_a_ref)
        stage_lines(jnp.minimum(z + 2, count - 1), lined_a_ref)
        stage_attributes(z + 1, lined_b_ref)
        return carry

    lax.fori_loop(0, count // 2, pair, 0)
    for z in range(count):
        for copy in copies(z):
            copy.wait()


def body(volume):
    depths, rows, cols = volume.shape
    il, xl = lax.axis_size("il"), lax.axis_size("xl")
    assert xl == 2 and depths == 2 * SLOTS + 2 and cols == 256
    bf16 = jnp.bfloat16
    whole = pl.BlockSpec(memory_space=pltpu.VMEM)
    side, top, bottom, top_corner, bottom_corner = pl.pallas_call(
        side_kernel,
        out_shape=(
            jax.ShapeDtypeStruct((3, rows, 128), bf16),
            jax.ShapeDtypeStruct((depths, SIDE, cols), bf16),
            jax.ShapeDtypeStruct((depths, SIDE, cols), bf16),
            jax.ShapeDtypeStruct((3, SIDE, 128), bf16),
            jax.ShapeDtypeStruct((3, SIDE, 128), bf16),
        ),
        in_specs=[whole],
        out_specs=(whole,) * 5,
        compiler_params=pltpu.CompilerParams(vmem_limit_bytes=32 << 20),
        name="side_kernel",
    )(volume)

    up = [(i, i + 1) for i in range(il - 1)]
    down = [(i + 1, i) for i in range(il - 1)]
    swap = [(0, 1), (1, 0)]

    def crossed(pairs):
        return [(s * 2 + x, t * 2 + 1 - x) for s, t in pairs for x in range(2)]

    last_rows = lax.ppermute(bottom, "il", up)
    next_rows = lax.ppermute(top, "il", down)
    side_in = lax.ppermute(side, "xl", swap)
    last_corner = lax.ppermute(bottom_corner, ("il", "xl"), crossed(up))
    next_corner = lax.ppermute(top_corner, ("il", "xl"), crossed(down))

    tables = Tables(rows, cols)
    count, padded = depths - 2, rows + 2 * SIDE
    out = jax.ShapeDtypeStruct((count, rows, cols), jnp.float32)
    anywhere = pl.BlockSpec(memory_space=pl.ANY)
    return pl.pallas_call(
        lambda *refs: main_kernel(tables, *refs),
        out_shape=(out,) * 3,
        in_specs=[whole] * 7,
        out_specs=(anywhere,) * 3,
        scratch_shapes=[
            pltpu.VMEM((depths, padded, cols), bf16),
            pltpu.VMEM((padded, 384), bf16),
            pltpu.VMEM((rows, padded), bf16),
            pltpu.VMEM((SLOTS, cols + 128, cols), bf16),
            pltpu.VMEM((SLOTS, 128, cols), bf16),
            pltpu.VMEM((2, 6 * rows, 128), bf16),
            pltpu.VMEM((6 * rows, cols + 128), bf16),
            pltpu.VMEM((6 * rows, cols + 128), bf16),
            pltpu.VMEM((count, rows, cols), jnp.float32),
            pltpu.VMEM((count, rows, cols), jnp.float32),
            pltpu.VMEM((count, rows, cols), jnp.float32),
            pltpu.SemaphoreType.DMA((count, 3)),
        ],
        compiler_params=pltpu.CompilerParams(vmem_limit_bytes=48 << 20),
        name="main_kernel",
    )(volume, side_in, next_rows, last_rows, next_corner, last_corner, jnp.asarray(tables.table))


def solution(mesh):
    spec = P(None, ("parts", "il"), "xl")
    return jax.shard_map(body, mesh=mesh, in_specs=(spec,), out_specs=(spec,) * 3, check_vma=False)
```

```python
import jax
import jax.numpy as jnp
import ml_dtypes
import numpy as np
from jax import lax
from jax.experimental import pallas as pl
from jax.experimental.pallas import tpu as pltpu
from jax.sharding import PartitionSpec as P

RADIUS = 9
REACH = RADIUS + 1
SIDE = 16
SLOTS = 8
TILES = 3
EDGE = 16
OWN = 2
FAR = -1000
WHOLE = pl.BlockSpec(memory_space=pltpu.VMEM)
IN_HBM = pl.BlockSpec(memory_space=pltpu.HBM)


def filter_taps():
    offsets = np.arange(2 * RADIUS + 1).astype(np.float32)
    sigma = np.float32(RADIUS / 3.0)
    shape = np.exp(np.float32(-0.5) * ((offsets - RADIUS) / sigma) ** 2)
    return (shape / np.sum(shape, dtype=np.float32)).astype(ml_dtypes.bfloat16).astype(np.float32)


def iota(shape, dim):
    return lax.broadcasted_iota(jnp.int32, shape, dim)


def band(source, target, scale=1.0):
    offset = jnp.abs(source - target)
    weights = jnp.zeros(offset.shape, jnp.float32)
    for distance, tap in enumerate(filter_taps()[RADIUS:]):
        weights = jnp.where(offset == distance, jnp.float32(scale * tap), weights)
    return weights


def difference(source, target):
    offset = source - target
    return jnp.where(offset == 1, 1.0, jnp.where(offset == -1, -1.0, 0.0)).astype(jnp.float32)


def dot(left, right):
    return jnp.dot(left, right, preferred_element_type=jnp.float32)


def halo_plane(lane, tile, depths):
    slot = lax.div(lane, SIDE)
    rest = jnp.where(slot == 0, 0, jnp.where(slot == 1, depths - 1, FAR))
    return jnp.where(tile < 2, 1 + SLOTS * tile + slot, rest)


def halo_column(lane, x, cols):
    place = lax.rem(lane, SIDE)
    return jnp.where(x == 0, cols - OWN + place, place - (SIDE - OWN))


def edge_position(index, rows):
    first = index < EDGE
    previous = index - 2 * EDGE - REACH
    following = rows + index - 3 * EDGE
    outer = jnp.where(index < 2 * EDGE + REACH, previous, jnp.where(index < 3 * EDGE, FAR + 2 * index, following))
    outer = jnp.where(index >= 3 * EDGE + REACH, FAR + 2 * index, outer)
    return jnp.where(first, index, jnp.where(index < 2 * EDGE, rows - 2 * EDGE + index, outer))


def pack_kernel(
    hbm_ref, vol_ref, send_ref, own_ref, lines_ref, diff_i_ref, diff_x_ref, smooth_ref, halo_ref, lines_e_ref, diff_e_ref, sem
):
    depths, rows, cols = vol_ref.shape
    load = pltpu.make_async_copy(hbm_ref, vol_ref, sem)
    load.start()
    x, il, last = lax.axis_index("xl"), lax.axis_index("il"), lax.axis_size("il") - 1
    bf16 = jnp.bfloat16

    target, source = iota((rows, rows), 0), iota((rows, rows), 1)
    inner = (source > 0) & (source < rows - 1)
    lines_ref[...] = jnp.where(inner, band(source, target, 0.25), 0.0).astype(bf16)
    diff_i_ref[...] = difference(source, target).astype(bf16)
    target, source = iota((2 * EDGE, 4 * EDGE), 0), iota((2 * EDGE, 4 * EDGE), 1)
    source_at, target_at = edge_position(source, rows), edge_position(target, rows)
    use = (source_at == 0) | (source_at == rows - 1)
    use = use | ((source_at < 0) & (il > 0)) | ((source_at >= rows) & (il < last))
    lines_e_ref[...] = jnp.where(use, band(source_at, target_at, 0.25), 0.0).astype(bf16)
    target, source = iota((4 * EDGE, 4 * EDGE), 0), iota((4 * EDGE, 4 * EDGE), 1)
    diff_e_ref[...] = difference(edge_position(source, rows), edge_position(target, rows)).astype(bf16)

    source, target = iota((cols, cols), 0), iota((cols, cols), 1)
    diff_x_ref[...] = difference(source, target).astype(bf16)
    moved = source == jnp.where(x == 0, cols - 1, 0)
    smooth_own = jnp.where(moved, 0.0, band(source, target)).astype(bf16)
    lane, target = iota((128, cols), 0), iota((128, cols), 1)
    place = lax.rem(lane, SIDE)
    repeated = place == jnp.where(x == 0, 0, SIDE - 1)
    smooth_halo = jnp.where(repeated, 0.0, band(halo_column(lane, x, cols), target))
    for index in range(SLOTS):
        smooth_ref[index, :cols, :] = smooth_own
        smooth_ref[index, cols:, :] = jnp.where(lax.div(lane, SIDE) == index, smooth_halo, 0.0).astype(bf16)

    source, target = iota((128, 128), 0), iota((128, 128), 1)
    same = lax.rem(source, SIDE) == lax.rem(target, SIDE)
    across = difference(lax.rem(source, SIDE), lax.rem(target, SIDE))
    for group in range(2):
        centre = halo_plane(target, group, depths)
        for tile in range(TILES):
            plane = halo_plane(source, tile, depths)
            part = slice(128 * tile, 128 * (tile + 1))
            halo_ref[group, part, :128] = jnp.where(same, difference(plane, centre), 0.0).astype(bf16)
            halo_ref[group, part, 128:] = jnp.where(plane == centre, across, 0.0).astype(bf16)

    source, lane = iota((cols, 256), 0), iota((cols, 256), 1)
    place = lax.rem(lane, SIDE)
    low, high = place < SIDE - OWN, place >= OWN
    sent = jnp.where(x == 0, jnp.where(low, cols - (SIDE - OWN) + place, FAR), jnp.where(high, place - OWN, FAR))
    low, high = place < OWN, place >= SIDE - OWN
    kept = jnp.where(x == 0, jnp.where(low, cols - OWN + place, FAR), jnp.where(high, place - (SIDE - OWN), FAR))
    pick = jnp.where(source == jnp.where(lane < 128, sent, kept), 1.0, 0.0).astype(bf16)
    slot = lax.div(lax.rem(iota((rows, 256), 1), 128), SIDE)

    load.wait()
    for tile in range(TILES):
        if tile < 2:
            planes = [(1 + SLOTS * tile + index, index) for index in range(SLOTS)]
        else:
            planes = [(0, 0), (depths - 1, 1)]
        packed = jnp.zeros((rows, 256), jnp.float32)
        for plane, index in planes:
            packed = jnp.where(slot == index, dot(vol_ref[plane], pick), packed)
        packed = packed.astype(bf16)
        send_ref[tile] = packed[:, :128]
        own_ref[tile] = packed[:, 128:]


def rows_kernel(vol_ref, own_ref, side_ref, halo_ref, first_ref, second_ref, packed_ref):
    depths, rows, cols = vol_ref.shape
    even = lax.rem(lax.axis_index("il"), 2) == 0

    def put(row, top, bottom):
        top, bottom = top[:REACH], bottom[EDGE - REACH :]
        lanes = top.shape[1]
        packed_ref[0, row : row + REACH, :lanes] = jnp.where(even, bottom, top)
        packed_ref[1, row : row + REACH, :lanes] = jnp.where(even, top, bottom)

    packed_ref[:, depths * REACH :, :] = jnp.zeros_like(packed_ref[:, depths * REACH :, :])
    for depth in range(depths):
        top = vol_ref[depth, :EDGE, :].astype(jnp.float32)
        bottom = vol_ref[depth, rows - EDGE :, :].astype(jnp.float32)
        put(REACH * depth, top, bottom)
    tiles = []
    for tile in range(TILES):
        merged = own_ref[tile].astype(jnp.float32) + side_ref[tile].astype(jnp.float32)
        halo_ref[:, 128 * tile : 128 * (tile + 1)] = merged.astype(jnp.bfloat16)
        tiles.append((merged[:EDGE], merged[rows - EDGE :]))
    tops = jnp.concatenate([tiles[0][0], tiles[1][0]], axis=1)
    bottoms = jnp.concatenate([tiles[0][1], tiles[1][1]], axis=1)
    put(REACH * depths, tops, bottoms)
    put(REACH * (depths + 1), *tiles[2])
    first_ref[...] = packed_ref[0].astype(jnp.bfloat16)
    second_ref[...] = packed_ref[1].astype(jnp.bfloat16)


def moments(grad_i, grad_x, grad_z):
    terms = (
        grad_i * grad_i,
        grad_x * grad_x,
        grad_z * grad_z,
        grad_i * grad_x,
        grad_i * grad_z,
        grad_x * grad_z,
    )
    return [term.astype(jnp.bfloat16) for term in terms]


def own_lines(start, count, vol_ref, lines_ref, diff_i_ref, diff_x_ref, inner_ref, part_ref):
    rows = vol_ref.shape[1]

    def step(k, carry):
        z = start + k
        centre = vol_ref[z + 1]
        grad_i = dot(diff_i_ref[...], centre)
        grad_x = dot(centre, diff_x_ref[...])
        grad_z = vol_ref[z + 2].astype(jnp.float32) - vol_ref[z].astype(jnp.float32)
        for comp, term in enumerate(moments(grad_i, grad_x, grad_z)):
            summed = dot(lines_ref[...], term)
            inner_ref[k, comp] = summed[EDGE : rows - EDGE].astype(jnp.bfloat16)
            part_ref[k, comp, :EDGE] = summed[:EDGE]
            part_ref[k, comp, EDGE:] = summed[rows - EDGE :]
        return carry

    lax.fori_loop(0, count, step, 0, unroll=2)


def lines_kernel(start, count, vol_ref, lines_ref, diff_i_ref, diff_x_ref, inner_ref, part_ref):
    own_lines(start, count, vol_ref, lines_ref, diff_i_ref, diff_x_ref, inner_ref, part_ref)


def lines_halo_kernel(
    start, count, vol_ref, lines_ref, diff_i_ref, diff_x_ref, halo_ref, diff_h_ref, inner_ref, part_ref, part_h_ref
):
    for group in range(2):
        both = dot(halo_ref[...], diff_h_ref[group])
        grad_i = dot(diff_i_ref[...], halo_ref[:, 128 * group : 128 * (group + 1)])
        for comp, term in enumerate(moments(grad_i, both[:, 128:], both[:, :128])):
            part_h_ref[group, comp] = dot(lines_ref[...], term)
    own_lines(start, count, vol_ref, lines_ref, diff_i_ref, diff_x_ref, inner_ref, part_ref)


def final_kernel(
    vol_ref, halo_ref, first_ref, second_ref, inner_a_ref, part_a_ref, inner_b_ref, part_b_ref, part_h_ref,
    smooth_ref, diff_x_ref, diff_h_ref, lines_e_ref, diff_e_ref,
    dip_i_ref, dip_x_ref, plan_ref,
    packed_ref, block_ref, block_h_ref, lined_h_ref, edge_a_ref, edge_b_ref,
    out_i_ref, out_x_ref, out_p_ref, sems,
):
    depths, rows, cols = vol_ref.shape
    count, half = depths - 2, inner_a_ref.shape[0]
    even = lax.rem(lax.axis_index("il"), 2) == 0
    bf16 = jnp.bfloat16

    first, second = first_ref[...].astype(jnp.float32), second_ref[...].astype(jnp.float32)
    packed_ref[0] = jnp.where(even, second, first)
    packed_ref[1] = jnp.where(even, first, second)
    for depth in range(depths):
        block_ref[depth, :EDGE] = vol_ref[depth, :EDGE]
        block_ref[depth, EDGE : 2 * EDGE] = vol_ref[depth, rows - EDGE :]
        for side in range(2):
            at = EDGE * (2 + side)
            block_ref[depth, at : at + EDGE] = packed_ref[side, REACH * depth : REACH * depth + EDGE].astype(bf16)
    block_h_ref[:EDGE] = halo_ref[:EDGE]
    block_h_ref[EDGE : 2 * EDGE] = halo_ref[rows - EDGE :]
    for side in range(2):
        at, row = EDGE * (2 + side), REACH * depths
        block_h_ref[at : at + EDGE, :256] = packed_ref[side, row : row + EDGE].astype(bf16)
        block_h_ref[at : at + EDGE, 256:] = packed_ref[side, row + REACH : row + REACH + EDGE, :128].astype(bf16)

    for group in range(2):
        both = dot(block_h_ref[...], diff_h_ref[group])
        grad_i = dot(diff_e_ref[...], block_h_ref[:, 128 * group : 128 * (group + 1)])
        for comp, term in enumerate(moments(grad_i, both[:, 128:], both[:, :128])):
            outer = dot(lines_e_ref[...], term)
            lined_h_ref[group, comp, :EDGE] = (part_h_ref[group, comp, :EDGE] + outer[:EDGE]).astype(bf16)
            lined_h_ref[group, comp, EDGE : rows - EDGE] = part_h_ref[group, comp, EDGE : rows - EDGE].astype(bf16)
            lined_h_ref[group, comp, rows - EDGE :] = (part_h_ref[group, comp, rows - EDGE :] + outer[EDGE:]).astype(bf16)

    def copies(z):
        pairs = ((out_i_ref, dip_i_ref), (out_x_ref, dip_x_ref), (out_p_ref, plan_ref))
        return [pltpu.make_async_copy(src.at[z], dst.at[z], sems.at[z, n]) for n, (src, dst) in enumerate(pairs)]

    def run(group, inner_ref, part_ref):
        def stage_edge(k, edge_ref):
            z = half * group + k
            centre = block_ref[z + 1]
            grad_i = dot(diff_e_ref[...], centre)
            grad_x = dot(centre, diff_x_ref[...])
            grad_z = block_ref[z + 2].astype(jnp.float32) - block_ref[z].astype(jnp.float32)
            for comp, term in enumerate(moments(grad_i, grad_x, grad_z)):
                edge_ref[comp] = (part_ref[k, comp] + dot(lines_e_ref[...], term)).astype(bf16)

        def stage_attributes(k, edge_ref):
            z = half * group + k
            weights = smooth_ref[k]

            def smoothed(comp):
                own = jnp.concatenate([edge_ref[comp, :EDGE], inner_ref[k, comp], edge_ref[comp, EDGE:]], axis=0)
                return dot(jnp.concatenate([own, lined_h_ref[group, comp]], axis=1), weights)

            a, b, c, d, e, f = [smoothed(comp) for comp in range(6)]
            low = c + 1e-6
            inverse = -1.0 / low
            out_i_ref[z] = e * inverse
            out_x_ref[z] = f * inverse
            spread = (a - b) * (a - c) + (b - c) * (b - c) + 3.0 * (d * d + e * e + f * f)
            out_p_ref[z] = jnp.sqrt(spread) / (a + b + low)
            for copy in copies(z):
                copy.start()

        stage_edge(0, edge_a_ref)

        def pair(pair_index, carry):
            k = 2 * pair_index
            stage_edge(k + 1, edge_b_ref)
            stage_attributes(k, edge_a_ref)
            stage_edge(jnp.minimum(k + 2, half - 1), edge_a_ref)
            stage_attributes(k + 1, edge_b_ref)
            return carry

        lax.fori_loop(0, half // 2, pair, 0)

    run(0, inner_a_ref, part_a_ref)
    run(1, inner_b_ref, part_b_ref)
    for z in range(count):
        for copy in copies(z):
            copy.wait()


def call(name, kernel, outs, scratch, operands, in_specs=None, out_specs=None, flops=0, limit=16):
    return pl.pallas_call(
        kernel,
        out_shape=tuple(jax.ShapeDtypeStruct(*out) for out in outs),
        in_specs=in_specs or [WHOLE] * len(operands),
        out_specs=out_specs or (WHOLE,) * len(outs),
        scratch_shapes=scratch,
        compiler_params=pltpu.CompilerParams(vmem_limit_bytes=limit << 20),
        name=name,
        cost_estimate=pl.CostEstimate(flops=flops, bytes_accessed=0, transcendentals=0),
    )(*operands)


def body(volume):
    depths, rows, cols = volume.shape
    il, xl = lax.axis_size("il"), lax.axis_size("xl")
    count = depths - 2
    assert xl == 2 and il % 2 == 0 and count == 2 * SLOTS and cols == 256
    bf16, f32 = jnp.bfloat16, jnp.float32
    packed_rows = -(-REACH * (depths + 2) // 16) * 16

    vol, send, own, lines, diff_i, diff_x, smooth, diff_h, lines_e, diff_e = call(
        "pack_kernel",
        pack_kernel,
        [
            (volume.shape, bf16),
            ((TILES, rows, 128), bf16),
            ((TILES, rows, 128), bf16),
            ((rows, rows), bf16),
            ((rows, rows), bf16),
            ((cols, cols), bf16),
            ((SLOTS, cols + 128, cols), bf16),
            ((2, 128 * TILES, 256), bf16),
            ((2 * EDGE, 4 * EDGE), bf16),
            ((4 * EDGE, 4 * EDGE), bf16),
        ],
        [pltpu.SemaphoreType.DMA],
        [volume],
        in_specs=[IN_HBM],
    )
    side = lax.ppermute(send, "xl", [(0, 1), (1, 0)])

    def own_outs(half):
        return [((half, 6, rows - 2 * EDGE, cols), bf16), ((half, 6, 2 * EDGE, cols), f32)]

    half = count // 2
    work = half * 1024 * 2 * 256 * 256
    inner_a, part_a = call(
        "lines_kernel",
        lambda *refs: lines_kernel(0, half, *refs),
        own_outs(half),
        [],
        [vol, lines, diff_i, diff_x],
        flops=work,
    )
    halo, first, second = call(
        "rows_kernel",
        rows_kernel,
        [((rows, 128 * TILES), bf16), ((packed_rows, cols), bf16), ((packed_rows, cols), bf16)],
        [pltpu.VMEM((2, packed_rows, cols), f32)],
        [vol, own, side],
    )
    one = [(i, i ^ 1) for i in range(il)]
    two = [pair for i in range(1, il - 1, 2) for pair in ((i, i + 1), (i + 1, i))]
    first_in = lax.ppermute(first, "il", one)
    second_in = lax.ppermute(second, "il", two)
    inner_b, part_b, part_h = call(
        "lines_halo_kernel",
        lambda *refs: lines_halo_kernel(half, half, *refs),
        own_outs(half) + [((2, 6, rows, 128), f32)],
        [],
        [vol, lines, diff_i, diff_x, halo, diff_h],
        flops=work,
    )
    return call(
        "final_kernel",
        final_kernel,
        [((count, rows, cols), f32)] * 3,
        [
            pltpu.VMEM((2, packed_rows, cols), f32),
            pltpu.VMEM((depths, 4 * EDGE, cols), bf16),
            pltpu.VMEM((4 * EDGE, 128 * TILES), bf16),
            pltpu.VMEM((2, 6, rows, 128), bf16),
            pltpu.VMEM((6, 2 * EDGE, cols), bf16),
            pltpu.VMEM((6, 2 * EDGE, cols), bf16),
            pltpu.VMEM((count, rows, cols), f32),
            pltpu.VMEM((count, rows, cols), f32),
            pltpu.VMEM((count, rows, cols), f32),
            pltpu.SemaphoreType.DMA((count, 3)),
        ],
        [vol, halo, first_in, second_in, inner_a, part_a, inner_b, part_b, part_h, smooth, diff_x, diff_h, lines_e, diff_e],
        out_specs=(IN_HBM,) * 3,
        flops=count * 2048 * 2 * 256 * 256,
        limit=24,
    )


def solution(mesh):
    spec = P(None, ("parts", "il"), "xl")
    return jax.shard_map(body, mesh=mesh, in_specs=(spec,), out_specs=(spec,) * 3, check_vma=False)
```

```python
import jax
import jax.numpy as jnp
import ml_dtypes
import numpy as np
from jax import lax
from jax.experimental import pallas as pl
from jax.experimental.pallas import tpu as pltpu
from jax.sharding import PartitionSpec as P

RADIUS = 9
REACH = RADIUS + 1
SIDE = 16
SLOTS = 8
TILES = 3
EDGE = 16
OWN = 2
TINY = float(np.finfo(np.float32).tiny)
FAR = -1000
WHOLE = pl.BlockSpec(memory_space=pltpu.VMEM)
IN_HBM = pl.BlockSpec(memory_space=pltpu.HBM)


def filter_taps():
    offsets = np.arange(2 * RADIUS + 1).astype(np.float32)
    sigma = np.float32(RADIUS / 3.0)
    shape = np.exp(np.float32(-0.5) * ((offsets - RADIUS) / sigma) ** 2)
    return (shape / np.sum(shape, dtype=np.float32)).astype(ml_dtypes.bfloat16).astype(np.float32)


def iota(shape, dim):
    return lax.broadcasted_iota(jnp.int32, shape, dim)


def band(source, target, scale=1.0):
    offset = jnp.abs(source - target)
    weights = jnp.zeros(offset.shape, jnp.float32)
    for distance, tap in enumerate(filter_taps()[RADIUS:]):
        weights = jnp.where(offset == distance, jnp.float32(scale * tap), weights)
    return weights


def difference(source, target):
    offset = source - target
    return jnp.where(offset == 1, 1.0, jnp.where(offset == -1, -1.0, 0.0)).astype(jnp.float32)


def dot(left, right):
    return jnp.dot(left, right, preferred_element_type=jnp.float32)


def reciprocal(value):
    guess = pl.reciprocal(value, approx=True)
    return guess * (2.0 - value * guess)


def halo_plane(lane, tile, depths):
    slot = lax.div(lane, SIDE)
    rest = jnp.where(slot == 0, 0, jnp.where(slot == 1, depths - 1, FAR))
    return jnp.where(tile < 2, 1 + SLOTS * tile + slot, rest)


def halo_column(lane, x, cols):
    place = lax.rem(lane, SIDE)
    return jnp.where(x == 0, cols - OWN + place, place - (SIDE - OWN))


def edge_position(index, rows):
    first = index < EDGE
    previous = index - 2 * EDGE - REACH
    following = rows + index - 3 * EDGE
    outer = jnp.where(index < 2 * EDGE + REACH, previous, jnp.where(index < 3 * EDGE, FAR + 2 * index, following))
    outer = jnp.where(index >= 3 * EDGE + REACH, FAR + 2 * index, outer)
    return jnp.where(first, index, jnp.where(index < 2 * EDGE, rows - 2 * EDGE + index, outer))


def tables_kernel(depths, lines_ref, diff_i_ref, diff_x_ref, smooth_ref, halo_ref, lines_e_ref, diff_e_ref, pick_ref):
    rows, cols = lines_ref.shape[0], diff_x_ref.shape[0]
    x, il, last = lax.axis_index("xl"), lax.axis_index("il"), lax.axis_size("il") - 1
    bf16 = jnp.bfloat16

    target, source = iota((rows, rows), 0), iota((rows, rows), 1)
    inner = (source > 0) & (source < rows - 1)
    lines_ref[...] = jnp.where(inner, band(source, target, 0.25), 0.0).astype(bf16)
    diff_i_ref[...] = difference(source, target).astype(bf16)
    target, source = iota((2 * EDGE, 4 * EDGE), 0), iota((2 * EDGE, 4 * EDGE), 1)
    source_at, target_at = edge_position(source, rows), edge_position(target, rows)
    use = (source_at == 0) | (source_at == rows - 1)
    use = use | ((source_at < 0) & (il > 0)) | ((source_at >= rows) & (il < last))
    lines_e_ref[...] = jnp.where(use, band(source_at, target_at, 0.25), 0.0).astype(bf16)
    target, source = iota((4 * EDGE, 4 * EDGE), 0), iota((4 * EDGE, 4 * EDGE), 1)
    diff_e_ref[...] = difference(edge_position(source, rows), edge_position(target, rows)).astype(bf16)

    source, target = iota((cols, cols), 0), iota((cols, cols), 1)
    diff_x_ref[...] = difference(source, target).astype(bf16)
    moved = source == jnp.where(x == 0, cols - 1, 0)
    smooth_own = jnp.where(moved, 0.0, band(source, target)).astype(bf16)
    lane, target = iota((128, cols), 0), iota((128, cols), 1)
    place = lax.rem(lane, SIDE)
    repeated = place == jnp.where(x == 0, 0, SIDE - 1)
    smooth_halo = jnp.where(repeated, 0.0, band(halo_column(lane, x, cols), target))
    for index in range(SLOTS):
        smooth_ref[index, :cols, :] = smooth_own
        smooth_ref[index, cols:, :] = jnp.where(lax.div(lane, SIDE) == index, smooth_halo, 0.0).astype(bf16)

    source, target = iota((128, 128), 0), iota((128, 128), 1)
    same = lax.rem(source, SIDE) == lax.rem(target, SIDE)
    across = difference(lax.rem(source, SIDE), lax.rem(target, SIDE))
    for group in range(2):
        centre = halo_plane(target, group, depths)
        for tile in range(TILES):
            plane = halo_plane(source, tile, depths)
            part = slice(128 * tile, 128 * (tile + 1))
            halo_ref[group, part, :128] = jnp.where(same, difference(plane, centre), 0.0).astype(bf16)
            halo_ref[group, part, 128:] = jnp.where(plane == centre, across, 0.0).astype(bf16)

    source, lane = iota((cols, 256), 0), iota((cols, 256), 1)
    place = lax.rem(lane, SIDE)
    low, high = place < SIDE - OWN, place >= OWN
    sent = jnp.where(x == 0, jnp.where(low, cols - (SIDE - OWN) + place, FAR), jnp.where(high, place - OWN, FAR))
    low, high = place < OWN, place >= SIDE - OWN
    kept = jnp.where(x == 0, jnp.where(low, cols - OWN + place, FAR), jnp.where(high, place - (SIDE - OWN), FAR))
    pick_ref[...] = jnp.where(source == jnp.where(lane < 128, sent, kept), 1.0, 0.0).astype(bf16)


def pack_kernel(vol_ref, pick_ref, copy_ref, send_ref, own_ref):
    depths, rows, cols = vol_ref.shape
    slot = lax.div(lax.rem(iota((rows, 256), 1), 128), SIDE)
    copy_ref[...] = vol_ref[...]
    for tile in range(TILES):
        if tile < 2:
            planes = [(1 + SLOTS * tile + index, index) for index in range(SLOTS)]
        else:
            planes = [(0, 0), (depths - 1, 1)]
        packed = jnp.zeros((rows, 256), jnp.float32)
        for plane, index in planes:
            packed = jnp.where(slot == index, dot(vol_ref[plane], pick_ref[...]), packed)
        packed = packed.astype(jnp.bfloat16)
        send_ref[tile] = packed[:, :128]
        own_ref[tile] = packed[:, 128:]


def rows_kernel(vol_ref, own_ref, side_ref, after_ref, halo_ref, first_ref, second_ref, packed_ref):
    depths, rows, cols = vol_ref.shape
    even = lax.rem(lax.axis_index("il"), 2) == 0

    def put(row, top, bottom):
        top, bottom = top[:REACH], bottom[EDGE - REACH :]
        lanes = top.shape[1]
        packed_ref[0, row : row + REACH, :lanes] = jnp.where(even, bottom, top)
        packed_ref[1, row : row + REACH, :lanes] = jnp.where(even, top, bottom)

    packed_ref[:, depths * REACH :, :] = jnp.zeros_like(packed_ref[:, depths * REACH :, :])
    for depth in range(depths):
        top = vol_ref[depth, :EDGE, :].astype(jnp.float32)
        bottom = vol_ref[depth, rows - EDGE :, :].astype(jnp.float32)
        put(REACH * depth, top, bottom)
    tiles = []
    for tile in range(TILES):
        merged = own_ref[tile].astype(jnp.float32) + side_ref[tile].astype(jnp.float32)
        halo_ref[:, 128 * tile : 128 * (tile + 1)] = merged.astype(jnp.bfloat16)
        tiles.append((merged[:EDGE], merged[rows - EDGE :]))
    tops = jnp.concatenate([tiles[0][0], tiles[1][0]], axis=1)
    bottoms = jnp.concatenate([tiles[0][1], tiles[1][1]], axis=1)
    put(REACH * depths, tops, bottoms)
    put(REACH * (depths + 1), *tiles[2])
    first_ref[...] = packed_ref[0].astype(jnp.bfloat16)
    second_ref[...] = packed_ref[1].astype(jnp.bfloat16)


def moments(grad_i, grad_x, grad_z):
    terms = (
        grad_i * grad_i,
        grad_x * grad_x,
        grad_z * grad_z,
        grad_i * grad_x,
        grad_i * grad_z,
        grad_x * grad_z,
    )
    return [term.astype(jnp.bfloat16) for term in terms]


def own_lines(start, count, vol_ref, lines_ref, diff_i_ref, diff_x_ref, inner_ref, part_ref, even_ref, odd_ref):
    rows = vol_ref.shape[1]

    def stage_moments(k, moments_ref):
        z = start + k
        centre = vol_ref[z + 1]
        grad_i = dot(diff_i_ref[...], centre)
        grad_x = dot(centre, diff_x_ref[...])
        grad_z = vol_ref[z + 2].astype(jnp.float32) - vol_ref[z].astype(jnp.float32)
        for comp, term in enumerate(moments(grad_i, grad_x, grad_z)):
            moments_ref[comp] = term

    def stage_lines(k, moments_ref):
        for comp in range(6):
            summed = dot(lines_ref[...], moments_ref[comp])
            inner_ref[k, comp] = summed[EDGE : rows - EDGE].astype(jnp.bfloat16)
            part_ref[k, comp, :EDGE] = summed[:EDGE]
            part_ref[k, comp, EDGE:] = summed[rows - EDGE :]

    stage_moments(0, even_ref)

    def pair(index, carry):
        k = 2 * index
        stage_moments(k + 1, odd_ref)
        stage_lines(k, even_ref)
        stage_moments(jnp.minimum(k + 2, count - 1), even_ref)
        stage_lines(k + 1, odd_ref)
        return carry

    lax.fori_loop(0, count // 2, pair, 0)


def lines_kernel(start, count, *refs):
    own_lines(start, count, *refs)


def lines_halo_kernel(
    start, count, vol_ref, lines_ref, diff_i_ref, diff_x_ref, halo_ref, diff_h_ref, inner_ref, part_ref, part_h_ref,
    even_ref, odd_ref,
):
    for group in range(2):
        both = dot(halo_ref[...], diff_h_ref[group])
        grad_i = dot(diff_i_ref[...], halo_ref[:, 128 * group : 128 * (group + 1)])
        for comp, term in enumerate(moments(grad_i, both[:, 128:], both[:, :128])):
            part_h_ref[group, comp] = dot(lines_ref[...], term)
    own_lines(start, count, vol_ref, lines_ref, diff_i_ref, diff_x_ref, inner_ref, part_ref, even_ref, odd_ref)


def final_kernel(
    vol_ref, halo_ref, first_ref, second_ref, inner_a_ref, part_a_ref, inner_b_ref, part_b_ref, part_h_ref,
    smooth_ref, diff_x_ref, diff_h_ref, lines_e_ref, diff_e_ref,
    dip_i_ref, dip_x_ref, plan_ref,
    packed_ref, block_ref, block_h_ref, lined_h_ref, edge_a_ref, edge_b_ref,
    out_i_ref, out_x_ref, out_p_ref, sems,
):
    depths, rows, cols = vol_ref.shape
    count, half = depths - 2, inner_a_ref.shape[0]
    even = lax.rem(lax.axis_index("il"), 2) == 0
    bf16 = jnp.bfloat16

    first, second = first_ref[...].astype(jnp.float32), second_ref[...].astype(jnp.float32)
    packed_ref[0] = jnp.where(even, second, first)
    packed_ref[1] = jnp.where(even, first, second)
    for depth in range(depths):
        block_ref[depth, :EDGE] = vol_ref[depth, :EDGE]
        block_ref[depth, EDGE : 2 * EDGE] = vol_ref[depth, rows - EDGE :]
        for side in range(2):
            at = EDGE * (2 + side)
            block_ref[depth, at : at + EDGE] = packed_ref[side, REACH * depth : REACH * depth + EDGE].astype(bf16)
    block_h_ref[:EDGE] = halo_ref[:EDGE]
    block_h_ref[EDGE : 2 * EDGE] = halo_ref[rows - EDGE :]
    for side in range(2):
        at, row = EDGE * (2 + side), REACH * depths
        block_h_ref[at : at + EDGE, :256] = packed_ref[side, row : row + EDGE].astype(bf16)
        block_h_ref[at : at + EDGE, 256:] = packed_ref[side, row + REACH : row + REACH + EDGE, :128].astype(bf16)

    for group in range(2):
        both = dot(block_h_ref[...], diff_h_ref[group])
        grad_i = dot(diff_e_ref[...], block_h_ref[:, 128 * group : 128 * (group + 1)])
        for comp, term in enumerate(moments(grad_i, both[:, 128:], both[:, :128])):
            outer = dot(lines_e_ref[...], term)
            lined_h_ref[group, comp, :EDGE] = (part_h_ref[group, comp, :EDGE] + outer[:EDGE]).astype(bf16)
            lined_h_ref[group, comp, EDGE : rows - EDGE] = part_h_ref[group, comp, EDGE : rows - EDGE].astype(bf16)
            lined_h_ref[group, comp, rows - EDGE :] = (part_h_ref[group, comp, rows - EDGE :] + outer[EDGE:]).astype(bf16)

    def copies(z):
        pairs = ((out_i_ref, dip_i_ref), (out_x_ref, dip_x_ref), (out_p_ref, plan_ref))
        return [pltpu.make_async_copy(src.at[z], dst.at[z], sems.at[z, n]) for n, (src, dst) in enumerate(pairs)]

    def run(group, inner_ref, part_ref):
        def stage_edge(k, edge_ref):
            z = half * group + k
            centre = block_ref[z + 1]
            grad_i = dot(diff_e_ref[...], centre)
            grad_x = dot(centre, diff_x_ref[...])
            grad_z = block_ref[z + 2].astype(jnp.float32) - block_ref[z].astype(jnp.float32)
            for comp, term in enumerate(moments(grad_i, grad_x, grad_z)):
                edge_ref[comp] = (part_ref[k, comp] + dot(lines_e_ref[...], term)).astype(bf16)

        def stage_attributes(k, edge_ref):
            z = half * group + k
            weights = smooth_ref[k]

            def smoothed(comp):
                own = jnp.concatenate([edge_ref[comp, :EDGE], inner_ref[k, comp], edge_ref[comp, EDGE:]], axis=0)
                return dot(jnp.concatenate([own, lined_h_ref[group, comp]], axis=1), weights)

            a, b, c, d, e, f = [smoothed(comp) for comp in range(6)]
            low = c + 1e-6
            inverse = reciprocal(low)
            out_i_ref[z] = -e * inverse
            out_x_ref[z] = -f * inverse
            spread = (a - b) * (a - c) + (b - c) * (b - c) + 3.0 * (d * d + e * e + f * f)
            root = spread * lax.rsqrt(jnp.maximum(spread, TINY))
            out_p_ref[z] = root * reciprocal(a + b + low)
            for copy in copies(z):
                copy.start()

        stage_edge(0, edge_a_ref)

        def pair(pair_index, carry):
            k = 2 * pair_index
            stage_edge(k + 1, edge_b_ref)
            stage_attributes(k, edge_a_ref)
            stage_edge(jnp.minimum(k + 2, half - 1), edge_a_ref)
            stage_attributes(k + 1, edge_b_ref)
            return carry

        lax.fori_loop(0, half // 2, pair, 0)

    run(0, inner_a_ref, part_a_ref)
    run(1, inner_b_ref, part_b_ref)
    for z in range(count):
        for copy in copies(z):
            copy.wait()


def call(name, kernel, outs, scratch, operands, in_specs=None, out_specs=None, flops=0, limit=16):
    return pl.pallas_call(
        kernel,
        out_shape=tuple(jax.ShapeDtypeStruct(*out) for out in outs),
        in_specs=in_specs or [WHOLE] * len(operands),
        out_specs=out_specs or (WHOLE,) * len(outs),
        scratch_shapes=scratch,
        compiler_params=pltpu.CompilerParams(vmem_limit_bytes=limit << 20),
        name=name,
        cost_estimate=pl.CostEstimate(flops=flops, bytes_accessed=0, transcendentals=0),
    )(*operands)


def body(volume):
    depths, rows, cols = volume.shape
    il, xl = lax.axis_size("il"), lax.axis_size("xl")
    count = depths - 2
    assert xl == 2 and il % 2 == 0 and count == 2 * SLOTS and cols == 256
    bf16, f32 = jnp.bfloat16, jnp.float32
    half = count // 2
    work = half * 1024 * 2 * 256 * 256
    packed_rows = -(-REACH * (depths + 2) // 16) * 16

    lines, diff_i, diff_x, smooth, diff_h, lines_e, diff_e, pick = call(
        "tables_kernel",
        lambda *refs: tables_kernel(depths, *refs),
        [
            ((rows, rows), bf16),
            ((rows, rows), bf16),
            ((cols, cols), bf16),
            ((SLOTS, cols + 128, cols), bf16),
            ((2, 128 * TILES, 256), bf16),
            ((2 * EDGE, 4 * EDGE), bf16),
            ((4 * EDGE, 4 * EDGE), bf16),
            ((cols, 256), bf16),
        ],
        [],
        [],
        flops=work,
    )
    halo_tile = ((TILES, rows, 128), bf16)
    vol, send, own = call("pack_kernel", pack_kernel, [(volume.shape, bf16), halo_tile, halo_tile], [], [volume, pick])
    side = lax.ppermute(send, "xl", [(0, 1), (1, 0)])

    def own_outs(half):
        return [((half, 6, rows - 2 * EDGE, cols), bf16), ((half, 6, 2 * EDGE, cols), f32)]

    inner_a, part_a = call(
        "lines_kernel",
        lambda *refs: lines_kernel(0, half, *refs),
        own_outs(half),
        [pltpu.VMEM((6, rows, cols), bf16)] * 2,
        [vol, lines, diff_i, diff_x],
        flops=work,
    )
    halo, first, second = call(
        "rows_kernel",
        rows_kernel,
        [((rows, 128 * TILES), bf16), ((packed_rows, cols), bf16), ((packed_rows, cols), bf16)],
        [pltpu.VMEM((2, packed_rows, cols), f32)],
        [vol, own, side, part_a],
        in_specs=[WHOLE] * 3 + [pl.BlockSpec(memory_space=pl.ANY)],
    )
    one = [(i, i ^ 1) for i in range(il)]
    two = [pair for i in range(1, il - 1, 2) for pair in ((i, i + 1), (i + 1, i))]
    first_in = lax.ppermute(first, "il", one)
    second_in = lax.ppermute(second, "il", two)
    inner_b, part_b, part_h = call(
        "lines_halo_kernel",
        lambda *refs: lines_halo_kernel(half, half, *refs),
        own_outs(half) + [((2, 6, rows, 128), f32)],
        [pltpu.VMEM((6, rows, cols), bf16)] * 2,
        [vol, lines, diff_i, diff_x, halo, diff_h],
        flops=work,
    )
    return call(
        "final_kernel",
        final_kernel,
        [((count, rows, cols), f32)] * 3,
        [
            pltpu.VMEM((2, packed_rows, cols), f32),
            pltpu.VMEM((depths, 4 * EDGE, cols), bf16),
            pltpu.VMEM((4 * EDGE, 128 * TILES), bf16),
            pltpu.VMEM((2, 6, rows, 128), bf16),
            pltpu.VMEM((6, 2 * EDGE, cols), bf16),
            pltpu.VMEM((6, 2 * EDGE, cols), bf16),
            pltpu.VMEM((count, rows, cols), f32),
            pltpu.VMEM((count, rows, cols), f32),
            pltpu.VMEM((count, rows, cols), f32),
            pltpu.SemaphoreType.DMA((count, 3)),
        ],
        [vol, halo, first_in, second_in, inner_a, part_a, inner_b, part_b, part_h, smooth, diff_x, diff_h, lines_e, diff_e],
        out_specs=(IN_HBM,) * 3,
        flops=count * 2048 * 2 * 256 * 256,
        limit=24,
    )


def solution(mesh):
    spec = P(None, ("parts", "il"), "xl")
    return jax.shard_map(body, mesh=mesh, in_specs=(spec,), out_specs=(spec,) * 3, check_vma=False)
```

```python
import jax
import jax.numpy as jnp
import ml_dtypes
import numpy as np
from jax import lax
from jax.experimental import pallas as pl
from jax.experimental.pallas import tpu as pltpu
from jax.sharding import PartitionSpec as P

RADIUS = 9
REACH = RADIUS + 1
SIDE = 16
SLOTS = 8
TILES = 3
EDGE = 16
OWN = 2
TINY = float(np.finfo(np.float32).tiny)
FAR = -1000
WHOLE = pl.BlockSpec(memory_space=pltpu.VMEM)
IN_HBM = pl.BlockSpec(memory_space=pltpu.HBM)


def filter_taps():
    offsets = np.arange(2 * RADIUS + 1).astype(np.float32)
    sigma = np.float32(RADIUS / 3.0)
    shape = np.exp(np.float32(-0.5) * ((offsets - RADIUS) / sigma) ** 2)
    return (shape / np.sum(shape, dtype=np.float32)).astype(ml_dtypes.bfloat16).astype(np.float32)


def iota(shape, dim):
    return lax.broadcasted_iota(jnp.int32, shape, dim)


def band(source, target, scale=1.0):
    offset = jnp.abs(source - target)
    weights = jnp.zeros(offset.shape, jnp.float32)
    for distance, tap in enumerate(filter_taps()[RADIUS:]):
        weights = jnp.where(offset == distance, jnp.float32(scale * tap), weights)
    return weights


def difference(source, target):
    offset = source - target
    return jnp.where(offset == 1, 1.0, jnp.where(offset == -1, -1.0, 0.0)).astype(jnp.float32)


def dot(left, right):
    return jnp.dot(left, right, preferred_element_type=jnp.float32)


def reciprocal(value):
    guess = pl.reciprocal(value, approx=True)
    return guess * (2.0 - value * guess)


def halo_plane(lane, tile, depths):
    slot = lax.div(lane, SIDE)
    rest = jnp.where(slot == 0, 0, jnp.where(slot == 1, depths - 1, FAR))
    return jnp.where(tile < 2, 1 + SLOTS * tile + slot, rest)


def halo_column(lane, x, cols):
    place = lax.rem(lane, SIDE)
    return jnp.where(x == 0, cols - OWN + place, place - (SIDE - OWN))


def edge_position(index, rows):
    first = index < EDGE
    previous = index - 2 * EDGE - REACH
    following = rows + index - 3 * EDGE
    outer = jnp.where(index < 2 * EDGE + REACH, previous, jnp.where(index < 3 * EDGE, FAR + 2 * index, following))
    outer = jnp.where(index >= 3 * EDGE + REACH, FAR + 2 * index, outer)
    return jnp.where(first, index, jnp.where(index < 2 * EDGE, rows - 2 * EDGE + index, outer))


def tables_kernel(depths, lines_ref, diff_i_ref, diff_x_ref, smooth_ref, halo_ref, lines_e_ref, diff_e_ref, pick_ref):
    rows, cols = lines_ref.shape[0], diff_x_ref.shape[0]
    x, il, last = lax.axis_index("xl"), lax.axis_index("il"), lax.axis_size("il") - 1
    bf16 = jnp.bfloat16

    target, source = iota((rows, rows), 0), iota((rows, rows), 1)
    inner = (source > 0) & (source < rows - 1)
    lines_ref[...] = jnp.where(inner, band(source, target, 0.25), 0.0).astype(bf16)
    diff_i_ref[...] = difference(source, target).astype(bf16)
    target, source = iota((2 * EDGE, 4 * EDGE), 0), iota((2 * EDGE, 4 * EDGE), 1)
    source_at, target_at = edge_position(source, rows), edge_position(target, rows)
    use = (source_at == 0) | (source_at == rows - 1)
    use = use | ((source_at < 0) & (il > 0)) | ((source_at >= rows) & (il < last))
    lines_e_ref[...] = jnp.where(use, band(source_at, target_at, 0.25), 0.0).astype(bf16)
    target, source = iota((4 * EDGE, 4 * EDGE), 0), iota((4 * EDGE, 4 * EDGE), 1)
    diff_e_ref[...] = difference(edge_position(source, rows), edge_position(target, rows)).astype(bf16)

    source, target = iota((cols, cols), 0), iota((cols, cols), 1)
    diff_x_ref[...] = difference(source, target).astype(bf16)
    moved = source == jnp.where(x == 0, cols - 1, 0)
    smooth_own = jnp.where(moved, 0.0, band(source, target)).astype(bf16)
    lane, target = iota((128, cols), 0), iota((128, cols), 1)
    place = lax.rem(lane, SIDE)
    repeated = place == jnp.where(x == 0, 0, SIDE - 1)
    smooth_halo = jnp.where(repeated, 0.0, band(halo_column(lane, x, cols), target))
    for index in range(SLOTS):
        smooth_ref[index, :cols, :] = smooth_own
        smooth_ref[index, cols:, :] = jnp.where(lax.div(lane, SIDE) == index, smooth_halo, 0.0).astype(bf16)

    source, target = iota((128, 128), 0), iota((128, 128), 1)
    same = lax.rem(source, SIDE) == lax.rem(target, SIDE)
    across = difference(lax.rem(source, SIDE), lax.rem(target, SIDE))
    for group in range(2):
        centre = halo_plane(target, group, depths)
        for tile in range(TILES):
            plane = halo_plane(source, tile, depths)
            part = slice(128 * tile, 128 * (tile + 1))
            halo_ref[group, part, :128] = jnp.where(same, difference(plane, centre), 0.0).astype(bf16)
            halo_ref[group, part, 128:] = jnp.where(plane == centre, across, 0.0).astype(bf16)

    source, lane = iota((cols, 256), 0), iota((cols, 256), 1)
    place = lax.rem(lane, SIDE)
    low, high = place < SIDE - OWN, place >= OWN
    sent = jnp.where(x == 0, jnp.where(low, cols - (SIDE - OWN) + place, FAR), jnp.where(high, place - OWN, FAR))
    low, high = place < OWN, place >= SIDE - OWN
    kept = jnp.where(x == 0, jnp.where(low, cols - OWN + place, FAR), jnp.where(high, place - (SIDE - OWN), FAR))
    pick_ref[...] = jnp.where(source == jnp.where(lane < 128, sent, kept), 1.0, 0.0).astype(bf16)


def pack_kernel(vol_ref, pick_ref, copy_ref, send_ref, own_ref):
    depths, rows, cols = vol_ref.shape
    slot = lax.div(lax.rem(iota((rows, 256), 1), 128), SIDE)
    copy_ref[...] = vol_ref[...]
    for tile in range(TILES):
        if tile < 2:
            planes = [(1 + SLOTS * tile + index, index) for index in range(SLOTS)]
        else:
            planes = [(0, 0), (depths - 1, 1)]
        packed = jnp.zeros((rows, 256), jnp.float32)
        for plane, index in planes:
            packed = jnp.where(slot == index, dot(vol_ref[plane], pick_ref[...]), packed)
        packed = packed.astype(jnp.bfloat16)
        send_ref[tile] = packed[:, :128]
        own_ref[tile] = packed[:, 128:]


def rows_kernel(vol_ref, own_ref, side_ref, after_ref, halo_ref, first_ref, second_ref, packed_ref):
    depths, rows, cols = vol_ref.shape
    even = lax.rem(lax.axis_index("il"), 2) == 0

    def put(row, top, bottom):
        top, bottom = top[:REACH], bottom[EDGE - REACH :]
        lanes = top.shape[1]
        packed_ref[0, row : row + REACH, :lanes] = jnp.where(even, bottom, top)
        packed_ref[1, row : row + REACH, :lanes] = jnp.where(even, top, bottom)

    packed_ref[:, depths * REACH :, :] = jnp.zeros_like(packed_ref[:, depths * REACH :, :])
    for depth in range(depths):
        top = vol_ref[depth, :EDGE, :].astype(jnp.float32)
        bottom = vol_ref[depth, rows - EDGE :, :].astype(jnp.float32)
        put(REACH * depth, top, bottom)
    tiles = []
    for tile in range(TILES):
        merged = own_ref[tile].astype(jnp.float32) + side_ref[tile].astype(jnp.float32)
        halo_ref[:, 128 * tile : 128 * (tile + 1)] = merged.astype(jnp.bfloat16)
        tiles.append((merged[:EDGE], merged[rows - EDGE :]))
    tops = jnp.concatenate([tiles[0][0], tiles[1][0]], axis=1)
    bottoms = jnp.concatenate([tiles[0][1], tiles[1][1]], axis=1)
    put(REACH * depths, tops, bottoms)
    put(REACH * (depths + 1), *tiles[2])
    first_ref[...] = packed_ref[0].astype(jnp.bfloat16)
    second_ref[...] = packed_ref[1].astype(jnp.bfloat16)


def moments(grad_i, grad_x, grad_z):
    terms = (
        grad_i * grad_i,
        grad_x * grad_x,
        grad_z * grad_z,
        grad_i * grad_x,
        grad_i * grad_z,
        grad_x * grad_z,
    )
    return [term.astype(jnp.bfloat16) for term in terms]


def store_chunks(summed, comp, inner_ref, part_ref):
    chunks = summed.shape[0] // EDGE
    for chunk in range(1, chunks - 1):
        inner_ref[chunk - 1, comp] = summed[EDGE * chunk : EDGE * (chunk + 1)].astype(jnp.bfloat16)
    part_ref[0, comp] = summed[:EDGE]
    part_ref[1, comp] = summed[EDGE * (chunks - 1) :]


def own_lines(start, count, vol_ref, lines_ref, diff_i_ref, diff_x_ref, inner_ref, part_ref, even_ref, odd_ref):
    rows = vol_ref.shape[1]

    def stage_moments(k, moments_ref):
        z = start + k
        centre = vol_ref[z + 1]
        grad_i = dot(diff_i_ref[...], centre)
        grad_x = dot(centre, diff_x_ref[...])
        grad_z = vol_ref[z + 2].astype(jnp.float32) - vol_ref[z].astype(jnp.float32)
        for comp, term in enumerate(moments(grad_i, grad_x, grad_z)):
            moments_ref[comp] = term

    def stage_lines(k, moments_ref):
        for comp in range(6):
            summed = dot(lines_ref[...], moments_ref[comp])
            store_chunks(summed, comp, inner_ref.at[k], part_ref.at[k])

    stage_moments(0, even_ref)

    def pair(index, carry):
        k = 2 * index
        stage_moments(k + 1, odd_ref)
        stage_lines(k, even_ref)
        stage_moments(jnp.minimum(k + 2, count - 1), even_ref)
        stage_lines(k + 1, odd_ref)
        return carry

    lax.fori_loop(0, count // 2, pair, 0)


def lines_kernel(start, count, *refs):
    own_lines(start, count, *refs)


def lines_halo_kernel(
    start, count, vol_ref, lines_ref, diff_i_ref, diff_x_ref, halo_ref, diff_h_ref, rows_ref,
    inner_ref, part_ref, inner_h_ref, part_h_ref, rows_out_ref, even_ref, odd_ref,
):
    rows_out_ref[...] = rows_ref[...]
    for group in range(2):
        both = dot(halo_ref[...], diff_h_ref[group])
        grad_i = dot(diff_i_ref[...], halo_ref[:, 128 * group : 128 * (group + 1)])
        for comp, term in enumerate(moments(grad_i, both[:, 128:], both[:, :128])):
            store_chunks(dot(lines_ref[...], term), comp, inner_h_ref.at[group], part_h_ref.at[group])
    own_lines(start, count, vol_ref, lines_ref, diff_i_ref, diff_x_ref, inner_ref, part_ref, even_ref, odd_ref)


def attributes(own, halo, weights, store):
    own = own.reshape(-1, own.shape[-1])
    halo = halo.reshape(-1, halo.shape[-1])
    tensor = dot(jnp.concatenate([own, halo], axis=1), weights)
    for chunk in range(tensor.shape[0] // (6 * EDGE)):
        base = 6 * EDGE * chunk
        a, b, c, d, e, f = [tensor[base + EDGE * comp : base + EDGE * (comp + 1)] for comp in range(6)]
        low = c + 1e-6
        inverse = reciprocal(low)
        spread = (a - b) * (a - c) + (b - c) * (b - c) + 3.0 * (d * d + e * e + f * f)
        root = spread * lax.rsqrt(jnp.maximum(spread, TINY))
        store(chunk, (-e * inverse, -f * inverse, root * reciprocal(a + b + low)))


def inner_kernel(inner_a_ref, inner_b_ref, inner_h_ref, smooth_ref, dip_i_ref, dip_x_ref, plan_ref, out_ref, sems):
    half, chunks = inner_a_ref.shape[:2]
    inner = EDGE * chunks
    targets = (dip_i_ref, dip_x_ref, plan_ref)

    def copies(pair):
        return [
            pltpu.make_async_copy(
                out_ref.at[n, pl.ds(half * group + 2 * pair, 2)],
                target.at[pl.ds(half * group + 2 * pair, 2), pl.ds(EDGE, inner)],
                sems.at[pair, group, n],
            )
            for group in range(2)
            for n, target in enumerate(targets)
        ]

    def step(pair, carry):
        for parity in range(2):
            k = 2 * pair + parity

            def store(chunk, values):
                group, row = chunk // chunks, EDGE * (chunk % chunks)
                for n, value in enumerate(values):
                    out_ref[n, half * group + k, row : row + EDGE] = value

            own = jnp.concatenate([inner_a_ref[k], inner_b_ref[k]], axis=0)
            attributes(own, inner_h_ref[...], smooth_ref[k], store)
        for copy in copies(pair):
            copy.start()
        return carry

    lax.fori_loop(0, half // 2, step, 0)
    for pair in range(half // 2):
        for copy in copies(pair):
            copy.wait()


def final_kernel(
    vol_ref, halo_ref, first_ref, second_ref, part_a_ref, part_b_ref, part_h_ref,
    smooth_ref, diff_x_ref, diff_h_ref, lines_e_ref, diff_e_ref, inner_i_ref, inner_x_ref, inner_p_ref,
    dip_i_ref, dip_x_ref, plan_ref,
    packed_ref, block_ref, block_h_ref, lined_h_ref, even_ref, odd_ref, out_ref, sems,
):
    depths, rows, cols = vol_ref.shape
    half = part_a_ref.shape[0]
    parts = (part_a_ref, part_b_ref)
    targets = (dip_i_ref, dip_x_ref, plan_ref)
    is_even = lax.rem(lax.axis_index("il"), 2) == 0
    bf16 = jnp.bfloat16

    first, second = first_ref[...].astype(jnp.float32), second_ref[...].astype(jnp.float32)
    packed_ref[0] = jnp.where(is_even, second, first)
    packed_ref[1] = jnp.where(is_even, first, second)
    for depth in range(depths):
        block_ref[depth, :EDGE] = vol_ref[depth, :EDGE]
        block_ref[depth, EDGE : 2 * EDGE] = vol_ref[depth, rows - EDGE :]
        for side in range(2):
            at = EDGE * (2 + side)
            block_ref[depth, at : at + EDGE] = packed_ref[side, REACH * depth : REACH * depth + EDGE].astype(bf16)
    block_h_ref[:EDGE] = halo_ref[:EDGE]
    block_h_ref[EDGE : 2 * EDGE] = halo_ref[rows - EDGE :]
    for side in range(2):
        at, row = EDGE * (2 + side), REACH * depths
        block_h_ref[at : at + EDGE, :256] = packed_ref[side, row : row + EDGE].astype(bf16)
        block_h_ref[at : at + EDGE, 256:] = packed_ref[side, row + REACH : row + REACH + EDGE, :128].astype(bf16)

    for group in range(2):
        both = dot(block_h_ref[...], diff_h_ref[group])
        grad_i = dot(diff_e_ref[...], block_h_ref[:, 128 * group : 128 * (group + 1)])
        for comp, term in enumerate(moments(grad_i, both[:, 128:], both[:, :128])):
            outer = dot(lines_e_ref[...], term)
            for end in range(2):
                summed = part_h_ref[group, end, comp] + outer[EDGE * end : EDGE * (end + 1)]
                lined_h_ref[group, end, comp] = summed.astype(bf16)

    def stage_edge(k, edge_ref):
        for group in range(2):
            z = half * group + k
            centre = block_ref[z + 1]
            grad_i = dot(diff_e_ref[...], centre)
            grad_x = dot(centre, diff_x_ref[...])
            grad_z = block_ref[z + 2].astype(jnp.float32) - block_ref[z].astype(jnp.float32)
            for comp, term in enumerate(moments(grad_i, grad_x, grad_z)):
                outer = dot(lines_e_ref[...], term)
                for end in range(2):
                    summed = parts[group][k, end, comp] + outer[EDGE * end : EDGE * (end + 1)]
                    edge_ref[group, end, comp] = summed.astype(bf16)

    def stage_attributes(k, edge_ref):
        def store(chunk, values):
            group, end = chunk // 2, chunk % 2
            for n, value in enumerate(values):
                out_ref[n, end, half * group + k] = value

        attributes(edge_ref[...], lined_h_ref[...], smooth_ref[k], store)

    def copies(pair):
        return [
            pltpu.make_async_copy(
                out_ref.at[n, end, pl.ds(half * group + 2 * pair, 2)],
                target.at[pl.ds(half * group + 2 * pair, 2), pl.ds((rows - EDGE) * end, EDGE)],
                sems.at[pair, group, end, n],
            )
            for group in range(2)
            for end in range(2)
            for n, target in enumerate(targets)
        ]

    stage_edge(0, even_ref)

    def step(pair, carry):
        k = 2 * pair
        stage_edge(k + 1, odd_ref)
        stage_attributes(k, even_ref)
        stage_edge(jnp.minimum(k + 2, half - 1), even_ref)
        stage_attributes(k + 1, odd_ref)
        for copy in copies(pair):
            copy.start()
        return carry

    lax.fori_loop(0, half // 2, step, 0)
    for pair in range(half // 2):
        for copy in copies(pair):
            copy.wait()


def call(name, kernel, outs, scratch, operands, in_specs=None, out_specs=None, flops=0, limit=16, aliases={}):
    return pl.pallas_call(
        kernel,
        out_shape=tuple(jax.ShapeDtypeStruct(*out) for out in outs),
        in_specs=in_specs or [WHOLE] * len(operands),
        out_specs=out_specs or (WHOLE,) * len(outs),
        scratch_shapes=scratch,
        compiler_params=pltpu.CompilerParams(vmem_limit_bytes=limit << 20),
        name=name,
        input_output_aliases=aliases,
        cost_estimate=pl.CostEstimate(flops=flops, bytes_accessed=0, transcendentals=0),
    )(*operands)


def body(volume):
    depths, rows, cols = volume.shape
    il, xl = lax.axis_size("il"), lax.axis_size("xl")
    count = depths - 2
    assert xl == 2 and il % 2 == 0 and count == 2 * SLOTS and cols == 256
    bf16, f32 = jnp.bfloat16, jnp.float32
    half = count // 2
    work = half * 1024 * 2 * 256 * 256
    packed_rows = -(-REACH * (depths + 2) // 16) * 16

    lines, diff_i, diff_x, smooth, diff_h, lines_e, diff_e, pick = call(
        "tables_kernel",
        lambda *refs: tables_kernel(depths, *refs),
        [
            ((rows, rows), bf16),
            ((rows, rows), bf16),
            ((cols, cols), bf16),
            ((SLOTS, cols + 128, cols), bf16),
            ((2, 128 * TILES, 256), bf16),
            ((2 * EDGE, 4 * EDGE), bf16),
            ((4 * EDGE, 4 * EDGE), bf16),
            ((cols, 256), bf16),
        ],
        [],
        [],
        flops=work,
    )
    halo_tile = ((TILES, rows, 128), bf16)
    vol, send, own = call("pack_kernel", pack_kernel, [(volume.shape, bf16), halo_tile, halo_tile], [], [volume, pick])
    side = lax.ppermute(send, "xl", [(0, 1), (1, 0)])

    chunks = rows // EDGE - 2

    def own_outs(count, lanes):
        return [((count, chunks, 6, EDGE, lanes), bf16), ((count, 2, 6, EDGE, lanes), f32)]

    inner_a, part_a = call(
        "lines_kernel",
        lambda *refs: lines_kernel(0, half, *refs),
        own_outs(half, cols),
        [pltpu.VMEM((6, rows, cols), bf16)] * 2,
        [vol, lines, diff_i, diff_x],
        flops=work,
    )
    halo, first, second = call(
        "rows_kernel",
        rows_kernel,
        [((rows, 128 * TILES), bf16), ((packed_rows, cols), bf16), ((packed_rows, cols), bf16)],
        [pltpu.VMEM((2, packed_rows, cols), f32)],
        [vol, own, side, part_a],
        in_specs=[WHOLE] * 3 + [pl.BlockSpec(memory_space=pl.ANY)],
    )
    one = [(i, i ^ 1) for i in range(il)]
    two = [pair for i in range(1, il - 1, 2) for pair in ((i, i + 1), (i + 1, i))]
    first_in = lax.ppermute(first, "il", one)
    inner_b, part_b, inner_h, part_h, second = call(
        "lines_halo_kernel",
        lambda *refs: lines_halo_kernel(half, half, *refs),
        own_outs(half, cols) + own_outs(2, 128) + [((packed_rows, cols), bf16)],
        [pltpu.VMEM((6, rows, cols), bf16)] * 2,
        [vol, lines, diff_i, diff_x, halo, diff_h, second],
        flops=work,
    )
    second_in = lax.ppermute(second, "il", two)
    outs = [((count, rows, cols), f32)] * 3
    inner_outs = call(
        "inner_kernel",
        inner_kernel,
        outs,
        [pltpu.VMEM((3, count, rows - 2 * EDGE, cols), f32), pltpu.SemaphoreType.DMA((half // 2, 2, 3))],
        [inner_a, inner_b, inner_h, smooth],
        out_specs=(IN_HBM,) * 3,
        flops=3 * work,
    )
    operands = [vol, halo, first_in, second_in, part_a, part_b, part_h, smooth, diff_x, diff_h, lines_e, diff_e]
    return call(
        "final_kernel",
        final_kernel,
        outs,
        [
            pltpu.VMEM((2, packed_rows, cols), f32),
            pltpu.VMEM((depths, 4 * EDGE, cols), bf16),
            pltpu.VMEM((4 * EDGE, 128 * TILES), bf16),
            pltpu.VMEM((2, 2, 6, EDGE, 128), bf16),
            pltpu.VMEM((2, 2, 6, EDGE, cols), bf16),
            pltpu.VMEM((2, 2, 6, EDGE, cols), bf16),
            pltpu.VMEM((3, 2, count, EDGE, cols), f32),
            pltpu.SemaphoreType.DMA((half // 2, 2, 2, 3)),
        ],
        operands + list(inner_outs),
        in_specs=[WHOLE] * len(operands) + [IN_HBM] * 3,
        out_specs=(IN_HBM,) * 3,
        flops=work,
        aliases={len(operands) + n: n for n in range(3)},
    )


def solution(mesh):
    spec = P(None, ("parts", "il"), "xl")
    return jax.shard_map(body, mesh=mesh, in_specs=(spec,), out_specs=(spec,) * 3, check_vma=False)
```

```python
import jax
import jax.numpy as jnp
import ml_dtypes
import numpy as np
from jax import lax
from jax.experimental import pallas as pl
from jax.experimental.pallas import tpu as pltpu
from jax.sharding import PartitionSpec as P

RADIUS = 9
REACH = RADIUS + 1
SIDE = 16
SLOTS = 8
TILES = 3
EDGE = 16
OWN = 2
TINY = float(np.finfo(np.float32).tiny)
FAR = -1000
WHOLE = pl.BlockSpec(memory_space=pltpu.VMEM)
IN_HBM = pl.BlockSpec(memory_space=pltpu.HBM)


def filter_taps():
    offsets = np.arange(2 * RADIUS + 1).astype(np.float32)
    sigma = np.float32(RADIUS / 3.0)
    shape = np.exp(np.float32(-0.5) * ((offsets - RADIUS) / sigma) ** 2)
    return (shape / np.sum(shape, dtype=np.float32)).astype(ml_dtypes.bfloat16).astype(np.float32)


def iota(shape, dim):
    return lax.broadcasted_iota(jnp.int32, shape, dim)


def band(source, target, scale=1.0):
    offset = jnp.abs(source - target)
    weights = jnp.zeros(offset.shape, jnp.float32)
    for distance, tap in enumerate(filter_taps()[RADIUS:]):
        weights = jnp.where(offset == distance, jnp.float32(scale * tap), weights)
    return weights


def difference(source, target):
    offset = source - target
    return jnp.where(offset == 1, 1.0, jnp.where(offset == -1, -1.0, 0.0)).astype(jnp.float32)


def dot(left, right):
    return jnp.dot(left, right, preferred_element_type=jnp.float32)


def reciprocal(value):
    guess = pl.reciprocal(value, approx=True)
    return guess * (2.0 - value * guess)


def halo_plane(lane, tile, depths):
    slot = lax.div(lane, SIDE)
    rest = jnp.where(slot == 0, 0, jnp.where(slot == 1, depths - 1, FAR))
    return jnp.where(tile < 2, 1 + SLOTS * tile + slot, rest)


def halo_column(lane, x, cols):
    place = lax.rem(lane, SIDE)
    return jnp.where(x == 0, cols - OWN + place, place - (SIDE - OWN))


def low_end(exchange):
    even = lax.rem(lax.axis_index("il"), 2) == 0
    return jnp.logical_not(even) if exchange == 0 else even


def tables_kernel(depths, lines_ref, diff_i_ref, diff_x_ref, smooth_ref, pack_h_ref, diff_h_ref, lines_e_ref, diff_e_ref, pick_ref):
    rows, cols = lines_ref.shape[0], diff_x_ref.shape[0]
    x, il, last = lax.axis_index("xl"), lax.axis_index("il"), lax.axis_size("il") - 1
    bf16 = jnp.bfloat16

    target, source = iota((rows, rows), 0), iota((rows, rows), 1)
    inner = (source > 0) & (source < rows - 1)
    lines_ref[...] = jnp.where(inner, band(source, target, 0.25), 0.0).astype(bf16)
    diff_i_ref[...] = difference(source, target).astype(bf16)
    span = EDGE * (depths - 2)
    target, source = iota((span, span), 0), iota((span, span), 1)
    depth = lax.div(source, EDGE) == lax.div(target, EDGE)
    target, source = lax.rem(target, EDGE), lax.rem(source, EDGE)
    diff_e_ref[...] = jnp.where(depth, difference(source, target), 0.0).astype(bf16)
    for exchange in range(2):
        low = low_end(exchange)
        source_at = jnp.where(low, source - REACH, rows - (EDGE - REACH) + source)
        target_at = jnp.where(low, target, rows - EDGE + target)
        first = jnp.where(low & (il > 0), -rows, 0)
        final = jnp.where(jnp.logical_not(low) & (il < last), 2 * rows, rows - 1)
        use = depth & (source_at >= first) & (source_at <= final) & ((source_at <= 0) | (source_at >= rows - 1))
        lines_e_ref[exchange] = jnp.where(use, band(source_at, target_at, 0.25), 0.0).astype(bf16)

    source, target = iota((cols, cols), 0), iota((cols, cols), 1)
    diff_x_ref[...] = difference(source, target).astype(bf16)
    moved = source == jnp.where(x == 0, cols - 1, 0)
    column = lax.rem(target + 128 * x, cols)
    smooth_ref[...] = jnp.where(moved, 0.0, band(source, column)).astype(bf16)
    source, target = iota((256, 256), 0), iota((256, 256), 1)
    place = lax.rem(source, SIDE)
    use = (lax.div(source, SIDE) == lax.div(target, SIDE)) & (place != jnp.where(x == 0, 0, SIDE - 1))
    column = jnp.where(x == 0, cols - SIDE, 0) + lax.rem(target, SIDE)
    pack_h_ref[...] = jnp.where(use, band(halo_column(place, x, cols), column), 0.0).astype(bf16)

    source, target = iota((128, 128), 0), iota((128, 128), 1)
    same = lax.rem(source, SIDE) == lax.rem(target, SIDE)
    across = difference(lax.rem(source, SIDE), lax.rem(target, SIDE))
    for group in range(2):
        centre = halo_plane(target, group, depths)
        for tile in range(TILES):
            plane = halo_plane(source, tile, depths)
            part, out = slice(128 * tile, 128 * (tile + 1)), 128 * group
            diff_h_ref[part, out : out + 128] = jnp.where(same, difference(plane, centre), 0.0).astype(bf16)
            diff_h_ref[part, 256 + out : 384 + out] = jnp.where(plane == centre, across, 0.0).astype(bf16)

    source, lane = iota((cols, 256), 0), iota((cols, 256), 1)
    place = lax.rem(lane, SIDE)
    low, high = place < SIDE - OWN, place >= OWN
    sent = jnp.where(x == 0, jnp.where(low, cols - (SIDE - OWN) + place, FAR), jnp.where(high, place - OWN, FAR))
    low, high = place < OWN, place >= SIDE - OWN
    kept = jnp.where(x == 0, jnp.where(low, cols - OWN + place, FAR), jnp.where(high, place - (SIDE - OWN), FAR))
    pick_ref[...] = jnp.where(source == jnp.where(lane < 128, sent, kept), 1.0, 0.0).astype(bf16)


def pack_kernel(vol_ref, pick_ref, copy_ref, send_ref, own_ref):
    depths, rows, cols = vol_ref.shape
    slot = lax.div(lax.rem(iota((rows, 256), 1), 128), SIDE)
    copy_ref[...] = vol_ref[...]
    for tile in range(TILES):
        if tile < 2:
            planes = [(1 + SLOTS * tile + index, index) for index in range(SLOTS)]
        else:
            planes = [(0, 0), (depths - 1, 1)]
        packed = jnp.zeros((rows, 256), jnp.float32)
        for plane, index in planes:
            packed = jnp.where(slot == index, dot(vol_ref[plane], pick_ref[...]), packed)
        packed = packed.astype(jnp.bfloat16)
        send_ref[tile] = packed[:, :128]
        own_ref[tile] = packed[:, 128:]


def rows_kernel(vol_ref, own_ref, side_ref, halo_ref, first_ref, second_ref, packed_ref):
    depths, rows, cols = vol_ref.shape
    even = lax.rem(lax.axis_index("il"), 2) == 0

    def put(row, top, bottom):
        top, bottom = top[:REACH], bottom[EDGE - REACH :]
        lanes = top.shape[1]
        packed_ref[0, row : row + REACH, :lanes] = jnp.where(even, bottom, top)
        packed_ref[1, row : row + REACH, :lanes] = jnp.where(even, top, bottom)

    packed_ref[:, depths * REACH :, :] = jnp.zeros_like(packed_ref[:, depths * REACH :, :])
    for depth in range(depths):
        top = vol_ref[depth, :EDGE, :].astype(jnp.float32)
        bottom = vol_ref[depth, rows - EDGE :, :].astype(jnp.float32)
        put(REACH * depth, top, bottom)
    tiles = []
    for tile in range(TILES):
        merged = own_ref[tile].astype(jnp.float32) + side_ref[tile].astype(jnp.float32)
        halo_ref[:, 128 * tile : 128 * (tile + 1)] = merged.astype(jnp.bfloat16)
        tiles.append((merged[:EDGE], merged[rows - EDGE :]))
    tops = jnp.concatenate([tiles[0][0], tiles[1][0]], axis=1)
    bottoms = jnp.concatenate([tiles[0][1], tiles[1][1]], axis=1)
    put(REACH * depths, tops, bottoms)
    put(REACH * (depths + 1), *tiles[2])
    first_ref[...] = packed_ref[0].astype(jnp.bfloat16)
    second_ref[...] = packed_ref[1].astype(jnp.bfloat16)


def moments(grad_i, grad_x, grad_z):
    terms = (
        grad_i * grad_i,
        grad_x * grad_x,
        grad_z * grad_z,
        grad_i * grad_x,
        grad_i * grad_z,
        grad_x * grad_z,
    )
    return [term.astype(jnp.bfloat16) for term in terms]


def store_chunks(summed, comp, inner_ref, part_ref):
    chunks = summed.shape[0] // EDGE
    for chunk in range(1, chunks - 1):
        inner_ref[chunk - 1, comp] = summed[EDGE * chunk : EDGE * (chunk + 1)].astype(jnp.bfloat16)
    part_ref[0, comp] = summed[:EDGE]
    part_ref[1, comp] = summed[EDGE * (chunks - 1) :]


def lines_kernel(
    vol_ref, halo_ref, rows_ref, lines_ref, diff_i_ref, diff_x_ref, diff_h_ref,
    inner_ref, part_ref, inner_h_ref, part_h_ref, rows_out_ref, even_ref, odd_ref,
):
    depths, rows, cols = vol_ref.shape
    count = depths - 2
    rows_out_ref[...] = rows_ref[...]
    both = dot(halo_ref[...], diff_h_ref[...])
    grad_i = dot(diff_i_ref[...], halo_ref[:, :256])
    for comp, term in enumerate(moments(grad_i, both[:, 256:], both[:, :256])):
        store_chunks(dot(lines_ref[...], term), comp, inner_h_ref, part_h_ref)

    def stage_moments(z, moments_ref):
        centre = vol_ref[pl.ds(z + 1, 2)]
        across = dot(centre.reshape(2 * rows, cols), diff_x_ref[...])
        for k in range(2):
            grad_i = dot(diff_i_ref[...], centre[k])
            grad_x = across[rows * k : rows * (k + 1)]
            grad_z = vol_ref[z + k + 2].astype(jnp.float32) - vol_ref[z + k].astype(jnp.float32)
            for comp, term in enumerate(moments(grad_i, grad_x, grad_z)):
                moments_ref[k, comp] = term

    def stage_lines(z, moments_ref):
        for k in range(2):
            for comp in range(6):
                store_chunks(dot(lines_ref[...], moments_ref[k, comp]), comp, inner_ref.at[z + k], part_ref.at[:, :, z + k])

    stage_moments(0, even_ref)

    def step(index, carry):
        z = 4 * index
        stage_moments(z + 2, odd_ref)
        stage_lines(z, even_ref)
        stage_moments(jnp.minimum(z + 4, count - 2), even_ref)
        stage_lines(z + 2, odd_ref)
        return carry

    lax.fori_loop(0, count // 4, step, 0)


def attributes(own, border, smooth_ref, store):
    x = lax.axis_index("xl")
    tensor = dot(own, smooth_ref[...])
    halves = (tensor[:, :128], tensor[:, 128:] + border)
    lanes = (pl.multiple_of(128 * x, 128), pl.multiple_of(128 - 128 * x, 128))
    for chunk in range(own.shape[0] // (6 * EDGE)):
        base = 6 * EDGE * chunk
        for half, lane in zip(halves, lanes):
            a, b, c, d, e, f = [half[base + EDGE * comp : base + EDGE * (comp + 1)] for comp in range(6)]
            low = c + 1e-6
            inverse = reciprocal(low)
            spread = (a - b) * (a - c) + (b - c) * (b - c) + 3.0 * (d * d + e * e + f * f)
            root = spread * lax.rsqrt(jnp.maximum(spread, TINY))
            store(chunk, pl.ds(lane, 128), (-e * inverse, -f * inverse, root * reciprocal(a + b + low)))


def border_of(packed, slot):
    base = jnp.where(lax.axis_index("xl") == 0, 128 - SIDE, 0)
    moved = pltpu.roll(packed, lax.rem(base - SIDE * slot + 128, 128), 1)
    return jnp.where(lax.div(iota(packed.shape, 1), SIDE) == lax.div(base, SIDE), moved, 0.0)


def inner_kernel(inner_ref, inner_h_ref, smooth_ref, pack_h_ref, dip_i_ref, dip_x_ref, plan_ref, border_ref, out_ref, sems):
    count, chunks = inner_ref.shape[:2]
    half, inner = count // 2, EDGE * chunks
    targets = (dip_i_ref, dip_x_ref, plan_ref)
    border_ref[...] = dot(inner_h_ref[...].reshape(6 * inner, 256), pack_h_ref[...])

    def copies(pair):
        return [
            pltpu.make_async_copy(
                out_ref.at[n, pl.ds(half * group + 2 * pair, 2)],
                target.at[pl.ds(half * group + 2 * pair, 2), pl.ds(EDGE, inner)],
                sems.at[pair, group, n],
            )
            for group in range(2)
            for n, target in enumerate(targets)
        ]

    def step(pair, carry):
        for parity in range(2):
            k = 2 * pair + parity
            for group in range(2):

                def store(chunk, lanes, values):
                    for n, value in enumerate(values):
                        out_ref[n, half * group + k, EDGE * chunk : EDGE * (chunk + 1), lanes] = value

                border = border_of(border_ref[:, 128 * group : 128 * (group + 1)], k)
                attributes(inner_ref[half * group + k].reshape(6 * inner, 256), border, smooth_ref, store)
        for copy in copies(pair):
            copy.start()
        return carry

    lax.fori_loop(0, half // 2, step, 0)
    for pair in range(half // 2):
        for copy in copies(pair):
            copy.wait()


def end_kernel(
    exchange, vol_ref, halo_ref, rows_ref, part_ref, part_h_ref,
    smooth_ref, pack_h_ref, diff_x_ref, diff_h_ref, lines_e_ref, diff_e_ref, in_i_ref, in_x_ref, in_p_ref,
    dip_i_ref, dip_x_ref, plan_ref,
    packed_ref, block_ref, block_h_ref, border_ref, edge_ref, out_ref, sems,
):
    depths, rows, cols = vol_ref.shape
    count, half = depths - 2, (depths - 2) // 2
    bf16, f32 = jnp.bfloat16, jnp.float32
    low = low_end(exchange)
    end = jnp.where(low, 0, 1)
    start = pl.multiple_of(jnp.where(low, 0, rows - EDGE), EDGE)
    targets = (dip_i_ref, dip_x_ref, plan_ref)

    packed_ref[:8] = jnp.zeros_like(packed_ref[:8])
    packed_ref[8:] = rows_ref[...].astype(f32)

    def joined(row, own):
        lanes = own.shape[1]
        before = packed_ref[8 + row : 8 + row + EDGE, :lanes]
        after = packed_ref[8 + row - (EDGE - REACH) : 8 + row + REACH, :lanes]
        own = own.astype(f32)
        place = iota(own.shape, 0)
        first = jnp.where(place < REACH, before, pltpu.roll(own, REACH, 0))
        second = jnp.where(place < EDGE - REACH, pltpu.roll(own, EDGE - REACH, 0), after)
        return jnp.where(low, first, second).astype(bf16)

    for depth in range(depths):
        block_ref[depth] = joined(REACH * depth, vol_ref[depth, pl.ds(start, EDGE)])
    own_h = halo_ref[pl.ds(start, EDGE)]
    block_h_ref[:, :256] = joined(REACH * depths, own_h[:, :256])
    block_h_ref[:, 256:] = joined(REACH * (depths + 1), own_h[:, 256:])

    both = dot(block_h_ref[...], diff_h_ref[...])
    grad_i = dot(diff_e_ref[:EDGE, :EDGE], block_h_ref[:, :256])
    lined_h = []
    for comp, term in enumerate(moments(grad_i, both[:, 256:], both[:, :256])):
        summed = part_h_ref[end, comp] + dot(lines_e_ref[exchange, :EDGE, :EDGE], term)
        lined_h.append(summed.astype(bf16))
    border_ref[...] = dot(jnp.concatenate(lined_h, axis=0), pack_h_ref[...])

    centre = block_ref[1 : count + 1].reshape(count * EDGE, cols)
    grad_i = dot(diff_e_ref[...], centre)
    grad_x = dot(centre, diff_x_ref[...])
    grad_z = block_ref[2:].astype(f32) - block_ref[:count].astype(f32)
    for comp, term in enumerate(moments(grad_i, grad_x, grad_z.reshape(count * EDGE, cols))):
        outer = dot(lines_e_ref[exchange], term)
        summed = part_ref[end, comp] + outer.reshape(count, EDGE, cols)
        edge_ref[:, comp] = summed.astype(bf16)

    def copies(pair):
        return [
            pltpu.make_async_copy(
                out_ref.at[n, pl.ds(half * group + 2 * pair, 2)],
                target.at[pl.ds(half * group + 2 * pair, 2), pl.ds(start, EDGE)],
                sems.at[pair, group, n],
            )
            for group in range(2)
            for n, target in enumerate(targets)
        ]

    def step(pair, carry):
        own, border, places = [], [], []
        for group in range(2):
            for parity in range(2):
                k = 2 * pair + parity
                places.append(half * group + k)
                own.append(edge_ref[half * group + k].reshape(6 * EDGE, cols))
                border.append(border_of(border_ref[:, 128 * group : 128 * (group + 1)], k))

        def store(chunk, lanes, values):
            for n, value in enumerate(values):
                out_ref[n, places[chunk], :, lanes] = value

        attributes(jnp.concatenate(own, axis=0), jnp.concatenate(border, axis=0), smooth_ref, store)
        for copy in copies(pair):
            copy.start()
        return carry

    lax.fori_loop(0, half // 2, step, 0)
    for pair in range(half // 2):
        for copy in copies(pair):
            copy.wait()


def call(name, kernel, outs, scratch, operands, in_specs=None, out_specs=None, flops=0, limit=16, aliases={}):
    return pl.pallas_call(
        kernel,
        out_shape=tuple(jax.ShapeDtypeStruct(*out) for out in outs),
        in_specs=in_specs or [WHOLE] * len(operands),
        out_specs=out_specs or (WHOLE,) * len(outs),
        scratch_shapes=scratch,
        compiler_params=pltpu.CompilerParams(vmem_limit_bytes=limit << 20),
        name=name,
        input_output_aliases=aliases,
        cost_estimate=pl.CostEstimate(flops=flops, bytes_accessed=0, transcendentals=0),
    )(*operands)


def body(volume):
    depths, rows, cols = volume.shape
    il, xl = lax.axis_size("il"), lax.axis_size("xl")
    count = depths - 2
    assert xl == 2 and il % 2 == 0 and count == 2 * SLOTS and cols == 256
    bf16, f32 = jnp.bfloat16, jnp.float32
    half = count // 2
    work = half * 1024 * 2 * 256 * 256
    packed_rows = -(-REACH * (depths + 2) // 16) * 16

    span = EDGE * count
    lines, diff_i, diff_x, smooth, pack_h, diff_h, lines_e, diff_e, pick = call(
        "tables_kernel",
        lambda *refs: tables_kernel(depths, *refs),
        [
            ((rows, rows), bf16),
            ((rows, rows), bf16),
            ((cols, cols), bf16),
            ((cols, cols), bf16),
            ((256, 256), bf16),
            ((128 * TILES, 512), bf16),
            ((2, span, span), bf16),
            ((span, span), bf16),
            ((cols, 256), bf16),
        ],
        [],
        [],
        flops=work,
    )
    halo_tile = ((TILES, rows, 128), bf16)
    vol, send, own = call("pack_kernel", pack_kernel, [(volume.shape, bf16), halo_tile, halo_tile], [], [volume, pick])
    side = lax.ppermute(send, "xl", [(0, 1), (1, 0)])
    packed = ((packed_rows, cols), bf16)
    halo, first, second = call(
        "rows_kernel",
        rows_kernel,
        [((rows, 128 * TILES), bf16), packed, packed],
        [pltpu.VMEM((2, packed_rows, cols), f32)],
        [vol, own, side],
    )
    one = [(i, i ^ 1) for i in range(il)]
    two = [pair for i in range(1, il - 1, 2) for pair in ((i, i + 1), (i + 1, i))]
    second_in = lax.ppermute(second, "il", two)
    chunks = rows // EDGE - 2
    inner, part, inner_h, part_h, first = call(
        "lines_kernel",
        lines_kernel,
        [
            ((count, chunks, 6, EDGE, cols), bf16),
            ((2, 6, count, EDGE, cols), f32),
            ((chunks, 6, EDGE, 256), bf16),
            ((2, 6, EDGE, 256), f32),
            packed,
        ],
        [pltpu.VMEM((2, 6, rows, cols), bf16)] * 2,
        [vol, halo, first, lines, diff_i, diff_x, diff_h],
        flops=2 * work,
    )
    first_in = lax.ppermute(first, "il", one)
    shapes = [((count, rows, cols), f32)] * 3
    sems = pltpu.SemaphoreType.DMA((half // 2, 2, 3))
    outs = call(
        "inner_kernel",
        inner_kernel,
        shapes,
        [pltpu.VMEM((6 * EDGE * chunks, 256), f32), pltpu.VMEM((3, count, EDGE * chunks, cols), f32), sems],
        [inner, inner_h, smooth, pack_h],
        out_specs=(IN_HBM,) * 3,
        flops=2 * work,
    )
    tables = [smooth, pack_h, diff_x, diff_h, lines_e, diff_e]
    for exchange, received in ((1, second_in), (0, first_in)):
        operands = [vol, halo, received, part, part_h, *tables]
        outs = call(
            "end_kernel",
            lambda *refs, exchange=exchange: end_kernel(exchange, *refs),
            shapes,
            [
                pltpu.VMEM((8 + packed_rows, cols), f32),
                pltpu.VMEM((depths, EDGE, cols), bf16),
                pltpu.VMEM((EDGE, 128 * TILES), bf16),
                pltpu.VMEM((6 * EDGE, 256), f32),
                pltpu.VMEM((count, 6, EDGE, cols), bf16),
                pltpu.VMEM((3, count, EDGE, cols), f32),
                sems,
            ],
            operands + list(outs),
            in_specs=[WHOLE] * len(operands) + [IN_HBM] * 3,
            out_specs=(IN_HBM,) * 3,
            flops=work,
            aliases={len(operands) + n: n for n in range(3)},
        )
    return outs


def solution(mesh):
    spec = P(None, ("parts", "il"), "xl")
    return jax.shard_map(body, mesh=mesh, in_specs=(spec,), out_specs=(spec,) * 3, check_vma=False)
```

```python
import jax
import jax.numpy as jnp
import ml_dtypes
import numpy as np
from jax import lax
from jax.experimental import pallas as pl
from jax.experimental.pallas import tpu as pltpu
from jax.sharding import PartitionSpec as P

RADIUS = 9
REACH = RADIUS + 1
SIDE = 16
SLOTS = 8
TILES = 3
EDGE = 16
OWN = 2
TINY = float(np.finfo(np.float32).tiny)
HEAD = 4
FAR = -1000
WHOLE = pl.BlockSpec(memory_space=pltpu.VMEM)
IN_HBM = pl.BlockSpec(memory_space=pltpu.HBM)
ANYWHERE = pl.BlockSpec(memory_space=pl.ANY)


def filter_taps():
    offsets = np.arange(2 * RADIUS + 1).astype(np.float32)
    sigma = np.float32(RADIUS / 3.0)
    shape = np.exp(np.float32(-0.5) * ((offsets - RADIUS) / sigma) ** 2)
    return (shape / np.sum(shape, dtype=np.float32)).astype(ml_dtypes.bfloat16).astype(np.float32)


def iota(shape, dim):
    return lax.broadcasted_iota(jnp.int32, shape, dim)


def band(source, target, scale=1.0):
    offset = jnp.abs(source - target)
    weights = jnp.zeros(offset.shape, jnp.float32)
    for distance, tap in enumerate(filter_taps()[RADIUS:]):
        weights = jnp.where(offset == distance, jnp.float32(scale * tap), weights)
    return weights


def difference(source, target):
    offset = source - target
    return jnp.where(offset == 1, 1.0, jnp.where(offset == -1, -1.0, 0.0)).astype(jnp.float32)


def dot(left, right):
    return jnp.dot(left, right, preferred_element_type=jnp.float32)


def reciprocal(value):
    guess = pl.reciprocal(value, approx=True)
    return guess * (2.0 - value * guess)


def halo_plane(lane, tile, depths):
    slot = lax.div(lane, SIDE)
    rest = jnp.where(slot == 0, 0, jnp.where(slot == 1, depths - 1, FAR))
    return jnp.where(tile < 2, 1 + SLOTS * tile + slot, rest)


def halo_column(lane, x, cols):
    place = lax.rem(lane, SIDE)
    return jnp.where(x == 0, cols - OWN + place, place - (SIDE - OWN))


def low_end(exchange):
    even = lax.rem(lax.axis_index("il"), 2) == 0
    return jnp.logical_not(even) if exchange == 0 else even


def tables_kernel(depths, lines_ref, diff_i_ref, diff_x_ref, smooth_ref, pack_h_ref, diff_h_ref, lines_e_ref, diff_e_ref, pick_ref):
    rows, cols = lines_ref.shape[0], diff_x_ref.shape[0]
    x, il, last = lax.axis_index("xl"), lax.axis_index("il"), lax.axis_size("il") - 1
    bf16 = jnp.bfloat16

    target, source = iota((rows, rows), 0), iota((rows, rows), 1)
    inner = (source > 0) & (source < rows - 1)
    lines_ref[...] = jnp.where(inner, band(source, target, 0.25), 0.0).astype(bf16)
    diff_i_ref[...] = difference(source, target).astype(bf16)
    span = EDGE * (depths - 2)
    target, source = iota((span, span), 0), iota((span, span), 1)
    depth = lax.div(source, EDGE) == lax.div(target, EDGE)
    target, source = lax.rem(target, EDGE), lax.rem(source, EDGE)
    diff_e_ref[...] = jnp.where(depth, difference(source, target), 0.0).astype(bf16)
    for exchange in range(2):
        low = low_end(exchange)
        source_at = jnp.where(low, source - REACH, rows - (EDGE - REACH) + source)
        target_at = jnp.where(low, target, rows - EDGE + target)
        first = jnp.where(low & (il > 0), -rows, 0)
        final = jnp.where(jnp.logical_not(low) & (il < last), 2 * rows, rows - 1)
        use = depth & (source_at >= first) & (source_at <= final) & ((source_at <= 0) | (source_at >= rows - 1))
        lines_e_ref[exchange] = jnp.where(use, band(source_at, target_at, 0.25), 0.0).astype(bf16)

    source, target = iota((cols, cols), 0), iota((cols, cols), 1)
    diff_x_ref[...] = difference(source, target).astype(bf16)
    moved = source == jnp.where(x == 0, cols - 1, 0)
    column = lax.rem(target + 128 * x, cols)
    smooth_ref[...] = jnp.where(moved, 0.0, band(source, column)).astype(bf16)
    source, target = iota((256, 256), 0), iota((256, 256), 1)
    place = lax.rem(source, SIDE)
    use = (lax.div(source, SIDE) == lax.div(target, SIDE)) & (place != jnp.where(x == 0, 0, SIDE - 1))
    column = jnp.where(x == 0, cols - SIDE, 0) + lax.rem(target, SIDE)
    pack_h_ref[...] = jnp.where(use, band(halo_column(place, x, cols), column), 0.0).astype(bf16)

    source, target = iota((128, 128), 0), iota((128, 128), 1)
    same = lax.rem(source, SIDE) == lax.rem(target, SIDE)
    across = difference(lax.rem(source, SIDE), lax.rem(target, SIDE))
    for group in range(2):
        centre = halo_plane(target, group, depths)
        for tile in range(TILES):
            plane = halo_plane(source, tile, depths)
            part, out = slice(128 * tile, 128 * (tile + 1)), 128 * group
            diff_h_ref[part, out : out + 128] = jnp.where(same, difference(plane, centre), 0.0).astype(bf16)
            diff_h_ref[part, 256 + out : 384 + out] = jnp.where(plane == centre, across, 0.0).astype(bf16)

    source, lane = iota((cols, 256), 0), iota((cols, 256), 1)
    place = lax.rem(lane, SIDE)
    low, high = place < SIDE - OWN, place >= OWN
    sent = jnp.where(x == 0, jnp.where(low, cols - (SIDE - OWN) + place, FAR), jnp.where(high, place - OWN, FAR))
    low, high = place < OWN, place >= SIDE - OWN
    kept = jnp.where(x == 0, jnp.where(low, cols - OWN + place, FAR), jnp.where(high, place - (SIDE - OWN), FAR))
    pick_ref[...] = jnp.where(source == jnp.where(lane < 128, sent, kept), 1.0, 0.0).astype(bf16)


def pack_kernel(vol_ref, pick_ref, copy_ref, send_ref, own_ref):
    depths, rows, cols = vol_ref.shape
    slot = lax.div(lax.rem(iota((rows, 256), 1), 128), SIDE)
    copy_ref[...] = vol_ref[...]
    for tile in range(TILES):
        if tile < 2:
            planes = [(1 + SLOTS * tile + index, index) for index in range(SLOTS)]
        else:
            planes = [(0, 0), (depths - 1, 1)]
        packed = jnp.zeros((rows, 256), jnp.float32)
        for plane, index in planes:
            packed = jnp.where(slot == index, dot(vol_ref[plane], pick_ref[...]), packed)
        packed = packed.astype(jnp.bfloat16)
        send_ref[tile] = packed[:, :128]
        own_ref[tile] = packed[:, 128:]


def rows_kernel(vol_ref, own_ref, side_ref, after_ref, halo_ref, ends_ref, packed_ref):
    depths, rows, cols = vol_ref.shape
    even = lax.rem(lax.axis_index("il"), 2) == 0

    def put(row, top, bottom):
        top, bottom = top[:REACH], bottom[EDGE - REACH :]
        lanes = top.shape[1]
        packed_ref[0, row : row + REACH, :lanes] = jnp.where(even, bottom, top)
        packed_ref[1, row : row + REACH, :lanes] = jnp.where(even, top, bottom)

    packed_ref[:, depths * REACH :, :] = jnp.zeros_like(packed_ref[:, depths * REACH :, :])
    for depth in range(depths):
        top = vol_ref[depth, :EDGE, :].astype(jnp.float32)
        bottom = vol_ref[depth, rows - EDGE :, :].astype(jnp.float32)
        put(REACH * depth, top, bottom)
    tiles = []
    for tile in range(TILES):
        merged = own_ref[tile].astype(jnp.float32) + side_ref[tile].astype(jnp.float32)
        halo_ref[:, 128 * tile : 128 * (tile + 1)] = merged.astype(jnp.bfloat16)
        tiles.append((merged[:EDGE], merged[rows - EDGE :]))
    tops = jnp.concatenate([tiles[0][0], tiles[1][0]], axis=1)
    bottoms = jnp.concatenate([tiles[0][1], tiles[1][1]], axis=1)
    put(REACH * depths, tops, bottoms)
    put(REACH * (depths + 1), *tiles[2])
    ends_ref[...] = packed_ref[...].astype(jnp.bfloat16)


def relay_kernel(ends_ref, after_ref, out_ref):
    out_ref[...] = ends_ref[1]


def moments(grad_i, grad_x, grad_z):
    terms = (
        grad_i * grad_i,
        grad_x * grad_x,
        grad_z * grad_z,
        grad_i * grad_x,
        grad_i * grad_z,
        grad_x * grad_z,
    )
    return [term.astype(jnp.bfloat16) for term in terms]


def store_chunks(summed, comp, inner_ref, part_ref):
    chunks = summed.shape[0] // EDGE
    for chunk in range(1, chunks - 1):
        inner_ref[chunk - 1, comp] = summed[EDGE * chunk : EDGE * (chunk + 1)].astype(jnp.bfloat16)
    part_ref[0, comp] = summed[:EDGE]
    part_ref[1, comp] = summed[EDGE * (chunks - 1) :]


def lines_kernel(vol_ref, lines_ref, diff_i_ref, diff_x_ref, inner_ref, part_ref, even_ref, odd_ref):
    own_lines(0, HEAD, vol_ref, lines_ref, diff_i_ref, diff_x_ref, inner_ref, part_ref, even_ref, odd_ref)


def more_lines_kernel(
    vol_ref, halo_ref, lines_ref, diff_i_ref, diff_x_ref, diff_h_ref, inner_in_ref, part_in_ref,
    inner_ref, part_ref, inner_h_ref, part_h_ref, even_ref, odd_ref,
):
    both = dot(halo_ref[...], diff_h_ref[...])
    grad_i = dot(diff_i_ref[...], halo_ref[:, :256])
    for comp, term in enumerate(moments(grad_i, both[:, 256:], both[:, :256])):
        store_chunks(dot(lines_ref[...], term), comp, inner_h_ref, part_h_ref)
    stop = vol_ref.shape[0] - 2
    own_lines(HEAD, stop, vol_ref, lines_ref, diff_i_ref, diff_x_ref, inner_ref, part_ref, even_ref, odd_ref)


def own_lines(first, stop, vol_ref, lines_ref, diff_i_ref, diff_x_ref, inner_ref, part_ref, even_ref, odd_ref):
    depths, rows, cols = vol_ref.shape

    def stage_moments(z, moments_ref):
        centre = vol_ref[pl.ds(z + 1, 2)]
        across = dot(centre.reshape(2 * rows, cols), diff_x_ref[...])
        for k in range(2):
            grad_i = dot(diff_i_ref[...], centre[k])
            grad_x = across[rows * k : rows * (k + 1)]
            grad_z = vol_ref[z + k + 2].astype(jnp.float32) - vol_ref[z + k].astype(jnp.float32)
            for comp, term in enumerate(moments(grad_i, grad_x, grad_z)):
                moments_ref[k, comp] = term

    def stage_lines(z, moments_ref):
        for k in range(2):
            for comp in range(6):
                store_chunks(dot(lines_ref[...], moments_ref[k, comp]), comp, inner_ref.at[z + k], part_ref.at[:, :, z + k])

    stage_moments(first, even_ref)

    def step(index, carry):
        z = first + 4 * index
        stage_moments(z + 2, odd_ref)
        stage_lines(z, even_ref)
        stage_moments(jnp.minimum(z + 4, stop - 2), even_ref)
        stage_lines(z + 2, odd_ref)
        return carry

    lax.fori_loop(0, (stop - first) // 4, step, 0)


def attributes(own, border, smooth_ref, store):
    x = lax.axis_index("xl")
    tensor = dot(own, smooth_ref[...])
    halves = (tensor[:, :128], tensor[:, 128:] + border)
    lanes = (pl.multiple_of(128 * x, 128), pl.multiple_of(128 - 128 * x, 128))
    for chunk in range(own.shape[0] // (6 * EDGE)):
        base = 6 * EDGE * chunk
        for half, lane in zip(halves, lanes):
            a, b, c, d, e, f = [half[base + EDGE * comp : base + EDGE * (comp + 1)] for comp in range(6)]
            low = c + 1e-6
            inverse = reciprocal(low)
            spread = (a - b) * (a - c) + (b - c) * (b - c) + 3.0 * (d * d + e * e + f * f)
            root = spread * lax.rsqrt(jnp.maximum(spread, TINY))
            store(chunk, pl.ds(lane, 128), (-e * inverse, -f * inverse, root * reciprocal(a + b + low)))


def border_of(packed, slot):
    base = jnp.where(lax.axis_index("xl") == 0, 128 - SIDE, 0)
    moved = pltpu.roll(packed, lax.rem(base - SIDE * slot + 128, 128), 1)
    return jnp.where(lax.div(iota(packed.shape, 1), SIDE) == lax.div(base, SIDE), moved, 0.0)


def inner_kernel(inner_ref, inner_h_ref, smooth_ref, pack_h_ref, out_ref, border_ref):
    count, chunks = inner_ref.shape[:2]
    half, inner = count // 2, EDGE * chunks
    border_ref[...] = dot(inner_h_ref[...].reshape(6 * inner, 256), pack_h_ref[...])

    def step(k, carry):
        for group in range(2):

            def store(chunk, lanes, values):
                for n, value in enumerate(values):
                    out_ref[n, half * group + k, EDGE * chunk : EDGE * (chunk + 1), lanes] = value

            border = border_of(border_ref[:, 128 * group : 128 * (group + 1)], k)
            attributes(inner_ref[half * group + k].reshape(6 * inner, 256), border, smooth_ref, store)
        return carry

    lax.fori_loop(0, half, step, 0, unroll=2)


def end_kernel(
    exchange, vol_ref, halo_ref, rows_ref, part_ref, part_h_ref,
    smooth_ref, pack_h_ref, diff_x_ref, diff_h_ref, lines_e_ref, diff_e_ref, done_ref, *refs,
):
    last = exchange == 1
    targets, refs = (refs[3:6], refs[6:]) if last else (refs[:3], refs[3:])
    if last:
        packed_ref, block_ref, block_h_ref, border_ref, edge_ref, out_ref, done_sems, sems = refs
    else:
        out_ref, packed_ref, block_ref, block_h_ref, border_ref, edge_ref, done_sems = refs
    depths, rows, cols = vol_ref.shape
    count, half = depths - 2, (depths - 2) // 2
    bf16, f32 = jnp.bfloat16, jnp.float32
    low = low_end(exchange)
    end = jnp.where(low, 0, 1)
    start = pl.multiple_of(jnp.where(low, 0, rows - EDGE), EDGE)
    done_start = pl.multiple_of(jnp.where(low, rows - EDGE, 0), EDGE) if last else EDGE
    finished = [
        pltpu.make_async_copy(done_ref.at[n], target.at[:, pl.ds(done_start, done_ref.shape[2])], done_sems.at[n])
        for n, target in enumerate(targets)
    ]
    for copy in finished:
        copy.start()

    packed_ref[:8] = jnp.zeros_like(packed_ref[:8])
    packed_ref[8:] = (rows_ref[...] if last else rows_ref[0]).astype(f32)

    def joined(row, own):
        lanes = own.shape[1]
        before = packed_ref[8 + row : 8 + row + EDGE, :lanes]
        after = packed_ref[8 + row - (EDGE - REACH) : 8 + row + REACH, :lanes]
        own = own.astype(f32)
        place = iota(own.shape, 0)
        first = jnp.where(place < REACH, before, pltpu.roll(own, REACH, 0))
        second = jnp.where(place < EDGE - REACH, pltpu.roll(own, EDGE - REACH, 0), after)
        return jnp.where(low, first, second).astype(bf16)

    for depth in range(depths):
        block_ref[depth] = joined(REACH * depth, vol_ref[depth, pl.ds(start, EDGE)])
    own_h = halo_ref[pl.ds(start, EDGE)]
    block_h_ref[:, :256] = joined(REACH * depths, own_h[:, :256])
    block_h_ref[:, 256:] = joined(REACH * (depths + 1), own_h[:, 256:])

    both = dot(block_h_ref[...], diff_h_ref[...])
    grad_i = dot(diff_e_ref[:EDGE, :EDGE], block_h_ref[:, :256])
    lined_h = []
    for comp, term in enumerate(moments(grad_i, both[:, 256:], both[:, :256])):
        summed = part_h_ref[end, comp] + dot(lines_e_ref[exchange, :EDGE, :EDGE], term)
        lined_h.append(summed.astype(bf16))
    border_ref[...] = dot(jnp.concatenate(lined_h, axis=0), pack_h_ref[...])

    centre = block_ref[1 : count + 1].reshape(count * EDGE, cols)
    grad_i = dot(diff_e_ref[...], centre)
    grad_x = dot(centre, diff_x_ref[...])
    grad_z = block_ref[2:].astype(f32) - block_ref[:count].astype(f32)
    for comp, term in enumerate(moments(grad_i, grad_x, grad_z.reshape(count * EDGE, cols))):
        outer = dot(lines_e_ref[exchange], term)
        summed = part_ref[end, comp] + outer.reshape(count, EDGE, cols)
        edge_ref[:, comp] = summed.astype(bf16)

    copies = []
    for pair in range(half // 2):
        own, border, places = [], [], []
        for group in range(2):
            for parity in range(2):
                k = 2 * pair + parity
                places.append(half * group + k)
                own.append(edge_ref[half * group + k].reshape(6 * EDGE, cols))
                border.append(border_of(border_ref[:, 128 * group : 128 * (group + 1)], k))

        def store(chunk, lanes, values):
            for n, value in enumerate(values):
                out_ref[n, places[chunk], :, lanes] = value

        attributes(jnp.concatenate(own, axis=0), jnp.concatenate(border, axis=0), smooth_ref, store)
        if last:
            for group in range(2):
                depth = pl.ds(half * group + 2 * pair, 2)
                for n, target in enumerate(targets):
                    copy = pltpu.make_async_copy(
                        out_ref.at[n, depth], target.at[depth, pl.ds(start, EDGE)], sems.at[pair, group, n]
                    )
                    copy.start()
                    copies.append(copy)
    for copy in finished + copies:
        copy.wait()


def call(name, kernel, outs, scratch, operands, in_specs=None, out_specs=None, flops=0, limit=16, aliases={}):
    return pl.pallas_call(
        kernel,
        out_shape=tuple(jax.ShapeDtypeStruct(*out) for out in outs),
        in_specs=in_specs or [WHOLE] * len(operands),
        out_specs=out_specs or (WHOLE,) * len(outs),
        scratch_shapes=scratch,
        compiler_params=pltpu.CompilerParams(vmem_limit_bytes=limit << 20),
        name=name,
        input_output_aliases=aliases,
        cost_estimate=pl.CostEstimate(flops=flops, bytes_accessed=0, transcendentals=0),
    )(*operands)


def body(volume):
    depths, rows, cols = volume.shape
    il, xl = lax.axis_size("il"), lax.axis_size("xl")
    count = depths - 2
    assert xl == 2 and il % 2 == 0 and count == 2 * SLOTS and cols == 256
    bf16, f32 = jnp.bfloat16, jnp.float32
    half = count // 2
    work = half * 1024 * 2 * 256 * 256
    packed_rows = -(-REACH * (depths + 2) // 16) * 16

    span = EDGE * count
    lines, diff_i, diff_x, smooth, pack_h, diff_h, lines_e, diff_e, pick = call(
        "tables_kernel",
        lambda *refs: tables_kernel(depths, *refs),
        [
            ((rows, rows), bf16),
            ((rows, rows), bf16),
            ((cols, cols), bf16),
            ((cols, cols), bf16),
            ((256, 256), bf16),
            ((128 * TILES, 512), bf16),
            ((2, span, span), bf16),
            ((span, span), bf16),
            ((cols, 256), bf16),
        ],
        [],
        [],
        flops=work,
    )
    halo_tile = ((TILES, rows, 128), bf16)
    vol, send, own = call("pack_kernel", pack_kernel, [(volume.shape, bf16), halo_tile, halo_tile], [], [volume, pick])
    side = lax.ppermute(send, "xl", [(0, 1), (1, 0)])
    chunks = rows // EDGE - 2
    lined = [((count, chunks, 6, EDGE, cols), bf16), ((2, 6, count, EDGE, cols), f32)]
    moment_slots = [pltpu.VMEM((2, 6, rows, cols), bf16)] * 2
    inner, part = call("lines_kernel", lines_kernel, lined, moment_slots, [vol, lines, diff_i, diff_x], flops=work // 4)
    halo, ends = call(
        "rows_kernel",
        rows_kernel,
        [((rows, 128 * TILES), bf16), ((2, packed_rows, cols), bf16)],
        [pltpu.VMEM((2, packed_rows, cols), f32)],
        [vol, own, side, part],
        in_specs=[WHOLE] * 3 + [ANYWHERE],
    )
    ends_in = lax.ppermute(ends, "il", [(i, i ^ 1) for i in range(il)])
    operands = [vol, halo, lines, diff_i, diff_x, diff_h, inner, part]
    inner, part, inner_h, part_h = call(
        "more_lines_kernel",
        more_lines_kernel,
        lined + [((chunks, 6, EDGE, 256), bf16), ((2, 6, EDGE, 256), f32)],
        moment_slots,
        operands,
        flops=2 * work,
        aliases={len(operands) - 2 + n: n for n in range(2)},
    )
    (done,) = call(
        "inner_kernel",
        inner_kernel,
        [((3, count, EDGE * chunks, cols), f32)],
        [pltpu.VMEM((6 * EDGE * chunks, 256), f32)],
        [inner, inner_h, smooth, pack_h],
        flops=2 * work,
    )
    (relayed,) = call(
        "relay_kernel", relay_kernel, [((packed_rows, cols), bf16)], [], [ends_in, done], in_specs=[WHOLE, ANYWHERE]
    )
    onward = [(i, i + 2) for i in range(0, il - 2, 2)] + [(i, i - 2) for i in range(3, il, 2)]
    relayed_in = lax.ppermute(relayed, "il", onward)

    outs = [((count, rows, cols), f32)] * 3
    end_rows = (3, count, EDGE, cols)
    tables = [smooth, pack_h, diff_x, diff_h, lines_e, diff_e]
    scratch = [
        pltpu.VMEM((8 + packed_rows, cols), f32),
        pltpu.VMEM((depths, EDGE, cols), bf16),
        pltpu.VMEM((EDGE, 128 * TILES), bf16),
        pltpu.VMEM((6 * EDGE, 256), f32),
        pltpu.VMEM((count, 6, EDGE, cols), bf16),
    ]
    sems = pltpu.SemaphoreType.DMA((3,))
    *outs_in, done = call(
        "near_end_kernel",
        lambda *refs: end_kernel(0, *refs),
        outs + [(end_rows, f32)],
        scratch + [sems],
        [vol, halo, ends_in, part, part_h, *tables, done],
        out_specs=(IN_HBM,) * 3 + (WHOLE,),
        flops=work,
    )
    operands = [vol, halo, relayed_in, part, part_h, *tables, done]
    return call(
        "far_end_kernel",
        lambda *refs: end_kernel(1, *refs),
        outs,
        scratch + [pltpu.VMEM(end_rows, f32), sems, pltpu.SemaphoreType.DMA((half // 2, 2, 3))],
        operands + outs_in,
        in_specs=[WHOLE] * len(operands) + [IN_HBM] * 3,
        out_specs=(IN_HBM,) * 3,
        flops=work,
        aliases={len(operands) + n: n for n in range(3)},
    )


def solution(mesh):
    spec = P(None, ("parts", "il"), "xl")
    return jax.shard_map(body, mesh=mesh, in_specs=(spec,), out_specs=(spec,) * 3, check_vma=False)
```

```python
import jax
import jax.numpy as jnp
import ml_dtypes
import numpy as np
from jax import lax
from jax.experimental import pallas as pl
from jax.experimental.pallas import tpu as pltpu
from jax.sharding import PartitionSpec as P

RADIUS = 9
REACH = RADIUS + 1
SIDE = 16
SLOTS = 8
TILES = 3
EDGE = 16
OWN = 2
TINY = float(np.finfo(np.float32).tiny)
HEAD = 4
PART = 4
FAR = -1000
WHOLE = pl.BlockSpec(memory_space=pltpu.VMEM)
IN_HBM = pl.BlockSpec(memory_space=pltpu.HBM)
ANYWHERE = pl.BlockSpec(memory_space=pl.ANY)


def filter_taps():
    offsets = np.arange(2 * RADIUS + 1).astype(np.float32)
    sigma = np.float32(RADIUS / 3.0)
    shape = np.exp(np.float32(-0.5) * ((offsets - RADIUS) / sigma) ** 2)
    return (shape / np.sum(shape, dtype=np.float32)).astype(ml_dtypes.bfloat16).astype(np.float32)


def iota(shape, dim):
    return lax.broadcasted_iota(jnp.int32, shape, dim)


def band(source, target, scale=1.0):
    offset = jnp.abs(source - target)
    weights = jnp.zeros(offset.shape, jnp.float32)
    for distance, tap in enumerate(filter_taps()[RADIUS:]):
        weights = jnp.where(offset == distance, jnp.float32(scale * tap), weights)
    return weights


def difference(source, target):
    offset = source - target
    return jnp.where(offset == 1, 1.0, jnp.where(offset == -1, -1.0, 0.0)).astype(jnp.float32)


def dot(left, right):
    return jnp.dot(left, right, preferred_element_type=jnp.float32)


def reciprocal(value):
    guess = pl.reciprocal(value, approx=True)
    return guess * (2.0 - value * guess)


def halo_plane(lane, tile, depths):
    slot = lax.div(lane, SIDE)
    rest = jnp.where(slot == 0, 0, jnp.where(slot == 1, depths - 1, FAR))
    return jnp.where(tile < 2, 1 + SLOTS * tile + slot, rest)


def halo_column(lane, x, cols):
    place = lax.rem(lane, SIDE)
    return jnp.where(x == 0, cols - OWN + place, place - (SIDE - OWN))


def low_end(exchange):
    even = lax.rem(lax.axis_index("il"), 2) == 0
    return jnp.logical_not(even) if exchange == 0 else even


def tables_kernel(depths, lines_ref, diff_i_ref, diff_x_ref, smooth_ref, pack_h_ref, diff_h_ref, lines_e_ref, diff_e_ref, pick_ref):
    rows, cols = lines_ref.shape[0], diff_x_ref.shape[0]
    x, il, last = lax.axis_index("xl"), lax.axis_index("il"), lax.axis_size("il") - 1
    bf16 = jnp.bfloat16

    target, source = iota((rows, rows), 0), iota((rows, rows), 1)
    inner = (source > 0) & (source < rows - 1)
    lines_ref[...] = jnp.where(inner, band(source, target, 0.25), 0.0).astype(bf16)
    diff_i_ref[...] = difference(source, target).astype(bf16)
    span = EDGE * (depths - 2)
    target, source = iota((span, span), 0), iota((span, span), 1)
    depth = lax.div(source, EDGE) == lax.div(target, EDGE)
    target, source = lax.rem(target, EDGE), lax.rem(source, EDGE)
    diff_e_ref[...] = jnp.where(depth, difference(source, target), 0.0).astype(bf16)
    for exchange in range(2):
        low = low_end(exchange)
        source_at = jnp.where(low, source - REACH, rows - (EDGE - REACH) + source)
        target_at = jnp.where(low, target, rows - EDGE + target)
        first = jnp.where(low & (il > 0), -rows, 0)
        final = jnp.where(jnp.logical_not(low) & (il < last), 2 * rows, rows - 1)
        use = depth & (source_at >= first) & (source_at <= final) & ((source_at <= 0) | (source_at >= rows - 1))
        lines_e_ref[exchange] = jnp.where(use, band(source_at, target_at, 0.25), 0.0).astype(bf16)

    source, target = iota((cols, cols), 0), iota((cols, cols), 1)
    diff_x_ref[...] = difference(source, target).astype(bf16)
    moved = source == jnp.where(x == 0, cols - 1, 0)
    column = lax.rem(target + 128 * x, cols)
    smooth_ref[...] = jnp.where(moved, 0.0, band(source, column)).astype(bf16)
    source, target = iota((256, 256), 0), iota((256, 256), 1)
    place = lax.rem(source, SIDE)
    use = (lax.div(source, SIDE) == lax.div(target, SIDE)) & (place != jnp.where(x == 0, 0, SIDE - 1))
    column = jnp.where(x == 0, cols - SIDE, 0) + lax.rem(target, SIDE)
    pack_h_ref[...] = jnp.where(use, band(halo_column(place, x, cols), column), 0.0).astype(bf16)

    source, target = iota((128, 128), 0), iota((128, 128), 1)
    same = lax.rem(source, SIDE) == lax.rem(target, SIDE)
    across = difference(lax.rem(source, SIDE), lax.rem(target, SIDE))
    for group in range(2):
        centre = halo_plane(target, group, depths)
        for tile in range(TILES):
            plane = halo_plane(source, tile, depths)
            part, out = slice(128 * tile, 128 * (tile + 1)), 128 * group
            diff_h_ref[part, out : out + 128] = jnp.where(same, difference(plane, centre), 0.0).astype(bf16)
            diff_h_ref[part, 256 + out : 384 + out] = jnp.where(plane == centre, across, 0.0).astype(bf16)

    source, lane = iota((cols, 256), 0), iota((cols, 256), 1)
    place = lax.rem(lane, SIDE)
    low, high = place < SIDE - OWN, place >= OWN
    sent = jnp.where(x == 0, jnp.where(low, cols - (SIDE - OWN) + place, FAR), jnp.where(high, place - OWN, FAR))
    low, high = place < OWN, place >= SIDE - OWN
    kept = jnp.where(x == 0, jnp.where(low, cols - OWN + place, FAR), jnp.where(high, place - (SIDE - OWN), FAR))
    pick_ref[...] = jnp.where(source == jnp.where(lane < 128, sent, kept), 1.0, 0.0).astype(bf16)


def pack_kernel(vol_ref, pick_ref, copy_ref, send_ref, own_ref):
    depths, rows, cols = vol_ref.shape
    slot = lax.div(lax.rem(iota((rows, 256), 1), 128), SIDE)
    copy_ref[...] = vol_ref[...]
    picked = dot(vol_ref[...].reshape(depths * rows, cols), pick_ref[...])
    for tile in range(TILES):
        if tile < 2:
            planes = [(1 + SLOTS * tile + index, index) for index in range(SLOTS)]
        else:
            planes = [(0, 0), (depths - 1, 1)]
        packed = jnp.zeros((rows, 256), jnp.float32)
        for plane, index in planes:
            packed = jnp.where(slot == index, picked[rows * plane : rows * (plane + 1)], packed)
        packed = packed.astype(jnp.bfloat16)
        send_ref[tile] = packed[:, :128]
        own_ref[tile] = packed[:, 128:]


def rows_kernel(vol_ref, own_ref, side_ref, after_ref, halo_ref, ends_ref, packed_ref):
    depths, rows, cols = vol_ref.shape
    even = lax.rem(lax.axis_index("il"), 2) == 0

    def put(row, top, bottom):
        top, bottom = top[:REACH], bottom[EDGE - REACH :]
        lanes = top.shape[1]
        packed_ref[0, row : row + REACH, :lanes] = jnp.where(even, bottom, top)
        packed_ref[1, row : row + REACH, :lanes] = jnp.where(even, top, bottom)

    packed_ref[:, depths * REACH :, :] = jnp.zeros_like(packed_ref[:, depths * REACH :, :])
    for depth in range(depths):
        top = vol_ref[depth, :EDGE, :].astype(jnp.float32)
        bottom = vol_ref[depth, rows - EDGE :, :].astype(jnp.float32)
        put(REACH * depth, top, bottom)
    tiles = []
    for tile in range(TILES):
        merged = own_ref[tile].astype(jnp.float32) + side_ref[tile].astype(jnp.float32)
        halo_ref[:, 128 * tile : 128 * (tile + 1)] = merged.astype(jnp.bfloat16)
        tiles.append((merged[:EDGE], merged[rows - EDGE :]))
    tops = jnp.concatenate([tiles[0][0], tiles[1][0]], axis=1)
    bottoms = jnp.concatenate([tiles[0][1], tiles[1][1]], axis=1)
    put(REACH * depths, tops, bottoms)
    put(REACH * (depths + 1), *tiles[2])
    ends_ref[...] = packed_ref[...].astype(jnp.bfloat16)


def relay_kernel(ends_ref, after_ref, out_ref):
    out_ref[...] = ends_ref[1]


def moments(grad_i, grad_x, grad_z):
    terms = (
        grad_i * grad_i,
        grad_x * grad_x,
        grad_z * grad_z,
        grad_i * grad_x,
        grad_i * grad_z,
        grad_x * grad_z,
    )
    return [term.astype(jnp.bfloat16) for term in terms]


def store_chunks(summed, comp, inner_ref, part_ref):
    chunks = summed.shape[0] // EDGE
    for chunk in range(1, chunks - 1):
        inner_ref[chunk - 1, comp] = summed[EDGE * chunk : EDGE * (chunk + 1)].astype(jnp.bfloat16)
    part_ref[0, comp] = summed[:EDGE]
    part_ref[1, comp] = summed[EDGE * (chunks - 1) :]


def lines_kernel(vol_ref, lines_ref, diff_i_ref, diff_x_ref, inner_ref, part_ref, even_ref, odd_ref):
    own_lines(0, HEAD, vol_ref, lines_ref, diff_i_ref, diff_x_ref, inner_ref, part_ref, even_ref, odd_ref)


def more_lines_kernel(
    vol_ref, halo_ref, lines_ref, diff_i_ref, diff_x_ref, diff_h_ref, inner_in_ref, part_in_ref,
    inner_ref, part_ref, inner_h_ref, part_h_ref, even_ref, odd_ref,
):
    both = dot(halo_ref[...], diff_h_ref[...])
    grad_i = dot(diff_i_ref[...], halo_ref[:, :256])
    for comp, term in enumerate(moments(grad_i, both[:, 256:], both[:, :256])):
        store_chunks(dot(lines_ref[...], term), comp, inner_h_ref, part_h_ref)
    stop = vol_ref.shape[0] - 2
    own_lines(HEAD, stop, vol_ref, lines_ref, diff_i_ref, diff_x_ref, inner_ref, part_ref, even_ref, odd_ref)


def own_lines(first, stop, vol_ref, lines_ref, diff_i_ref, diff_x_ref, inner_ref, part_ref, even_ref, odd_ref):
    depths, rows, cols = vol_ref.shape

    def stage_moments(z, moments_ref):
        centre = vol_ref[pl.ds(z + 1, 2)]
        across = dot(centre.reshape(2 * rows, cols), diff_x_ref[...])
        for k in range(2):
            grad_i = dot(diff_i_ref[...], centre[k])
            grad_x = across[rows * k : rows * (k + 1)]
            grad_z = vol_ref[z + k + 2].astype(jnp.float32) - vol_ref[z + k].astype(jnp.float32)
            for comp, term in enumerate(moments(grad_i, grad_x, grad_z)):
                moments_ref[k, comp] = term

    def stage_lines(z, moments_ref):
        for k in range(2):
            for comp in range(6):
                store_chunks(dot(lines_ref[...], moments_ref[k, comp]), comp, inner_ref.at[z + k], part_ref.at[:, :, z + k])

    stage_moments(first, even_ref)

    def step(index, carry):
        z = first + 4 * index
        stage_moments(z + 2, odd_ref)
        stage_lines(z, even_ref)
        stage_moments(jnp.minimum(z + 4, stop - 2), even_ref)
        stage_lines(z + 2, odd_ref)
        return carry

    lax.fori_loop(0, (stop - first) // 4, step, 0)


def attributes(own, border, smooth_ref, store):
    x = lax.axis_index("xl")
    tensor = dot(own, smooth_ref[...])
    halves = (tensor[:, :128], tensor[:, 128:] + border)
    lanes = (pl.multiple_of(128 * x, 128), pl.multiple_of(128 - 128 * x, 128))
    for chunk in range(own.shape[0] // (6 * EDGE)):
        base = 6 * EDGE * chunk
        for half, lane in zip(halves, lanes):
            a, b, c, d, e, f = [half[base + EDGE * comp : base + EDGE * (comp + 1)] for comp in range(6)]
            low = c + 1e-6
            inverse = reciprocal(low)
            spread = (a - b) * (a - c) + (b - c) * (b - c) + 3.0 * (d * d + e * e + f * f)
            root = spread * lax.rsqrt(jnp.maximum(spread, TINY))
            store(chunk, pl.ds(lane, 128), (-e * inverse, -f * inverse, root * reciprocal(a + b + low)))


def border_of(packed, slot):
    base = jnp.where(lax.axis_index("xl") == 0, 128 - SIDE, 0)
    moved = pltpu.roll(packed, lax.rem(base - SIDE * slot + 128, 128), 1)
    return jnp.where(lax.div(iota(packed.shape, 1), SIDE) == lax.div(base, SIDE), moved, 0.0)


def inner_kernel(
    inner_ref, inner_h_ref, smooth_ref, pack_h_ref, dip_i_ref, dip_x_ref, plan_ref, later_ref, border_ref, out_ref, sems
):
    count, chunks = inner_ref.shape[:2]
    half, inner = count // 2, EDGE * chunks
    targets = (dip_i_ref, dip_x_ref, plan_ref)
    border_ref[...] = dot(inner_h_ref[...].reshape(6 * inner, 256), pack_h_ref[...])

    def finish(k, target_ref):
        for group in range(2):

            def store(chunk, lanes, values):
                for n, value in enumerate(values):
                    target_ref[n, group, k % (half // 2), EDGE * chunk : EDGE * (chunk + 1), lanes] = value

            border = border_of(border_ref[:, 128 * group : 128 * (group + 1)], k)
            attributes(inner_ref[half * group + k].reshape(6 * inner, 256), border, smooth_ref, store)

    def copies(pair):
        return [
            pltpu.make_async_copy(
                out_ref.at[n, group, pl.ds(2 * pair, 2)],
                target.at[pl.ds(half * group + 2 * pair, 2), pl.ds(EDGE, inner)],
                sems.at[pair, group, n],
            )
            for group in range(2)
            for n, target in enumerate(targets)
        ]

    def first(pair, carry):
        finish(2 * pair, out_ref)
        finish(2 * pair + 1, out_ref)
        for copy in copies(pair):
            copy.start()
        return carry

    def second(pair, carry):
        finish(2 * pair, later_ref)
        finish(2 * pair + 1, later_ref)
        return carry

    lax.fori_loop(0, half // 4, first, 0)
    lax.fori_loop(half // 4, half // 2, second, 0)
    for pair in range(half // 4):
        for copy in copies(pair):
            copy.wait()


def end_kernel(
    exchange, vol_ref, halo_ref, rows_ref, part_ref, part_h_ref,
    smooth_ref, pack_h_ref, diff_x_ref, diff_h_ref, lines_e_ref, diff_e_ref, done_ref, *refs,
):
    last = exchange == 1
    targets, refs = refs[3:6], refs[6:]
    if last:
        packed_ref, block_ref, block_h_ref, border_ref, edge_ref, out_ref, done_sems, sems = refs
    else:
        out_ref, packed_ref, block_ref, block_h_ref, border_ref, edge_ref, done_sems = refs
    depths, rows, cols = vol_ref.shape
    count, half = depths - 2, (depths - 2) // 2
    bf16, f32 = jnp.bfloat16, jnp.float32
    low = low_end(exchange)
    end = jnp.where(low, 0, 1)
    start = pl.multiple_of(jnp.where(low, 0, rows - EDGE), EDGE)
    other = pl.multiple_of(jnp.where(low, rows - EDGE, 0), EDGE)
    finished = []
    for n, target in enumerate(targets):
        for group in range(2):
            if last:
                source = done_ref.at[n, pl.ds(half * group, half)]
                place = target.at[pl.ds(half * group, half), pl.ds(other, EDGE)]
            else:
                source = done_ref.at[n, group]
                place = target.at[pl.ds(half * group + half // 2, half // 2), pl.ds(EDGE, rows - 2 * EDGE)]
            finished.append(pltpu.make_async_copy(source, place, done_sems.at[n, group]))
    for copy in finished:
        copy.start()

    packed_ref[:8] = jnp.zeros_like(packed_ref[:8])
    if last:
        il = lax.axis_index("il")
        outside = (low & (il == 0)) | (jnp.logical_not(low) & (il == lax.axis_size("il") - 1))
        packed_ref[8:] = jnp.where(outside, 0.0, rows_ref[...].astype(f32))
    else:
        packed_ref[8:] = rows_ref[0].astype(f32)

    def joined(row, own):
        lanes = own.shape[1]
        before = packed_ref[8 + row : 8 + row + EDGE, :lanes]
        after = packed_ref[8 + row - (EDGE - REACH) : 8 + row + REACH, :lanes]
        own = own.astype(f32)
        place = iota(own.shape, 0)
        first = jnp.where(place < REACH, before, pltpu.roll(own, REACH, 0))
        second = jnp.where(place < EDGE - REACH, pltpu.roll(own, EDGE - REACH, 0), after)
        return jnp.where(low, first, second).astype(bf16)

    for depth in range(depths):
        block_ref[depth] = joined(REACH * depth, vol_ref[depth, pl.ds(start, EDGE)])
    own_h = halo_ref[pl.ds(start, EDGE)]
    block_h_ref[:, :256] = joined(REACH * depths, own_h[:, :256])
    block_h_ref[:, 256:] = joined(REACH * (depths + 1), own_h[:, 256:])

    both = dot(block_h_ref[...], diff_h_ref[...])
    grad_i = dot(diff_e_ref[:EDGE, :EDGE], block_h_ref[:, :256])
    lined_h = []
    for comp, term in enumerate(moments(grad_i, both[:, 256:], both[:, :256])):
        summed = part_h_ref[end, comp] + dot(lines_e_ref[exchange, :EDGE, :EDGE], term)
        lined_h.append(summed.astype(bf16))
    border_ref[...] = dot(jnp.concatenate(lined_h, axis=0), pack_h_ref[...])

    centre = block_ref[1 : count + 1].reshape(count * EDGE, cols)
    grad_i = dot(diff_e_ref[...], centre)
    grad_x = dot(centre, diff_x_ref[...])
    grad_z = block_ref[2:].astype(f32) - block_ref[:count].astype(f32)
    for comp, term in enumerate(moments(grad_i, grad_x, grad_z.reshape(count * EDGE, cols))):
        outer = dot(lines_e_ref[exchange], term)
        summed = part_ref[end, comp] + outer.reshape(count, EDGE, cols)
        edge_ref[:, comp] = summed.astype(bf16)

    copies = []
    for pair in range(half // PART):
        own, border, places = [], [], []
        for group in range(2):
            for parity in range(PART):
                k = PART * pair + parity
                places.append(half * group + k)
                own.append(edge_ref[half * group + k].reshape(6 * EDGE, cols))
                border.append(border_of(border_ref[:, 128 * group : 128 * (group + 1)], k))

        def store(chunk, lanes, values):
            for n, value in enumerate(values):
                out_ref[n, places[chunk], :, lanes] = value

        attributes(jnp.concatenate(own, axis=0), jnp.concatenate(border, axis=0), smooth_ref, store)
        if last:
            for group in range(2):
                depth = pl.ds(half * group + PART * pair, PART)
                for n, target in enumerate(targets):
                    copy = pltpu.make_async_copy(
                        out_ref.at[n, depth], target.at[depth, pl.ds(start, EDGE)], sems.at[pair, group, n]
                    )
                    copy.start()
                    copies.append(copy)
    for copy in finished + copies:
        copy.wait()


def call(name, kernel, outs, scratch, operands, in_specs=None, out_specs=None, flops=0, limit=16, aliases={}):
    return pl.pallas_call(
        kernel,
        out_shape=tuple(jax.ShapeDtypeStruct(*out) for out in outs),
        in_specs=in_specs or [WHOLE] * len(operands),
        out_specs=out_specs or (WHOLE,) * len(outs),
        scratch_shapes=scratch,
        compiler_params=pltpu.CompilerParams(vmem_limit_bytes=limit << 20),
        name=name,
        input_output_aliases=aliases,
        cost_estimate=pl.CostEstimate(flops=flops, bytes_accessed=0, transcendentals=0),
    )(*operands)


def body(volume):
    depths, rows, cols = volume.shape
    il, xl = lax.axis_size("il"), lax.axis_size("xl")
    count = depths - 2
    assert xl == 2 and il % 2 == 0 and count == 2 * SLOTS and cols == 256
    bf16, f32 = jnp.bfloat16, jnp.float32
    half = count // 2
    work = half * 1024 * 2 * 256 * 256
    packed_rows = -(-REACH * (depths + 2) // 16) * 16

    span = EDGE * count
    lines, diff_i, diff_x, smooth, pack_h, diff_h, lines_e, diff_e, pick = call(
        "tables_kernel",
        lambda *refs: tables_kernel(depths, *refs),
        [
            ((rows, rows), bf16),
            ((rows, rows), bf16),
            ((cols, cols), bf16),
            ((cols, cols), bf16),
            ((256, 256), bf16),
            ((128 * TILES, 512), bf16),
            ((2, span, span), bf16),
            ((span, span), bf16),
            ((cols, 256), bf16),
        ],
        [],
        [],
        flops=work,
    )
    halo_tile = ((TILES, rows, 128), bf16)
    vol, send, own = call("pack_kernel", pack_kernel, [(volume.shape, bf16), halo_tile, halo_tile], [], [volume, pick])
    side = lax.ppermute(send, "xl", [(0, 1), (1, 0)])
    chunks = rows // EDGE - 2
    lined = [((count, chunks, 6, EDGE, cols), bf16), ((2, 6, count, EDGE, cols), f32)]
    moment_slots = [pltpu.VMEM((2, 6, rows, cols), bf16)] * 2
    inner, part = call("lines_kernel", lines_kernel, lined, moment_slots, [vol, lines, diff_i, diff_x], flops=work // 4)
    halo, ends = call(
        "rows_kernel",
        rows_kernel,
        [((rows, 128 * TILES), bf16), ((2, packed_rows, cols), bf16)],
        [pltpu.VMEM((2, packed_rows, cols), f32)],
        [vol, own, side, part],
        in_specs=[WHOLE] * 3 + [ANYWHERE],
    )
    ends_in = lax.ppermute(ends, "il", [(i, i ^ 1) for i in range(il)])
    operands = [vol, halo, lines, diff_i, diff_x, diff_h, inner, part]
    inner, part, inner_h, part_h = call(
        "more_lines_kernel",
        more_lines_kernel,
        lined + [((chunks, 6, EDGE, 256), bf16), ((2, 6, EDGE, 256), f32)],
        moment_slots,
        operands,
        flops=2 * work,
        aliases={len(operands) - 2 + n: n for n in range(2)},
    )
    outs = [((count, rows, cols), f32)] * 3
    saved = (3, 2, half // 2, EDGE * chunks, cols)
    *outs_in, done = call(
        "inner_kernel",
        inner_kernel,
        outs + [(saved, f32)],
        [
            pltpu.VMEM((6 * EDGE * chunks, 256), f32),
            pltpu.VMEM(saved, f32),
            pltpu.SemaphoreType.DMA((half // 4, 2, 3)),
        ],
        [inner, inner_h, smooth, pack_h],
        out_specs=(IN_HBM,) * 3 + (WHOLE,),
        flops=2 * work,
    )
    (relayed,) = call(
        "relay_kernel", relay_kernel, [((packed_rows, cols), bf16)], [], [ends_in, done], in_specs=[WHOLE, ANYWHERE]
    )
    onward = [(i, i + 2) for i in range(0, il - 2, 2)] + [(il - 2, il - 1)]
    onward += [(i, i - 2) for i in range(3, il, 2)] + [(1, 0)]
    relayed_in = lax.ppermute(relayed, "il", onward)

    end_rows = (3, count, EDGE, cols)
    tables = [smooth, pack_h, diff_x, diff_h, lines_e, diff_e]
    scratch = [
        pltpu.VMEM((8 + packed_rows, cols), f32),
        pltpu.VMEM((depths, EDGE, cols), bf16),
        pltpu.VMEM((EDGE, 128 * TILES), bf16),
        pltpu.VMEM((6 * EDGE, 256), f32),
        pltpu.VMEM((count, 6, EDGE, cols), bf16),
    ]
    sems = pltpu.SemaphoreType.DMA((3, 2))
    operands = [vol, halo, ends_in, part, part_h, *tables, done]
    *outs_in, done = call(
        "near_end_kernel",
        lambda *refs: end_kernel(0, *refs),
        outs + [(end_rows, f32)],
        scratch + [sems],
        operands + outs_in,
        in_specs=[WHOLE] * len(operands) + [IN_HBM] * 3,
        out_specs=(IN_HBM,) * 3 + (WHOLE,),
        flops=work,
        aliases={len(operands) + n: n for n in range(3)},
    )
    operands = [vol, halo, relayed_in, part, part_h, *tables, done]
    return call(
        "far_end_kernel",
        lambda *refs: end_kernel(1, *refs),
        outs,
        scratch + [pltpu.VMEM(end_rows, f32), sems, pltpu.SemaphoreType.DMA((half // PART, 2, 3))],
        operands + outs_in,
        in_specs=[WHOLE] * len(operands) + [IN_HBM] * 3,
        out_specs=(IN_HBM,) * 3,
        flops=work,
        aliases={len(operands) + n: n for n in range(3)},
    )


def solution(mesh):
    spec = P(None, ("parts", "il"), "xl")
    return jax.shard_map(body, mesh=mesh, in_specs=(spec,), out_specs=(spec,) * 3, check_vma=False)
```

```python
import jax
import jax.numpy as jnp
import ml_dtypes
import numpy as np
from jax import lax
from jax.experimental import pallas as pl
from jax.experimental.pallas import tpu as pltpu
from jax.sharding import PartitionSpec as P

RADIUS = 9
REACH = RADIUS + 1
SIDE = 16
SLOTS = 8
TILES = 3
EDGE = 16
OWN = 2
TINY = float(np.finfo(np.float32).tiny)
HEAD = 2
AHEAD = 2
FAR = -1000
WHOLE = pl.BlockSpec(memory_space=pltpu.VMEM)
IN_HBM = pl.BlockSpec(memory_space=pltpu.HBM)
ANYWHERE = pl.BlockSpec(memory_space=pl.ANY)


def filter_taps():
    offsets = np.arange(2 * RADIUS + 1).astype(np.float32)
    sigma = np.float32(RADIUS / 3.0)
    shape = np.exp(np.float32(-0.5) * ((offsets - RADIUS) / sigma) ** 2)
    return (shape / np.sum(shape, dtype=np.float32)).astype(ml_dtypes.bfloat16).astype(np.float32)


def iota(shape, dim):
    return lax.broadcasted_iota(jnp.int32, shape, dim)


def band(source, target, scale=1.0):
    offset = jnp.abs(source - target)
    weights = jnp.zeros(offset.shape, jnp.float32)
    for distance, tap in enumerate(filter_taps()[RADIUS:]):
        weights = jnp.where(offset == distance, jnp.float32(scale * tap), weights)
    return weights


def difference(source, target):
    offset = source - target
    return jnp.where(offset == 1, 1.0, jnp.where(offset == -1, -1.0, 0.0)).astype(jnp.float32)


def dot(left, right):
    return jnp.dot(left, right, preferred_element_type=jnp.float32)


def reciprocal(value):
    guess = pl.reciprocal(value, approx=True)
    return guess * (2.0 - value * guess)


def halo_plane(lane, tile, depths):
    slot = lax.div(lane, SIDE)
    rest = jnp.where(slot == 0, 0, jnp.where(slot == 1, depths - 1, FAR))
    return jnp.where(tile < 2, 1 + SLOTS * tile + slot, rest)


def halo_column(lane, x, cols):
    place = lax.rem(lane, SIDE)
    return jnp.where(x == 0, cols - OWN + place, place - (SIDE - OWN))


def low_end(exchange):
    even = lax.rem(lax.axis_index("il"), 2) == 0
    return jnp.logical_not(even) if exchange == 0 else even


def tables_kernel(depths, lines_ref, diff_i_ref, diff_x_ref, smooth_ref, pack_h_ref, diff_h_ref, lines_e_ref, diff_e_ref, pick_ref):
    rows, cols = lines_ref.shape[0], diff_x_ref.shape[0]
    x, il, last = lax.axis_index("xl"), lax.axis_index("il"), lax.axis_size("il") - 1
    bf16 = jnp.bfloat16

    target, source = iota((rows, rows), 0), iota((rows, rows), 1)
    inner = (source > 0) & (source < rows - 1)
    lines_ref[...] = jnp.where(inner, band(source, target, 0.25), 0.0).astype(bf16)
    diff_i_ref[...] = difference(source, target).astype(bf16)
    span = EDGE * (depths - 2)
    target, source = iota((span, span), 0), iota((span, span), 1)
    depth = lax.div(source, EDGE) == lax.div(target, EDGE)
    target, source = lax.rem(target, EDGE), lax.rem(source, EDGE)
    diff_e_ref[...] = jnp.where(depth, difference(source, target), 0.0).astype(bf16)
    for exchange in range(2):
        low = low_end(exchange)
        source_at = jnp.where(low, source - REACH, rows - (EDGE - REACH) + source)
        target_at = jnp.where(low, target, rows - EDGE + target)
        first = jnp.where(low & (il > 0), -rows, 0)
        final = jnp.where(jnp.logical_not(low) & (il < last), 2 * rows, rows - 1)
        use = depth & (source_at >= first) & (source_at <= final) & ((source_at <= 0) | (source_at >= rows - 1))
        lines_e_ref[exchange] = jnp.where(use, band(source_at, target_at, 0.25), 0.0).astype(bf16)

    source, target = iota((cols, cols), 0), iota((cols, cols), 1)
    diff_x_ref[...] = difference(source, target).astype(bf16)
    moved = source == jnp.where(x == 0, cols - 1, 0)
    column = lax.rem(target + 128 * x, cols)
    smooth_ref[...] = jnp.where(moved, 0.0, band(source, column)).astype(bf16)
    source, target = iota((256, 256), 0), iota((256, 256), 1)
    place = lax.rem(source, SIDE)
    use = (lax.div(source, SIDE) == lax.div(target, SIDE)) & (place != jnp.where(x == 0, 0, SIDE - 1))
    column = jnp.where(x == 0, cols - SIDE, 0) + lax.rem(target, SIDE)
    pack_h_ref[...] = jnp.where(use, band(halo_column(place, x, cols), column), 0.0).astype(bf16)

    source, target = iota((128, 128), 0), iota((128, 128), 1)
    same = lax.rem(source, SIDE) == lax.rem(target, SIDE)
    across = difference(lax.rem(source, SIDE), lax.rem(target, SIDE))
    for group in range(2):
        centre = halo_plane(target, group, depths)
        for tile in range(TILES):
            plane = halo_plane(source, tile, depths)
            part, out = slice(128 * tile, 128 * (tile + 1)), 128 * group
            diff_h_ref[part, out : out + 128] = jnp.where(same, difference(plane, centre), 0.0).astype(bf16)
            diff_h_ref[part, 256 + out : 384 + out] = jnp.where(plane == centre, across, 0.0).astype(bf16)

    source, lane = iota((cols, 256), 0), iota((cols, 256), 1)
    place = lax.rem(lane, SIDE)
    low, high = place < SIDE - OWN, place >= OWN
    sent = jnp.where(x == 0, jnp.where(low, cols - (SIDE - OWN) + place, FAR), jnp.where(high, place - OWN, FAR))
    low, high = place < OWN, place >= SIDE - OWN
    kept = jnp.where(x == 0, jnp.where(low, cols - OWN + place, FAR), jnp.where(high, place - (SIDE - OWN), FAR))
    pick_ref[...] = jnp.where(source == jnp.where(lane < 128, sent, kept), 1.0, 0.0).astype(bf16)


def pack_kernel(vol_ref, pick_ref, copy_ref, send_ref, own_ref):
    depths, rows, cols = vol_ref.shape
    slot = lax.div(lax.rem(iota((rows, 256), 1), 128), SIDE)
    copy_ref[...] = vol_ref[...]
    picked = dot(vol_ref[...].reshape(depths * rows, cols), pick_ref[...])
    for tile in range(TILES):
        if tile < 2:
            planes = [(1 + SLOTS * tile + index, index) for index in range(SLOTS)]
        else:
            planes = [(0, 0), (depths - 1, 1)]
        packed = jnp.zeros((rows, 256), jnp.float32)
        for plane, index in planes:
            packed = jnp.where(slot == index, picked[rows * plane : rows * (plane + 1)], packed)
        packed = packed.astype(jnp.bfloat16)
        send_ref[tile] = packed[:, :128]
        own_ref[tile] = packed[:, 128:]


def rows_kernel(vol_ref, own_ref, side_ref, after_ref, halo_ref, near_ref, far_ref, packed_ref):
    depths, rows, cols = vol_ref.shape
    even = lax.rem(lax.axis_index("il"), 2) == 0

    def put(row, top, bottom):
        top, bottom = top[:REACH], bottom[EDGE - REACH :]
        lanes = top.shape[1]
        packed_ref[0, row : row + REACH, :lanes] = jnp.where(even, bottom, top)
        packed_ref[1, row : row + REACH, :lanes] = jnp.where(even, top, bottom)

    packed_ref[:, depths * REACH :, :] = jnp.zeros_like(packed_ref[:, depths * REACH :, :])
    for depth in range(depths):
        top = vol_ref[depth, :EDGE, :].astype(jnp.float32)
        bottom = vol_ref[depth, rows - EDGE :, :].astype(jnp.float32)
        put(REACH * depth, top, bottom)
    tiles = []
    for tile in range(TILES):
        merged = own_ref[tile].astype(jnp.float32) + side_ref[tile].astype(jnp.float32)
        halo_ref[:, 128 * tile : 128 * (tile + 1)] = merged.astype(jnp.bfloat16)
        tiles.append((merged[:EDGE], merged[rows - EDGE :]))
    tops = jnp.concatenate([tiles[0][0], tiles[1][0]], axis=1)
    bottoms = jnp.concatenate([tiles[0][1], tiles[1][1]], axis=1)
    put(REACH * depths, tops, bottoms)
    put(REACH * (depths + 1), *tiles[2])
    near_ref[...] = packed_ref[0].astype(jnp.bfloat16)
    far_ref[...] = packed_ref[1].astype(jnp.bfloat16)


def relay_kernel(rows_ref, after_ref, out_ref):
    out_ref[...] = rows_ref[...]


def moments(grad_i, grad_x, grad_z):
    terms = (
        grad_i * grad_i,
        grad_x * grad_x,
        grad_z * grad_z,
        grad_i * grad_x,
        grad_i * grad_z,
        grad_x * grad_z,
    )
    return [term.astype(jnp.bfloat16) for term in terms]


def store_chunks(summed, comp, inner_ref, part_ref):
    chunks = summed.shape[0] // EDGE
    for chunk in range(1, chunks - 1):
        inner_ref[chunk - 1, comp] = summed[EDGE * chunk : EDGE * (chunk + 1)].astype(jnp.bfloat16)
    part_ref[0, comp] = summed[:EDGE]
    part_ref[1, comp] = summed[EDGE * (chunks - 1) :]


def make_moments(pair, vol_ref, diff_i_ref, diff_x_ref, moments_ref):
    depths, rows, cols = vol_ref.shape
    planes = [vol_ref[2 * pair + k] for k in range(4)]
    across = dot(jnp.concatenate(planes[1:3], axis=0), diff_x_ref[...])
    for k in range(2):
        grad_i = dot(diff_i_ref[...], planes[k + 1])
        grad_x = across[rows * k : rows * (k + 1)]
        grad_z = planes[k + 2].astype(jnp.float32) - planes[k].astype(jnp.float32)
        for comp, term in enumerate(moments(grad_i, grad_x, grad_z)):
            moments_ref[k, comp] = term


def make_lines(pair, lines_ref, moments_ref, inner_ref, part_ref):
    for k in range(2):
        z = 2 * pair + k
        for comp in range(6):
            store_chunks(dot(lines_ref[...], moments_ref[k, comp]), comp, inner_ref.at[z], part_ref.at[:, :, z])


def lines_kernel(vol_ref, lines_ref, diff_i_ref, diff_x_ref, inner_ref, part_ref, even_ref, odd_ref):
    slots = (even_ref, odd_ref)
    for pair in range(HEAD):
        make_moments(pair, vol_ref, diff_i_ref, diff_x_ref, slots[pair % 2])
        make_lines(pair, lines_ref, slots[pair % 2], inner_ref, part_ref)


def attributes(own, border, smooth_ref, store):
    x = lax.axis_index("xl")
    tensor = dot(own, smooth_ref[...])
    halves = (tensor[:, :128], tensor[:, 128:] + border)
    lanes = (pl.multiple_of(128 * x, 128), pl.multiple_of(128 - 128 * x, 128))
    for chunk in range(own.shape[0] // (6 * EDGE)):
        base = 6 * EDGE * chunk
        for half, lane in zip(halves, lanes):
            a, b, c, d, e, f = [half[base + EDGE * comp : base + EDGE * (comp + 1)] for comp in range(6)]
            low = c + 1e-6
            inverse = reciprocal(low)
            spread = (a - b) * (a - c) + (b - c) * (b - c) + 3.0 * (d * d + e * e + f * f)
            root = spread * lax.rsqrt(jnp.maximum(spread, TINY))
            store(chunk, pl.ds(lane, 128), (-e * inverse, -f * inverse, root * reciprocal(a + b + low)))


def border_of(packed, slot):
    base = jnp.where(lax.axis_index("xl") == 0, 128 - SIDE, 0)
    moved = pltpu.roll(packed, lax.rem(base - SIDE * slot + 128, 128), 1)
    return jnp.where(lax.div(iota(packed.shape, 1), SIDE) == lax.div(base, SIDE), moved, 0.0)


def own_kernel(
    stage, vol_ref, lines_ref, diff_i_ref, diff_x_ref, smooth_ref, halo_ref, diff_h_ref, pack_h_ref,
    inner_in_ref, part_in_ref, *refs,
):
    if stage == 0:
        inner_ref, part_ref, *targets, later_ref, part_h_ref, border_ref, even_ref, odd_ref, out_ref, sems = refs
        both = dot(halo_ref[...], diff_h_ref[...])
        grad_i = dot(diff_i_ref[...], halo_ref[:, :256])
        lined_h = [[] for chunk in range(inner_ref.shape[1])]
        for comp, term in enumerate(moments(grad_i, both[:, 256:], both[:, :256])):
            summed = dot(lines_ref[...], term)
            for chunk, parts in enumerate(lined_h):
                parts.append(summed[EDGE * (chunk + 1) : EDGE * (chunk + 2)].astype(jnp.bfloat16))
            part_h_ref[0, comp] = summed[:EDGE]
            part_h_ref[1, comp] = summed[EDGE * (len(lined_h) + 1) :]
        border_ref[...] = dot(jnp.concatenate(sum(lined_h, []), axis=0), pack_h_ref[...])
        finished = []
    else:
        border_ref, done_ref, *refs = refs
        inner_ref, part_ref, *targets, later_ref, even_ref, odd_ref, out_ref, sems, done_sems = refs[3:]
        finished = []
    count, chunks = inner_ref.shape[:2]
    pairs, inner = count // 4, EDGE * chunks
    slots = (even_ref, odd_ref)

    def place(target, pair):
        return target.at[pl.ds(2 * pair, 2), pl.ds(EDGE, inner)]

    if stage == 1:
        for n, target in enumerate(targets):
            finished.append(pltpu.make_async_copy(done_ref.at[n], place(target, pairs - 1), done_sems.at[n]))
            finished[-1].start()

    ahead = list(range(HEAD, pairs + AHEAD) if stage == 0 else range(pairs + AHEAD, 2 * pairs))
    for step in range(pairs):
        pair = pairs * stage + step
        todo = ahead[step : step + 1]
        for q in todo:
            make_moments(q, vol_ref, diff_i_ref, diff_x_ref, slots[q % 2])
        for k in range(2):
            z = 2 * pair + k

            def store(chunk, lanes, values):
                rows = slice(EDGE * chunk, EDGE * (chunk + 1))
                for n, value in enumerate(values):
                    if step == pairs - 1:
                        later_ref[n, k, rows, lanes] = value
                    else:
                        out_ref[n, 2 * step + k, rows, lanes] = value

            border = border_of(border_ref[:, 128 * stage : 128 * (stage + 1)], z % SLOTS)
            attributes(inner_ref[z].reshape(6 * inner, 256), border, smooth_ref, store)
        for q in todo:
            make_lines(q, lines_ref, slots[q % 2], inner_ref, part_ref)
        if step < pairs - 1:
            for n, target in enumerate(targets):
                source = out_ref.at[n, pl.ds(2 * step, 2)]
                finished.append(pltpu.make_async_copy(source, place(target, pair), sems.at[step, n]))
                finished[-1].start()
    for copy in finished:
        copy.wait()


def end_kernel(
    exchange, vol_ref, halo_ref, rows_ref, part_ref, part_h_ref,
    smooth_ref, pack_h_ref, diff_x_ref, diff_h_ref, lines_e_ref, diff_e_ref, done_ref, *refs,
):
    last = exchange == 1
    targets, refs = refs[3:6], refs[6:]
    if last:
        packed_ref, block_ref, block_h_ref, border_ref, edge_ref, out_ref, done_sems, sems = refs
    else:
        out_ref, packed_ref, block_ref, block_h_ref, border_ref, edge_ref, done_sems = refs
    depths, rows, cols = vol_ref.shape
    count, half = depths - 2, (depths - 2) // 2
    bf16, f32 = jnp.bfloat16, jnp.float32
    low = low_end(exchange)
    end = jnp.where(low, 0, 1)
    start = pl.multiple_of(jnp.where(low, 0, rows - EDGE), EDGE)
    other = pl.multiple_of(jnp.where(low, rows - EDGE, 0), EDGE)
    finished = []
    for n, target in enumerate(targets):
        if last:
            place = target.at[:, pl.ds(other, EDGE)]
        else:
            place = target.at[pl.ds(count - 2, 2), pl.ds(EDGE, rows - 2 * EDGE)]
        finished.append(pltpu.make_async_copy(done_ref.at[n], place, done_sems.at[n]))
    for copy in finished:
        copy.start()

    packed_ref[:8] = jnp.zeros_like(packed_ref[:8])
    if last:
        il = lax.axis_index("il")
        outside = (low & (il == 0)) | (jnp.logical_not(low) & (il == lax.axis_size("il") - 1))
        packed_ref[8:] = jnp.where(outside, 0.0, rows_ref[...].astype(f32))
    else:
        packed_ref[8:] = rows_ref[...].astype(f32)

    def joined(row, own):
        lanes = own.shape[1]
        before = packed_ref[8 + row : 8 + row + EDGE, :lanes]
        after = packed_ref[8 + row - (EDGE - REACH) : 8 + row + REACH, :lanes]
        own = own.astype(f32)
        place = iota(own.shape, 0)
        first = jnp.where(place < REACH, before, pltpu.roll(own, REACH, 0))
        second = jnp.where(place < EDGE - REACH, pltpu.roll(own, EDGE - REACH, 0), after)
        return jnp.where(low, first, second).astype(bf16)

    for depth in range(depths):
        block_ref[depth] = joined(REACH * depth, vol_ref[depth, pl.ds(start, EDGE)])
    own_h = halo_ref[pl.ds(start, EDGE)]
    block_h_ref[:, :256] = joined(REACH * depths, own_h[:, :256])
    block_h_ref[:, 256:] = joined(REACH * (depths + 1), own_h[:, 256:])

    both = dot(block_h_ref[...], diff_h_ref[...])
    grad_i = dot(diff_e_ref[:EDGE, :EDGE], block_h_ref[:, :256])
    lined_h = []
    for comp, term in enumerate(moments(grad_i, both[:, 256:], both[:, :256])):
        summed = part_h_ref[end, comp] + dot(lines_e_ref[exchange, :EDGE, :EDGE], term)
        lined_h.append(summed.astype(bf16))
    border_ref[...] = dot(jnp.concatenate(lined_h, axis=0), pack_h_ref[...])

    span = EDGE * half
    copies = []
    for group in range(2):
        first = half * group
        centre = block_ref[first + 1 : first + half + 1].reshape(span, cols)
        grad_i = dot(diff_e_ref[:span, :span], centre)
        grad_x = dot(centre, diff_x_ref[...])
        grad_z = block_ref[first + 2 : first + half + 2].astype(f32) - block_ref[first : first + half].astype(f32)
        for comp, term in enumerate(moments(grad_i, grad_x, grad_z.reshape(span, cols))):
            outer = dot(lines_e_ref[exchange, :span, :span], term)
            summed = part_ref[end, comp, first : first + half] + outer.reshape(half, EDGE, cols)
            edge_ref[first : first + half, comp] = summed.astype(bf16)
    for group in range(2):
        first = half * group
        border = [border_of(border_ref[:, 128 * group : 128 * (group + 1)], k) for k in range(half)]

        def store(chunk, lanes, values):
            for n, value in enumerate(values):
                out_ref[n, first + chunk, :, lanes] = value

        own = edge_ref[first : first + half].reshape(6 * span, cols)
        attributes(own, jnp.concatenate(border, axis=0), smooth_ref, store)
        if last:
            depth = pl.ds(first, half)
            for n, target in enumerate(targets):
                copy = pltpu.make_async_copy(out_ref.at[n, depth], target.at[depth, pl.ds(start, EDGE)], sems.at[group, n])
                copy.start()
                copies.append(copy)
    for copy in finished + copies:
        copy.wait()


def call(name, kernel, outs, scratch, operands, in_specs=None, out_specs=None, flops=0, limit=16, aliases={}):
    return pl.pallas_call(
        kernel,
        out_shape=tuple(jax.ShapeDtypeStruct(*out) for out in outs),
        in_specs=in_specs or [WHOLE] * len(operands),
        out_specs=out_specs or (WHOLE,) * len(outs),
        scratch_shapes=scratch,
        compiler_params=pltpu.CompilerParams(vmem_limit_bytes=limit << 20),
        name=name,
        input_output_aliases=aliases,
        cost_estimate=pl.CostEstimate(flops=flops, bytes_accessed=0, transcendentals=0),
    )(*operands)


def body(volume):
    depths, rows, cols = volume.shape
    il, xl = lax.axis_size("il"), lax.axis_size("xl")
    count = depths - 2
    assert xl == 2 and il % 2 == 0 and count == 2 * SLOTS and cols == 256
    bf16, f32 = jnp.bfloat16, jnp.float32
    half = count // 2
    work = half * 1024 * 2 * 256 * 256
    packed_rows = -(-REACH * (depths + 2) // 16) * 16

    span = EDGE * count
    lines, diff_i, diff_x, smooth, pack_h, diff_h, lines_e, diff_e, pick = call(
        "tables_kernel",
        lambda *refs: tables_kernel(depths, *refs),
        [
            ((rows, rows), bf16),
            ((rows, rows), bf16),
            ((cols, cols), bf16),
            ((cols, cols), bf16),
            ((256, 256), bf16),
            ((128 * TILES, 512), bf16),
            ((2, span, span), bf16),
            ((span, span), bf16),
            ((cols, 256), bf16),
        ],
        [],
        [],
        flops=work,
    )
    halo_tile = ((TILES, rows, 128), bf16)
    vol, send, own = call("pack_kernel", pack_kernel, [(volume.shape, bf16), halo_tile, halo_tile], [], [volume, pick])
    side = lax.ppermute(send, "xl", [(0, 1), (1, 0)])
    chunks = rows // EDGE - 2
    lined = [((count, chunks, 6, EDGE, cols), bf16), ((2, 6, count, EDGE, cols), f32)]
    moment_slots = [pltpu.VMEM((2, 6, rows, cols), bf16)] * 2
    inner, part = call("lines_kernel", lines_kernel, lined, moment_slots, [vol, lines, diff_i, diff_x], flops=work // 4)
    packed = ((packed_rows, cols), bf16)
    halo, near, far = call(
        "rows_kernel",
        rows_kernel,
        [((rows, 128 * TILES), bf16), packed, packed],
        [pltpu.VMEM((2, packed_rows, cols), f32)],
        [vol, own, side, part],
        in_specs=[WHOLE] * 3 + [ANYWHERE],
    )
    swap = [(i, i ^ 1) for i in range(il)]
    onward = [(i, i + 2) for i in range(0, il - 2, 2)] + [(il - 2, il - 1)]
    onward += [(i, i - 2) for i in range(3, il, 2)] + [(1, 0)]
    far_in = lax.ppermute(far, "il", swap)
    near_in = lax.ppermute(near, "il", swap)

    outs = [((count, rows, cols), f32)] * 3
    saved = ((3, 2, EDGE * chunks, cols), f32)
    border = ((6 * EDGE * chunks, 256), f32)
    ready = [((3, count // 2 - 2, EDGE * chunks, cols), f32)]
    own_scratch = moment_slots + [pltpu.VMEM(*ready[0]), pltpu.SemaphoreType.DMA((count // 4 - 1, 3))]
    shared = [vol, lines, diff_i, diff_x, smooth, halo, diff_h, pack_h]
    inner, part, *outs_in, done, part_h, border = call(
        "first_own_kernel",
        lambda *refs: own_kernel(0, *refs),
        lined + outs + [saved, ((2, 6, EDGE, 256), f32), border],
        own_scratch,
        shared + [inner, part],
        out_specs=(WHOLE,) * 2 + (IN_HBM,) * 3 + (WHOLE,) * 3,
        flops=3 * work,
        aliases={len(shared) + n: n for n in range(2)},
    )
    (relayed,) = call("relay_kernel", relay_kernel, [packed], [], [far_in, done], in_specs=[WHOLE, ANYWHERE])
    relayed_in = lax.ppermute(relayed, "il", onward)
    inner, part, *outs_in, done = call(
        "second_own_kernel",
        lambda *refs: own_kernel(1, *refs),
        lined + outs + [saved],
        own_scratch + [pltpu.SemaphoreType.DMA((3,))],
        shared + [inner, part, border, done] + outs_in,
        in_specs=[WHOLE] * (len(shared) + 4) + [IN_HBM] * 3,
        out_specs=(WHOLE,) * 2 + (IN_HBM,) * 3 + (WHOLE,),
        flops=3 * work,
        aliases={len(shared): 0, len(shared) + 1: 1} | {len(shared) + 4 + n: 2 + n for n in range(3)},
    )

    end_rows = (3, count, EDGE, cols)
    tables = [smooth, pack_h, diff_x, diff_h, lines_e, diff_e]
    scratch = [
        pltpu.VMEM((8 + packed_rows, cols), f32),
        pltpu.VMEM((depths, EDGE, cols), bf16),
        pltpu.VMEM((EDGE, 128 * TILES), bf16),
        pltpu.VMEM((6 * EDGE, 256), f32),
        pltpu.VMEM((count, 6, EDGE, cols), bf16),
    ]
    sems = pltpu.SemaphoreType.DMA((3,))
    operands = [vol, halo, near_in, part, part_h, *tables, done]
    *outs_in, done = call(
        "near_end_kernel",
        lambda *refs: end_kernel(0, *refs),
        outs + [(end_rows, f32)],
        scratch + [sems],
        operands + outs_in,
        in_specs=[WHOLE] * len(operands) + [IN_HBM] * 3,
        out_specs=(IN_HBM,) * 3 + (WHOLE,),
        flops=work,
        aliases={len(operands) + n: n for n in range(3)},
    )
    operands = [vol, halo, relayed_in, part, part_h, *tables, done]
    return call(
        "far_end_kernel",
        lambda *refs: end_kernel(1, *refs),
        outs,
        scratch + [pltpu.VMEM(end_rows, f32), sems, pltpu.SemaphoreType.DMA((2, 3))],
        operands + outs_in,
        in_specs=[WHOLE] * len(operands) + [IN_HBM] * 3,
        out_specs=(IN_HBM,) * 3,
        flops=work,
        aliases={len(operands) + n: n for n in range(3)},
    )


def solution(mesh):
    spec = P(None, ("parts", "il"), "xl")
    return jax.shard_map(body, mesh=mesh, in_specs=(spec,), out_specs=(spec,) * 3, check_vma=False)
```

```python
import jax
import jax.numpy as jnp
import ml_dtypes
import numpy as np
from jax import lax
from jax.experimental import pallas as pl
from jax.experimental.pallas import tpu as pltpu
from jax.sharding import PartitionSpec as P

RADIUS = 9
REACH = RADIUS + 1
SIDE = 16
SLOTS = 8
TILES = 3
EDGE = 16
OWN = 2
TINY = float(np.finfo(np.float32).tiny)
HEAD = 2
AHEAD = 2
FAR = -1000
WHOLE = pl.BlockSpec(memory_space=pltpu.VMEM)
IN_HBM = pl.BlockSpec(memory_space=pltpu.HBM)
ANYWHERE = pl.BlockSpec(memory_space=pl.ANY)


def filter_taps():
    offsets = np.arange(2 * RADIUS + 1).astype(np.float32)
    sigma = np.float32(RADIUS / 3.0)
    shape = np.exp(np.float32(-0.5) * ((offsets - RADIUS) / sigma) ** 2)
    return (shape / np.sum(shape, dtype=np.float32)).astype(ml_dtypes.bfloat16).astype(np.float32)


def iota(shape, dim):
    return lax.broadcasted_iota(jnp.int32, shape, dim)


def band(source, target, scale=1.0):
    offset = jnp.abs(source - target)
    weights = jnp.zeros(offset.shape, jnp.float32)
    for distance, tap in enumerate(filter_taps()[RADIUS:]):
        weights = jnp.where(offset == distance, jnp.float32(scale * tap), weights)
    return weights


def difference(source, target):
    offset = source - target
    return jnp.where(offset == 1, 1.0, jnp.where(offset == -1, -1.0, 0.0)).astype(jnp.float32)


def dot(left, right):
    return jnp.dot(left, right, preferred_element_type=jnp.float32)


def reciprocal(value):
    guess = pl.reciprocal(value, approx=True)
    return guess * (2.0 - value * guess)


def halo_plane(lane, tile, depths):
    slot = lax.div(lane, SIDE)
    rest = jnp.where(slot == 0, 0, jnp.where(slot == 1, depths - 1, FAR))
    return jnp.where(tile < 2, 1 + SLOTS * tile + slot, rest)


def halo_column(lane, x, cols):
    place = lax.rem(lane, SIDE)
    return jnp.where(x == 0, cols - OWN + place, place - (SIDE - OWN))


def low_end(exchange):
    even = lax.rem(lax.axis_index("il"), 2) == 0
    return jnp.logical_not(even) if exchange == 0 else even


def tables_kernel(depths, lines_ref, diff_i_ref, diff_x_ref, smooth_ref, pack_h_ref, diff_h_ref, lines_e_ref, diff_e_ref, pick_ref, mask_ref):
    rows, cols = lines_ref.shape[0], diff_x_ref.shape[0]
    x, il, last = lax.axis_index("xl"), lax.axis_index("il"), lax.axis_size("il") - 1
    bf16 = jnp.bfloat16

    target, source = iota((rows, rows), 0), iota((rows, rows), 1)
    inner = (source > 0) & (source < rows - 1)
    lines_ref[...] = jnp.where(inner, band(source, target, 0.25), 0.0).astype(bf16)
    diff_i_ref[...] = difference(source, target).astype(bf16)
    span = EDGE * (depths - 2)
    target, source = iota((span, span), 0), iota((span, span), 1)
    depth = lax.div(source, EDGE) == lax.div(target, EDGE)
    target, source = lax.rem(target, EDGE), lax.rem(source, EDGE)
    diff_e_ref[...] = jnp.where(depth, difference(source, target), 0.0).astype(bf16)
    for exchange in range(2):
        low = low_end(exchange)
        source_at = jnp.where(low, source - REACH, rows - (EDGE - REACH) + source)
        target_at = jnp.where(low, target, rows - EDGE + target)
        first = jnp.where(low & (il > 0), -rows, 0)
        final = jnp.where(jnp.logical_not(low) & (il < last), 2 * rows, rows - 1)
        use = depth & (source_at >= first) & (source_at <= final) & ((source_at <= 0) | (source_at >= rows - 1))
        lines_e_ref[exchange] = jnp.where(use, band(source_at, target_at, 0.25), 0.0).astype(bf16)

    source, target = iota((cols, cols), 0), iota((cols, cols), 1)
    diff_x_ref[...] = difference(source, target).astype(bf16)
    moved = source == jnp.where(x == 0, cols - 1, 0)
    column = lax.rem(target + 128 * x, cols)
    smooth_ref[...] = jnp.where(moved, 0.0, band(source, column)).astype(bf16)
    source, target = iota((256, 256), 0), iota((256, 256), 1)
    place = lax.rem(source, SIDE)
    use = (lax.div(source, SIDE) == lax.div(target, SIDE)) & (place != jnp.where(x == 0, 0, SIDE - 1))
    column = jnp.where(x == 0, cols - SIDE, 0) + lax.rem(target, SIDE)
    pack_h_ref[...] = jnp.where(use, band(halo_column(place, x, cols), column), 0.0).astype(bf16)

    source, target = iota((128, 128), 0), iota((128, 128), 1)
    same = lax.rem(source, SIDE) == lax.rem(target, SIDE)
    across = difference(lax.rem(source, SIDE), lax.rem(target, SIDE))
    for group in range(2):
        centre = halo_plane(target, group, depths)
        for tile in range(TILES):
            plane = halo_plane(source, tile, depths)
            part, out = slice(128 * tile, 128 * (tile + 1)), 128 * group
            diff_h_ref[part, out : out + 128] = jnp.where(same, difference(plane, centre), 0.0).astype(bf16)
            diff_h_ref[part, 256 + out : 384 + out] = jnp.where(plane == centre, across, 0.0).astype(bf16)

    source, lane = iota((cols, 256), 0), iota((cols, 256), 1)
    place = lax.rem(lane, SIDE)
    low, high = place < SIDE - OWN, place >= OWN
    sent = jnp.where(x == 0, jnp.where(low, cols - (SIDE - OWN) + place, FAR), jnp.where(high, place - OWN, FAR))
    low, high = place < OWN, place >= SIDE - OWN
    kept = jnp.where(x == 0, jnp.where(low, cols - OWN + place, FAR), jnp.where(high, place - (SIDE - OWN), FAR))
    pick_ref[...] = jnp.where(source == jnp.where(lane < 128, sent, kept), 1.0, 0.0).astype(bf16)
    lane = iota((8, 128), 1)
    border = jnp.where(x == 0, lane - (128 - SIDE), lane)
    mask_ref[...] = jnp.where((border >= 0) & (border < SIDE), 1.0, 0.0)


def pack_kernel(vol_ref, pick_ref, copy_ref, send_ref, own_ref):
    depths, rows, cols = vol_ref.shape
    slot = lax.div(lax.rem(iota((rows, 256), 1), 128), SIDE)
    copy_ref[...] = vol_ref[...]
    picked = dot(vol_ref[...].reshape(depths * rows, cols), pick_ref[...])
    for tile in range(TILES):
        if tile < 2:
            planes = [(1 + SLOTS * tile + index, index) for index in range(SLOTS)]
        else:
            planes = [(0, 0), (depths - 1, 1)]
        packed = jnp.zeros((rows, 256), jnp.float32)
        for plane, index in planes:
            packed = jnp.where(slot == index, picked[rows * plane : rows * (plane + 1)], packed)
        packed = packed.astype(jnp.bfloat16)
        send_ref[tile] = packed[:, :128]
        own_ref[tile] = packed[:, 128:]


def rows_kernel(vol_ref, own_ref, side_ref, after_ref, halo_ref, near_ref, far_ref, packed_ref):
    depths, rows, cols = vol_ref.shape
    even = lax.rem(lax.axis_index("il"), 2) == 0

    def put(row, top, bottom):
        top, bottom = top[:REACH], bottom[EDGE - REACH :]
        lanes = top.shape[1]
        packed_ref[0, row : row + REACH, :lanes] = jnp.where(even, bottom, top)
        packed_ref[1, row : row + REACH, :lanes] = jnp.where(even, top, bottom)

    packed_ref[:, depths * REACH :, :] = jnp.zeros_like(packed_ref[:, depths * REACH :, :])
    for depth in range(depths):
        top = vol_ref[depth, :EDGE, :].astype(jnp.float32)
        bottom = vol_ref[depth, rows - EDGE :, :].astype(jnp.float32)
        put(REACH * depth, top, bottom)
    tiles = []
    for tile in range(TILES):
        merged = own_ref[tile].astype(jnp.float32) + side_ref[tile].astype(jnp.float32)
        halo_ref[:, 128 * tile : 128 * (tile + 1)] = merged.astype(jnp.bfloat16)
        tiles.append((merged[:EDGE], merged[rows - EDGE :]))
    tops = jnp.concatenate([tiles[0][0], tiles[1][0]], axis=1)
    bottoms = jnp.concatenate([tiles[0][1], tiles[1][1]], axis=1)
    put(REACH * depths, tops, bottoms)
    put(REACH * (depths + 1), *tiles[2])
    near_ref[...] = packed_ref[0].astype(jnp.bfloat16)
    far_ref[...] = packed_ref[1].astype(jnp.bfloat16)


def relay_kernel(rows_ref, after_ref, out_ref):
    out_ref[...] = rows_ref[...]


def moments(grad_i, grad_x, grad_z):
    terms = (
        grad_i * grad_i,
        grad_x * grad_x,
        grad_z * grad_z,
        grad_i * grad_x,
        grad_i * grad_z,
        grad_x * grad_z,
    )
    return [term.astype(jnp.bfloat16) for term in terms]


def store_chunks(summed, comp, inner_ref, part_ref):
    chunks = summed.shape[0] // EDGE
    for chunk in range(1, chunks - 1):
        inner_ref[chunk - 1, comp] = summed[EDGE * chunk : EDGE * (chunk + 1)].astype(jnp.bfloat16)
    part_ref[0, comp] = summed[:EDGE]
    part_ref[1, comp] = summed[EDGE * (chunks - 1) :]


def make_moments(pair, vol_ref, diff_i_ref, diff_x_ref, moments_ref):
    depths, rows, cols = vol_ref.shape
    planes = [vol_ref[2 * pair + k] for k in range(4)]
    across = dot(jnp.concatenate(planes[1:3], axis=0), diff_x_ref[...])
    for k in range(2):
        grad_i = dot(diff_i_ref[...], planes[k + 1])
        grad_x = across[rows * k : rows * (k + 1)]
        grad_z = planes[k + 2].astype(jnp.float32) - planes[k].astype(jnp.float32)
        for comp, term in enumerate(moments(grad_i, grad_x, grad_z)):
            moments_ref[k, comp] = term


def make_lines(pair, lines_ref, moments_ref, inner_ref, part_ref):
    for k in range(2):
        z = 2 * pair + k
        for comp in range(6):
            store_chunks(dot(lines_ref[...], moments_ref[k, comp]), comp, inner_ref.at[z], part_ref.at[:, :, z])


def lines_kernel(vol_ref, lines_ref, diff_i_ref, diff_x_ref, inner_ref, part_ref, even_ref, odd_ref):
    slots = (even_ref, odd_ref)
    for pair in range(HEAD):
        make_moments(pair, vol_ref, diff_i_ref, diff_x_ref, slots[pair % 2])
        make_lines(pair, lines_ref, slots[pair % 2], inner_ref, part_ref)


def attributes(own, border, smooth_ref, store):
    x = lax.axis_index("xl")
    tensor = dot(own, smooth_ref[...])
    halves = (tensor[:, :128], tensor[:, 128:] + border)
    lanes = (pl.multiple_of(128 * x, 128), pl.multiple_of(128 - 128 * x, 128))
    for chunk in range(own.shape[0] // (6 * EDGE)):
        base = 6 * EDGE * chunk
        for half, lane in zip(halves, lanes):
            a, b, c, d, e, f = [half[base + EDGE * comp : base + EDGE * (comp + 1)] for comp in range(6)]
            low = c + 1e-6
            guess = pl.reciprocal(low, approx=True)
            inverse = guess * (low * guess - 2.0)
            spread = (a - b) * (a - c) + (b - c) * (b - c) + 3.0 * (d * d + e * e + f * f)
            root = spread * lax.rsqrt(jnp.maximum(spread, TINY))
            store(chunk, pl.ds(lane, 128), (e * inverse, f * inverse, root * reciprocal(a + b + low)))


def border_of(packed, slot, mask_ref):
    base = jnp.where(lax.axis_index("xl") == 0, 128 - SIDE, 0)
    moved = pltpu.roll(packed, lax.rem(base - SIDE * slot + 128, 128), 1)
    return (moved.reshape(-1, 8, 128) * mask_ref[...]).reshape(packed.shape)


def own_kernel(
    stage, vol_ref, lines_ref, diff_i_ref, diff_x_ref, smooth_ref, halo_ref, diff_h_ref, pack_h_ref, mask_ref,
    inner_in_ref, part_in_ref, *refs,
):
    if stage == 0:
        inner_ref, part_ref, *targets, later_ref, part_h_ref, border_ref, even_ref, odd_ref, out_ref, sems = refs
        both = dot(halo_ref[...], diff_h_ref[...])
        grad_i = dot(diff_i_ref[...], halo_ref[:, :256])
        lined_h = [[] for chunk in range(inner_ref.shape[1])]
        for comp, term in enumerate(moments(grad_i, both[:, 256:], both[:, :256])):
            summed = dot(lines_ref[...], term)
            for chunk, parts in enumerate(lined_h):
                parts.append(summed[EDGE * (chunk + 1) : EDGE * (chunk + 2)].astype(jnp.bfloat16))
            part_h_ref[0, comp] = summed[:EDGE]
            part_h_ref[1, comp] = summed[EDGE * (len(lined_h) + 1) :]
        border_ref[...] = dot(jnp.concatenate(sum(lined_h, []), axis=0), pack_h_ref[...])
        finished = []
    else:
        border_ref, done_ref, *refs = refs
        inner_ref, part_ref, *targets, later_ref, even_ref, odd_ref, out_ref, sems, done_sems = refs[3:]
        finished = []
    count, chunks = inner_ref.shape[:2]
    pairs, inner = count // 4, EDGE * chunks
    slots = (even_ref, odd_ref)

    def place(target, pair):
        return target.at[pl.ds(2 * pair, 2), pl.ds(EDGE, inner)]

    if stage == 1:
        for n, target in enumerate(targets):
            finished.append(pltpu.make_async_copy(done_ref.at[n], place(target, pairs - 1), done_sems.at[n]))
            finished[-1].start()

    ahead = list(range(HEAD, pairs + AHEAD) if stage == 0 else range(pairs + AHEAD, 2 * pairs))
    for step in range(pairs):
        pair = pairs * stage + step
        todo = ahead[step : step + 1]
        for q in todo:
            make_moments(q, vol_ref, diff_i_ref, diff_x_ref, slots[q % 2])
        for k in range(2):
            z = 2 * pair + k

            def store(chunk, lanes, values):
                rows = slice(EDGE * chunk, EDGE * (chunk + 1))
                for n, value in enumerate(values):
                    if step == pairs - 1:
                        later_ref[n, k, rows, lanes] = value
                    else:
                        out_ref[n, 2 * step + k, rows, lanes] = value

            border = border_of(border_ref[:, 128 * stage : 128 * (stage + 1)], z % SLOTS, mask_ref)
            attributes(inner_ref[z].reshape(6 * inner, 256), border, smooth_ref, store)
        for q in todo:
            make_lines(q, lines_ref, slots[q % 2], inner_ref, part_ref)
        if step < pairs - 1:
            for n, target in enumerate(targets):
                source = out_ref.at[n, pl.ds(2 * step, 2)]
                finished.append(pltpu.make_async_copy(source, place(target, pair), sems.at[step, n]))
                finished[-1].start()
    for copy in finished:
        copy.wait()


def end_kernel(
    exchange, vol_ref, halo_ref, rows_ref, part_ref, part_h_ref,
    smooth_ref, pack_h_ref, diff_x_ref, diff_h_ref, lines_e_ref, diff_e_ref, mask_ref, done_ref, *refs,
):
    last = exchange == 1
    targets, refs = refs[3:6], refs[6:]
    if last:
        packed_ref, block_ref, block_h_ref, border_ref, edge_ref, out_ref, done_sems, sems = refs
    else:
        out_ref, packed_ref, block_ref, block_h_ref, border_ref, edge_ref, done_sems = refs
    depths, rows, cols = vol_ref.shape
    count, half = depths - 2, (depths - 2) // 2
    bf16, f32 = jnp.bfloat16, jnp.float32
    low = low_end(exchange)
    end = jnp.where(low, 0, 1)
    start = pl.multiple_of(jnp.where(low, 0, rows - EDGE), EDGE)
    other = pl.multiple_of(jnp.where(low, rows - EDGE, 0), EDGE)
    finished = []
    for n, target in enumerate(targets):
        if last:
            place = target.at[:, pl.ds(other, EDGE)]
        else:
            place = target.at[pl.ds(count - 2, 2), pl.ds(EDGE, rows - 2 * EDGE)]
        finished.append(pltpu.make_async_copy(done_ref.at[n], place, done_sems.at[n]))
    for copy in finished:
        copy.start()

    packed_ref[:8] = jnp.zeros_like(packed_ref[:8])
    if last:
        il = lax.axis_index("il")
        outside = (low & (il == 0)) | (jnp.logical_not(low) & (il == lax.axis_size("il") - 1))
        packed_ref[8:] = jnp.where(outside, 0.0, rows_ref[...].astype(f32))
    else:
        packed_ref[8:] = rows_ref[...].astype(f32)

    def joined(row, own):
        lanes = own.shape[1]
        before = packed_ref[8 + row : 8 + row + EDGE, :lanes]
        after = packed_ref[8 + row - (EDGE - REACH) : 8 + row + REACH, :lanes]
        own = own.astype(f32)
        place = iota(own.shape, 0)
        first = jnp.where(place < REACH, before, pltpu.roll(own, REACH, 0))
        second = jnp.where(place < EDGE - REACH, pltpu.roll(own, EDGE - REACH, 0), after)
        return jnp.where(low, first, second).astype(bf16)

    for depth in range(depths):
        block_ref[depth] = joined(REACH * depth, vol_ref[depth, pl.ds(start, EDGE)])
    own_h = halo_ref[pl.ds(start, EDGE)]
    block_h_ref[:, :256] = joined(REACH * depths, own_h[:, :256])
    block_h_ref[:, 256:] = joined(REACH * (depths + 1), own_h[:, 256:])

    both = dot(block_h_ref[...], diff_h_ref[...])
    grad_i = dot(diff_e_ref[:EDGE, :EDGE], block_h_ref[:, :256])
    lined_h = []
    for comp, term in enumerate(moments(grad_i, both[:, 256:], both[:, :256])):
        summed = part_h_ref[end, comp] + dot(lines_e_ref[exchange, :EDGE, :EDGE], term)
        lined_h.append(summed.astype(bf16))
    border_ref[...] = dot(jnp.concatenate(lined_h, axis=0), pack_h_ref[...])

    span = EDGE * half
    copies = []
    for group in range(2):
        first = half * group
        centre = block_ref[first + 1 : first + half + 1].reshape(span, cols)
        grad_i = dot(diff_e_ref[:span, :span], centre)
        grad_x = dot(centre, diff_x_ref[...])
        grad_z = block_ref[first + 2 : first + half + 2].astype(f32) - block_ref[first : first + half].astype(f32)
        for comp, term in enumerate(moments(grad_i, grad_x, grad_z.reshape(span, cols))):
            outer = dot(lines_e_ref[exchange, :span, :span], term)
            summed = part_ref[end, comp, first : first + half] + outer.reshape(half, EDGE, cols)
            edge_ref[first : first + half, comp] = summed.astype(bf16)
    for group in range(2):
        first = half * group
        border = [border_of(border_ref[:, 128 * group : 128 * (group + 1)], k, mask_ref) for k in range(half)]

        def store(chunk, lanes, values):
            for n, value in enumerate(values):
                out_ref[n, first + chunk, :, lanes] = value

        own = edge_ref[first : first + half].reshape(6 * span, cols)
        attributes(own, jnp.concatenate(border, axis=0), smooth_ref, store)
        if last:
            depth = pl.ds(first, half)
            for n, target in enumerate(targets):
                copy = pltpu.make_async_copy(out_ref.at[n, depth], target.at[depth, pl.ds(start, EDGE)], sems.at[group, n])
                copy.start()
                copies.append(copy)
    for copy in finished + copies:
        copy.wait()


def call(name, kernel, outs, scratch, operands, in_specs=None, out_specs=None, flops=0, limit=16, aliases={}):
    return pl.pallas_call(
        kernel,
        out_shape=tuple(jax.ShapeDtypeStruct(*out) for out in outs),
        in_specs=in_specs or [WHOLE] * len(operands),
        out_specs=out_specs or (WHOLE,) * len(outs),
        scratch_shapes=scratch,
        compiler_params=pltpu.CompilerParams(vmem_limit_bytes=limit << 20),
        name=name,
        input_output_aliases=aliases,
        cost_estimate=pl.CostEstimate(flops=flops, bytes_accessed=0, transcendentals=0),
    )(*operands)


def body(volume):
    depths, rows, cols = volume.shape
    il, xl = lax.axis_size("il"), lax.axis_size("xl")
    count = depths - 2
    assert xl == 2 and il % 2 == 0 and count == 2 * SLOTS and cols == 256
    bf16, f32 = jnp.bfloat16, jnp.float32
    half = count // 2
    work = half * 1024 * 2 * 256 * 256
    packed_rows = -(-REACH * (depths + 2) // 16) * 16

    span = EDGE * count
    lines, diff_i, diff_x, smooth, pack_h, diff_h, lines_e, diff_e, pick, mask = call(
        "tables_kernel",
        lambda *refs: tables_kernel(depths, *refs),
        [
            ((rows, rows), bf16),
            ((rows, rows), bf16),
            ((cols, cols), bf16),
            ((cols, cols), bf16),
            ((256, 256), bf16),
            ((128 * TILES, 512), bf16),
            ((2, span, span), bf16),
            ((span, span), bf16),
            ((cols, 256), bf16),
            ((8, 128), f32),
        ],
        [],
        [],
        flops=work,
    )
    halo_tile = ((TILES, rows, 128), bf16)
    vol, send, own = call("pack_kernel", pack_kernel, [(volume.shape, bf16), halo_tile, halo_tile], [], [volume, pick])
    side = lax.ppermute(send, "xl", [(0, 1), (1, 0)])
    chunks = rows // EDGE - 2
    lined = [((count, chunks, 6, EDGE, cols), bf16), ((2, 6, count, EDGE, cols), f32)]
    moment_slots = [pltpu.VMEM((2, 6, rows, cols), bf16)] * 2
    inner, part = call("lines_kernel", lines_kernel, lined, moment_slots, [vol, lines, diff_i, diff_x], flops=work // 4)
    packed = ((packed_rows, cols), bf16)
    halo, near, far = call(
        "rows_kernel",
        rows_kernel,
        [((rows, 128 * TILES), bf16), packed, packed],
        [pltpu.VMEM((2, packed_rows, cols), f32)],
        [vol, own, side, part],
        in_specs=[WHOLE] * 3 + [ANYWHERE],
    )
    swap = [(i, i ^ 1) for i in range(il)]
    onward = [(i, i + 2) for i in range(0, il - 2, 2)] + [(il - 2, il - 1)]
    onward += [(i, i - 2) for i in range(3, il, 2)] + [(1, 0)]
    far_in = lax.ppermute(far, "il", swap)
    near_in = lax.ppermute(near, "il", swap)

    outs = [((count, rows, cols), f32)] * 3
    saved = ((3, 2, EDGE * chunks, cols), f32)
    border = ((6 * EDGE * chunks, 256), f32)
    ready = [((3, count // 2 - 2, EDGE * chunks, cols), f32)]
    own_scratch = moment_slots + [pltpu.VMEM(*ready[0]), pltpu.SemaphoreType.DMA((count // 4 - 1, 3))]
    shared = [vol, lines, diff_i, diff_x, smooth, halo, diff_h, pack_h, mask]
    inner, part, *outs_in, done, part_h, border = call(
        "first_own_kernel",
        lambda *refs: own_kernel(0, *refs),
        lined + outs + [saved, ((2, 6, EDGE, 256), f32), border],
        own_scratch,
        shared + [inner, part],
        out_specs=(WHOLE,) * 2 + (IN_HBM,) * 3 + (WHOLE,) * 3,
        flops=3 * work,
        aliases={len(shared) + n: n for n in range(2)},
    )
    (relayed,) = call("relay_kernel", relay_kernel, [packed], [], [far_in, done], in_specs=[WHOLE, ANYWHERE])
    relayed_in = lax.ppermute(relayed, "il", onward)
    inner, part, *outs_in, done = call(
        "second_own_kernel",
        lambda *refs: own_kernel(1, *refs),
        lined + outs + [saved],
        own_scratch + [pltpu.SemaphoreType.DMA((3,))],
        shared + [inner, part, border, done] + outs_in,
        in_specs=[WHOLE] * (len(shared) + 4) + [IN_HBM] * 3,
        out_specs=(WHOLE,) * 2 + (IN_HBM,) * 3 + (WHOLE,),
        flops=3 * work,
        aliases={len(shared): 0, len(shared) + 1: 1} | {len(shared) + 4 + n: 2 + n for n in range(3)},
    )

    end_rows = (3, count, EDGE, cols)
    tables = [smooth, pack_h, diff_x, diff_h, lines_e, diff_e, mask]
    scratch = [
        pltpu.VMEM((8 + packed_rows, cols), f32),
        pltpu.VMEM((depths, EDGE, cols), bf16),
        pltpu.VMEM((EDGE, 128 * TILES), bf16),
        pltpu.VMEM((6 * EDGE, 256), f32),
        pltpu.VMEM((count, 6, EDGE, cols), bf16),
    ]
    sems = pltpu.SemaphoreType.DMA((3,))
    operands = [vol, halo, near_in, part, part_h, *tables, done]
    *outs_in, done = call(
        "near_end_kernel",
        lambda *refs: end_kernel(0, *refs),
        outs + [(end_rows, f32)],
        scratch + [sems],
        operands + outs_in,
        in_specs=[WHOLE] * len(operands) + [IN_HBM] * 3,
        out_specs=(IN_HBM,) * 3 + (WHOLE,),
        flops=work,
        aliases={len(operands) + n: n for n in range(3)},
    )
    operands = [vol, halo, relayed_in, part, part_h, *tables, done]
    return call(
        "far_end_kernel",
        lambda *refs: end_kernel(1, *refs),
        outs,
        scratch + [pltpu.VMEM(end_rows, f32), sems, pltpu.SemaphoreType.DMA((2, 3))],
        operands + outs_in,
        in_specs=[WHOLE] * len(operands) + [IN_HBM] * 3,
        out_specs=(IN_HBM,) * 3,
        flops=work,
        aliases={len(operands) + n: n for n in range(3)},
    )


def solution(mesh):
    spec = P(None, ("parts", "il"), "xl")
    return jax.shard_map(body, mesh=mesh, in_specs=(spec,), out_specs=(spec,) * 3, check_vma=False)
```

```python
import jax
import jax.numpy as jnp
import ml_dtypes
import numpy as np
from jax import lax
from jax.experimental import pallas as pl
from jax.experimental.pallas import tpu as pltpu
from jax.sharding import PartitionSpec as P

RADIUS = 9
REACH = RADIUS + 1
SIDE = 16
SLOTS = 8
TILES = 3
EDGE = 16
OWN = 2
TINY = float(np.finfo(np.float32).tiny)
HEAD = 2
AHEAD = 2
FAR = -1000
WHOLE = pl.BlockSpec(memory_space=pltpu.VMEM)
IN_HBM = pl.BlockSpec(memory_space=pltpu.HBM)
ANYWHERE = pl.BlockSpec(memory_space=pl.ANY)


def filter_taps():
    offsets = np.arange(2 * RADIUS + 1).astype(np.float32)
    sigma = np.float32(RADIUS / 3.0)
    shape = np.exp(np.float32(-0.5) * ((offsets - RADIUS) / sigma) ** 2)
    return (shape / np.sum(shape, dtype=np.float32)).astype(ml_dtypes.bfloat16).astype(np.float32)


def iota(shape, dim):
    return lax.broadcasted_iota(jnp.int32, shape, dim)


def band(source, target, scale=1.0):
    offset = jnp.abs(source - target)
    weights = jnp.zeros(offset.shape, jnp.float32)
    for distance, tap in enumerate(filter_taps()[RADIUS:]):
        weights = jnp.where(offset == distance, jnp.float32(scale * tap), weights)
    return weights


def difference(source, target):
    offset = source - target
    return jnp.where(offset == 1, 1.0, jnp.where(offset == -1, -1.0, 0.0)).astype(jnp.float32)


def dot(left, right):
    return jnp.dot(left, right, preferred_element_type=jnp.float32)


def reciprocal(value):
    guess = pl.reciprocal(value, approx=True)
    return guess * (2.0 - value * guess)


def halo_plane(lane, tile, depths):
    slot = lax.div(lane, SIDE)
    rest = jnp.where(slot == 0, 0, jnp.where(slot == 1, depths - 1, FAR))
    return jnp.where(tile < 2, 1 + SLOTS * tile + slot, rest)


def halo_column(lane, x, cols):
    place = lax.rem(lane, SIDE)
    return jnp.where(x == 0, cols - OWN + place, place - (SIDE - OWN))


def low_end(exchange):
    even = lax.rem(lax.axis_index("il"), 2) == 0
    return jnp.logical_not(even) if exchange == 0 else even


def tables_kernel(depths, lines_ref, diff_i_ref, diff_x_ref, smooth_ref, pack_h_ref, diff_h_ref, lines_e_ref, diff_e_ref, pick_ref, mask_ref):
    rows, cols = lines_ref.shape[0], diff_x_ref.shape[0]
    x, il, last = lax.axis_index("xl"), lax.axis_index("il"), lax.axis_size("il") - 1
    bf16 = jnp.bfloat16

    target, source = iota((rows, rows), 0), iota((rows, rows), 1)
    inner = (source > 0) & (source < rows - 1)
    lines_ref[...] = jnp.where(inner, band(source, target, 0.25), 0.0).astype(bf16)
    diff_i_ref[...] = difference(source, target).astype(bf16)
    span = EDGE * (depths - 2)
    target, source = iota((span, span), 0), iota((span, span), 1)
    depth = lax.div(source, EDGE) == lax.div(target, EDGE)
    target, source = lax.rem(target, EDGE), lax.rem(source, EDGE)
    diff_e_ref[...] = jnp.where(depth, difference(source, target), 0.0).astype(bf16)
    for exchange in range(2):
        low = low_end(exchange)
        source_at = jnp.where(low, source - REACH, rows - (EDGE - REACH) + source)
        target_at = jnp.where(low, target, rows - EDGE + target)
        first = jnp.where(low & (il > 0), -rows, 0)
        final = jnp.where(jnp.logical_not(low) & (il < last), 2 * rows, rows - 1)
        use = depth & (source_at >= first) & (source_at <= final) & ((source_at <= 0) | (source_at >= rows - 1))
        lines_e_ref[exchange] = jnp.where(use, band(source_at, target_at, 0.25), 0.0).astype(bf16)

    source, target = iota((cols, cols), 0), iota((cols, cols), 1)
    diff_x_ref[...] = difference(source, target).astype(bf16)
    moved = source == jnp.where(x == 0, cols - 1, 0)
    column = lax.rem(target + 128 * x, cols)
    smooth_ref[...] = jnp.where(moved, 0.0, band(source, column)).astype(bf16)
    source, target = iota((256, 256), 0), iota((256, 256), 1)
    place = lax.rem(source, SIDE)
    use = (lax.div(source, SIDE) == lax.div(target, SIDE)) & (place != jnp.where(x == 0, 0, SIDE - 1))
    column = jnp.where(x == 0, cols - SIDE, 0) + lax.rem(target, SIDE)
    pack_h_ref[...] = jnp.where(use, band(halo_column(place, x, cols), column), 0.0).astype(bf16)

    source, target = iota((128, 128), 0), iota((128, 128), 1)
    same = lax.rem(source, SIDE) == lax.rem(target, SIDE)
    across = difference(lax.rem(source, SIDE), lax.rem(target, SIDE))
    for group in range(2):
        centre = halo_plane(target, group, depths)
        for tile in range(TILES):
            plane = halo_plane(source, tile, depths)
            part, out = slice(128 * tile, 128 * (tile + 1)), 128 * group
            diff_h_ref[part, out : out + 128] = jnp.where(same, difference(plane, centre), 0.0).astype(bf16)
            diff_h_ref[part, 256 + out : 384 + out] = jnp.where(plane == centre, across, 0.0).astype(bf16)

    source, lane = iota((cols, 256), 0), iota((cols, 256), 1)
    place = lax.rem(lane, SIDE)
    low, high = place < SIDE - OWN, place >= OWN
    sent = jnp.where(x == 0, jnp.where(low, cols - (SIDE - OWN) + place, FAR), jnp.where(high, place - OWN, FAR))
    low, high = place < OWN, place >= SIDE - OWN
    kept = jnp.where(x == 0, jnp.where(low, cols - OWN + place, FAR), jnp.where(high, place - (SIDE - OWN), FAR))
    pick_ref[...] = jnp.where(source == jnp.where(lane < 128, sent, kept), 1.0, 0.0).astype(bf16)
    lane = iota((8, 128), 1)
    border = jnp.where(x == 0, lane - (128 - SIDE), lane)
    mask_ref[...] = jnp.where((border >= 0) & (border < SIDE), 1.0, 0.0)


def pack_kernel(vol_ref, pick_ref, copy_ref, send_ref, own_ref):
    depths, rows, cols = vol_ref.shape
    slot = lax.div(lax.rem(iota((rows, 256), 1), 128), SIDE)
    copy_ref[...] = vol_ref[...]
    picked = dot(vol_ref[...].reshape(depths * rows, cols), pick_ref[...])
    for tile in range(TILES):
        if tile < 2:
            planes = [(1 + SLOTS * tile + index, index) for index in range(SLOTS)]
        else:
            planes = [(0, 0), (depths - 1, 1)]
        packed = jnp.zeros((rows, 256), jnp.float32)
        for plane, index in planes:
            packed = jnp.where(slot == index, picked[rows * plane : rows * (plane + 1)], packed)
        packed = packed.astype(jnp.bfloat16)
        send_ref[tile] = packed[:, :128]
        own_ref[tile] = packed[:, 128:]


def rows_kernel(vol_ref, own_ref, side_ref, after_ref, halo_ref, near_ref, far_ref, packed_ref):
    depths, rows, cols = vol_ref.shape
    even = lax.rem(lax.axis_index("il"), 2) == 0

    def put(row, top, bottom):
        top, bottom = top[:REACH], bottom[EDGE - REACH :]
        lanes = top.shape[1]
        packed_ref[0, row : row + REACH, :lanes] = jnp.where(even, bottom, top)
        packed_ref[1, row : row + REACH, :lanes] = jnp.where(even, top, bottom)

    packed_ref[:, depths * REACH :, :] = jnp.zeros_like(packed_ref[:, depths * REACH :, :])
    for depth in range(depths):
        top = vol_ref[depth, :EDGE, :].astype(jnp.float32)
        bottom = vol_ref[depth, rows - EDGE :, :].astype(jnp.float32)
        put(REACH * depth, top, bottom)
    tiles = []
    for tile in range(TILES):
        merged = own_ref[tile].astype(jnp.float32) + side_ref[tile].astype(jnp.float32)
        halo_ref[:, 128 * tile : 128 * (tile + 1)] = merged.astype(jnp.bfloat16)
        tiles.append((merged[:EDGE], merged[rows - EDGE :]))
    tops = jnp.concatenate([tiles[0][0], tiles[1][0]], axis=1)
    bottoms = jnp.concatenate([tiles[0][1], tiles[1][1]], axis=1)
    put(REACH * depths, tops, bottoms)
    put(REACH * (depths + 1), *tiles[2])
    near_ref[...] = packed_ref[0].astype(jnp.bfloat16)
    far_ref[...] = packed_ref[1].astype(jnp.bfloat16)


def relay_kernel(rows_ref, after_ref, out_ref):
    out_ref[...] = rows_ref[...]


def moments(grad_i, grad_x, grad_z):
    terms = (
        grad_i * grad_i,
        grad_x * grad_x,
        grad_z * grad_z,
        grad_i * grad_x,
        grad_i * grad_z,
        grad_x * grad_z,
    )
    return [term.astype(jnp.bfloat16) for term in terms]


def store_chunks(summed, comp, inner_ref, part_ref):
    chunks = summed.shape[0] // EDGE
    for chunk in range(1, chunks - 1):
        inner_ref[chunk - 1, comp] = summed[EDGE * chunk : EDGE * (chunk + 1)].astype(jnp.bfloat16)
    part_ref[0, comp] = summed[:EDGE]
    part_ref[1, comp] = summed[EDGE * (chunks - 1) :]


def make_moments(pair, vol_ref, diff_i_ref, diff_x_ref, moments_ref):
    depths, rows, cols = vol_ref.shape
    planes = [vol_ref[2 * pair + k] for k in range(4)]
    across = dot(jnp.concatenate(planes[1:3], axis=0), diff_x_ref[...])
    for k in range(2):
        grad_i = dot(diff_i_ref[...], planes[k + 1])
        grad_x = across[rows * k : rows * (k + 1)]
        grad_z = planes[k + 2].astype(jnp.float32) - planes[k].astype(jnp.float32)
        for comp, term in enumerate(moments(grad_i, grad_x, grad_z)):
            moments_ref[k, comp] = term


def make_lines(z, comp, lines_ref, moments_ref, inner_ref, part_ref):
    store_chunks(dot(lines_ref[...], moments_ref[z % 2, comp]), comp, inner_ref.at[z], part_ref.at[:, :, z])


def lines_kernel(vol_ref, lines_ref, diff_i_ref, diff_x_ref, inner_ref, part_ref, even_ref, odd_ref):
    slots = (even_ref, odd_ref)
    for pair in range(HEAD):
        make_moments(pair, vol_ref, diff_i_ref, diff_x_ref, slots[pair % 2])
        for k in range(2):
            for comp in range(6):
                make_lines(2 * pair + k, comp, lines_ref, slots[pair % 2], inner_ref, part_ref)


def tensor_of(own, smooth_ref, tensor_ref):
    tensor_ref[...] = dot(own.reshape(-1, own.shape[-1]), smooth_ref[...])


def attributes(tensor, border, store):
    x = lax.axis_index("xl")
    halves = (tensor[:, :128], tensor[:, 128:] + border)
    lanes = (pl.multiple_of(128 * x, 128), pl.multiple_of(128 - 128 * x, 128))
    for half, lane in zip(halves, lanes):
        a, b, c, d, e, f = [half[EDGE * comp : EDGE * (comp + 1)] for comp in range(6)]
        low = c + 1e-6
        guess = pl.reciprocal(low, approx=True)
        inverse = guess * (low * guess - 2.0)
        spread = (a - b) * (a - c) + (b - c) * (b - c) + 3.0 * (d * d + e * e + f * f)
        root = spread * lax.rsqrt(jnp.maximum(spread, TINY))
        store(pl.ds(lane, 128), (e * inverse, f * inverse, root * reciprocal(a + b + low)))


def border_of(packed, slot, mask_ref):
    base = jnp.where(lax.axis_index("xl") == 0, 128 - SIDE, 0)
    moved = pltpu.roll(packed, lax.rem(base - SIDE * slot + 128, 128), 1)
    return (moved.reshape(-1, 8, 128) * mask_ref[...]).reshape(packed.shape)


def own_kernel(
    stage, vol_ref, lines_ref, diff_i_ref, diff_x_ref, smooth_ref, halo_ref, diff_h_ref, pack_h_ref, mask_ref,
    inner_in_ref, part_in_ref, *refs,
):
    if stage == 0:
        inner_ref, part_ref, *targets, later_ref, part_h_ref, border_ref, even_ref, odd_ref, tensor_ref, out_ref, sems = refs
        both = dot(halo_ref[...], diff_h_ref[...])
        grad_i = dot(diff_i_ref[...], halo_ref[:, :256])
        lined_h = [[] for chunk in range(inner_ref.shape[1])]
        for comp, term in enumerate(moments(grad_i, both[:, 256:], both[:, :256])):
            summed = dot(lines_ref[...], term)
            for chunk, parts in enumerate(lined_h):
                parts.append(summed[EDGE * (chunk + 1) : EDGE * (chunk + 2)].astype(jnp.bfloat16))
            part_h_ref[0, comp] = summed[:EDGE]
            part_h_ref[1, comp] = summed[EDGE * (len(lined_h) + 1) :]
        border_ref[...] = dot(jnp.concatenate(sum(lined_h, []), axis=0), pack_h_ref[...])
        finished = []
    else:
        border_ref, done_ref, *refs = refs
        inner_ref, part_ref, *targets, later_ref, even_ref, odd_ref, tensor_ref, out_ref, sems, done_sems = refs[3:]
        finished = []
    count, chunks = inner_ref.shape[:2]
    pairs, inner = count // 4, EDGE * chunks
    slots = (even_ref, odd_ref)

    def place(target, pair):
        return target.at[pl.ds(2 * pair, 2), pl.ds(EDGE, inner)]

    if stage == 1:
        for n, target in enumerate(targets):
            finished.append(pltpu.make_async_copy(done_ref.at[n], place(target, pairs - 1), done_sems.at[n]))
            finished[-1].start()

    half = count // 2
    ahead = range(2 * HEAD, half + 2 * AHEAD) if stage == 0 else range(half + 2 * AHEAD, count)
    tensor_of(inner_ref[half * stage], smooth_ref, tensor_ref.at[0])
    for step in range(half):
        z = half * stage + step
        later = ahead[step] if step < len(ahead) else None
        if later is not None and later % 2 == 0:
            make_moments(later // 2, vol_ref, diff_i_ref, diff_x_ref, slots[later // 2 % 2])
        if step < half - 1:
            tensor_of(inner_ref[z + 1], smooth_ref, tensor_ref.at[(step + 1) % 2])
        for chunk in range(chunks):
            rows = slice(EDGE * chunk, EDGE * (chunk + 1))
            part = slice(6 * EDGE * chunk, 6 * EDGE * (chunk + 1))

            def store(lanes, values):
                for n, value in enumerate(values):
                    if step >= half - 2:
                        later_ref[n, step % 2, rows, lanes] = value
                    else:
                        out_ref[n, step, rows, lanes] = value

            border = border_of(border_ref[part, 128 * stage : 128 * (stage + 1)], z % SLOTS, mask_ref)
            attributes(tensor_ref[step % 2, part], border, store)
            if later is not None:
                make_lines(later, chunk, lines_ref, slots[later // 2 % 2], inner_ref, part_ref)
        if step % 2 == 1 and step < half - 2:
            for n, target in enumerate(targets):
                source = out_ref.at[n, pl.ds(step - 1, 2)]
                finished.append(pltpu.make_async_copy(source, place(target, z // 2), sems.at[step // 2, n]))
                finished[-1].start()
    for copy in finished:
        copy.wait()


def end_kernel(
    exchange, vol_ref, halo_ref, rows_ref, part_ref, part_h_ref,
    smooth_ref, pack_h_ref, diff_x_ref, diff_h_ref, lines_e_ref, diff_e_ref, mask_ref, done_ref, *refs,
):
    last = exchange == 1
    targets, refs = refs[3:6], refs[6:]
    if last:
        packed_ref, block_ref, block_h_ref, border_ref, edge_ref, tensor_ref, out_ref, done_sems, sems = refs
    else:
        out_ref, packed_ref, block_ref, block_h_ref, border_ref, edge_ref, tensor_ref, done_sems = refs
    depths, rows, cols = vol_ref.shape
    count, half = depths - 2, (depths - 2) // 2
    bf16, f32 = jnp.bfloat16, jnp.float32
    low = low_end(exchange)
    end = jnp.where(low, 0, 1)
    start = pl.multiple_of(jnp.where(low, 0, rows - EDGE), EDGE)
    other = pl.multiple_of(jnp.where(low, rows - EDGE, 0), EDGE)
    finished = []
    for n, target in enumerate(targets):
        if last:
            place = target.at[:, pl.ds(other, EDGE)]
        else:
            place = target.at[pl.ds(count - 2, 2), pl.ds(EDGE, rows - 2 * EDGE)]
        finished.append(pltpu.make_async_copy(done_ref.at[n], place, done_sems.at[n]))
    for copy in finished:
        copy.start()

    packed_ref[:8] = jnp.zeros_like(packed_ref[:8])
    if last:
        il = lax.axis_index("il")
        outside = (low & (il == 0)) | (jnp.logical_not(low) & (il == lax.axis_size("il") - 1))
        packed_ref[8:] = jnp.where(outside, 0.0, rows_ref[...].astype(f32))
    else:
        packed_ref[8:] = rows_ref[...].astype(f32)

    def joined(row, own):
        lanes = own.shape[1]
        before = packed_ref[8 + row : 8 + row + EDGE, :lanes]
        after = packed_ref[8 + row - (EDGE - REACH) : 8 + row + REACH, :lanes]
        own = own.astype(f32)
        place = iota(own.shape, 0)
        first = jnp.where(place < REACH, before, pltpu.roll(own, REACH, 0))
        second = jnp.where(place < EDGE - REACH, pltpu.roll(own, EDGE - REACH, 0), after)
        return jnp.where(low, first, second).astype(bf16)

    for depth in range(depths):
        block_ref[depth] = joined(REACH * depth, vol_ref[depth, pl.ds(start, EDGE)])
    own_h = halo_ref[pl.ds(start, EDGE)]
    block_h_ref[:, :256] = joined(REACH * depths, own_h[:, :256])
    block_h_ref[:, 256:] = joined(REACH * (depths + 1), own_h[:, 256:])

    both = dot(block_h_ref[...], diff_h_ref[...])
    grad_i = dot(diff_e_ref[:EDGE, :EDGE], block_h_ref[:, :256])
    lined_h = []
    for comp, term in enumerate(moments(grad_i, both[:, 256:], both[:, :256])):
        summed = part_h_ref[end, comp] + dot(lines_e_ref[exchange, :EDGE, :EDGE], term)
        lined_h.append(summed.astype(bf16))
    border_ref[...] = dot(jnp.concatenate(lined_h, axis=0), pack_h_ref[...])

    span = EDGE * half
    copies = []
    def make_block_moments(group):
        first = half * group
        centre = block_ref[first + 1 : first + half + 1].reshape(span, cols)
        grad_i = dot(diff_e_ref[:span, :span], centre)
        grad_x = dot(centre, diff_x_ref[...])
        grad_z = block_ref[first + 2 : first + half + 2].astype(f32) - block_ref[first : first + half].astype(f32)
        return moments(grad_i, grad_x, grad_z.reshape(span, cols))

    def make_edge(group, comp, term):
        first = half * group
        outer = dot(lines_e_ref[exchange, :span, :span], term)
        summed = part_ref[end, comp, first : first + half] + outer.reshape(half, EDGE, cols)
        edge_ref[first : first + half, comp] = summed.astype(bf16)

    def finish(group, k):
        def store(lanes, values):
            for n, value in enumerate(values):
                out_ref[n, half * group + k, :, lanes] = value

        border = border_of(border_ref[:, 128 * group : 128 * (group + 1)], k, mask_ref)
        attributes(tensor_ref[group, 6 * EDGE * k : 6 * EDGE * (k + 1)], border, store)

    def send(group):
        depth = pl.ds(half * group, half)
        for n, target in enumerate(targets):
            copy = pltpu.make_async_copy(out_ref.at[n, depth], target.at[depth, pl.ds(start, EDGE)], sems.at[group, n])
            copy.start()
            copies.append(copy)

    for comp, term in enumerate(make_block_moments(0)):
        make_edge(0, comp, term)
    later = make_block_moments(1)
    tensor_of(edge_ref[:half], smooth_ref, tensor_ref.at[0])
    for k in range(half):
        if k < 6:
            make_edge(1, k, later[k])
        finish(0, k)
    if last:
        send(0)
    tensor_of(edge_ref[half:], smooth_ref, tensor_ref.at[1])
    for k in range(half):
        finish(1, k)
    if last:
        send(1)
    for copy in finished + copies:
        copy.wait()


def call(name, kernel, outs, scratch, operands, in_specs=None, out_specs=None, flops=0, limit=16, aliases={}):
    return pl.pallas_call(
        kernel,
        out_shape=tuple(jax.ShapeDtypeStruct(*out) for out in outs),
        in_specs=in_specs or [WHOLE] * len(operands),
        out_specs=out_specs or (WHOLE,) * len(outs),
        scratch_shapes=scratch,
        compiler_params=pltpu.CompilerParams(vmem_limit_bytes=limit << 20),
        name=name,
        input_output_aliases=aliases,
        cost_estimate=pl.CostEstimate(flops=flops, bytes_accessed=0, transcendentals=0),
    )(*operands)


def body(volume):
    depths, rows, cols = volume.shape
    il, xl = lax.axis_size("il"), lax.axis_size("xl")
    count = depths - 2
    assert xl == 2 and il % 2 == 0 and count == 2 * SLOTS and rows == 128 and cols == 256
    bf16, f32 = jnp.bfloat16, jnp.float32
    half = count // 2
    work = half * 1024 * 2 * 256 * 256
    packed_rows = -(-REACH * (depths + 2) // 16) * 16

    span = EDGE * count
    lines, diff_i, diff_x, smooth, pack_h, diff_h, lines_e, diff_e, pick, mask = call(
        "tables_kernel",
        lambda *refs: tables_kernel(depths, *refs),
        [
            ((rows, rows), bf16),
            ((rows, rows), bf16),
            ((cols, cols), bf16),
            ((cols, cols), bf16),
            ((256, 256), bf16),
            ((128 * TILES, 512), bf16),
            ((2, span, span), bf16),
            ((span, span), bf16),
            ((cols, 256), bf16),
            ((8, 128), f32),
        ],
        [],
        [],
        flops=work,
    )
    halo_tile = ((TILES, rows, 128), bf16)
    vol, send, own = call("pack_kernel", pack_kernel, [(volume.shape, bf16), halo_tile, halo_tile], [], [volume, pick])
    side = lax.ppermute(send, "xl", [(0, 1), (1, 0)])
    chunks = rows // EDGE - 2
    lined = [((count, chunks, 6, EDGE, cols), bf16), ((2, 6, count, EDGE, cols), f32)]
    moment_slots = [pltpu.VMEM((2, 6, rows, cols), bf16)] * 2
    inner, part = call("lines_kernel", lines_kernel, lined, moment_slots, [vol, lines, diff_i, diff_x], flops=work // 4)
    packed = ((packed_rows, cols), bf16)
    halo, near, far = call(
        "rows_kernel",
        rows_kernel,
        [((rows, 128 * TILES), bf16), packed, packed],
        [pltpu.VMEM((2, packed_rows, cols), f32)],
        [vol, own, side, part],
        in_specs=[WHOLE] * 3 + [ANYWHERE],
    )
    swap = [(i, i ^ 1) for i in range(il)]
    onward = [(i, i + 2) for i in range(0, il - 2, 2)] + [(il - 2, il - 1)]
    onward += [(i, i - 2) for i in range(3, il, 2)] + [(1, 0)]
    far_in = lax.ppermute(far, "il", swap)
    near_in = lax.ppermute(near, "il", swap)

    outs = [((count, rows, cols), f32)] * 3
    saved = ((3, 2, EDGE * chunks, cols), f32)
    border = ((6 * EDGE * chunks, 256), f32)
    ready = [((3, count // 2 - 2, EDGE * chunks, cols), f32)]
    own_scratch = moment_slots + [pltpu.VMEM((2, 6 * EDGE * chunks, cols), f32), pltpu.VMEM(*ready[0]), pltpu.SemaphoreType.DMA((count // 4 - 1, 3))]
    shared = [vol, lines, diff_i, diff_x, smooth, halo, diff_h, pack_h, mask]
    inner, part, *outs_in, done, part_h, border = call(
        "first_own_kernel",
        lambda *refs: own_kernel(0, *refs),
        lined + outs + [saved, ((2, 6, EDGE, 256), f32), border],
        own_scratch,
        shared + [inner, part],
        out_specs=(WHOLE,) * 2 + (IN_HBM,) * 3 + (WHOLE,) * 3,
        flops=3 * work,
        aliases={len(shared) + n: n for n in range(2)},
    )
    (relayed,) = call("relay_kernel", relay_kernel, [packed], [], [far_in, done], in_specs=[WHOLE, ANYWHERE])
    relayed_in = lax.ppermute(relayed, "il", onward)
    inner, part, *outs_in, done = call(
        "second_own_kernel",
        lambda *refs: own_kernel(1, *refs),
        lined + outs + [saved],
        own_scratch + [pltpu.SemaphoreType.DMA((3,))],
        shared + [inner, part, border, done] + outs_in,
        in_specs=[WHOLE] * (len(shared) + 4) + [IN_HBM] * 3,
        out_specs=(WHOLE,) * 2 + (IN_HBM,) * 3 + (WHOLE,),
        flops=3 * work,
        aliases={len(shared): 0, len(shared) + 1: 1} | {len(shared) + 4 + n: 2 + n for n in range(3)},
    )

    end_rows = (3, count, EDGE, cols)
    tables = [smooth, pack_h, diff_x, diff_h, lines_e, diff_e, mask]
    scratch = [
        pltpu.VMEM((8 + packed_rows, cols), f32),
        pltpu.VMEM((depths, EDGE, cols), bf16),
        pltpu.VMEM((EDGE, 128 * TILES), bf16),
        pltpu.VMEM((6 * EDGE, 256), f32),
        pltpu.VMEM((count, 6, EDGE, cols), bf16),
        pltpu.VMEM((2, half * 6 * EDGE, cols), f32),
    ]
    sems = pltpu.SemaphoreType.DMA((3,))
    operands = [vol, halo, near_in, part, part_h, *tables, done]
    *outs_in, done = call(
        "near_end_kernel",
        lambda *refs: end_kernel(0, *refs),
        outs + [(end_rows, f32)],
        scratch + [sems],
        operands + outs_in,
        in_specs=[WHOLE] * len(operands) + [IN_HBM] * 3,
        out_specs=(IN_HBM,) * 3 + (WHOLE,),
        flops=work,
        aliases={len(operands) + n: n for n in range(3)},
    )
    operands = [vol, halo, relayed_in, part, part_h, *tables, done]
    return call(
        "far_end_kernel",
        lambda *refs: end_kernel(1, *refs),
        outs,
        scratch + [pltpu.VMEM(end_rows, f32), sems, pltpu.SemaphoreType.DMA((2, 3))],
        operands + outs_in,
        in_specs=[WHOLE] * len(operands) + [IN_HBM] * 3,
        out_specs=(IN_HBM,) * 3,
        flops=work,
        aliases={len(operands) + n: n for n in range(3)},
    )


def solution(mesh):
    spec = P(None, ("parts", "il"), "xl")
    return jax.shard_map(body, mesh=mesh, in_specs=(spec,), out_specs=(spec,) * 3, check_vma=False)
```

```python
import jax
import jax.numpy as jnp
import ml_dtypes
import numpy as np
from jax import lax
from jax.experimental import pallas as pl
from jax.experimental.pallas import tpu as pltpu
from jax.sharding import PartitionSpec as P

RADIUS = 9
REACH = RADIUS + 1
SIDE = 16
SLOTS = 8
TILES = 3
EDGE = 16
OWN = 2
TINY = float(np.finfo(np.float32).tiny)
HEAD = 2
AHEAD = 2
FAR = -1000
WHOLE = pl.BlockSpec(memory_space=pltpu.VMEM)
IN_HBM = pl.BlockSpec(memory_space=pltpu.HBM)
ANYWHERE = pl.BlockSpec(memory_space=pl.ANY)


def filter_taps():
    offsets = np.arange(2 * RADIUS + 1).astype(np.float32)
    sigma = np.float32(RADIUS / 3.0)
    shape = np.exp(np.float32(-0.5) * ((offsets - RADIUS) / sigma) ** 2)
    return (shape / np.sum(shape, dtype=np.float32)).astype(ml_dtypes.bfloat16).astype(np.float32)


def iota(shape, dim):
    return lax.broadcasted_iota(jnp.int32, shape, dim)


def band(source, target, scale=1.0):
    offset = jnp.abs(source - target)
    weights = jnp.zeros(offset.shape, jnp.float32)
    for distance, tap in enumerate(filter_taps()[RADIUS:]):
        weights = jnp.where(offset == distance, jnp.float32(scale * tap), weights)
    return weights


def difference(source, target):
    offset = source - target
    return jnp.where(offset == 1, 1.0, jnp.where(offset == -1, -1.0, 0.0)).astype(jnp.float32)


def dot(left, right):
    return jnp.dot(left, right, preferred_element_type=jnp.float32)


def reciprocal(value):
    guess = pl.reciprocal(value, approx=True)
    return guess * (2.0 - value * guess)


def halo_plane(lane, tile, depths):
    slot = lax.div(lane, SIDE)
    rest = jnp.where(slot == 0, 0, jnp.where(slot == 1, depths - 1, FAR))
    return jnp.where(tile < 2, 1 + SLOTS * tile + slot, rest)


def halo_column(lane, x, cols):
    place = lax.rem(lane, SIDE)
    return jnp.where(x == 0, cols - OWN + place, place - (SIDE - OWN))


def low_end(exchange):
    even = lax.rem(lax.axis_index("il"), 2) == 0
    return jnp.logical_not(even) if exchange == 0 else even


def tables_kernel(depths, lines_ref, diff_i_ref, smooth_ref, pack_h_ref, diff_h_ref, lines_e_ref, diff_e_ref, pick_ref, mask_ref):
    rows, cols = lines_ref.shape[0], smooth_ref.shape[0]
    x, il, last = lax.axis_index("xl"), lax.axis_index("il"), lax.axis_size("il") - 1
    bf16 = jnp.bfloat16

    target, source = iota((rows, rows), 0), iota((rows, rows), 1)
    inner = (source > 0) & (source < rows - 1)
    lines_ref[...] = jnp.where(inner, band(source, target, 0.25), 0.0).astype(bf16)
    diff_i_ref[...] = difference(source, target).astype(bf16)
    span = EDGE * SLOTS
    target, source = iota((span, span), 0), iota((span, span), 1)
    depth = lax.div(source, EDGE) == lax.div(target, EDGE)
    target, source = lax.rem(target, EDGE), lax.rem(source, EDGE)
    diff_e_ref[...] = difference(source, target)[:EDGE, :EDGE].astype(bf16)
    for exchange in range(2):
        low = low_end(exchange)
        source_at = jnp.where(low, source - REACH, rows - (EDGE - REACH) + source)
        target_at = jnp.where(low, target, rows - EDGE + target)
        first = jnp.where(low & (il > 0), -rows, 0)
        final = jnp.where(jnp.logical_not(low) & (il < last), 2 * rows, rows - 1)
        use = depth & (source_at >= first) & (source_at <= final) & ((source_at <= 0) | (source_at >= rows - 1))
        lines_e_ref[exchange] = jnp.where(use, band(source_at, target_at, 0.25), 0.0).astype(bf16)

    source, target = iota((cols, cols), 0), iota((cols, cols), 1)
    moved = source == jnp.where(x == 0, cols - 1, 0)
    column = lax.rem(target + 128 * x, cols)
    smooth_ref[...] = jnp.where(moved, 0.0, band(source, column)).astype(bf16)
    source, target = iota((256, 256), 0), iota((256, 256), 1)
    place = lax.rem(source, SIDE)
    use = (lax.div(source, SIDE) == lax.div(target, SIDE)) & (place != jnp.where(x == 0, 0, SIDE - 1))
    column = jnp.where(x == 0, cols - SIDE, 0) + lax.rem(target, SIDE)
    pack_h_ref[...] = jnp.where(use, band(halo_column(place, x, cols), column), 0.0).astype(bf16)

    source, target = iota((128, 128), 0), iota((128, 128), 1)
    same = lax.rem(source, SIDE) == lax.rem(target, SIDE)
    across = difference(lax.rem(source, SIDE), lax.rem(target, SIDE))
    for group in range(2):
        centre = halo_plane(target, group, depths)
        for tile in range(TILES):
            plane = halo_plane(source, tile, depths)
            part, out = slice(128 * tile, 128 * (tile + 1)), 128 * group
            diff_h_ref[part, out : out + 128] = jnp.where(same, difference(plane, centre), 0.0).astype(bf16)
            diff_h_ref[part, 256 + out : 384 + out] = jnp.where(plane == centre, across, 0.0).astype(bf16)

    source, lane = iota((cols, 256), 0), iota((cols, 256), 1)
    place = lax.rem(lane, SIDE)
    low, high = place < SIDE - OWN, place >= OWN
    sent = jnp.where(x == 0, jnp.where(low, cols - (SIDE - OWN) + place, FAR), jnp.where(high, place - OWN, FAR))
    low, high = place < OWN, place >= SIDE - OWN
    kept = jnp.where(x == 0, jnp.where(low, cols - OWN + place, FAR), jnp.where(high, place - (SIDE - OWN), FAR))
    pick_ref[...] = jnp.where(source == jnp.where(lane < 128, sent, kept), 1.0, 0.0).astype(bf16)
    lane = iota((8, 128), 1)
    border = jnp.where(x == 0, lane - (128 - SIDE), lane)
    mask_ref[0] = jnp.where((border >= 0) & (border < SIDE), 1.0, 0.0)
    mask_ref[1] = jnp.where(lane > 0, 1.0, 0.0)
    mask_ref[2] = jnp.where(lane < 127, 1.0, 0.0)


def pack_kernel(vol_ref, pick_ref, copy_ref, send_ref, own_ref):
    depths, rows, cols = vol_ref.shape
    slot = lax.div(lax.rem(iota((rows, 256), 1), 128), SIDE)
    copy_ref[...] = vol_ref[...]
    picked = dot(vol_ref[...].reshape(depths * rows, cols), pick_ref[...])
    for tile in range(TILES):
        if tile < 2:
            planes = [(1 + SLOTS * tile + index, index) for index in range(SLOTS)]
        else:
            planes = [(0, 0), (depths - 1, 1)]
        packed = jnp.zeros((rows, 256), jnp.float32)
        for plane, index in planes:
            packed = jnp.where(slot == index, picked[rows * plane : rows * (plane + 1)], packed)
        packed = packed.astype(jnp.bfloat16)
        send_ref[tile] = packed[:, :128]
        own_ref[tile] = packed[:, 128:]


def rows_kernel(vol_ref, own_ref, side_ref, after_ref, halo_ref, near_ref, far_ref, packed_ref):
    depths, rows, cols = vol_ref.shape
    even = lax.rem(lax.axis_index("il"), 2) == 0

    def put(row, top, bottom):
        top, bottom = top[:REACH], bottom[EDGE - REACH :]
        lanes = top.shape[1]
        packed_ref[0, row : row + REACH, :lanes] = jnp.where(even, bottom, top)
        packed_ref[1, row : row + REACH, :lanes] = jnp.where(even, top, bottom)

    packed_ref[:, depths * REACH :, :] = jnp.zeros_like(packed_ref[:, depths * REACH :, :])
    for depth in range(depths):
        top = vol_ref[depth, :EDGE, :].astype(jnp.float32)
        bottom = vol_ref[depth, rows - EDGE :, :].astype(jnp.float32)
        put(REACH * depth, top, bottom)
    tiles = []
    for tile in range(TILES):
        merged = own_ref[tile].astype(jnp.float32) + side_ref[tile].astype(jnp.float32)
        halo_ref[:, 128 * tile : 128 * (tile + 1)] = merged.astype(jnp.bfloat16)
        tiles.append((merged[:EDGE], merged[rows - EDGE :]))
    tops = jnp.concatenate([tiles[0][0], tiles[1][0]], axis=1)
    bottoms = jnp.concatenate([tiles[0][1], tiles[1][1]], axis=1)
    put(REACH * depths, tops, bottoms)
    put(REACH * (depths + 1), *tiles[2])
    near_ref[...] = packed_ref[0].astype(jnp.bfloat16)
    far_ref[...] = packed_ref[1].astype(jnp.bfloat16)


def relay_kernel(rows_ref, after_ref, out_ref):
    out_ref[...] = rows_ref[...]


def moments(grad_i, grad_x, grad_z):
    terms = (
        grad_i * grad_i,
        grad_x * grad_x,
        grad_z * grad_z,
        grad_i * grad_x,
        grad_i * grad_z,
        grad_x * grad_z,
    )
    return [term.astype(jnp.bfloat16) for term in terms]


def store_chunks(summed, comp, inner_ref, part_ref):
    chunks = summed.shape[0] // EDGE
    for chunk in range(1, chunks - 1):
        inner_ref[chunk - 1, comp] = summed[EDGE * chunk : EDGE * (chunk + 1)].astype(jnp.bfloat16)
    part_ref[0, comp] = summed[:EDGE]
    part_ref[1, comp] = summed[EDGE * (chunks - 1) :]


def gradients(before, centre, after, mask_ref):
    rows, cols = centre.shape
    left, right = pltpu.roll(centre, 1, 1), pltpu.roll(centre, cols - 1, 1)
    left_0 = (left[:, :128].reshape(-1, 8, 128) * mask_ref[1]).reshape(rows, 128)
    right_1 = (right[:, cols - 128 :].reshape(-1, 8, 128) * mask_ref[2]).reshape(rows, 128)
    grad_x = jnp.concatenate([right[:, : cols - 128] - left_0, right_1 - left[:, 128:]], axis=1)
    return pltpu.roll(centre, rows - 1, 0) - pltpu.roll(centre, 1, 0), grad_x, after - before


def make_moments(pair, vol_ref, mask_ref, moments_ref):
    planes = [vol_ref[2 * pair + k].astype(jnp.float32) for k in range(4)]
    for k in range(2):
        for comp, term in enumerate(moments(*gradients(*planes[k : k + 3], mask_ref))):
            moments_ref[k, comp] = term


def make_lines(z, comp, lines_ref, moments_ref, inner_ref, part_ref):
    store_chunks(dot(lines_ref[...], moments_ref[z % 2, comp]), comp, inner_ref.at[z], part_ref.at[:, :, z])


def lines_kernel(vol_ref, lines_ref, mask_ref, inner_ref, part_ref, even_ref, odd_ref):
    slots = (even_ref, odd_ref)
    for pair in range(HEAD):
        make_moments(pair, vol_ref, mask_ref, slots[pair % 2])
        for k in range(2):
            for comp in range(6):
                make_lines(2 * pair + k, comp, lines_ref, slots[pair % 2], inner_ref, part_ref)


def tensor_of(own, smooth_ref, tensor_ref):
    tensor_ref[...] = dot(own.reshape(-1, own.shape[-1]), smooth_ref[...])


def attributes(tensor, border, store):
    x = lax.axis_index("xl")
    halves = (tensor[:, :128], tensor[:, 128:] + border)
    lanes = (pl.multiple_of(128 * x, 128), pl.multiple_of(128 - 128 * x, 128))
    for half, lane in zip(halves, lanes):
        a, b, c, d, e, f = [half[EDGE * comp : EDGE * (comp + 1)] for comp in range(6)]
        low = c + 1e-6
        guess = pl.reciprocal(low, approx=True)
        inverse = guess * (low * guess - 2.0)
        spread = (a - b) * (a - c) + (b - c) * (b - c) + 3.0 * (d * d + e * e + f * f)
        root = spread * lax.rsqrt(jnp.maximum(spread, TINY))
        store(pl.ds(lane, 128), (e * inverse, f * inverse, root * reciprocal(a + b + low)))


def border_of(packed, slot, mask_ref):
    base = jnp.where(lax.axis_index("xl") == 0, 128 - SIDE, 0)
    moved = pltpu.roll(packed, lax.rem(base - SIDE * slot + 128, 128), 1)
    return (moved.reshape(-1, 8, 128) * mask_ref[0]).reshape(packed.shape)


def own_kernel(
    stage, vol_ref, lines_ref, diff_i_ref, smooth_ref, halo_ref, diff_h_ref, pack_h_ref, mask_ref,
    inner_in_ref, part_in_ref, *refs,
):
    if stage == 0:
        inner_ref, part_ref, *targets, later_ref, part_h_ref, border_ref, even_ref, odd_ref, tensor_ref, out_ref, sems = refs
        both = dot(halo_ref[...], diff_h_ref[...])
        grad_i = dot(diff_i_ref[...], halo_ref[:, :256])
        lined_h = [[] for chunk in range(inner_ref.shape[1])]
        for comp, term in enumerate(moments(grad_i, both[:, 256:], both[:, :256])):
            summed = dot(lines_ref[...], term)
            for chunk, parts in enumerate(lined_h):
                parts.append(summed[EDGE * (chunk + 1) : EDGE * (chunk + 2)].astype(jnp.bfloat16))
            part_h_ref[0, comp] = summed[:EDGE]
            part_h_ref[1, comp] = summed[EDGE * (len(lined_h) + 1) :]
        border_ref[...] = dot(jnp.concatenate(sum(lined_h, []), axis=0), pack_h_ref[...])
        finished = []
    else:
        border_ref, done_ref, *refs = refs
        inner_ref, part_ref, *targets, later_ref, even_ref, odd_ref, tensor_ref, out_ref, sems, done_sems = refs[3:]
        finished = []
    count, chunks = inner_ref.shape[:2]
    pairs, inner = count // 4, EDGE * chunks
    slots = (even_ref, odd_ref)

    def place(target, pair):
        return target.at[pl.ds(2 * pair, 2), pl.ds(EDGE, inner)]

    if stage == 1:
        for n, target in enumerate(targets):
            finished.append(pltpu.make_async_copy(done_ref.at[n], place(target, pairs - 1), done_sems.at[n]))
            finished[-1].start()

    half = count // 2
    ahead = range(2 * HEAD, half + 2 * AHEAD) if stage == 0 else range(half + 2 * AHEAD, count)
    tensor_of(inner_ref[half * stage], smooth_ref, tensor_ref.at[0])
    for step in range(half):
        z = half * stage + step
        later = ahead[step] if step < len(ahead) else None
        if later is not None and later % 2 == 0:
            make_moments(later // 2, vol_ref, mask_ref, slots[later // 2 % 2])
        if step < half - 1:
            tensor_of(inner_ref[z + 1], smooth_ref, tensor_ref.at[(step + 1) % 2])
        for chunk in range(chunks):
            rows = slice(EDGE * chunk, EDGE * (chunk + 1))
            part = slice(6 * EDGE * chunk, 6 * EDGE * (chunk + 1))

            def store(lanes, values):
                for n, value in enumerate(values):
                    if step >= half - 2:
                        later_ref[n, step % 2, rows, lanes] = value
                    else:
                        out_ref[n, step, rows, lanes] = value

            border = border_of(border_ref[part, 128 * stage : 128 * (stage + 1)], z % SLOTS, mask_ref)
            attributes(tensor_ref[step % 2, part], border, store)
            if later is not None:
                make_lines(later, chunk, lines_ref, slots[later // 2 % 2], inner_ref, part_ref)
        if step % 2 == 1 and step < half - 2:
            for n, target in enumerate(targets):
                source = out_ref.at[n, pl.ds(step - 1, 2)]
                finished.append(pltpu.make_async_copy(source, place(target, z // 2), sems.at[step // 2, n]))
                finished[-1].start()
    for copy in finished:
        copy.wait()


def end_kernel(
    exchange, vol_ref, halo_ref, rows_ref, part_ref, part_h_ref,
    smooth_ref, pack_h_ref, diff_h_ref, lines_e_ref, diff_e_ref, mask_ref, done_ref, *refs,
):
    last = exchange == 1
    targets, refs = refs[3:6], refs[6:]
    if last:
        packed_ref, block_ref, block_h_ref, border_ref, edge_ref, tensor_ref, out_ref, done_sems, sems = refs
    else:
        out_ref, packed_ref, block_ref, block_h_ref, border_ref, edge_ref, tensor_ref, done_sems = refs
    depths, rows, cols = vol_ref.shape
    count, half = depths - 2, (depths - 2) // 2
    bf16, f32 = jnp.bfloat16, jnp.float32
    low = low_end(exchange)
    end = jnp.where(low, 0, 1)
    start = pl.multiple_of(jnp.where(low, 0, rows - EDGE), EDGE)
    other = pl.multiple_of(jnp.where(low, rows - EDGE, 0), EDGE)
    finished = []
    for n, target in enumerate(targets):
        if last:
            place = target.at[:, pl.ds(other, EDGE)]
        else:
            place = target.at[pl.ds(count - 2, 2), pl.ds(EDGE, rows - 2 * EDGE)]
        finished.append(pltpu.make_async_copy(done_ref.at[n], place, done_sems.at[n]))
    for copy in finished:
        copy.start()

    packed_ref[:8] = jnp.zeros_like(packed_ref[:8])
    if last:
        il = lax.axis_index("il")
        outside = (low & (il == 0)) | (jnp.logical_not(low) & (il == lax.axis_size("il") - 1))
        packed_ref[8:] = jnp.where(outside, 0.0, rows_ref[...].astype(f32))
    else:
        packed_ref[8:] = rows_ref[...].astype(f32)

    def joined(row, own):
        lanes = own.shape[1]
        before = packed_ref[8 + row : 8 + row + EDGE, :lanes]
        after = packed_ref[8 + row - (EDGE - REACH) : 8 + row + REACH, :lanes]
        own = own.astype(f32)
        place = iota(own.shape, 0)
        first = jnp.where(place < REACH, before, pltpu.roll(own, REACH, 0))
        second = jnp.where(place < EDGE - REACH, pltpu.roll(own, EDGE - REACH, 0), after)
        return jnp.where(low, first, second).astype(bf16)

    for depth in range(depths):
        block_ref[depth] = joined(REACH * depth, vol_ref[depth, pl.ds(start, EDGE)])
    own_h = halo_ref[pl.ds(start, EDGE)]
    block_h_ref[:, :256] = joined(REACH * depths, own_h[:, :256])
    block_h_ref[:, 256:] = joined(REACH * (depths + 1), own_h[:, 256:])

    both = dot(block_h_ref[...], diff_h_ref[...])
    grad_i = dot(diff_e_ref[...], block_h_ref[:, :256])
    lined_h = []
    for comp, term in enumerate(moments(grad_i, both[:, 256:], both[:, :256])):
        summed = part_h_ref[end, comp] + dot(lines_e_ref[exchange, :EDGE, :EDGE], term)
        lined_h.append(summed.astype(bf16))
    border_ref[...] = dot(jnp.concatenate(lined_h, axis=0), pack_h_ref[...])

    span = EDGE * half
    copies = []
    def make_block_moments(group):
        first = half * group
        planes = [block_ref[first + k : first + half + k].astype(f32).reshape(span, cols) for k in range(3)]
        return moments(*gradients(*planes, mask_ref))

    def make_edge(group, comp, term):
        first = half * group
        outer = dot(lines_e_ref[exchange, :span, :span], term)
        summed = part_ref[end, comp, first : first + half] + outer.reshape(half, EDGE, cols)
        edge_ref[first : first + half, comp] = summed.astype(bf16)

    def finish(group, k):
        def store(lanes, values):
            for n, value in enumerate(values):
                out_ref[n, half * group + k, :, lanes] = value

        border = border_of(border_ref[:, 128 * group : 128 * (group + 1)], k, mask_ref)
        attributes(tensor_ref[group, 6 * EDGE * k : 6 * EDGE * (k + 1)], border, store)

    def send(group):
        depth = pl.ds(half * group, half)
        for n, target in enumerate(targets):
            copy = pltpu.make_async_copy(out_ref.at[n, depth], target.at[depth, pl.ds(start, EDGE)], sems.at[group, n])
            copy.start()
            copies.append(copy)

    for comp, term in enumerate(make_block_moments(0)):
        make_edge(0, comp, term)
    later = make_block_moments(1)
    tensor_of(edge_ref[:half], smooth_ref, tensor_ref.at[0])
    for k in range(half):
        if k < 6:
            make_edge(1, k, later[k])
        finish(0, k)
    if last:
        send(0)
    tensor_of(edge_ref[half:], smooth_ref, tensor_ref.at[1])
    for k in range(half):
        finish(1, k)
    if last:
        send(1)
    for copy in finished + copies:
        copy.wait()


def call(name, kernel, outs, scratch, operands, in_specs=None, out_specs=None, flops=0, limit=16, aliases={}):
    return pl.pallas_call(
        kernel,
        out_shape=tuple(jax.ShapeDtypeStruct(*out) for out in outs),
        in_specs=in_specs or [WHOLE] * len(operands),
        out_specs=out_specs or (WHOLE,) * len(outs),
        scratch_shapes=scratch,
        compiler_params=pltpu.CompilerParams(vmem_limit_bytes=limit << 20),
        name=name,
        input_output_aliases=aliases,
        cost_estimate=pl.CostEstimate(flops=flops, bytes_accessed=0, transcendentals=0),
    )(*operands)


def body(volume):
    depths, rows, cols = volume.shape
    il, xl = lax.axis_size("il"), lax.axis_size("xl")
    count = depths - 2
    assert xl == 2 and il % 2 == 0 and count == 2 * SLOTS and rows == 128 and cols == 256
    bf16, f32 = jnp.bfloat16, jnp.float32
    half = count // 2
    work = half * 1024 * 2 * 256 * 256
    packed_rows = -(-REACH * (depths + 2) // 16) * 16

    span = EDGE * SLOTS
    lines, diff_i, smooth, pack_h, diff_h, lines_e, diff_e, pick, mask = call(
        "tables_kernel",
        lambda *refs: tables_kernel(depths, *refs),
        [
            ((rows, rows), bf16),
            ((rows, rows), bf16),
            ((cols, cols), bf16),
            ((256, 256), bf16),
            ((128 * TILES, 512), bf16),
            ((2, span, span), bf16),
            ((EDGE, EDGE), bf16),
            ((cols, 256), bf16),
            ((3, 8, 128), f32),
        ],
        [],
        [],
        flops=work,
    )
    halo_tile = ((TILES, rows, 128), bf16)
    vol, send, own = call("pack_kernel", pack_kernel, [(volume.shape, bf16), halo_tile, halo_tile], [], [volume, pick])
    side = lax.ppermute(send, "xl", [(0, 1), (1, 0)])
    chunks = rows // EDGE - 2
    lined = [((count, chunks, 6, EDGE, cols), bf16), ((2, 6, count, EDGE, cols), f32)]
    moment_slots = [pltpu.VMEM((2, 6, rows, cols), bf16)] * 2
    inner, part = call("lines_kernel", lines_kernel, lined, moment_slots, [vol, lines, mask], flops=work // 4)
    packed = ((packed_rows, cols), bf16)
    halo, near, far = call(
        "rows_kernel",
        rows_kernel,
        [((rows, 128 * TILES), bf16), packed, packed],
        [pltpu.VMEM((2, packed_rows, cols), f32)],
        [vol, own, side, part],
        in_specs=[WHOLE] * 3 + [ANYWHERE],
    )
    swap = [(i, i ^ 1) for i in range(il)]
    onward = [(i, i + 2) for i in range(0, il - 2, 2)] + [(il - 2, il - 1)]
    onward += [(i, i - 2) for i in range(3, il, 2)] + [(1, 0)]
    far_in = lax.ppermute(far, "il", swap)
    near_in = lax.ppermute(near, "il", swap)

    outs = [((count, rows, cols), f32)] * 3
    saved = ((3, 2, EDGE * chunks, cols), f32)
    border = ((6 * EDGE * chunks, 256), f32)
    ready = [((3, count // 2 - 2, EDGE * chunks, cols), f32)]
    own_scratch = moment_slots + [pltpu.VMEM((2, 6 * EDGE * chunks, cols), f32), pltpu.VMEM(*ready[0]), pltpu.SemaphoreType.DMA((count // 4 - 1, 3))]
    shared = [vol, lines, diff_i, smooth, halo, diff_h, pack_h, mask]
    inner, part, *outs_in, done, part_h, border = call(
        "first_own_kernel",
        lambda *refs: own_kernel(0, *refs),
        lined + outs + [saved, ((2, 6, EDGE, 256), f32), border],
        own_scratch,
        shared + [inner, part],
        out_specs=(WHOLE,) * 2 + (IN_HBM,) * 3 + (WHOLE,) * 3,
        flops=3 * work,
        aliases={len(shared) + n: n for n in range(2)},
    )
    (relayed,) = call("relay_kernel", relay_kernel, [packed], [], [far_in, done], in_specs=[WHOLE, ANYWHERE])
    relayed_in = lax.ppermute(relayed, "il", onward)
    inner, part, *outs_in, done = call(
        "second_own_kernel",
        lambda *refs: own_kernel(1, *refs),
        lined + outs + [saved],
        own_scratch + [pltpu.SemaphoreType.DMA((3,))],
        shared + [inner, part, border, done] + outs_in,
        in_specs=[WHOLE] * (len(shared) + 4) + [IN_HBM] * 3,
        out_specs=(WHOLE,) * 2 + (IN_HBM,) * 3 + (WHOLE,),
        flops=3 * work,
        aliases={len(shared): 0, len(shared) + 1: 1} | {len(shared) + 4 + n: 2 + n for n in range(3)},
    )

    end_rows = (3, count, EDGE, cols)
    tables = [smooth, pack_h, diff_h, lines_e, diff_e, mask]
    scratch = [
        pltpu.VMEM((8 + packed_rows, cols), f32),
        pltpu.VMEM((depths, EDGE, cols), bf16),
        pltpu.VMEM((EDGE, 128 * TILES), bf16),
        pltpu.VMEM((6 * EDGE, 256), f32),
        pltpu.VMEM((count, 6, EDGE, cols), bf16),
        pltpu.VMEM((2, half * 6 * EDGE, cols), f32),
    ]
    sems = pltpu.SemaphoreType.DMA((3,))
    operands = [vol, halo, near_in, part, part_h, *tables, done]
    *outs_in, done = call(
        "near_end_kernel",
        lambda *refs: end_kernel(0, *refs),
        outs + [(end_rows, f32)],
        scratch + [sems],
        operands + outs_in,
        in_specs=[WHOLE] * len(operands) + [IN_HBM] * 3,
        out_specs=(IN_HBM,) * 3 + (WHOLE,),
        flops=work,
        aliases={len(operands) + n: n for n in range(3)},
    )
    operands = [vol, halo, relayed_in, part, part_h, *tables, done]
    return call(
        "far_end_kernel",
        lambda *refs: end_kernel(1, *refs),
        outs,
        scratch + [pltpu.VMEM(end_rows, f32), sems, pltpu.SemaphoreType.DMA((2, 3))],
        operands + outs_in,
        in_specs=[WHOLE] * len(operands) + [IN_HBM] * 3,
        out_specs=(IN_HBM,) * 3,
        flops=work,
        aliases={len(operands) + n: n for n in range(3)},
    )


def solution(mesh):
    spec = P(None, ("parts", "il"), "xl")
    return jax.shard_map(body, mesh=mesh, in_specs=(spec,), out_specs=(spec,) * 3, check_vma=False)
```

```python
import jax
import jax.numpy as jnp
import ml_dtypes
import numpy as np
from jax import lax
from jax.experimental import pallas as pl
from jax.experimental.pallas import tpu as pltpu
from jax.sharding import PartitionSpec as P

RADIUS = 9
REACH = RADIUS + 1
SIDE = 16
SLOTS = 8
TILES = 3
EDGE = 16
OWN = 2
TINY = float(np.finfo(np.float32).tiny)
HEAD = 2
FAR = -1000
WHOLE = pl.BlockSpec(memory_space=pltpu.VMEM)
IN_HBM = pl.BlockSpec(memory_space=pltpu.HBM)
ANYWHERE = pl.BlockSpec(memory_space=pl.ANY)


def filter_taps():
    offsets = np.arange(2 * RADIUS + 1).astype(np.float32)
    sigma = np.float32(RADIUS / 3.0)
    shape = np.exp(np.float32(-0.5) * ((offsets - RADIUS) / sigma) ** 2)
    return (shape / np.sum(shape, dtype=np.float32)).astype(ml_dtypes.bfloat16).astype(np.float32)


def iota(shape, dim):
    return lax.broadcasted_iota(jnp.int32, shape, dim)


def band(source, target, scale=1.0):
    offset = jnp.abs(source - target)
    weights = jnp.zeros(offset.shape, jnp.float32)
    for distance, tap in enumerate(filter_taps()[RADIUS:]):
        weights = jnp.where(offset == distance, jnp.float32(scale * tap), weights)
    return weights


def difference(source, target):
    offset = source - target
    return jnp.where(offset == 1, 1.0, jnp.where(offset == -1, -1.0, 0.0)).astype(jnp.float32)


def dot(left, right):
    return jnp.dot(left, right, preferred_element_type=jnp.float32)


def reciprocal(value):
    guess = pl.reciprocal(value, approx=True)
    return guess * (2.0 - value * guess)


def halo_plane(lane, tile, depths):
    slot = lax.div(lane, SIDE)
    rest = jnp.where(slot == 0, 0, jnp.where(slot == 1, depths - 1, FAR))
    return jnp.where(tile < 2, 1 + SLOTS * tile + slot, rest)


def halo_column(lane, x, cols):
    place = lax.rem(lane, SIDE)
    return jnp.where(x == 0, cols - OWN + place, place - (SIDE - OWN))


def low_end(exchange):
    even = lax.rem(lax.axis_index("il"), 2) == 0
    return jnp.logical_not(even) if exchange == 0 else even


def tables_kernel(depths, lines_ref, diff_i_ref, smooth_ref, pack_h_ref, diff_h_ref, lines_e_ref, diff_e_ref, pick_ref, mask_ref):
    rows, cols = lines_ref.shape[0], smooth_ref.shape[0]
    x, il, last = lax.axis_index("xl"), lax.axis_index("il"), lax.axis_size("il") - 1
    bf16 = jnp.bfloat16

    target, source = iota((rows, rows), 0), iota((rows, rows), 1)
    inner = (source > 0) & (source < rows - 1)
    lines_ref[...] = jnp.where(inner, band(source, target, 0.25), 0.0).astype(bf16)
    diff_i_ref[...] = difference(source, target).astype(bf16)
    span = EDGE * SLOTS
    target, source = iota((span, span), 0), iota((span, span), 1)
    depth = lax.div(source, EDGE) == lax.div(target, EDGE)
    target, source = lax.rem(target, EDGE), lax.rem(source, EDGE)
    diff_e_ref[...] = difference(source, target)[:EDGE, :EDGE].astype(bf16)
    for exchange in range(2):
        low = low_end(exchange)
        source_at = jnp.where(low, source - REACH, rows - (EDGE - REACH) + source)
        target_at = jnp.where(low, target, rows - EDGE + target)
        first = jnp.where(low & (il > 0), -rows, 0)
        final = jnp.where(jnp.logical_not(low) & (il < last), 2 * rows, rows - 1)
        use = depth & (source_at >= first) & (source_at <= final) & ((source_at <= 0) | (source_at >= rows - 1))
        lines_e_ref[exchange] = jnp.where(use, band(source_at, target_at, 0.25), 0.0).astype(bf16)

    source, target = iota((cols, cols), 0), iota((cols, cols), 1)
    moved = source == jnp.where(x == 0, cols - 1, 0)
    column = lax.rem(target + 128 * x, cols)
    smooth_ref[...] = jnp.where(moved, 0.0, band(source, column)).astype(bf16)
    source, target = iota((256, 256), 0), iota((256, 256), 1)
    place = lax.rem(source, SIDE)
    use = (lax.div(source, SIDE) == lax.div(target, SIDE)) & (place != jnp.where(x == 0, 0, SIDE - 1))
    column = jnp.where(x == 0, cols - SIDE, 0) + lax.rem(target, SIDE)
    pack_h_ref[...] = jnp.where(use, band(halo_column(place, x, cols), column), 0.0).astype(bf16)

    source, target = iota((128, 128), 0), iota((128, 128), 1)
    same = lax.rem(source, SIDE) == lax.rem(target, SIDE)
    across = difference(lax.rem(source, SIDE), lax.rem(target, SIDE))
    for group in range(2):
        centre = halo_plane(target, group, depths)
        for tile in range(TILES):
            plane = halo_plane(source, tile, depths)
            part, out = slice(128 * tile, 128 * (tile + 1)), 128 * group
            diff_h_ref[part, out : out + 128] = jnp.where(same, difference(plane, centre), 0.0).astype(bf16)
            diff_h_ref[part, 256 + out : 384 + out] = jnp.where(plane == centre, across, 0.0).astype(bf16)

    source, lane = iota((cols, 256), 0), iota((cols, 256), 1)
    place = lax.rem(lane, SIDE)
    low, high = place < SIDE - OWN, place >= OWN
    sent = jnp.where(x == 0, jnp.where(low, cols - (SIDE - OWN) + place, FAR), jnp.where(high, place - OWN, FAR))
    low, high = place < OWN, place >= SIDE - OWN
    kept = jnp.where(x == 0, jnp.where(low, cols - OWN + place, FAR), jnp.where(high, place - (SIDE - OWN), FAR))
    pick_ref[...] = jnp.where(source == jnp.where(lane < 128, sent, kept), 1.0, 0.0).astype(bf16)
    lane = iota((8, 128), 1)
    border = jnp.where(x == 0, lane - (128 - SIDE), lane)
    mask_ref[0] = jnp.where((border >= 0) & (border < SIDE), 1.0, 0.0)
    mask_ref[1] = jnp.where(lane > 0, 1.0, 0.0)
    mask_ref[2] = jnp.where(lane < 127, 1.0, 0.0)


def pack_kernel(vol_ref, pick_ref, copy_ref, send_ref, own_ref):
    depths, rows, cols = vol_ref.shape
    slot = lax.div(lax.rem(iota((rows, 256), 1), 128), SIDE)
    copy_ref[...] = vol_ref[...]
    picked = dot(vol_ref[...].reshape(depths * rows, cols), pick_ref[...])
    for tile in range(TILES):
        if tile < 2:
            planes = [(1 + SLOTS * tile + index, index) for index in range(SLOTS)]
        else:
            planes = [(0, 0), (depths - 1, 1)]
        packed = jnp.zeros((rows, 256), jnp.float32)
        for plane, index in planes:
            packed = jnp.where(slot == index, picked[rows * plane : rows * (plane + 1)], packed)
        packed = packed.astype(jnp.bfloat16)
        send_ref[tile] = packed[:, :128]
        own_ref[tile] = packed[:, 128:]


def rows_kernel(vol_ref, own_ref, side_ref, after_ref, halo_ref, near_ref, far_ref, packed_ref):
    depths, rows, cols = vol_ref.shape
    even = lax.rem(lax.axis_index("il"), 2) == 0

    def put(row, top, bottom):
        top, bottom = top[:REACH], bottom[EDGE - REACH :]
        lanes = top.shape[1]
        packed_ref[0, row : row + REACH, :lanes] = jnp.where(even, bottom, top)
        packed_ref[1, row : row + REACH, :lanes] = jnp.where(even, top, bottom)

    packed_ref[:, depths * REACH :, :] = jnp.zeros_like(packed_ref[:, depths * REACH :, :])
    for depth in range(depths):
        top = vol_ref[depth, :EDGE, :].astype(jnp.float32)
        bottom = vol_ref[depth, rows - EDGE :, :].astype(jnp.float32)
        put(REACH * depth, top, bottom)
    tiles = []
    for tile in range(TILES):
        merged = own_ref[tile].astype(jnp.float32) + side_ref[tile].astype(jnp.float32)
        halo_ref[:, 128 * tile : 128 * (tile + 1)] = merged.astype(jnp.bfloat16)
        tiles.append((merged[:EDGE], merged[rows - EDGE :]))
    tops = jnp.concatenate([tiles[0][0], tiles[1][0]], axis=1)
    bottoms = jnp.concatenate([tiles[0][1], tiles[1][1]], axis=1)
    put(REACH * depths, tops, bottoms)
    put(REACH * (depths + 1), *tiles[2])
    near_ref[...] = packed_ref[0].astype(jnp.bfloat16)
    far_ref[...] = packed_ref[1].astype(jnp.bfloat16)


def relay_kernel(rows_ref, after_ref, out_ref):
    out_ref[...] = rows_ref[...]


def moments(grad_i, grad_x, grad_z):
    terms = (
        grad_i * grad_i,
        grad_x * grad_x,
        grad_z * grad_z,
        grad_i * grad_x,
        grad_i * grad_z,
        grad_x * grad_z,
    )
    return [term.astype(jnp.bfloat16) for term in terms]


def store_chunks(summed, comp, inner_ref, part_ref):
    chunks = summed.shape[0] // EDGE
    for chunk in range(1, chunks - 1):
        inner_ref[chunk - 1, comp] = summed[EDGE * chunk : EDGE * (chunk + 1)].astype(jnp.bfloat16)
    part_ref[0, comp] = summed[:EDGE]
    part_ref[1, comp] = summed[EDGE * (chunks - 1) :]


def gradients(before, centre, after, mask_ref):
    rows, cols = centre.shape
    left, right = pltpu.roll(centre, 1, 1), pltpu.roll(centre, cols - 1, 1)
    left_0 = (left[:, :128].reshape(-1, 8, 128) * mask_ref[1]).reshape(rows, 128)
    right_1 = (right[:, cols - 128 :].reshape(-1, 8, 128) * mask_ref[2]).reshape(rows, 128)
    grad_x = jnp.concatenate([right[:, : cols - 128] - left_0, right_1 - left[:, 128:]], axis=1)
    return pltpu.roll(centre, rows - 1, 0) - pltpu.roll(centre, 1, 0), grad_x, after - before


def make_moments(pair, vol_ref, mask_ref, moments_ref):
    planes = [vol_ref[2 * pair + k].astype(jnp.float32) for k in range(4)]
    for k in range(2):
        for comp, term in enumerate(moments(*gradients(*planes[k : k + 3], mask_ref))):
            moments_ref[k, comp] = term


def make_lines(pair, k, comp, lines_ref, moments_ref, inner_ref, part_ref):
    z = 2 * pair + k
    store_chunks(dot(lines_ref[...], moments_ref[k, comp]), comp, inner_ref.at[z], part_ref.at[:, :, z])


def lines_kernel(vol_ref, lines_ref, mask_ref, inner_ref, part_ref, moments_ref):
    def step(pair, carry):
        make_moments(pair, vol_ref, mask_ref, moments_ref)
        for k in range(2):
            for comp in range(6):
                make_lines(pair, k, comp, lines_ref, moments_ref, inner_ref, part_ref)
        return carry

    lax.fori_loop(0, HEAD, step, 0)


def tensor_of(own, smooth_ref, tensor_ref):
    tensor_ref[...] = dot(own.reshape(-1, own.shape[-1]), smooth_ref[...])


def attributes(tensor, border, store):
    x = lax.axis_index("xl")
    halves = (tensor[:, :128], tensor[:, 128:] + border)
    lanes = (pl.multiple_of(128 * x, 128), pl.multiple_of(128 - 128 * x, 128))
    for half, lane in zip(halves, lanes):
        a, b, c, d, e, f = [half[EDGE * comp : EDGE * (comp + 1)] for comp in range(6)]
        low = c + 1e-6
        guess = pl.reciprocal(low, approx=True)
        inverse = guess * (low * guess - 2.0)
        spread = (a - b) * (a - c) + (b - c) * (b - c) + 3.0 * (d * d + e * e + f * f)
        root = spread * lax.rsqrt(jnp.maximum(spread, TINY))
        store(pl.ds(lane, 128), (e * inverse, f * inverse, root * reciprocal(a + b + low)))


def border_of(packed, slot, mask_ref):
    base = jnp.where(lax.axis_index("xl") == 0, 128 - SIDE, 0)
    moved = pltpu.roll(packed, lax.rem(base - SIDE * slot + 128, 128), 1)
    return (moved.reshape(-1, 8, 128) * mask_ref[0]).reshape(packed.shape)


def own_kernel(
    stage, vol_ref, lines_ref, diff_i_ref, smooth_ref, halo_ref, diff_h_ref, pack_h_ref, mask_ref,
    inner_in_ref, part_in_ref, *refs,
):
    if stage == 0:
        inner_ref, part_ref, *targets, out_ref, part_h_ref, border_ref, moments_ref, tensor_ref, sems = refs
        both = dot(halo_ref[...], diff_h_ref[...])
        grad_i = dot(diff_i_ref[...], halo_ref[:, :256])
        lined_h = [[] for chunk in range(inner_ref.shape[1])]
        for comp, term in enumerate(moments(grad_i, both[:, 256:], both[:, :256])):
            summed = dot(lines_ref[...], term)
            for chunk, parts in enumerate(lined_h):
                parts.append(summed[EDGE * (chunk + 1) : EDGE * (chunk + 2)].astype(jnp.bfloat16))
            part_h_ref[0, comp] = summed[:EDGE]
            part_h_ref[1, comp] = summed[EDGE * (len(lined_h) + 1) :]
        border_ref[...] = dot(jnp.concatenate(sum(lined_h, []), axis=0), pack_h_ref[...])
    else:
        border_ref, done_ref, *refs = refs
        inner_ref, part_ref, *targets, out_ref, moments_ref, tensor_ref, sems, done_sems = refs[3:]
    count, chunks = inner_ref.shape[:2]
    pairs, inner = count // 4, EDGE * chunks
    origin = pairs * stage

    def copies(source_ref, step, pair, sem):
        rows = pl.ds(EDGE, inner)
        return [
            pltpu.make_async_copy(source_ref.at[n, pl.ds(2 * step, 2)], target.at[pl.ds(2 * pair, 2), rows], sem.at[n])
            for n, target in enumerate(targets)
        ]

    finished = []
    if stage == 1:
        finished += copies(done_ref, pairs - 1, pairs - 1, done_sems)
        for copy in finished:
            copy.start()

    def make_tensors(pair):
        for k in range(2):
            tensor_of(inner_ref[2 * pair + k], smooth_ref, tensor_ref.at[k])

    def run(first, stop, ahead):
        def step(index, carry):
            pair = origin + index
            for k in range(2):
                slot = lax.rem(2 * pair + k, SLOTS)
                for chunk in range(chunks):
                    rows = slice(EDGE * chunk, EDGE * (chunk + 1))
                    part = slice(6 * EDGE * chunk, 6 * EDGE * (chunk + 1))

                    def store(lanes, values):
                        for n, value in enumerate(values):
                            out_ref[n, 2 * index + k, rows, lanes] = value

                    border = border_of(border_ref[part, 128 * stage : 128 * (stage + 1)], slot, mask_ref)
                    attributes(tensor_ref[k, part], border, store)
                    if ahead:
                        make_lines(pair + ahead, k, chunk, lines_ref, moments_ref, inner_ref, part_ref)
            make_tensors(jnp.minimum(pair + 1, 2 * pairs - 1))
            if ahead:
                make_moments(jnp.minimum(pair + ahead + 1, 2 * pairs - 1), vol_ref, mask_ref, moments_ref)

            @pl.when(index < pairs - 1)
            def _():
                for copy in copies(out_ref, index, pair, sems.at[index]):
                    copy.start()

            return carry

        lax.fori_loop(first, stop, step, 0)

    make_tensors(origin)
    if stage == 0:
        make_moments(HEAD, vol_ref, mask_ref, moments_ref)
        run(0, pairs, HEAD)
    else:
        make_moments(pairs + HEAD, vol_ref, mask_ref, moments_ref)
        run(0, pairs - HEAD, HEAD)
        run(pairs - HEAD, pairs, 0)
    for step in range(pairs - 1):
        finished += copies(out_ref, step, origin + step, sems.at[step])
    for copy in finished:
        copy.wait()


def end_kernel(
    exchange, vol_ref, halo_ref, rows_ref, part_ref, part_h_ref,
    smooth_ref, pack_h_ref, diff_h_ref, lines_e_ref, diff_e_ref, mask_ref, done_ref, *refs,
):
    last = exchange == 1
    targets, refs = refs[3:6], refs[6:]
    if last:
        packed_ref, block_ref, block_h_ref, border_ref, edge_ref, tensor_ref, out_ref, done_sems, sems = refs
    else:
        out_ref, packed_ref, block_ref, block_h_ref, border_ref, edge_ref, tensor_ref, done_sems = refs
    depths, rows, cols = vol_ref.shape
    count, half = depths - 2, (depths - 2) // 2
    bf16, f32 = jnp.bfloat16, jnp.float32
    low = low_end(exchange)
    end = jnp.where(low, 0, 1)
    start = pl.multiple_of(jnp.where(low, 0, rows - EDGE), EDGE)
    other = pl.multiple_of(jnp.where(low, rows - EDGE, 0), EDGE)
    finished = []
    for n, target in enumerate(targets):
        if last:
            copy = pltpu.make_async_copy(done_ref.at[n], target.at[:, pl.ds(other, EDGE)], done_sems.at[n])
        else:
            place = target.at[pl.ds(count - 2, 2), pl.ds(EDGE, rows - 2 * EDGE)]
            copy = pltpu.make_async_copy(done_ref.at[n, pl.ds(half - 2, 2)], place, done_sems.at[n])
        finished.append(copy)
    for copy in finished:
        copy.start()

    packed_ref[:8] = jnp.zeros_like(packed_ref[:8])
    if last:
        il = lax.axis_index("il")
        outside = (low & (il == 0)) | (jnp.logical_not(low) & (il == lax.axis_size("il") - 1))
        packed_ref[8:] = jnp.where(outside, 0.0, rows_ref[...].astype(f32))
    else:
        packed_ref[8:] = rows_ref[...].astype(f32)

    def joined(row, own):
        lanes = own.shape[1]
        before = packed_ref[8 + row : 8 + row + EDGE, :lanes]
        after = packed_ref[8 + row - (EDGE - REACH) : 8 + row + REACH, :lanes]
        own = own.astype(f32)
        place = iota(own.shape, 0)
        first = jnp.where(place < REACH, before, pltpu.roll(own, REACH, 0))
        second = jnp.where(place < EDGE - REACH, pltpu.roll(own, EDGE - REACH, 0), after)
        return jnp.where(low, first, second).astype(bf16)

    for depth in range(depths):
        block_ref[depth] = joined(REACH * depth, vol_ref[depth, pl.ds(start, EDGE)])
    own_h = halo_ref[pl.ds(start, EDGE)]
    block_h_ref[:, :256] = joined(REACH * depths, own_h[:, :256])
    block_h_ref[:, 256:] = joined(REACH * (depths + 1), own_h[:, 256:])

    both = dot(block_h_ref[...], diff_h_ref[...])
    grad_i = dot(diff_e_ref[...], block_h_ref[:, :256])
    lined_h = []
    for comp, term in enumerate(moments(grad_i, both[:, 256:], both[:, :256])):
        summed = part_h_ref[end, comp] + dot(lines_e_ref[exchange, :EDGE, :EDGE], term)
        lined_h.append(summed.astype(bf16))
    border_ref[...] = dot(jnp.concatenate(lined_h, axis=0), pack_h_ref[...])

    span = EDGE * half
    copies = []
    def make_block_moments(group):
        first = half * group
        planes = [block_ref[first + k : first + half + k].astype(f32).reshape(span, cols) for k in range(3)]
        return moments(*gradients(*planes, mask_ref))

    def make_edge(group, comp, term):
        first = half * group
        outer = dot(lines_e_ref[exchange, :span, :span], term)
        summed = part_ref[end, comp, first : first + half] + outer.reshape(half, EDGE, cols)
        edge_ref[first : first + half, comp] = summed.astype(bf16)

    def finish(group, k):
        def store(lanes, values):
            for n, value in enumerate(values):
                out_ref[n, half * group + k, :, lanes] = value

        border = border_of(border_ref[:, 128 * group : 128 * (group + 1)], k, mask_ref)
        attributes(tensor_ref[group, 6 * EDGE * k : 6 * EDGE * (k + 1)], border, store)

    def send(group):
        depth = pl.ds(half * group, half)
        for n, target in enumerate(targets):
            copy = pltpu.make_async_copy(out_ref.at[n, depth], target.at[depth, pl.ds(start, EDGE)], sems.at[group, n])
            copy.start()
            copies.append(copy)

    for group in range(2):
        for comp, term in enumerate(make_block_moments(group)):
            make_edge(group, comp, term)
    for group in range(2):
        tensor_of(edge_ref[half * group : half * (group + 1)], smooth_ref, tensor_ref.at[group])
        for k in range(half):
            finish(group, k)
        if last:
            send(group)
    for copy in finished + copies:
        copy.wait()


def call(name, kernel, outs, scratch, operands, in_specs=None, out_specs=None, flops=0, limit=16, aliases={}):
    return pl.pallas_call(
        kernel,
        out_shape=tuple(jax.ShapeDtypeStruct(*out) for out in outs),
        in_specs=in_specs or [WHOLE] * len(operands),
        out_specs=out_specs or (WHOLE,) * len(outs),
        scratch_shapes=scratch,
        compiler_params=pltpu.CompilerParams(vmem_limit_bytes=limit << 20),
        name=name,
        input_output_aliases=aliases,
        cost_estimate=pl.CostEstimate(flops=flops, bytes_accessed=0, transcendentals=0),
    )(*operands)


def body(volume):
    depths, rows, cols = volume.shape
    il, xl = lax.axis_size("il"), lax.axis_size("xl")
    count = depths - 2
    assert xl == 2 and il % 2 == 0 and count == 2 * SLOTS and rows == 128 and cols == 256
    bf16, f32 = jnp.bfloat16, jnp.float32
    half = count // 2
    work = half * 1024 * 2 * 256 * 256
    packed_rows = -(-REACH * (depths + 2) // 16) * 16

    span = EDGE * SLOTS
    lines, diff_i, smooth, pack_h, diff_h, lines_e, diff_e, pick, mask = call(
        "tables_kernel",
        lambda *refs: tables_kernel(depths, *refs),
        [
            ((rows, rows), bf16),
            ((rows, rows), bf16),
            ((cols, cols), bf16),
            ((256, 256), bf16),
            ((128 * TILES, 512), bf16),
            ((2, span, span), bf16),
            ((EDGE, EDGE), bf16),
            ((cols, 256), bf16),
            ((3, 8, 128), f32),
        ],
        [],
        [],
        flops=work,
    )
    halo_tile = ((TILES, rows, 128), bf16)
    vol, send, own = call("pack_kernel", pack_kernel, [(volume.shape, bf16), halo_tile, halo_tile], [], [volume, pick])
    side = lax.ppermute(send, "xl", [(0, 1), (1, 0)])
    chunks = rows // EDGE - 2
    lined = [((count, chunks, 6, EDGE, cols), bf16), ((2, 6, count, EDGE, cols), f32)]
    moment_slots = [pltpu.VMEM((2, 6, rows, cols), bf16)]
    inner, part = call("lines_kernel", lines_kernel, lined, moment_slots, [vol, lines, mask], flops=work // 4)
    packed = ((packed_rows, cols), bf16)
    halo, near, far = call(
        "rows_kernel",
        rows_kernel,
        [((rows, 128 * TILES), bf16), packed, packed],
        [pltpu.VMEM((2, packed_rows, cols), f32)],
        [vol, own, side, part],
        in_specs=[WHOLE] * 3 + [ANYWHERE],
    )
    swap = [(i, i ^ 1) for i in range(il)]
    onward = [(i, i + 2) for i in range(0, il - 2, 2)] + [(il - 2, il - 1)]
    onward += [(i, i - 2) for i in range(3, il, 2)] + [(1, 0)]
    far_in = lax.ppermute(far, "il", swap)
    near_in = lax.ppermute(near, "il", swap)

    outs = [((count, rows, cols), f32)] * 3
    saved = ((3, half, EDGE * chunks, cols), f32)
    border = ((6 * EDGE * chunks, 256), f32)
    own_scratch = moment_slots + [pltpu.VMEM((2, 6 * EDGE * chunks, cols), f32), pltpu.SemaphoreType.DMA((half // 2 - 1, 3))]
    shared = [vol, lines, diff_i, smooth, halo, diff_h, pack_h, mask]
    inner, part, *outs_in, done, part_h, border = call(
        "first_own_kernel",
        lambda *refs: own_kernel(0, *refs),
        lined + outs + [saved, ((2, 6, EDGE, 256), f32), border],
        own_scratch,
        shared + [inner, part],
        out_specs=(WHOLE,) * 2 + (IN_HBM,) * 3 + (WHOLE,) * 3,
        flops=3 * work,
        aliases={len(shared) + n: n for n in range(2)},
    )
    (relayed,) = call("relay_kernel", relay_kernel, [packed], [], [far_in, done], in_specs=[WHOLE, ANYWHERE])
    relayed_in = lax.ppermute(relayed, "il", onward)
    inner, part, *outs_in, done = call(
        "second_own_kernel",
        lambda *refs: own_kernel(1, *refs),
        lined + outs + [saved],
        own_scratch + [pltpu.SemaphoreType.DMA((3,))],
        shared + [inner, part, border, done] + outs_in,
        in_specs=[WHOLE] * (len(shared) + 4) + [IN_HBM] * 3,
        out_specs=(WHOLE,) * 2 + (IN_HBM,) * 3 + (WHOLE,),
        flops=3 * work,
        aliases={len(shared): 0, len(shared) + 1: 1} | {len(shared) + 4 + n: 2 + n for n in range(3)},
    )

    end_rows = (3, count, EDGE, cols)
    tables = [smooth, pack_h, diff_h, lines_e, diff_e, mask]
    scratch = [
        pltpu.VMEM((8 + packed_rows, cols), f32),
        pltpu.VMEM((depths, EDGE, cols), bf16),
        pltpu.VMEM((EDGE, 128 * TILES), bf16),
        pltpu.VMEM((6 * EDGE, 256), f32),
        pltpu.VMEM((count, 6, EDGE, cols), bf16),
        pltpu.VMEM((2, half * 6 * EDGE, cols), f32),
    ]
    sems = pltpu.SemaphoreType.DMA((3,))
    operands = [vol, halo, near_in, part, part_h, *tables, done]
    *outs_in, done = call(
        "near_end_kernel",
        lambda *refs: end_kernel(0, *refs),
        outs + [(end_rows, f32)],
        scratch + [sems],
        operands + outs_in,
        in_specs=[WHOLE] * len(operands) + [IN_HBM] * 3,
        out_specs=(IN_HBM,) * 3 + (WHOLE,),
        flops=work,
        aliases={len(operands) + n: n for n in range(3)},
    )
    operands = [vol, halo, relayed_in, part, part_h, *tables, done]
    return call(
        "far_end_kernel",
        lambda *refs: end_kernel(1, *refs),
        outs,
        scratch + [pltpu.VMEM(end_rows, f32), sems, pltpu.SemaphoreType.DMA((2, 3))],
        operands + outs_in,
        in_specs=[WHOLE] * len(operands) + [IN_HBM] * 3,
        out_specs=(IN_HBM,) * 3,
        flops=work,
        aliases={len(operands) + n: n for n in range(3)},
    )


def solution(mesh):
    spec = P(None, ("parts", "il"), "xl")
    return jax.shard_map(body, mesh=mesh, in_specs=(spec,), out_specs=(spec,) * 3, check_vma=False)
```

```python
import jax
import jax.numpy as jnp
import ml_dtypes
import numpy as np
from jax import lax
from jax.experimental import pallas as pl
from jax.experimental.pallas import tpu as pltpu
from jax.sharding import PartitionSpec as P

RADIUS = 9
REACH = RADIUS + 1
SIDE = 16
SLOTS = 8
TILES = 3
EDGE = 16
OWN = 2
TINY = float(np.finfo(np.float32).tiny)
HEAD = 2
AHEAD = 2
FAR = -1000
WHOLE = pl.BlockSpec(memory_space=pltpu.VMEM)
IN_HBM = pl.BlockSpec(memory_space=pltpu.HBM)
ANYWHERE = pl.BlockSpec(memory_space=pl.ANY)


def filter_taps():
    offsets = np.arange(2 * RADIUS + 1).astype(np.float32)
    sigma = np.float32(RADIUS / 3.0)
    shape = np.exp(np.float32(-0.5) * ((offsets - RADIUS) / sigma) ** 2)
    return (shape / np.sum(shape, dtype=np.float32)).astype(ml_dtypes.bfloat16).astype(np.float32)


def iota(shape, dim):
    return lax.broadcasted_iota(jnp.int32, shape, dim)


def band(source, target, scale=1.0):
    offset = jnp.abs(source - target)
    weights = jnp.zeros(offset.shape, jnp.float32)
    for distance, tap in enumerate(filter_taps()[RADIUS:]):
        weights = jnp.where(offset == distance, jnp.float32(scale * tap), weights)
    return weights


def difference(source, target):
    offset = source - target
    return jnp.where(offset == 1, 1.0, jnp.where(offset == -1, -1.0, 0.0)).astype(jnp.float32)


def dot(left, right):
    return jnp.dot(left, right, preferred_element_type=jnp.float32)


def halo_plane(lane, tile, depths):
    slot = lax.div(lane, SIDE)
    rest = jnp.where(slot == 0, 0, jnp.where(slot == 1, depths - 1, FAR))
    return jnp.where(tile < 2, 1 + SLOTS * tile + slot, rest)


def halo_column(lane, x, cols):
    place = lax.rem(lane, SIDE)
    return jnp.where(x == 0, cols - OWN + place, place - (SIDE - OWN))


def low_end(exchange):
    even = lax.rem(lax.axis_index("il"), 2) == 0
    return jnp.logical_not(even) if exchange == 0 else even


def tables_kernel(depths, lines_ref, diff_i_ref, diff_x_ref, diff_z_ref, smooth_ref, pack_h_ref, diff_h_ref, lines_e_ref, diff_e_ref, pick_ref, mask_ref):
    rows, cols = lines_ref.shape[0], diff_x_ref.shape[0]
    x, il, last = lax.axis_index("xl"), lax.axis_index("il"), lax.axis_size("il") - 1
    bf16 = jnp.bfloat16

    target, source = iota((rows, rows), 0), iota((rows, rows), 1)
    inner = (source > 0) & (source < rows - 1)
    lines_ref[...] = jnp.where(inner, band(source, target, 0.25), 0.0).astype(bf16)
    diff_i_ref[...] = difference(source, target).astype(bf16)
    target, source = iota((rows, 2 * rows), 0), iota((rows, 2 * rows), 1)
    diff_z_ref[...] = jnp.where(source == target + rows, 1.0, jnp.where(source == target, -1.0, 0.0)).astype(bf16)
    span = EDGE * SLOTS
    target, source = iota((span, span), 0), iota((span, span), 1)
    depth = lax.div(source, EDGE) == lax.div(target, EDGE)
    target, source = lax.rem(target, EDGE), lax.rem(source, EDGE)
    diff_e_ref[...] = jnp.where(depth, difference(source, target), 0.0).astype(bf16)
    for exchange in range(2):
        low = low_end(exchange)
        source_at = jnp.where(low, source - REACH, rows - (EDGE - REACH) + source)
        target_at = jnp.where(low, target, rows - EDGE + target)
        first = jnp.where(low & (il > 0), -rows, 0)
        final = jnp.where(jnp.logical_not(low) & (il < last), 2 * rows, rows - 1)
        use = depth & (source_at >= first) & (source_at <= final) & ((source_at <= 0) | (source_at >= rows - 1))
        lines_e_ref[exchange] = jnp.where(use, band(source_at, target_at, 0.25), 0.0).astype(bf16)

    source, target = iota((cols, cols), 0), iota((cols, cols), 1)
    diff_x_ref[...] = difference(source, target).astype(bf16)
    moved = source == jnp.where(x == 0, cols - 1, 0)
    column = lax.rem(target + 128 * x, cols)
    smooth_ref[...] = jnp.where(moved, 0.0, band(source, column)).astype(bf16)
    source, target = iota((256, 256), 0), iota((256, 256), 1)
    place = lax.rem(source, SIDE)
    use = (lax.div(source, SIDE) == lax.div(target, SIDE)) & (place != jnp.where(x == 0, 0, SIDE - 1))
    column = jnp.where(x == 0, cols - SIDE, 0) + lax.rem(target, SIDE)
    pack_h_ref[...] = jnp.where(use, band(halo_column(place, x, cols), column), 0.0).astype(bf16)

    source, target = iota((128, 128), 0), iota((128, 128), 1)
    same = lax.rem(source, SIDE) == lax.rem(target, SIDE)
    across = difference(lax.rem(source, SIDE), lax.rem(target, SIDE))
    for group in range(2):
        centre = halo_plane(target, group, depths)
        for tile in range(TILES):
            plane = halo_plane(source, tile, depths)
            part, out = slice(128 * tile, 128 * (tile + 1)), 128 * group
            diff_h_ref[part, out : out + 128] = jnp.where(same, difference(plane, centre), 0.0).astype(bf16)
            diff_h_ref[part, 256 + out : 384 + out] = jnp.where(plane == centre, across, 0.0).astype(bf16)

    source, lane = iota((cols, 256), 0), iota((cols, 256), 1)
    place = lax.rem(lane, SIDE)
    low, high = place < SIDE - OWN, place >= OWN
    sent = jnp.where(x == 0, jnp.where(low, cols - (SIDE - OWN) + place, FAR), jnp.where(high, place - OWN, FAR))
    low, high = place < OWN, place >= SIDE - OWN
    kept = jnp.where(x == 0, jnp.where(low, cols - OWN + place, FAR), jnp.where(high, place - (SIDE - OWN), FAR))
    pick_ref[...] = jnp.where(source == jnp.where(lane < 128, sent, kept), 1.0, 0.0).astype(bf16)
    lane = iota((8, 128), 1)
    border = jnp.where(x == 0, lane - (128 - SIDE), lane)
    mask_ref[...] = jnp.where((border >= 0) & (border < SIDE), 1.0, 0.0)


def pack_kernel(vol_ref, pick_ref, copy_ref, send_ref, own_ref):
    depths, rows, cols = vol_ref.shape
    slot = lax.div(lax.rem(iota((rows, 256), 1), 128), SIDE)
    copy_ref[...] = vol_ref[...]
    picked = dot(vol_ref[...].reshape(depths * rows, cols), pick_ref[...])
    for tile in range(TILES):
        if tile < 2:
            planes = [(1 + SLOTS * tile + index, index) for index in range(SLOTS)]
        else:
            planes = [(0, 0), (depths - 1, 1)]
        packed = jnp.zeros((rows, 256), jnp.float32)
        for plane, index in planes:
            packed = jnp.where(slot == index, picked[rows * plane : rows * (plane + 1)], packed)
        packed = packed.astype(jnp.bfloat16)
        send_ref[tile] = packed[:, :128]
        own_ref[tile] = packed[:, 128:]


def rows_kernel(vol_ref, own_ref, side_ref, after_ref, halo_ref, near_ref, far_ref, packed_ref):
    depths, rows, cols = vol_ref.shape
    even = lax.rem(lax.axis_index("il"), 2) == 0

    def put(row, top, bottom):
        top, bottom = top[:REACH], bottom[EDGE - REACH :]
        lanes = top.shape[1]
        packed_ref[0, row : row + REACH, :lanes] = jnp.where(even, bottom, top)
        packed_ref[1, row : row + REACH, :lanes] = jnp.where(even, top, bottom)

    packed_ref[:, depths * REACH :, :] = jnp.zeros_like(packed_ref[:, depths * REACH :, :])
    for depth in range(depths):
        top = vol_ref[depth, :EDGE, :].astype(jnp.float32)
        bottom = vol_ref[depth, rows - EDGE :, :].astype(jnp.float32)
        put(REACH * depth, top, bottom)
    tiles = []
    for tile in range(TILES):
        merged = own_ref[tile].astype(jnp.float32) + side_ref[tile].astype(jnp.float32)
        halo_ref[:, 128 * tile : 128 * (tile + 1)] = merged.astype(jnp.bfloat16)
        tiles.append((merged[:EDGE], merged[rows - EDGE :]))
    tops = jnp.concatenate([tiles[0][0], tiles[1][0]], axis=1)
    bottoms = jnp.concatenate([tiles[0][1], tiles[1][1]], axis=1)
    put(REACH * depths, tops, bottoms)
    put(REACH * (depths + 1), *tiles[2])
    near_ref[...] = packed_ref[0].astype(jnp.bfloat16)
    far_ref[...] = packed_ref[1].astype(jnp.bfloat16)


def relay_kernel(rows_ref, after_ref, out_ref):
    out_ref[...] = rows_ref[...]


def moments(grad_i, grad_x, grad_z):
    terms = (
        grad_i * grad_i,
        grad_x * grad_x,
        grad_z * grad_z,
        grad_i * grad_x,
        grad_i * grad_z,
        grad_x * grad_z,
    )
    return [term.astype(jnp.bfloat16) for term in terms]


def store_chunks(summed, comp, inner_ref, part_ref):
    chunks = summed.shape[0] // EDGE
    for chunk in range(1, chunks - 1):
        inner_ref[chunk - 1, comp] = summed[EDGE * chunk : EDGE * (chunk + 1)].astype(jnp.bfloat16)
    part_ref[0, comp] = summed[:EDGE]
    part_ref[1, comp] = summed[EDGE * (chunks - 1) :]


def make_moments(pair, vol_ref, diff_i_ref, diff_x_ref, diff_z_ref, moments_ref):
    rows = vol_ref.shape[1]
    planes = [vol_ref[2 * pair + k] for k in range(4)]
    across = dot(jnp.concatenate(planes[1:3], axis=0), diff_x_ref[...])
    for k in range(2):
        grad_i = dot(diff_i_ref[...], planes[k + 1])
        grad_x = across[rows * k : rows * (k + 1)]
        grad_z = dot(diff_z_ref[...], jnp.concatenate([planes[k], planes[k + 2]], axis=0))
        for comp, term in enumerate(moments(grad_i, grad_x, grad_z)):
            moments_ref[k, comp] = term


def make_lines(z, comp, lines_ref, moments_ref, inner_ref, part_ref):
    store_chunks(dot(lines_ref[...], moments_ref[z % 2, comp]), comp, inner_ref.at[z], part_ref.at[:, :, z])


def lines_kernel(vol_ref, lines_ref, diff_i_ref, diff_x_ref, diff_z_ref, inner_ref, part_ref, even_ref, odd_ref):
    slots = (even_ref, odd_ref)
    for pair in range(HEAD):
        make_moments(pair, vol_ref, diff_i_ref, diff_x_ref, diff_z_ref, slots[pair % 2])
        for k in range(2):
            for comp in range(6):
                make_lines(2 * pair + k, comp, lines_ref, slots[pair % 2], inner_ref, part_ref)


def tensor_of(own, smooth_ref, tensor_ref):
    tensor_ref[...] = dot(own.reshape(-1, own.shape[-1]), smooth_ref[...])


def attributes(tensor, border, store):
    x = lax.axis_index("xl")
    halves = (tensor[:, :128], tensor[:, 128:] + border)
    lanes = (pl.multiple_of(128 * x, 128), pl.multiple_of(128 - 128 * x, 128))
    for half, lane in zip(halves, lanes):
        a, b, c, d, e, f = [half[EDGE * comp : EDGE * (comp + 1)] for comp in range(6)]
        low = -1e-6 - c
        inverse = pl.reciprocal(low, approx=True)
        spread = (a - b) * (a - c) + (b - c) * (b - c) + 3.0 * (d * d + e * e + f * f)
        root = spread * lax.rsqrt(jnp.maximum(spread, TINY))
        store(pl.ds(lane, 128), (e * inverse, f * inverse, root * pl.reciprocal(a + b - low, approx=True)))


def border_of(packed, slot, mask_ref):
    base = jnp.where(lax.axis_index("xl") == 0, 128 - SIDE, 0)
    moved = pltpu.roll(packed, lax.rem(base - SIDE * slot + 128, 128), 1)
    return (moved.reshape(-1, 8, 128) * mask_ref[...]).reshape(packed.shape)


def own_kernel(
    stage, vol_ref, lines_ref, diff_i_ref, diff_x_ref, diff_z_ref, smooth_ref, halo_ref, diff_h_ref, pack_h_ref, mask_ref,
    inner_in_ref, part_in_ref, *refs,
):
    if stage == 0:
        inner_ref, part_ref, *targets, later_ref, part_h_ref, border_ref, even_ref, odd_ref, tensor_ref, out_ref, sems = refs
        both = dot(halo_ref[...], diff_h_ref[...])
        grad_i = dot(diff_i_ref[...], halo_ref[:, :256])
        lined_h = [[] for chunk in range(inner_ref.shape[1])]
        for comp, term in enumerate(moments(grad_i, both[:, 256:], both[:, :256])):
            summed = dot(lines_ref[...], term)
            for chunk, parts in enumerate(lined_h):
                parts.append(summed[EDGE * (chunk + 1) : EDGE * (chunk + 2)].astype(jnp.bfloat16))
            part_h_ref[0, comp] = summed[:EDGE]
            part_h_ref[1, comp] = summed[EDGE * (len(lined_h) + 1) :]
        border_ref[...] = dot(jnp.concatenate(sum(lined_h, []), axis=0), pack_h_ref[...])
        finished = []
    else:
        border_ref, done_ref, *refs = refs
        inner_ref, part_ref, *targets, later_ref, even_ref, odd_ref, tensor_ref, out_ref, sems, done_sems = refs[3:]
        finished = []
    count, chunks = inner_ref.shape[:2]
    pairs, inner = count // 4, EDGE * chunks
    slots = (even_ref, odd_ref)

    def place(target, pair):
        return target.at[pl.ds(2 * pair, 2), pl.ds(EDGE, inner)]

    if stage == 1:
        for n, target in enumerate(targets):
            finished.append(pltpu.make_async_copy(done_ref.at[n], place(target, pairs - 1), done_sems.at[n]))
            finished[-1].start()

    half = count // 2
    ahead = range(2 * HEAD, half + 2 * AHEAD) if stage == 0 else range(half + 2 * AHEAD, count)
    tensor_of(inner_ref[half * stage], smooth_ref, tensor_ref.at[0])
    for step in range(half):
        z = half * stage + step
        later = ahead[step] if step < len(ahead) else None
        if later is not None and later % 2 == 0:
            make_moments(later // 2, vol_ref, diff_i_ref, diff_x_ref, diff_z_ref, slots[later // 2 % 2])
        if step < half - 1:
            tensor_of(inner_ref[z + 1], smooth_ref, tensor_ref.at[(step + 1) % 2])
        for chunk in range(chunks):
            rows = slice(EDGE * chunk, EDGE * (chunk + 1))
            part = slice(6 * EDGE * chunk, 6 * EDGE * (chunk + 1))

            def store(lanes, values):
                for n, value in enumerate(values):
                    if step >= half - 2:
                        later_ref[n, step % 2, rows, lanes] = value
                    else:
                        out_ref[n, step, rows, lanes] = value

            border = border_of(border_ref[part, 128 * stage : 128 * (stage + 1)], z % SLOTS, mask_ref)
            attributes(tensor_ref[step % 2, part], border, store)
            if later is not None:
                make_lines(later, chunk, lines_ref, slots[later // 2 % 2], inner_ref, part_ref)
        if step % 2 == 1 and step < half - 2:
            for n, target in enumerate(targets):
                source = out_ref.at[n, pl.ds(step - 1, 2)]
                finished.append(pltpu.make_async_copy(source, place(target, z // 2), sems.at[step // 2, n]))
                finished[-1].start()
    for copy in finished:
        copy.wait()


def end_kernel(
    exchange, vol_ref, halo_ref, rows_ref, part_ref, part_h_ref,
    smooth_ref, pack_h_ref, diff_x_ref, diff_z_ref, diff_h_ref, lines_e_ref, diff_e_ref, mask_ref, done_ref, *refs,
):
    last = exchange == 1
    targets, refs = refs[3:6], refs[6:]
    if last:
        packed_ref, block_ref, block_h_ref, border_ref, edge_ref, tensor_ref, out_ref, done_sems, sems = refs
    else:
        out_ref, packed_ref, block_ref, block_h_ref, border_ref, edge_ref, tensor_ref, done_sems = refs
    depths, rows, cols = vol_ref.shape
    count, half = depths - 2, (depths - 2) // 2
    bf16, f32 = jnp.bfloat16, jnp.float32
    low = low_end(exchange)
    end = jnp.where(low, 0, 1)
    start = pl.multiple_of(jnp.where(low, 0, rows - EDGE), EDGE)
    other = pl.multiple_of(jnp.where(low, rows - EDGE, 0), EDGE)
    finished = []
    for n, target in enumerate(targets):
        if last:
            place = target.at[:, pl.ds(other, EDGE)]
        else:
            place = target.at[pl.ds(count - 2, 2), pl.ds(EDGE, rows - 2 * EDGE)]
        finished.append(pltpu.make_async_copy(done_ref.at[n], place, done_sems.at[n]))
    for copy in finished:
        copy.start()

    packed_ref[:8] = jnp.zeros_like(packed_ref[:8])
    if last:
        il = lax.axis_index("il")
        outside = (low & (il == 0)) | (jnp.logical_not(low) & (il == lax.axis_size("il") - 1))
        packed_ref[8:] = jnp.where(outside, 0.0, rows_ref[...].astype(f32))
    else:
        packed_ref[8:] = rows_ref[...].astype(f32)

    def joined(row, own):
        lanes = own.shape[1]
        before = packed_ref[8 + row : 8 + row + EDGE, :lanes]
        after = packed_ref[8 + row - (EDGE - REACH) : 8 + row + REACH, :lanes]
        own = own.astype(f32)
        place = iota(own.shape, 0)
        first = jnp.where(place < REACH, before, pltpu.roll(own, REACH, 0))
        second = jnp.where(place < EDGE - REACH, pltpu.roll(own, EDGE - REACH, 0), after)
        return jnp.where(low, first, second).astype(bf16)

    for depth in range(depths):
        block_ref[depth] = joined(REACH * depth, vol_ref[depth, pl.ds(start, EDGE)])
    own_h = halo_ref[pl.ds(start, EDGE)]
    block_h_ref[:, :256] = joined(REACH * depths, own_h[:, :256])
    block_h_ref[:, 256:] = joined(REACH * (depths + 1), own_h[:, 256:])

    both = dot(block_h_ref[...], diff_h_ref[...])
    grad_i = dot(diff_e_ref[:EDGE, :EDGE], block_h_ref[:, :256])
    lined_h = []
    for comp, term in enumerate(moments(grad_i, both[:, 256:], both[:, :256])):
        summed = part_h_ref[end, comp] + dot(lines_e_ref[exchange, :EDGE, :EDGE], term)
        lined_h.append(summed.astype(bf16))
    border_ref[...] = dot(jnp.concatenate(lined_h, axis=0), pack_h_ref[...])

    span = EDGE * half
    copies = []
    def make_block_moments(group):
        first = half * group
        planes = [block_ref[first + k : first + half + k].reshape(span, cols) for k in range(3)]
        grad_i = dot(diff_e_ref[...], planes[1])
        grad_x = dot(planes[1], diff_x_ref[...])
        return moments(grad_i, grad_x, dot(diff_z_ref[...], jnp.concatenate([planes[0], planes[2]], axis=0)))

    def make_edge(group, comp, term):
        first = half * group
        outer = dot(lines_e_ref[exchange, :span, :span], term)
        summed = part_ref[end, comp, first : first + half] + outer.reshape(half, EDGE, cols)
        edge_ref[first : first + half, comp] = summed.astype(bf16)

    def finish(group, k):
        def store(lanes, values):
            for n, value in enumerate(values):
                out_ref[n, half * group + k, :, lanes] = value

        border = border_of(border_ref[:, 128 * group : 128 * (group + 1)], k, mask_ref)
        attributes(tensor_ref[group, 6 * EDGE * k : 6 * EDGE * (k + 1)], border, store)

    def send(group):
        depth = pl.ds(half * group, half)
        for n, target in enumerate(targets):
            copy = pltpu.make_async_copy(out_ref.at[n, depth], target.at[depth, pl.ds(start, EDGE)], sems.at[group, n])
            copy.start()
            copies.append(copy)

    for group in range(2):
        for comp, term in enumerate(make_block_moments(group)):
            make_edge(group, comp, term)
    for group in range(2):
        tensor_of(edge_ref[half * group : half * (group + 1)], smooth_ref, tensor_ref.at[group])
        for k in range(half):
            finish(group, k)
        if last:
            send(group)
    for copy in finished + copies:
        copy.wait()


def call(name, kernel, outs, scratch, operands, in_specs=None, out_specs=None, flops=0, limit=16, aliases={}):
    return pl.pallas_call(
        kernel,
        out_shape=tuple(jax.ShapeDtypeStruct(*out) for out in outs),
        in_specs=in_specs or [WHOLE] * len(operands),
        out_specs=out_specs or (WHOLE,) * len(outs),
        scratch_shapes=scratch,
        compiler_params=pltpu.CompilerParams(vmem_limit_bytes=limit << 20),
        name=name,
        input_output_aliases=aliases,
        cost_estimate=pl.CostEstimate(flops=flops, bytes_accessed=0, transcendentals=0),
    )(*operands)


def body(volume):
    depths, rows, cols = volume.shape
    il, xl = lax.axis_size("il"), lax.axis_size("xl")
    count = depths - 2
    assert xl == 2 and il % 2 == 0 and count == 2 * SLOTS and rows == 128 and cols == 256
    bf16, f32 = jnp.bfloat16, jnp.float32
    half = count // 2
    work = half * 1024 * 2 * 256 * 256
    packed_rows = -(-REACH * (depths + 2) // 16) * 16

    span = EDGE * SLOTS
    lines, diff_i, diff_x, diff_z, smooth, pack_h, diff_h, lines_e, diff_e, pick, mask = call(
        "tables_kernel",
        lambda *refs: tables_kernel(depths, *refs),
        [
            ((rows, rows), bf16),
            ((rows, rows), bf16),
            ((cols, cols), bf16),
            ((rows, 2 * rows), bf16),
            ((cols, cols), bf16),
            ((256, 256), bf16),
            ((128 * TILES, 512), bf16),
            ((2, span, span), bf16),
            ((span, span), bf16),
            ((cols, 256), bf16),
            ((8, 128), f32),
        ],
        [],
        [],
        flops=work,
    )
    halo_tile = ((TILES, rows, 128), bf16)
    vol, send, own = call("pack_kernel", pack_kernel, [(volume.shape, bf16), halo_tile, halo_tile], [], [volume, pick])
    side = lax.ppermute(send, "xl", [(0, 1), (1, 0)])
    chunks = rows // EDGE - 2
    lined = [((count, chunks, 6, EDGE, cols), bf16), ((2, 6, count, EDGE, cols), f32)]
    moment_slots = [pltpu.VMEM((2, 6, rows, cols), bf16)] * 2
    inner, part = call("lines_kernel", lines_kernel, lined, moment_slots, [vol, lines, diff_i, diff_x, diff_z], flops=work // 4)
    packed = ((packed_rows, cols), bf16)
    halo, near, far = call(
        "rows_kernel",
        rows_kernel,
        [((rows, 128 * TILES), bf16), packed, packed],
        [pltpu.VMEM((2, packed_rows, cols), f32)],
        [vol, own, side, part],
        in_specs=[WHOLE] * 3 + [ANYWHERE],
    )
    swap = [(i, i ^ 1) for i in range(il)]
    onward = [(i, i + 2) for i in range(0, il - 2, 2)] + [(il - 2, il - 1)]
    onward += [(i, i - 2) for i in range(3, il, 2)] + [(1, 0)]
    far_in = lax.ppermute(far, "il", swap)
    near_in = lax.ppermute(near, "il", swap)

    outs = [((count, rows, cols), f32)] * 3
    saved = ((3, 2, EDGE * chunks, cols), f32)
    border = ((6 * EDGE * chunks, 256), f32)
    ready = [((3, count // 2 - 2, EDGE * chunks, cols), f32)]
    own_scratch = moment_slots + [pltpu.VMEM((2, 6 * EDGE * chunks, cols), f32), pltpu.VMEM(*ready[0]), pltpu.SemaphoreType.DMA((count // 4 - 1, 3))]
    shared = [vol, lines, diff_i, diff_x, diff_z, smooth, halo, diff_h, pack_h, mask]
    inner, part, *outs_in, done, part_h, border = call(
        "first_own_kernel",
        lambda *refs: own_kernel(0, *refs),
        lined + outs + [saved, ((2, 6, EDGE, 256), f32), border],
        own_scratch,
        shared + [inner, part],
        out_specs=(WHOLE,) * 2 + (IN_HBM,) * 3 + (WHOLE,) * 3,
        flops=3 * work,
        aliases={len(shared) + n: n for n in range(2)},
    )
    (relayed,) = call("relay_kernel", relay_kernel, [packed], [], [far_in, done], in_specs=[WHOLE, ANYWHERE])
    relayed_in = lax.ppermute(relayed, "il", onward)
    inner, part, *outs_in, done = call(
        "second_own_kernel",
        lambda *refs: own_kernel(1, *refs),
        lined + outs + [saved],
        own_scratch + [pltpu.SemaphoreType.DMA((3,))],
        shared + [inner, part, border, done] + outs_in,
        in_specs=[WHOLE] * (len(shared) + 4) + [IN_HBM] * 3,
        out_specs=(WHOLE,) * 2 + (IN_HBM,) * 3 + (WHOLE,),
        flops=3 * work,
        aliases={len(shared): 0, len(shared) + 1: 1} | {len(shared) + 4 + n: 2 + n for n in range(3)},
    )

    end_rows = (3, count, EDGE, cols)
    tables = [smooth, pack_h, diff_x, diff_z, diff_h, lines_e, diff_e, mask]
    scratch = [
        pltpu.VMEM((8 + packed_rows, cols), f32),
        pltpu.VMEM((depths, EDGE, cols), bf16),
        pltpu.VMEM((EDGE, 128 * TILES), bf16),
        pltpu.VMEM((6 * EDGE, 256), f32),
        pltpu.VMEM((count, 6, EDGE, cols), bf16),
        pltpu.VMEM((2, half * 6 * EDGE, cols), f32),
    ]
    sems = pltpu.SemaphoreType.DMA((3,))
    operands = [vol, halo, near_in, part, part_h, *tables, done]
    *outs_in, done = call(
        "near_end_kernel",
        lambda *refs: end_kernel(0, *refs),
        outs + [(end_rows, f32)],
        scratch + [sems],
        operands + outs_in,
        in_specs=[WHOLE] * len(operands) + [IN_HBM] * 3,
        out_specs=(IN_HBM,) * 3 + (WHOLE,),
        flops=work,
        aliases={len(operands) + n: n for n in range(3)},
    )
    operands = [vol, halo, relayed_in, part, part_h, *tables, done]
    return call(
        "far_end_kernel",
        lambda *refs: end_kernel(1, *refs),
        outs,
        scratch + [pltpu.VMEM(end_rows, f32), sems, pltpu.SemaphoreType.DMA((2, 3))],
        operands + outs_in,
        in_specs=[WHOLE] * len(operands) + [IN_HBM] * 3,
        out_specs=(IN_HBM,) * 3,
        flops=work,
        aliases={len(operands) + n: n for n in range(3)},
    )


def solution(mesh):
    spec = P(None, ("parts", "il"), "xl")
    return jax.shard_map(body, mesh=mesh, in_specs=(spec,), out_specs=(spec,) * 3, check_vma=False)
```

```python
import jax
import jax.numpy as jnp
import ml_dtypes
import numpy as np
from jax import lax
from jax.experimental import pallas as pl
from jax.experimental.pallas import tpu as pltpu
from jax.sharding import PartitionSpec as P

RADIUS = 9
REACH = RADIUS + 1
SIDE = 16
SLOTS = 8
TILES = 3
EDGE = 16
OWN = 2
TINY = float(np.finfo(np.float32).tiny)
HEAD = 2
AHEAD = 2
FAR = -1000
WHOLE = pl.BlockSpec(memory_space=pltpu.VMEM)
IN_HBM = pl.BlockSpec(memory_space=pltpu.HBM)
ANYWHERE = pl.BlockSpec(memory_space=pl.ANY)


def filter_taps():
    offsets = np.arange(2 * RADIUS + 1).astype(np.float32)
    sigma = np.float32(RADIUS / 3.0)
    shape = np.exp(np.float32(-0.5) * ((offsets - RADIUS) / sigma) ** 2)
    return (shape / np.sum(shape, dtype=np.float32)).astype(ml_dtypes.bfloat16).astype(np.float32)


def iota(shape, dim):
    return lax.broadcasted_iota(jnp.int32, shape, dim)


def band(source, target, scale=1.0):
    offset = jnp.abs(source - target)
    weights = jnp.zeros(offset.shape, jnp.float32)
    for distance, tap in enumerate(filter_taps()[RADIUS:]):
        weights = jnp.where(offset == distance, jnp.float32(scale * tap), weights)
    return weights


def difference(source, target):
    offset = source - target
    return jnp.where(offset == 1, 1.0, jnp.where(offset == -1, -1.0, 0.0)).astype(jnp.float32)


def dot(left, right):
    return jnp.dot(left, right, preferred_element_type=jnp.float32)


def halo_plane(lane, tile, depths):
    slot = lax.div(lane, SIDE)
    rest = jnp.where(slot == 0, 0, jnp.where(slot == 1, depths - 1, FAR))
    return jnp.where(tile < 2, 1 + SLOTS * tile + slot, rest)


def halo_column(lane, x, cols):
    place = lax.rem(lane, SIDE)
    return jnp.where(x == 0, cols - OWN + place, place - (SIDE - OWN))


def low_end(exchange):
    even = lax.rem(lax.axis_index("il"), 2) == 0
    return jnp.logical_not(even) if exchange == 0 else even


def tables_kernel(depths, lines_ref, diff_i_ref, smooth_ref, pack_h_ref, diff_h_ref, lines_e_ref, diff_e_ref, pick_ref, mask_ref):
    rows, cols = lines_ref.shape[0], smooth_ref.shape[0]
    x, il, last = lax.axis_index("xl"), lax.axis_index("il"), lax.axis_size("il") - 1
    bf16 = jnp.bfloat16

    target, source = iota((rows, rows), 0), iota((rows, rows), 1)
    inner = (source > 0) & (source < rows - 1)
    lines_ref[...] = jnp.where(inner, band(source, target, 0.25), 0.0).astype(bf16)
    diff_i_ref[...] = difference(source, target).astype(bf16)
    span = EDGE * SLOTS
    target, source = iota((span, span), 0), iota((span, span), 1)
    depth = lax.div(source, EDGE) == lax.div(target, EDGE)
    target, source = lax.rem(target, EDGE), lax.rem(source, EDGE)
    diff_e_ref[...] = difference(source, target)[:EDGE, :EDGE].astype(bf16)
    for exchange in range(2):
        low = low_end(exchange)
        source_at = jnp.where(low, source - REACH, rows - (EDGE - REACH) + source)
        target_at = jnp.where(low, target, rows - EDGE + target)
        first = jnp.where(low & (il > 0), -rows, 0)
        final = jnp.where(jnp.logical_not(low) & (il < last), 2 * rows, rows - 1)
        use = depth & (source_at >= first) & (source_at <= final) & ((source_at <= 0) | (source_at >= rows - 1))
        lines_e_ref[exchange] = jnp.where(use, band(source_at, target_at, 0.25), 0.0).astype(bf16)

    source, target = iota((cols, cols), 0), iota((cols, cols), 1)
    moved = source == jnp.where(x == 0, cols - 1, 0)
    column = lax.rem(target + 128 * x, cols)
    smooth_ref[...] = jnp.where(moved, 0.0, band(source, column)).astype(bf16)
    source, target = iota((256, 256), 0), iota((256, 256), 1)
    place = lax.rem(source, SIDE)
    use = (lax.div(source, SIDE) == lax.div(target, SIDE)) & (place != jnp.where(x == 0, 0, SIDE - 1))
    column = jnp.where(x == 0, cols - SIDE, 0) + lax.rem(target, SIDE)
    pack_h_ref[...] = jnp.where(use, band(halo_column(place, x, cols), column), 0.0).astype(bf16)

    source, target = iota((128, 128), 0), iota((128, 128), 1)
    same = lax.rem(source, SIDE) == lax.rem(target, SIDE)
    across = difference(lax.rem(source, SIDE), lax.rem(target, SIDE))
    for group in range(2):
        centre = halo_plane(target, group, depths)
        for tile in range(TILES):
            plane = halo_plane(source, tile, depths)
            part, out = slice(128 * tile, 128 * (tile + 1)), 128 * group
            diff_h_ref[part, out : out + 128] = jnp.where(same, difference(plane, centre), 0.0).astype(bf16)
            diff_h_ref[part, 256 + out : 384 + out] = jnp.where(plane == centre, across, 0.0).astype(bf16)

    source, lane = iota((cols, 256), 0), iota((cols, 256), 1)
    place = lax.rem(lane, SIDE)
    low, high = place < SIDE - OWN, place >= OWN
    sent = jnp.where(x == 0, jnp.where(low, cols - (SIDE - OWN) + place, FAR), jnp.where(high, place - OWN, FAR))
    low, high = place < OWN, place >= SIDE - OWN
    kept = jnp.where(x == 0, jnp.where(low, cols - OWN + place, FAR), jnp.where(high, place - (SIDE - OWN), FAR))
    pick_ref[...] = jnp.where(source == jnp.where(lane < 128, sent, kept), 1.0, 0.0).astype(bf16)
    lane = iota((8, 128), 1)
    border = jnp.where(x == 0, lane - (128 - SIDE), lane)
    mask_ref[0] = jnp.where((border >= 0) & (border < SIDE), 1.0, 0.0)
    mask_ref[1] = jnp.where(lane > 0, 1.0, 0.0)
    mask_ref[2] = jnp.where(lane < 127, 1.0, 0.0)


def pack_kernel(vol_ref, pick_ref, copy_ref, send_ref, own_ref):
    depths, rows, cols = vol_ref.shape
    slot = lax.div(lax.rem(iota((rows, 256), 1), 128), SIDE)
    copy_ref[...] = vol_ref[...]
    picked = dot(vol_ref[...].reshape(depths * rows, cols), pick_ref[...])
    for tile in range(TILES):
        if tile < 2:
            planes = [(1 + SLOTS * tile + index, index) for index in range(SLOTS)]
        else:
            planes = [(0, 0), (depths - 1, 1)]
        packed = jnp.zeros((rows, 256), jnp.float32)
        for plane, index in planes:
            packed = jnp.where(slot == index, picked[rows * plane : rows * (plane + 1)], packed)
        packed = packed.astype(jnp.bfloat16)
        send_ref[tile] = packed[:, :128]
        own_ref[tile] = packed[:, 128:]


def rows_kernel(vol_ref, own_ref, side_ref, after_ref, halo_ref, near_ref, far_ref, packed_ref):
    depths, rows, cols = vol_ref.shape
    even = lax.rem(lax.axis_index("il"), 2) == 0

    def put(row, top, bottom):
        top, bottom = top[:REACH], bottom[EDGE - REACH :]
        lanes = top.shape[1]
        packed_ref[0, row : row + REACH, :lanes] = jnp.where(even, bottom, top)
        packed_ref[1, row : row + REACH, :lanes] = jnp.where(even, top, bottom)

    packed_ref[:, depths * REACH :, :] = jnp.zeros_like(packed_ref[:, depths * REACH :, :])
    for depth in range(depths):
        top = vol_ref[depth, :EDGE, :].astype(jnp.float32)
        bottom = vol_ref[depth, rows - EDGE :, :].astype(jnp.float32)
        put(REACH * depth, top, bottom)
    tiles = []
    for tile in range(TILES):
        merged = own_ref[tile].astype(jnp.float32) + side_ref[tile].astype(jnp.float32)
        halo_ref[:, 128 * tile : 128 * (tile + 1)] = merged.astype(jnp.bfloat16)
        tiles.append((merged[:EDGE], merged[rows - EDGE :]))
    tops = jnp.concatenate([tiles[0][0], tiles[1][0]], axis=1)
    bottoms = jnp.concatenate([tiles[0][1], tiles[1][1]], axis=1)
    put(REACH * depths, tops, bottoms)
    put(REACH * (depths + 1), *tiles[2])
    near_ref[...] = packed_ref[0].astype(jnp.bfloat16)
    far_ref[...] = packed_ref[1].astype(jnp.bfloat16)


def moments(grad_i, grad_x, grad_z):
    terms = (
        grad_i * grad_i,
        grad_x * grad_x,
        grad_z * grad_z,
        grad_i * grad_x,
        grad_i * grad_z,
        grad_x * grad_z,
    )
    return [term.astype(jnp.bfloat16) for term in terms]


def store_chunks(summed, comp, inner_ref, part_ref):
    chunks = summed.shape[0] // EDGE
    for chunk in range(1, chunks - 1):
        inner_ref[chunk - 1, comp] = summed[EDGE * chunk : EDGE * (chunk + 1)].astype(jnp.bfloat16)
    part_ref[0, comp] = summed[:EDGE]
    part_ref[1, comp] = summed[EDGE * (chunks - 1) :]


def gradients(before, centre, after, mask_ref):
    rows, cols = centre.shape
    left, right = pltpu.roll(centre, 1, 1), pltpu.roll(centre, cols - 1, 1)
    left_0 = (left[:, :128].reshape(-1, 8, 128) * mask_ref[1]).reshape(rows, 128)
    right_1 = (right[:, cols - 128 :].reshape(-1, 8, 128) * mask_ref[2]).reshape(rows, 128)
    grad_x = jnp.concatenate([right[:, : cols - 128] - left_0, right_1 - left[:, 128:]], axis=1)
    return pltpu.roll(centre, rows - 1, 0) - pltpu.roll(centre, 1, 0), grad_x, after - before


def make_moments(pair, vol_ref, mask_ref, moments_ref):
    planes = [vol_ref[2 * pair + k].astype(jnp.float32) for k in range(4)]
    for k in range(2):
        for comp, term in enumerate(moments(*gradients(*planes[k : k + 3], mask_ref))):
            moments_ref[k, comp] = term


def make_lines(z, comp, lines_ref, moments_ref, inner_ref, part_ref):
    store_chunks(dot(lines_ref[...], moments_ref[z % 2, comp]), comp, inner_ref.at[z], part_ref.at[:, :, z])


def lines_kernel(vol_ref, lines_ref, mask_ref, inner_ref, part_ref, even_ref, odd_ref):
    slots = (even_ref, odd_ref)
    for pair in range(HEAD):
        make_moments(pair, vol_ref, mask_ref, slots[pair % 2])
        for k in range(2):
            for comp in range(6):
                make_lines(2 * pair + k, comp, lines_ref, slots[pair % 2], inner_ref, part_ref)


def tensor_of(own, smooth_ref, tensor_ref):
    tensor_ref[...] = dot(own.reshape(-1, own.shape[-1]), smooth_ref[...])


def attributes(tensor, border, store):
    x = lax.axis_index("xl")
    halves = (tensor[:, :128], tensor[:, 128:] + border)
    lanes = (pl.multiple_of(128 * x, 128), pl.multiple_of(128 - 128 * x, 128))
    for half, lane in zip(halves, lanes):
        a, b, c, d, e, f = [half[EDGE * comp : EDGE * (comp + 1)] for comp in range(6)]
        low = -1e-6 - c
        inverse = pl.reciprocal(low, approx=True)
        spread = (a - b) * (a - c) + (b - c) * (b - c) + 3.0 * (d * d + e * e + f * f)
        root = spread * lax.rsqrt(jnp.maximum(spread, TINY))
        store(pl.ds(lane, 128), (e * inverse, f * inverse, root * pl.reciprocal(a + b - low, approx=True)))


def border_of(packed, slot, mask_ref):
    base = jnp.where(lax.axis_index("xl") == 0, 128 - SIDE, 0)
    moved = pltpu.roll(packed, lax.rem(base - SIDE * slot + 128, 128), 1)
    return (moved.reshape(-1, 8, 128) * mask_ref[0]).reshape(packed.shape)


def own_kernel(
    vol_ref, lines_ref, diff_i_ref, smooth_ref, halo_ref, diff_h_ref, pack_h_ref, mask_ref, inner_in_ref, part_in_ref,
    part_ref, dip_i_ref, dip_x_ref, plan_ref, later_ref, part_h_ref,
    inner_ref, border_ref, even_ref, odd_ref, tensor_ref, out_ref, sems,
):
    count, chunks = inner_ref.shape[:2]
    inner = EDGE * chunks
    slots = (even_ref, odd_ref)
    targets = (dip_i_ref, dip_x_ref, plan_ref)
    inner_ref[: 2 * HEAD] = inner_in_ref[...]

    both = dot(halo_ref[...], diff_h_ref[...])
    grad_i = dot(diff_i_ref[...], halo_ref[:, :256])
    lined_h = [[] for chunk in range(chunks)]
    for comp, term in enumerate(moments(grad_i, both[:, 256:], both[:, :256])):
        summed = dot(lines_ref[...], term)
        for chunk, parts in enumerate(lined_h):
            parts.append(summed[EDGE * (chunk + 1) : EDGE * (chunk + 2)].astype(jnp.bfloat16))
        part_h_ref[0, comp] = summed[:EDGE]
        part_h_ref[1, comp] = summed[EDGE * (chunks + 1) :]
    border_ref[...] = dot(jnp.concatenate(sum(lined_h, []), axis=0), pack_h_ref[...])

    copies = []
    tensor_of(inner_ref[0], smooth_ref, tensor_ref.at[0])
    for z in range(count):
        later = z + 2 * HEAD if z + 2 * HEAD < count else None
        if later is not None and later % 2 == 0:
            make_moments(later // 2, vol_ref, mask_ref, slots[later // 2 % 2])
        if z < count - 1:
            tensor_of(inner_ref[z + 1], smooth_ref, tensor_ref.at[(z + 1) % 2])
        group = 128 * (z // SLOTS)
        for chunk in range(chunks):
            rows = slice(EDGE * chunk, EDGE * (chunk + 1))
            part = slice(6 * EDGE * chunk, 6 * EDGE * (chunk + 1))

            def store(lanes, values):
                for n, value in enumerate(values):
                    if z >= count - 2:
                        later_ref[n, z % 2, rows, lanes] = value
                    else:
                        out_ref[n, z, rows, lanes] = value

            border = border_of(border_ref[part, group : group + 128], z % SLOTS, mask_ref)
            attributes(tensor_ref[z % 2, part], border, store)
            if later is not None:
                make_lines(later, chunk, lines_ref, slots[later // 2 % 2], inner_ref, part_ref)
        if z % 2 == 1 and z < count - 2:
            depth = pl.ds(z - 1, 2)
            for n, target in enumerate(targets):
                place = target.at[depth, pl.ds(EDGE, inner)]
                copies.append(pltpu.make_async_copy(out_ref.at[n, depth], place, sems.at[z // 2, n]))
                copies[-1].start()
    for copy in copies:
        copy.wait()


def end_kernel(
    exchange, vol_ref, halo_ref, rows_ref, part_ref, part_h_ref,
    smooth_ref, pack_h_ref, diff_h_ref, lines_e_ref, diff_e_ref, mask_ref, done_ref, *refs,
):
    last = exchange == 1
    targets, refs = refs[3:6], refs[6:]
    if last:
        packed_ref, block_ref, block_h_ref, border_ref, edge_ref, out_ref, done_sems, sems = refs
    else:
        out_ref, packed_ref, block_ref, block_h_ref, border_ref, edge_ref, done_sems = refs
    depths, rows, cols = vol_ref.shape
    count, half = depths - 2, (depths - 2) // 2
    bf16, f32 = jnp.bfloat16, jnp.float32
    low = low_end(exchange)
    end = jnp.where(low, 0, 1)
    start = pl.multiple_of(jnp.where(low, 0, rows - EDGE), EDGE)
    other = pl.multiple_of(jnp.where(low, rows - EDGE, 0), EDGE)
    finished = []
    for n, target in enumerate(targets):
        if last:
            place = target.at[:, pl.ds(other, EDGE)]
        else:
            place = target.at[pl.ds(count - 2, 2), pl.ds(EDGE, rows - 2 * EDGE)]
        finished.append(pltpu.make_async_copy(done_ref.at[n], place, done_sems.at[n]))
    for copy in finished:
        copy.start()

    packed_ref[:8] = jnp.zeros_like(packed_ref[:8])
    if last:
        il = lax.axis_index("il")
        outside = (low & (il == 0)) | (jnp.logical_not(low) & (il == lax.axis_size("il") - 1))
        packed_ref[8:] = jnp.where(outside, 0.0, rows_ref[...].astype(f32))
    else:
        packed_ref[8:] = rows_ref[...].astype(f32)

    def joined(row, own):
        lanes = own.shape[1]
        before = packed_ref[8 + row : 8 + row + EDGE, :lanes]
        after = packed_ref[8 + row - (EDGE - REACH) : 8 + row + REACH, :lanes]
        own = own.astype(f32)
        place = iota(own.shape, 0)
        first = jnp.where(place < REACH, before, pltpu.roll(own, REACH, 0))
        second = jnp.where(place < EDGE - REACH, pltpu.roll(own, EDGE - REACH, 0), after)
        return jnp.where(low, first, second).astype(bf16)

    for depth in range(depths):
        block_ref[depth] = joined(REACH * depth, vol_ref[depth, pl.ds(start, EDGE)])
    own_h = halo_ref[pl.ds(start, EDGE)]
    block_h_ref[:, :256] = joined(REACH * depths, own_h[:, :256])
    block_h_ref[:, 256:] = joined(REACH * (depths + 1), own_h[:, 256:])

    both = dot(block_h_ref[...], diff_h_ref[...])
    grad_i = dot(diff_e_ref[...], block_h_ref[:, :256])
    lined_h = []
    for comp, term in enumerate(moments(grad_i, both[:, 256:], both[:, :256])):
        summed = part_h_ref[end, comp] + dot(lines_e_ref[exchange, :EDGE, :EDGE], term)
        lined_h.append(summed.astype(bf16))
    border_ref[...] = dot(jnp.concatenate(lined_h, axis=0), pack_h_ref[...])

    span = EDGE * half
    copies = []
    def make_block_moments(group):
        first = half * group
        planes = [block_ref[first + k : first + half + k].astype(f32).reshape(span, cols) for k in range(3)]
        return moments(*gradients(*planes, mask_ref))

    def make_edge(group, comp, term):
        first = half * group
        outer = dot(lines_e_ref[exchange, :span, :span], term)
        summed = part_ref[end, comp, first : first + half] + outer.reshape(half, EDGE, cols)
        edge_ref[first : first + half, comp] = summed.astype(bf16)

    def finish(group, k, tensor):
        def store(lanes, values):
            for n, value in enumerate(values):
                out_ref[n, half * group + k, :, lanes] = value

        border = border_of(border_ref[:, 128 * group : 128 * (group + 1)], k, mask_ref)
        attributes(tensor, border, store)

    def send(group):
        depth = pl.ds(half * group, half)
        for n, target in enumerate(targets):
            copy = pltpu.make_async_copy(out_ref.at[n, depth], target.at[depth, pl.ds(start, EDGE)], sems.at[group, n])
            copy.start()
            copies.append(copy)

    for group in range(2):
        for comp, term in enumerate(make_block_moments(group)):
            make_edge(group, comp, term)
    for group in range(2):
        tensor = dot(edge_ref[half * group : half * (group + 1)].reshape(6 * span, cols), smooth_ref[...])
        for k in range(half):
            finish(group, k, tensor[6 * EDGE * k : 6 * EDGE * (k + 1)])
        if last:
            send(group)
    for copy in finished + copies:
        copy.wait()


def call(name, kernel, outs, scratch, operands, in_specs=None, out_specs=None, flops=0, limit=16, aliases={}):
    return pl.pallas_call(
        kernel,
        out_shape=tuple(jax.ShapeDtypeStruct(*out) for out in outs),
        in_specs=in_specs or [WHOLE] * len(operands),
        out_specs=out_specs or (WHOLE,) * len(outs),
        scratch_shapes=scratch,
        compiler_params=pltpu.CompilerParams(vmem_limit_bytes=limit << 20),
        name=name,
        input_output_aliases=aliases,
        cost_estimate=pl.CostEstimate(flops=flops, bytes_accessed=0, transcendentals=0),
    )(*operands)


def body(volume):
    depths, rows, cols = volume.shape
    il, xl = lax.axis_size("il"), lax.axis_size("xl")
    count = depths - 2
    assert xl == 2 and il % 2 == 0 and count == 2 * SLOTS and rows == 128 and cols == 256
    bf16, f32 = jnp.bfloat16, jnp.float32
    half = count // 2
    work = half * 1024 * 2 * 256 * 256
    packed_rows = -(-REACH * (depths + 2) // 16) * 16

    span = EDGE * SLOTS
    lines, diff_i, smooth, pack_h, diff_h, lines_e, diff_e, pick, mask = call(
        "tables_kernel",
        lambda *refs: tables_kernel(depths, *refs),
        [
            ((rows, rows), bf16),
            ((rows, rows), bf16),
            ((cols, cols), bf16),
            ((256, 256), bf16),
            ((128 * TILES, 512), bf16),
            ((2, span, span), bf16),
            ((EDGE, EDGE), bf16),
            ((cols, 256), bf16),
            ((3, 8, 128), f32),
        ],
        [],
        [],
        flops=work,
    )
    halo_tile = ((TILES, rows, 128), bf16)
    vol, send, own = call("pack_kernel", pack_kernel, [(volume.shape, bf16), halo_tile, halo_tile], [], [volume, pick])
    side = lax.ppermute(send, "xl", [(0, 1), (1, 0)])
    chunks = rows // EDGE - 2
    moment_slots = [pltpu.VMEM((2, 6, rows, cols), bf16)] * 2
    partial = ((2, 6, count, EDGE, cols), f32)
    inner, part = call(
        "lines_kernel",
        lines_kernel,
        [((2 * HEAD, chunks, 6, EDGE, cols), bf16), partial],
        moment_slots,
        [vol, lines, mask],
        flops=work // 4,
    )
    packed = ((packed_rows, cols), bf16)
    halo, near, far = call(
        "rows_kernel",
        rows_kernel,
        [((rows, 128 * TILES), bf16), packed, packed],
        [pltpu.VMEM((2, packed_rows, cols), f32)],
        [vol, own, side, part],
        in_specs=[WHOLE] * 3 + [ANYWHERE],
    )
    pairs = [(i, i + 1) for i in range(1, il - 1, 2)]
    far_in = lax.ppermute(far, "il", pairs + [(j, i) for i, j in pairs] + [(0, 0), (il - 1, il - 1)])
    near_in = lax.ppermute(near, "il", [(i, i ^ 1) for i in range(il)])

    outs = [((count, rows, cols), f32)] * 3
    operands = [vol, lines, diff_i, smooth, halo, diff_h, pack_h, mask, inner, part]
    part, *outs_in, done, part_h = call(
        "own_kernel",
        own_kernel,
        [partial, *outs, ((3, 2, EDGE * chunks, cols), f32), ((2, 6, EDGE, 256), f32)],
        [
            pltpu.VMEM((count, chunks, 6, EDGE, cols), bf16),
            pltpu.VMEM((6 * EDGE * chunks, 256), f32),
            *moment_slots,
            pltpu.VMEM((2, 6 * EDGE * chunks, cols), f32),
            pltpu.VMEM((3, count - 2, EDGE * chunks, cols), f32),
            pltpu.SemaphoreType.DMA((half - 1, 3)),
        ],
        operands,
        out_specs=(WHOLE,) + (IN_HBM,) * 3 + (WHOLE,) * 2,
        flops=5 * work,
        limit=24,
        aliases={len(operands) - 1: 0},
    )

    end_rows = (3, count, EDGE, cols)
    tables = [smooth, pack_h, diff_h, lines_e, diff_e, mask]
    scratch = [
        pltpu.VMEM((8 + packed_rows, cols), f32),
        pltpu.VMEM((depths, EDGE, cols), bf16),
        pltpu.VMEM((EDGE, 128 * TILES), bf16),
        pltpu.VMEM((6 * EDGE, 256), f32),
        pltpu.VMEM((count, 6, EDGE, cols), bf16),
    ]
    sems = pltpu.SemaphoreType.DMA((3,))
    operands = [vol, halo, near_in, part, part_h, *tables, done]
    *outs_in, done = call(
        "near_end_kernel",
        lambda *refs: end_kernel(0, *refs),
        outs + [(end_rows, f32)],
        scratch + [sems],
        operands + outs_in,
        in_specs=[WHOLE] * len(operands) + [IN_HBM] * 3,
        out_specs=(IN_HBM,) * 3 + (WHOLE,),
        flops=work,
        aliases={len(operands) + n: n for n in range(3)},
    )
    operands = [vol, halo, far_in, part, part_h, *tables, done]
    return call(
        "far_end_kernel",
        lambda *refs: end_kernel(1, *refs),
        outs,
        scratch + [pltpu.VMEM(end_rows, f32), sems, pltpu.SemaphoreType.DMA((2, 3))],
        operands + outs_in,
        in_specs=[WHOLE] * len(operands) + [IN_HBM] * 3,
        out_specs=(IN_HBM,) * 3,
        flops=work,
        aliases={len(operands) + n: n for n in range(3)},
    )


def solution(mesh):
    spec = P(None, ("parts", "il"), "xl")
    return jax.shard_map(body, mesh=mesh, in_specs=(spec,), out_specs=(spec,) * 3, check_vma=False)
```

```python
import jax
import jax.numpy as jnp
import ml_dtypes
import numpy as np
from jax import lax
from jax.experimental import pallas as pl
from jax.experimental.pallas import tpu as pltpu
from jax.sharding import PartitionSpec as P

RADIUS = 9
REACH = RADIUS + 1
SIDE = 16
SLOTS = 8
TILES = 3
EDGE = 16
OWN = 2
TINY = float(np.finfo(np.float32).tiny)
HEAD = 2
AHEAD = 2
FAR = -1000
WHOLE = pl.BlockSpec(memory_space=pltpu.VMEM)
IN_HBM = pl.BlockSpec(memory_space=pltpu.HBM)
ANYWHERE = pl.BlockSpec(memory_space=pl.ANY)


def filter_taps():
    offsets = np.arange(2 * RADIUS + 1).astype(np.float32)
    sigma = np.float32(RADIUS / 3.0)
    shape = np.exp(np.float32(-0.5) * ((offsets - RADIUS) / sigma) ** 2)
    return (shape / np.sum(shape, dtype=np.float32)).astype(ml_dtypes.bfloat16).astype(np.float32)


def iota(shape, dim):
    return lax.broadcasted_iota(jnp.int32, shape, dim)


def band(source, target, scale=1.0):
    offset = jnp.abs(source - target)
    weights = jnp.zeros(offset.shape, jnp.float32)
    for distance, tap in enumerate(filter_taps()[RADIUS:]):
        weights = jnp.where(offset == distance, jnp.float32(scale * tap), weights)
    return weights


def difference(source, target):
    offset = source - target
    return jnp.where(offset == 1, 1.0, jnp.where(offset == -1, -1.0, 0.0)).astype(jnp.float32)


def dot(left, right):
    return jnp.dot(left, right, preferred_element_type=jnp.float32)


def halo_plane(lane, tile, depths):
    slot = lax.div(lane, SIDE)
    rest = jnp.where(slot == 0, 0, jnp.where(slot == 1, depths - 1, FAR))
    return jnp.where(tile < 2, 1 + SLOTS * tile + slot, rest)


def halo_column(lane, x, cols):
    place = lax.rem(lane, SIDE)
    return jnp.where(x == 0, cols - OWN + place, place - (SIDE - OWN))


def low_end(exchange):
    even = lax.rem(lax.axis_index("il"), 2) == 0
    return jnp.logical_not(even) if exchange == 0 else even


def tables_kernel(depths, lines_ref, diff_i_ref, smooth_ref, pack_h_ref, diff_h_ref, lines_e_ref, diff_e_ref, pick_ref, mask_ref):
    rows, cols = lines_ref.shape[0], smooth_ref.shape[0]
    x, il, last = lax.axis_index("xl"), lax.axis_index("il"), lax.axis_size("il") - 1
    bf16 = jnp.bfloat16

    target, source = iota((rows, rows), 0), iota((rows, rows), 1)
    inner = (source > 0) & (source < rows - 1)
    lines_ref[...] = jnp.where(inner, band(source, target, 0.25), 0.0).astype(bf16)
    diff_i_ref[...] = difference(source, target).astype(bf16)
    span = EDGE * SLOTS
    target, source = iota((span, span), 0), iota((span, span), 1)
    depth = lax.div(source, EDGE) == lax.div(target, EDGE)
    target, source = lax.rem(target, EDGE), lax.rem(source, EDGE)
    diff_e_ref[...] = difference(source, target)[:EDGE, :EDGE].astype(bf16)
    for exchange in range(2):
        low = low_end(exchange)
        source_at = jnp.where(low, source - REACH, rows - (EDGE - REACH) + source)
        target_at = jnp.where(low, target, rows - EDGE + target)
        first = jnp.where(low & (il > 0), -rows, 0)
        final = jnp.where(jnp.logical_not(low) & (il < last), 2 * rows, rows - 1)
        use = depth & (source_at >= first) & (source_at <= final) & ((source_at <= 0) | (source_at >= rows - 1))
        lines_e_ref[exchange] = jnp.where(use, band(source_at, target_at, 0.25), 0.0).astype(bf16)

    source, target = iota((cols, cols), 0), iota((cols, cols), 1)
    moved = source == jnp.where(x == 0, cols - 1, 0)
    column = lax.rem(target + 128 * x, cols)
    smooth_ref[...] = jnp.where(moved, 0.0, band(source, column)).astype(bf16)
    source, target = iota((256, 256), 0), iota((256, 256), 1)
    place = lax.rem(source, SIDE)
    use = (lax.div(source, SIDE) == lax.div(target, SIDE)) & (place != jnp.where(x == 0, 0, SIDE - 1))
    column = jnp.where(x == 0, cols - SIDE, 0) + lax.rem(target, SIDE)
    pack_h_ref[...] = jnp.where(use, band(halo_column(place, x, cols), column), 0.0).astype(bf16)

    source, target = iota((128, 128), 0), iota((128, 128), 1)
    same = lax.rem(source, SIDE) == lax.rem(target, SIDE)
    across = difference(lax.rem(source, SIDE), lax.rem(target, SIDE))
    for group in range(2):
        centre = halo_plane(target, group, depths)
        for tile in range(TILES):
            plane = halo_plane(source, tile, depths)
            part, out = slice(128 * tile, 128 * (tile + 1)), 128 * group
            diff_h_ref[part, out : out + 128] = jnp.where(same, difference(plane, centre), 0.0).astype(bf16)
            diff_h_ref[part, 256 + out : 384 + out] = jnp.where(plane == centre, across, 0.0).astype(bf16)

    source, lane = iota((cols, 256), 0), iota((cols, 256), 1)
    place = lax.rem(lane, SIDE)
    low, high = place < SIDE - OWN, place >= OWN
    sent = jnp.where(x == 0, jnp.where(low, cols - (SIDE - OWN) + place, FAR), jnp.where(high, place - OWN, FAR))
    low, high = place < OWN, place >= SIDE - OWN
    kept = jnp.where(x == 0, jnp.where(low, cols - OWN + place, FAR), jnp.where(high, place - (SIDE - OWN), FAR))
    pick_ref[...] = jnp.where(source == jnp.where(lane < 128, sent, kept), 1.0, 0.0).astype(bf16)
    lane = iota((8, 128), 1)
    border = jnp.where(x == 0, lane - (128 - SIDE), lane)
    mask_ref[0] = jnp.where((border >= 0) & (border < SIDE), 1.0, 0.0)
    mask_ref[1] = jnp.where(lane > 0, 1.0, 0.0)
    mask_ref[2] = jnp.where(lane < 127, 1.0, 0.0)


def pack_kernel(vol_ref, pick_ref, copy_ref, send_ref, own_ref):
    depths, rows, cols = vol_ref.shape
    slot = lax.div(lax.rem(iota((rows, 256), 1), 128), SIDE)
    copy_ref[...] = vol_ref[...]
    picked = dot(vol_ref[...].reshape(depths * rows, cols), pick_ref[...])
    for tile in range(TILES):
        if tile < 2:
            planes = [(1 + SLOTS * tile + index, index) for index in range(SLOTS)]
        else:
            planes = [(0, 0), (depths - 1, 1)]
        packed = jnp.zeros((rows, 256), jnp.float32)
        for plane, index in planes:
            packed = jnp.where(slot == index, picked[rows * plane : rows * (plane + 1)], packed)
        packed = packed.astype(jnp.bfloat16)
        send_ref[tile] = packed[:, :128]
        own_ref[tile] = packed[:, 128:]


def rows_kernel(vol_ref, own_ref, side_ref, after_ref, halo_ref, near_ref, far_ref, packed_ref):
    depths, rows, cols = vol_ref.shape
    even = lax.rem(lax.axis_index("il"), 2) == 0

    def put(row, top, bottom):
        top, bottom = top[:REACH], bottom[EDGE - REACH :]
        lanes = top.shape[1]
        packed_ref[0, row : row + REACH, :lanes] = jnp.where(even, bottom, top)
        packed_ref[1, row : row + REACH, :lanes] = jnp.where(even, top, bottom)

    packed_ref[:, depths * REACH :, :] = jnp.zeros_like(packed_ref[:, depths * REACH :, :])
    for depth in range(depths):
        top = vol_ref[depth, :EDGE, :].astype(jnp.float32)
        bottom = vol_ref[depth, rows - EDGE :, :].astype(jnp.float32)
        put(REACH * depth, top, bottom)
    tiles = []
    for tile in range(TILES):
        merged = own_ref[tile].astype(jnp.float32) + side_ref[tile].astype(jnp.float32)
        halo_ref[:, 128 * tile : 128 * (tile + 1)] = merged.astype(jnp.bfloat16)
        tiles.append((merged[:EDGE], merged[rows - EDGE :]))
    tops = jnp.concatenate([tiles[0][0], tiles[1][0]], axis=1)
    bottoms = jnp.concatenate([tiles[0][1], tiles[1][1]], axis=1)
    put(REACH * depths, tops, bottoms)
    put(REACH * (depths + 1), *tiles[2])
    near_ref[...] = packed_ref[0].astype(jnp.bfloat16)
    far_ref[...] = packed_ref[1].astype(jnp.bfloat16)


def moments(grad_i, grad_x, grad_z):
    terms = (
        grad_i * grad_i,
        grad_x * grad_x,
        grad_z * grad_z,
        grad_i * grad_x,
        grad_i * grad_z,
        grad_x * grad_z,
    )
    return [term.astype(jnp.bfloat16) for term in terms]


def store_chunks(summed, comp, inner_ref, part_ref):
    chunks = summed.shape[0] // EDGE
    for chunk in range(1, chunks - 1):
        inner_ref[chunk - 1, comp] = summed[EDGE * chunk : EDGE * (chunk + 1)].astype(jnp.bfloat16)
    part_ref[0, comp] = summed[:EDGE]
    part_ref[1, comp] = summed[EDGE * (chunks - 1) :]


def gradients(before, centre, after, mask_ref):
    rows, cols = centre.shape
    left, right = pltpu.roll(centre, 1, 1), pltpu.roll(centre, cols - 1, 1)
    left_0 = (left[:, :128].reshape(-1, 8, 128) * mask_ref[1]).reshape(rows, 128)
    right_1 = (right[:, cols - 128 :].reshape(-1, 8, 128) * mask_ref[2]).reshape(rows, 128)
    grad_x = jnp.concatenate([right[:, : cols - 128] - left_0, right_1 - left[:, 128:]], axis=1)
    return pltpu.roll(centre, rows - 1, 0) - pltpu.roll(centre, 1, 0), grad_x, after - before


def make_moments(pair, vol_ref, mask_ref, moments_ref):
    planes = [vol_ref[2 * pair + k].astype(jnp.float32) for k in range(4)]
    for k in range(2):
        for comp, term in enumerate(moments(*gradients(*planes[k : k + 3], mask_ref))):
            moments_ref[k, comp] = term


def make_lines(z, comp, lines_ref, moments_ref, inner_ref, part_ref):
    store_chunks(dot(lines_ref[...], moments_ref[z % 2, comp]), comp, inner_ref.at[z], part_ref.at[:, :, z])


def lines_kernel(vol_ref, lines_ref, mask_ref, inner_ref, part_ref, even_ref, odd_ref):
    slots = (even_ref, odd_ref)
    for pair in range(HEAD):
        make_moments(pair, vol_ref, mask_ref, slots[pair % 2])
        for k in range(2):
            for comp in range(6):
                make_lines(2 * pair + k, comp, lines_ref, slots[pair % 2], inner_ref, part_ref)


def tensor_of(own, smooth_ref, tensor_ref):
    tensor_ref[...] = dot(own.reshape(-1, own.shape[-1]), smooth_ref[...])


def attributes(tensor, border, store):
    x = lax.axis_index("xl")
    halves = (tensor[:, :128], tensor[:, 128:] + border)
    lanes = (pl.multiple_of(128 * x, 128), pl.multiple_of(128 - 128 * x, 128))
    for half, lane in zip(halves, lanes):
        a, b, c, d, e, f = [half[EDGE * comp : EDGE * (comp + 1)] for comp in range(6)]
        low = -1e-6 - c
        inverse = pl.reciprocal(low, approx=True)
        spread = (a - b) * (a - c) + (b - c) * (b - c) + 3.0 * (d * d + e * e + f * f)
        root = spread * lax.rsqrt(jnp.maximum(spread, TINY))
        store(pl.ds(lane, 128), (e * inverse, f * inverse, root * pl.reciprocal(a + b - low, approx=True)))


def border_of(packed, slot, mask_ref):
    base = jnp.where(lax.axis_index("xl") == 0, 128 - SIDE, 0)
    moved = pltpu.roll(packed, lax.rem(base - SIDE * slot + 128, 128), 1)
    return (moved.reshape(-1, 8, 128) * mask_ref[0]).reshape(packed.shape)


def own_kernel(
    vol_ref, lines_ref, diff_i_ref, smooth_ref, halo_ref, diff_h_ref, pack_h_ref, mask_ref, inner_in_ref, part_in_ref,
    part_ref, dip_i_ref, dip_x_ref, plan_ref, later_ref, part_h_ref,
    inner_ref, border_ref, even_ref, odd_ref, tensor_ref, out_ref, sems,
):
    count, chunks = inner_ref.shape[:2]
    inner = EDGE * chunks
    slots = (even_ref, odd_ref)
    targets = (dip_i_ref, dip_x_ref, plan_ref)
    inner_ref[: 2 * HEAD] = inner_in_ref[...]

    both = dot(halo_ref[...], diff_h_ref[...])
    grad_i = dot(diff_i_ref[...], halo_ref[:, :256])
    lined_h = [[] for chunk in range(chunks)]
    for comp, term in enumerate(moments(grad_i, both[:, 256:], both[:, :256])):
        summed = dot(lines_ref[...], term)
        for chunk, parts in enumerate(lined_h):
            parts.append(summed[EDGE * (chunk + 1) : EDGE * (chunk + 2)].astype(jnp.bfloat16))
        part_h_ref[0, comp] = summed[:EDGE]
        part_h_ref[1, comp] = summed[EDGE * (chunks + 1) :]
    border_ref[...] = dot(jnp.concatenate(sum(lined_h, []), axis=0), pack_h_ref[...])

    copies = []
    tensor_of(inner_ref[0], smooth_ref, tensor_ref.at[0])
    for z in range(count):
        later = z + 2 * HEAD if z + 2 * HEAD < count else None
        if later is not None and later % 2 == 0:
            make_moments(later // 2, vol_ref, mask_ref, slots[later // 2 % 2])
        if z < count - 1:
            tensor_of(inner_ref[z + 1], smooth_ref, tensor_ref.at[(z + 1) % 2])
        group = 128 * (z // SLOTS)
        for chunk in range(chunks):
            rows = slice(EDGE * chunk, EDGE * (chunk + 1))
            part = slice(6 * EDGE * chunk, 6 * EDGE * (chunk + 1))

            def store(lanes, values):
                for n, value in enumerate(values):
                    if z >= count - 2:
                        later_ref[n, z % 2, rows, lanes] = value
                    else:
                        out_ref[n, z, rows, lanes] = value

            border = border_of(border_ref[part, group : group + 128], z % SLOTS, mask_ref)
            attributes(tensor_ref[z % 2, part], border, store)
            if later is not None:
                make_lines(later, chunk, lines_ref, slots[later // 2 % 2], inner_ref, part_ref)
        if z % 2 == 1 and z < count - 2:
            depth = pl.ds(z - 1, 2)
            for n, target in enumerate(targets):
                place = target.at[depth, pl.ds(EDGE, inner)]
                copies.append(pltpu.make_async_copy(out_ref.at[n, depth], place, sems.at[z // 2, n]))
                copies[-1].start()
    for copy in copies:
        copy.wait()


def end_kernel(
    exchange, vol_ref, halo_ref, rows_ref, part_ref, part_h_ref,
    smooth_ref, pack_h_ref, diff_h_ref, lines_e_ref, diff_e_ref, mask_ref, done_ref, *refs,
):
    last = exchange == 1
    targets, refs = refs[3:6], refs[6:]
    if last:
        packed_ref, block_ref, block_h_ref, border_ref, edge_ref, out_ref, done_sems, sems = refs
    else:
        out_ref, packed_ref, block_ref, block_h_ref, border_ref, edge_ref, done_sems = refs
    depths, rows, cols = vol_ref.shape
    count, half = depths - 2, (depths - 2) // 2
    bf16, f32 = jnp.bfloat16, jnp.float32
    low = low_end(exchange)
    end = jnp.where(low, 0, 1)
    start = pl.multiple_of(jnp.where(low, 0, rows - EDGE), EDGE)
    other = pl.multiple_of(jnp.where(low, rows - EDGE, 0), EDGE)
    finished = []
    for n, target in enumerate(targets):
        if last:
            place = target.at[:, pl.ds(other, EDGE)]
        else:
            place = target.at[pl.ds(count - 2, 2), pl.ds(EDGE, rows - 2 * EDGE)]
        finished.append(pltpu.make_async_copy(done_ref.at[n], place, done_sems.at[n]))
    for copy in finished:
        copy.start()

    packed_ref[:8] = jnp.zeros_like(packed_ref[:8])
    if last:
        il = lax.axis_index("il")
        outside = (low & (il == 0)) | (jnp.logical_not(low) & (il == lax.axis_size("il") - 1))
        packed_ref[8:] = jnp.where(outside, 0.0, rows_ref[...].astype(f32))
    else:
        packed_ref[8:] = rows_ref[...].astype(f32)

    def joined(row, own):
        lanes = own.shape[1]
        before = packed_ref[8 + row : 8 + row + EDGE, :lanes]
        after = packed_ref[8 + row - (EDGE - REACH) : 8 + row + REACH, :lanes]
        own = own.astype(f32)
        place = iota(own.shape, 0)
        first = jnp.where(place < REACH, before, pltpu.roll(own, REACH, 0))
        second = jnp.where(place < EDGE - REACH, pltpu.roll(own, EDGE - REACH, 0), after)
        return jnp.where(low, first, second).astype(bf16)

    for depth in range(depths):
        block_ref[depth] = joined(REACH * depth, vol_ref[depth, pl.ds(start, EDGE)])
    own_h = halo_ref[pl.ds(start, EDGE)]
    block_h_ref[:, :256] = joined(REACH * depths, own_h[:, :256])
    block_h_ref[:, 256:] = joined(REACH * (depths + 1), own_h[:, 256:])

    both = dot(block_h_ref[...], diff_h_ref[...])
    grad_i = dot(diff_e_ref[...], block_h_ref[:, :256])
    lined_h = []
    for comp, term in enumerate(moments(grad_i, both[:, 256:], both[:, :256])):
        summed = part_h_ref[end, comp] + dot(lines_e_ref[exchange, :EDGE, :EDGE], term)
        lined_h.append(summed.astype(bf16))
    border_ref[...] = dot(jnp.concatenate(lined_h, axis=0), pack_h_ref[...])

    span = EDGE * half
    copies = []
    def make_block_moments(group):
        first = half * group
        planes = [block_ref[first + k : first + half + k].astype(f32).reshape(span, cols) for k in range(3)]
        return moments(*gradients(*planes, mask_ref))

    def make_edge(group, comp, term):
        first = half * group
        outer = dot(lines_e_ref[exchange, :span, :span], term)
        summed = part_ref[end, comp, first : first + half] + outer.reshape(half, EDGE, cols)
        edge_ref[first : first + half, comp] = summed.astype(bf16)

    def finish(group, k, tensor):
        def store(lanes, values):
            for n, value in enumerate(values):
                out_ref[n, half * group + k, :, lanes] = value

        border = border_of(border_ref[:, 128 * group : 128 * (group + 1)], k, mask_ref)
        attributes(tensor, border, store)

    def send(group):
        depth = pl.ds(half * group, half)
        for n, target in enumerate(targets):
            copy = pltpu.make_async_copy(out_ref.at[n, depth], target.at[depth, pl.ds(start, EDGE)], sems.at[group, n])
            copy.start()
            copies.append(copy)

    for group in range(2):
        for comp, term in enumerate(make_block_moments(group)):
            make_edge(group, comp, term)
    for group in range(2):
        tensor = dot(edge_ref[half * group : half * (group + 1)].reshape(6 * span, cols), smooth_ref[...])
        for k in range(half):
            finish(group, k, tensor[6 * EDGE * k : 6 * EDGE * (k + 1)])
        if last:
            send(group)
    for copy in finished + copies:
        copy.wait()


def call(name, kernel, outs, scratch, operands, in_specs=None, out_specs=None, flops=0, limit=16, aliases={}):
    return pl.pallas_call(
        kernel,
        out_shape=tuple(jax.ShapeDtypeStruct(*out) for out in outs),
        in_specs=in_specs or [WHOLE] * len(operands),
        out_specs=out_specs or (WHOLE,) * len(outs),
        scratch_shapes=scratch,
        compiler_params=pltpu.CompilerParams(vmem_limit_bytes=limit << 20),
        name=name,
        input_output_aliases=aliases,
        cost_estimate=pl.CostEstimate(flops=flops, bytes_accessed=0, transcendentals=0),
    )(*operands)


def body(volume):
    depths, rows, cols = volume.shape
    il, xl = lax.axis_size("il"), lax.axis_size("xl")
    count = depths - 2
    assert xl == 2 and il % 2 == 0 and count == 2 * SLOTS and rows == 128 and cols == 256
    bf16, f32 = jnp.bfloat16, jnp.float32
    half = count // 2
    work = half * 1024 * 2 * 256 * 256
    packed_rows = -(-REACH * (depths + 2) // 16) * 16

    span = EDGE * SLOTS
    lines, diff_i, smooth, pack_h, diff_h, lines_e, diff_e, pick, mask = call(
        "tables_kernel",
        lambda *refs: tables_kernel(depths, *refs),
        [
            ((rows, rows), bf16),
            ((rows, rows), bf16),
            ((cols, cols), bf16),
            ((256, 256), bf16),
            ((128 * TILES, 512), bf16),
            ((2, span, span), bf16),
            ((EDGE, EDGE), bf16),
            ((cols, 256), bf16),
            ((3, 8, 128), f32),
        ],
        [],
        [],
        flops=work,
    )
    halo_tile = ((TILES, rows, 128), bf16)
    vol, send, own = call("pack_kernel", pack_kernel, [(volume.shape, bf16), halo_tile, halo_tile], [], [volume, pick])
    side = lax.ppermute(send, "xl", [(0, 1), (1, 0)])
    chunks = rows // EDGE - 2
    moment_slots = [pltpu.VMEM((2, 6, rows, cols), bf16)] * 2
    partial = ((2, 6, count, EDGE, cols), f32)
    inner, part = call(
        "lines_kernel",
        lines_kernel,
        [((2 * HEAD, chunks, 6, EDGE, cols), bf16), partial],
        moment_slots,
        [vol, lines, mask],
        flops=work // 4,
    )
    packed = ((packed_rows, cols), bf16)
    halo, near, far = call(
        "rows_kernel",
        rows_kernel,
        [((rows, 128 * TILES), bf16), packed, packed],
        [pltpu.VMEM((2, packed_rows, cols), f32)],
        [vol, own, side, part],
        in_specs=[WHOLE] * 3 + [ANYWHERE],
    )
    near_in = lax.ppermute(near, "il", [(i, i ^ 1) for i in range(il)])
    pairs = [(i, i + 1) for i in range(1, il - 1, 2)]
    far_in = lax.ppermute(far, "il", pairs + [(j, i) for i, j in pairs] + [(0, 0), (il - 1, il - 1)])

    outs = [((count, rows, cols), f32)] * 3
    operands = [vol, lines, diff_i, smooth, halo, diff_h, pack_h, mask, inner, part]
    part, *outs_in, done, part_h = call(
        "own_kernel",
        own_kernel,
        [partial, *outs, ((3, 2, EDGE * chunks, cols), f32), ((2, 6, EDGE, 256), f32)],
        [
            pltpu.VMEM((count, chunks, 6, EDGE, cols), bf16),
            pltpu.VMEM((6 * EDGE * chunks, 256), f32),
            *moment_slots,
            pltpu.VMEM((2, 6 * EDGE * chunks, cols), f32),
            pltpu.VMEM((3, count - 2, EDGE * chunks, cols), f32),
            pltpu.SemaphoreType.DMA((half - 1, 3)),
        ],
        operands,
        out_specs=(WHOLE,) + (IN_HBM,) * 3 + (WHOLE,) * 2,
        flops=5 * work,
        limit=24,
        aliases={len(operands) - 1: 0},
    )

    end_rows = (3, count, EDGE, cols)
    tables = [smooth, pack_h, diff_h, lines_e, diff_e, mask]
    scratch = [
        pltpu.VMEM((8 + packed_rows, cols), f32),
        pltpu.VMEM((depths, EDGE, cols), bf16),
        pltpu.VMEM((EDGE, 128 * TILES), bf16),
        pltpu.VMEM((6 * EDGE, 256), f32),
        pltpu.VMEM((count, 6, EDGE, cols), bf16),
    ]
    sems = pltpu.SemaphoreType.DMA((3,))
    operands = [vol, halo, near_in, part, part_h, *tables, done]
    *outs_in, done = call(
        "near_end_kernel",
        lambda *refs: end_kernel(0, *refs),
        outs + [(end_rows, f32)],
        scratch + [sems],
        operands + outs_in,
        in_specs=[WHOLE] * len(operands) + [IN_HBM] * 3,
        out_specs=(IN_HBM,) * 3 + (WHOLE,),
        flops=work,
        aliases={len(operands) + n: n for n in range(3)},
    )
    operands = [vol, halo, far_in, part, part_h, *tables, done]
    return call(
        "far_end_kernel",
        lambda *refs: end_kernel(1, *refs),
        outs,
        scratch + [pltpu.VMEM(end_rows, f32), sems, pltpu.SemaphoreType.DMA((2, 3))],
        operands + outs_in,
        in_specs=[WHOLE] * len(operands) + [IN_HBM] * 3,
        out_specs=(IN_HBM,) * 3,
        flops=work,
        aliases={len(operands) + n: n for n in range(3)},
    )


def solution(mesh):
    spec = P(None, ("parts", "il"), "xl")
    return jax.shard_map(body, mesh=mesh, in_specs=(spec,), out_specs=(spec,) * 3, check_vma=False)
```

```python
import jax
import jax.numpy as jnp
import ml_dtypes
import numpy as np
from jax import lax
from jax.experimental import pallas as pl
from jax.experimental.pallas import tpu as pltpu
from jax.sharding import PartitionSpec as P

RADIUS = 9
REACH = RADIUS + 1
SIDE = 16
SLOTS = 8
TILES = 3
EDGE = 16
OWN = 2
TINY = float(np.finfo(np.float32).tiny)
HEAD = 2
AHEAD = 2
FAR = -1000
WHOLE = pl.BlockSpec(memory_space=pltpu.VMEM)
IN_HBM = pl.BlockSpec(memory_space=pltpu.HBM)
ANYWHERE = pl.BlockSpec(memory_space=pl.ANY)


def filter_taps():
    offsets = np.arange(2 * RADIUS + 1).astype(np.float32)
    sigma = np.float32(RADIUS / 3.0)
    shape = np.exp(np.float32(-0.5) * ((offsets - RADIUS) / sigma) ** 2)
    return (shape / np.sum(shape, dtype=np.float32)).astype(ml_dtypes.bfloat16).astype(np.float32)


def iota(shape, dim):
    return lax.broadcasted_iota(jnp.int32, shape, dim)


def band(source, target, scale=1.0):
    offset = jnp.abs(source - target)
    weights = jnp.zeros(offset.shape, jnp.float32)
    for distance, tap in enumerate(filter_taps()[RADIUS:]):
        weights = jnp.where(offset == distance, jnp.float32(scale * tap), weights)
    return weights


def difference(source, target):
    offset = source - target
    return jnp.where(offset == 1, 1.0, jnp.where(offset == -1, -1.0, 0.0)).astype(jnp.float32)


def dot(left, right):
    return jnp.dot(left, right, preferred_element_type=jnp.float32)


def halo_plane(lane, tile, depths):
    slot = lax.div(lane, SIDE)
    rest = jnp.where(slot == 0, 0, jnp.where(slot == 1, depths - 1, FAR))
    return jnp.where(tile < 2, 1 + SLOTS * tile + slot, rest)


def halo_column(lane, x, cols):
    place = lax.rem(lane, SIDE)
    return jnp.where(x == 0, cols - OWN + place, place - (SIDE - OWN))


def low_end(exchange):
    even = lax.rem(lax.axis_index("il"), 2) == 0
    return jnp.logical_not(even) if exchange == 0 else even


def tables_kernel(depths, lines_ref, diff_i_ref, smooth_ref, pack_h_ref, diff_h_ref, lines_e_ref, diff_e_ref, pick_ref, mask_ref):
    rows, cols = lines_ref.shape[0], smooth_ref.shape[0]
    x, il, last = lax.axis_index("xl"), lax.axis_index("il"), lax.axis_size("il") - 1
    bf16 = jnp.bfloat16

    target, source = iota((rows, rows), 0), iota((rows, rows), 1)
    inner = (source > 0) & (source < rows - 1)
    lines_ref[...] = jnp.where(inner, band(source, target, 0.25), 0.0).astype(bf16)
    diff_i_ref[...] = difference(source, target).astype(bf16)
    span = EDGE * SLOTS
    target, source = iota((span, span), 0), iota((span, span), 1)
    depth = lax.div(source, EDGE) == lax.div(target, EDGE)
    target, source = lax.rem(target, EDGE), lax.rem(source, EDGE)
    diff_e_ref[...] = difference(source, target)[:EDGE, :EDGE].astype(bf16)
    for exchange in range(2):
        low = low_end(exchange)
        source_at = jnp.where(low, source - REACH, rows - (EDGE - REACH) + source)
        target_at = jnp.where(low, target, rows - EDGE + target)
        first = jnp.where(low & (il > 0), -rows, 0)
        final = jnp.where(jnp.logical_not(low) & (il < last), 2 * rows, rows - 1)
        use = depth & (source_at >= first) & (source_at <= final) & ((source_at <= 0) | (source_at >= rows - 1))
        lines_e_ref[exchange] = jnp.where(use, band(source_at, target_at, 0.25), 0.0).astype(bf16)

    source, target = iota((cols, cols), 0), iota((cols, cols), 1)
    moved = source == jnp.where(x == 0, cols - 1, 0)
    column = lax.rem(target + 128 * x, cols)
    smooth_ref[...] = jnp.where(moved, 0.0, band(source, column)).astype(bf16)
    source, target = iota((256, 256), 0), iota((256, 256), 1)
    place = lax.rem(source, SIDE)
    use = (lax.div(source, SIDE) == lax.div(target, SIDE)) & (place != jnp.where(x == 0, 0, SIDE - 1))
    column = jnp.where(x == 0, cols - SIDE, 0) + lax.rem(target, SIDE)
    pack_h_ref[...] = jnp.where(use, band(halo_column(place, x, cols), column), 0.0).astype(bf16)

    source, target = iota((128, 128), 0), iota((128, 128), 1)
    same = lax.rem(source, SIDE) == lax.rem(target, SIDE)
    across = difference(lax.rem(source, SIDE), lax.rem(target, SIDE))
    for group in range(2):
        centre = halo_plane(target, group, depths)
        for tile in range(TILES):
            plane = halo_plane(source, tile, depths)
            part, out = slice(128 * tile, 128 * (tile + 1)), 128 * group
            diff_h_ref[part, out : out + 128] = jnp.where(same, difference(plane, centre), 0.0).astype(bf16)
            diff_h_ref[part, 256 + out : 384 + out] = jnp.where(plane == centre, across, 0.0).astype(bf16)

    source, lane = iota((cols, 256), 0), iota((cols, 256), 1)
    place = lax.rem(lane, SIDE)
    low, high = place < SIDE - OWN, place >= OWN
    sent = jnp.where(x == 0, jnp.where(low, cols - (SIDE - OWN) + place, FAR), jnp.where(high, place - OWN, FAR))
    low, high = place < OWN, place >= SIDE - OWN
    kept = jnp.where(x == 0, jnp.where(low, cols - OWN + place, FAR), jnp.where(high, place - (SIDE - OWN), FAR))
    pick_ref[...] = jnp.where(source == jnp.where(lane < 128, sent, kept), 1.0, 0.0).astype(bf16)
    lane = iota((8, 128), 1)
    border = jnp.where(x == 0, lane - (128 - SIDE), lane)
    mask_ref[0] = jnp.where((border >= 0) & (border < SIDE), 1.0, 0.0)
    mask_ref[1] = jnp.where(lane > 0, 1.0, 0.0)
    mask_ref[2] = jnp.where(lane < 127, 1.0, 0.0)


def pack_kernel(vol_ref, pick_ref, copy_ref, send_ref, own_ref):
    depths, rows, cols = vol_ref.shape
    slot = lax.div(lax.rem(iota((rows, 256), 1), 128), SIDE)
    copy_ref[...] = vol_ref[...]
    picked = dot(vol_ref[...].reshape(depths * rows, cols), pick_ref[...])
    for tile in range(TILES):
        if tile < 2:
            planes = [(1 + SLOTS * tile + index, index) for index in range(SLOTS)]
        else:
            planes = [(0, 0), (depths - 1, 1)]
        packed = jnp.zeros((rows, 256), jnp.float32)
        for plane, index in planes:
            packed = jnp.where(slot == index, picked[rows * plane : rows * (plane + 1)], packed)
        packed = packed.astype(jnp.bfloat16)
        send_ref[tile] = packed[:, :128]
        own_ref[tile] = packed[:, 128:]


def rows_kernel(vol_ref, own_ref, side_ref, after_ref, halo_ref, near_ref, far_ref, packed_ref):
    depths, rows, cols = vol_ref.shape
    even = lax.rem(lax.axis_index("il"), 2) == 0

    def put(row, top, bottom):
        top, bottom = top[:REACH], bottom[EDGE - REACH :]
        lanes = top.shape[1]
        packed_ref[0, row : row + REACH, :lanes] = jnp.where(even, bottom, top)
        packed_ref[1, row : row + REACH, :lanes] = jnp.where(even, top, bottom)

    packed_ref[:, depths * REACH :, :] = jnp.zeros_like(packed_ref[:, depths * REACH :, :])
    for depth in range(depths):
        top = vol_ref[depth, :EDGE, :].astype(jnp.float32)
        bottom = vol_ref[depth, rows - EDGE :, :].astype(jnp.float32)
        put(REACH * depth, top, bottom)
    tiles = []
    for tile in range(TILES):
        merged = own_ref[tile].astype(jnp.float32) + side_ref[tile].astype(jnp.float32)
        halo_ref[:, 128 * tile : 128 * (tile + 1)] = merged.astype(jnp.bfloat16)
        tiles.append((merged[:EDGE], merged[rows - EDGE :]))
    tops = jnp.concatenate([tiles[0][0], tiles[1][0]], axis=1)
    bottoms = jnp.concatenate([tiles[0][1], tiles[1][1]], axis=1)
    put(REACH * depths, tops, bottoms)
    put(REACH * (depths + 1), *tiles[2])
    near_ref[...] = packed_ref[0].astype(jnp.bfloat16)
    far_ref[...] = packed_ref[1].astype(jnp.bfloat16)


def relay_kernel(rows_ref, after_ref, out_ref):
    out_ref[...] = rows_ref[...]


def moments(grad_i, grad_x, grad_z):
    terms = (
        grad_i * grad_i,
        grad_x * grad_x,
        grad_z * grad_z,
        grad_i * grad_x,
        grad_i * grad_z,
        grad_x * grad_z,
    )
    return [term.astype(jnp.bfloat16) for term in terms]


def store_chunks(summed, comp, inner_ref, part_ref):
    chunks = summed.shape[0] // EDGE
    for chunk in range(1, chunks - 1):
        inner_ref[chunk - 1, comp] = summed[EDGE * chunk : EDGE * (chunk + 1)].astype(jnp.bfloat16)
    part_ref[0, comp] = summed[:EDGE]
    part_ref[1, comp] = summed[EDGE * (chunks - 1) :]


def gradients(before, centre, after, mask_ref):
    rows, cols = centre.shape
    left, right = pltpu.roll(centre, 1, 1), pltpu.roll(centre, cols - 1, 1)
    left_0 = (left[:, :128].reshape(-1, 8, 128) * mask_ref[1]).reshape(rows, 128)
    right_1 = (right[:, cols - 128 :].reshape(-1, 8, 128) * mask_ref[2]).reshape(rows, 128)
    grad_x = jnp.concatenate([right[:, : cols - 128] - left_0, right_1 - left[:, 128:]], axis=1)
    return pltpu.roll(centre, rows - 1, 0) - pltpu.roll(centre, 1, 0), grad_x, after - before


def make_moments(pair, vol_ref, mask_ref, moments_ref):
    planes = [vol_ref[2 * pair + k].astype(jnp.float32) for k in range(4)]
    for k in range(2):
        for comp, term in enumerate(moments(*gradients(*planes[k : k + 3], mask_ref))):
            moments_ref[k, comp] = term


def make_lines(z, comp, lines_ref, moments_ref, inner_ref, part_ref):
    store_chunks(dot(lines_ref[...], moments_ref[z % 2, comp]), comp, inner_ref.at[z], part_ref.at[:, :, z])


def lines_kernel(vol_ref, lines_ref, mask_ref, inner_ref, part_ref, even_ref, odd_ref):
    slots = (even_ref, odd_ref)
    for pair in range(HEAD):
        make_moments(pair, vol_ref, mask_ref, slots[pair % 2])
        for k in range(2):
            for comp in range(6):
                make_lines(2 * pair + k, comp, lines_ref, slots[pair % 2], inner_ref, part_ref)


def tensor_of(own, smooth_ref, tensor_ref):
    tensor_ref[...] = dot(own.reshape(-1, own.shape[-1]), smooth_ref[...])


def attributes(tensor, border, store):
    x = lax.axis_index("xl")
    halves = (tensor[:, :128], tensor[:, 128:] + border)
    lanes = (pl.multiple_of(128 * x, 128), pl.multiple_of(128 - 128 * x, 128))
    for half, lane in zip(halves, lanes):
        a, b, c, d, e, f = [half[EDGE * comp : EDGE * (comp + 1)] for comp in range(6)]
        low = -1e-6 - c
        inverse = pl.reciprocal(low, approx=True)
        spread = (a - b) * (a - c) + (b - c) * (b - c) + 3.0 * (d * d + e * e + f * f)
        root = spread * lax.rsqrt(jnp.maximum(spread, TINY))
        store(pl.ds(lane, 128), (e * inverse, f * inverse, root * pl.reciprocal(a + b - low, approx=True)))


def border_of(packed, slot, mask_ref):
    base = jnp.where(lax.axis_index("xl") == 0, 128 - SIDE, 0)
    moved = pltpu.roll(packed, lax.rem(base - SIDE * slot + 128, 128), 1)
    return (moved.reshape(-1, 8, 128) * mask_ref[0]).reshape(packed.shape)


def own_kernel(
    stage, vol_ref, lines_ref, diff_i_ref, smooth_ref, halo_ref, diff_h_ref, pack_h_ref, mask_ref,
    inner_in_ref, part_in_ref, *refs,
):
    if stage == 0:
        inner_ref, part_ref, *targets, later_ref, part_h_ref, border_ref, even_ref, odd_ref, tensor_ref, out_ref, sems = refs
        both = dot(halo_ref[...], diff_h_ref[...])
        grad_i = dot(diff_i_ref[...], halo_ref[:, :256])
        lined_h = [[] for chunk in range(inner_ref.shape[1])]
        for comp, term in enumerate(moments(grad_i, both[:, 256:], both[:, :256])):
            summed = dot(lines_ref[...], term)
            for chunk, parts in enumerate(lined_h):
                parts.append(summed[EDGE * (chunk + 1) : EDGE * (chunk + 2)].astype(jnp.bfloat16))
            part_h_ref[0, comp] = summed[:EDGE]
            part_h_ref[1, comp] = summed[EDGE * (len(lined_h) + 1) :]
        border_ref[...] = dot(jnp.concatenate(sum(lined_h, []), axis=0), pack_h_ref[...])
        finished = []
    else:
        border_ref, done_ref, *refs = refs
        inner_ref, part_ref, *targets, later_ref, even_ref, odd_ref, tensor_ref, out_ref, sems, done_sems = refs[3:]
        finished = []
    count, chunks = inner_ref.shape[:2]
    pairs, inner = count // 4, EDGE * chunks
    slots = (even_ref, odd_ref)

    def place(target, pair):
        return target.at[pl.ds(2 * pair, 2), pl.ds(EDGE, inner)]

    if stage == 1:
        for n, target in enumerate(targets):
            finished.append(pltpu.make_async_copy(done_ref.at[n], place(target, pairs - 1), done_sems.at[n]))
            finished[-1].start()

    half = count // 2
    ahead = range(2 * HEAD, half + 2 * AHEAD) if stage == 0 else range(half + 2 * AHEAD, count)
    tensor_of(inner_ref[half * stage], smooth_ref, tensor_ref.at[0])
    for step in range(half):
        z = half * stage + step
        later = ahead[step] if step < len(ahead) else None
        if later is not None and later % 2 == 0:
            make_moments(later // 2, vol_ref, mask_ref, slots[later // 2 % 2])
        if step < half - 1:
            tensor_of(inner_ref[z + 1], smooth_ref, tensor_ref.at[(step + 1) % 2])
        for chunk in range(chunks):
            rows = slice(EDGE * chunk, EDGE * (chunk + 1))
            part = slice(6 * EDGE * chunk, 6 * EDGE * (chunk + 1))

            def store(lanes, values):
                for n, value in enumerate(values):
                    if step >= half - 2:
                        later_ref[n, step % 2, rows, lanes] = value
                    else:
                        out_ref[n, step, rows, lanes] = value

            border = border_of(border_ref[part, 128 * stage : 128 * (stage + 1)], z % SLOTS, mask_ref)
            attributes(tensor_ref[step % 2, part], border, store)
            if later is not None:
                make_lines(later, chunk, lines_ref, slots[later // 2 % 2], inner_ref, part_ref)
        if step % 2 == 1 and step < half - 2:
            for n, target in enumerate(targets):
                source = out_ref.at[n, pl.ds(step - 1, 2)]
                finished.append(pltpu.make_async_copy(source, place(target, z // 2), sems.at[step // 2, n]))
                finished[-1].start()
    for copy in finished:
        copy.wait()


def end_kernel(
    exchange, vol_ref, halo_ref, rows_ref, part_ref, part_h_ref,
    smooth_ref, pack_h_ref, diff_h_ref, lines_e_ref, diff_e_ref, mask_ref, done_ref, *refs,
):
    last = exchange == 1
    targets, refs = refs[3:6], refs[6:]
    if last:
        packed_ref, block_ref, block_h_ref, border_ref, edge_ref, out_ref, done_sems, sems = refs
    else:
        out_ref, packed_ref, block_ref, block_h_ref, border_ref, edge_ref, done_sems = refs
    depths, rows, cols = vol_ref.shape
    count, half = depths - 2, (depths - 2) // 2
    bf16, f32 = jnp.bfloat16, jnp.float32
    low = low_end(exchange)
    end = jnp.where(low, 0, 1)
    start = pl.multiple_of(jnp.where(low, 0, rows - EDGE), EDGE)
    other = pl.multiple_of(jnp.where(low, rows - EDGE, 0), EDGE)
    finished = []
    for n, target in enumerate(targets):
        if last:
            place = target.at[:, pl.ds(other, EDGE)]
        else:
            place = target.at[pl.ds(count - 2, 2), pl.ds(EDGE, rows - 2 * EDGE)]
        finished.append(pltpu.make_async_copy(done_ref.at[n], place, done_sems.at[n]))
    for copy in finished:
        copy.start()

    packed_ref[:8] = jnp.zeros_like(packed_ref[:8])
    if last:
        il = lax.axis_index("il")
        outside = (low & (il == 0)) | (jnp.logical_not(low) & (il == lax.axis_size("il") - 1))
        packed_ref[8:] = jnp.where(outside, 0.0, rows_ref[...].astype(f32))
    else:
        packed_ref[8:] = rows_ref[...].astype(f32)

    def joined(row, own):
        lanes = own.shape[1]
        before = packed_ref[8 + row : 8 + row + EDGE, :lanes]
        after = packed_ref[8 + row - (EDGE - REACH) : 8 + row + REACH, :lanes]
        own = own.astype(f32)
        place = iota(own.shape, 0)
        first = jnp.where(place < REACH, before, pltpu.roll(own, REACH, 0))
        second = jnp.where(place < EDGE - REACH, pltpu.roll(own, EDGE - REACH, 0), after)
        return jnp.where(low, first, second).astype(bf16)

    for depth in range(depths):
        block_ref[depth] = joined(REACH * depth, vol_ref[depth, pl.ds(start, EDGE)])
    own_h = halo_ref[pl.ds(start, EDGE)]
    block_h_ref[:, :256] = joined(REACH * depths, own_h[:, :256])
    block_h_ref[:, 256:] = joined(REACH * (depths + 1), own_h[:, 256:])

    both = dot(block_h_ref[...], diff_h_ref[...])
    grad_i = dot(diff_e_ref[...], block_h_ref[:, :256])
    lined_h = []
    for comp, term in enumerate(moments(grad_i, both[:, 256:], both[:, :256])):
        summed = part_h_ref[end, comp] + dot(lines_e_ref[exchange, :EDGE, :EDGE], term)
        lined_h.append(summed.astype(bf16))
    border_ref[...] = dot(jnp.concatenate(lined_h, axis=0), pack_h_ref[...])

    span = EDGE * half
    copies = []
    def make_block_moments(group):
        first = half * group
        planes = [block_ref[first + k : first + half + k].astype(f32).reshape(span, cols) for k in range(3)]
        return moments(*gradients(*planes, mask_ref))

    def make_edge(group, comp, term):
        first = half * group
        outer = dot(lines_e_ref[exchange, :span, :span], term)
        summed = part_ref[end, comp, first : first + half] + outer.reshape(half, EDGE, cols)
        edge_ref[first : first + half, comp] = summed.astype(bf16)

    def finish(group, k, tensor):
        def store(lanes, values):
            for n, value in enumerate(values):
                out_ref[n, half * group + k, :, lanes] = value

        border = border_of(border_ref[:, 128 * group : 128 * (group + 1)], k, mask_ref)
        attributes(tensor, border, store)

    def send(group):
        depth = pl.ds(half * group, half)
        for n, target in enumerate(targets):
            copy = pltpu.make_async_copy(out_ref.at[n, depth], target.at[depth, pl.ds(start, EDGE)], sems.at[group, n])
            copy.start()
            copies.append(copy)

    for group in range(2):
        for comp, term in enumerate(make_block_moments(group)):
            make_edge(group, comp, term)
    for group in range(2):
        tensor = dot(edge_ref[half * group : half * (group + 1)].reshape(6 * span, cols), smooth_ref[...])
        for k in range(half):
            finish(group, k, tensor[6 * EDGE * k : 6 * EDGE * (k + 1)])
        if last:
            send(group)
    for copy in finished + copies:
        copy.wait()


def call(name, kernel, outs, scratch, operands, in_specs=None, out_specs=None, flops=0, limit=16, aliases={}):
    return pl.pallas_call(
        kernel,
        out_shape=tuple(jax.ShapeDtypeStruct(*out) for out in outs),
        in_specs=in_specs or [WHOLE] * len(operands),
        out_specs=out_specs or (WHOLE,) * len(outs),
        scratch_shapes=scratch,
        compiler_params=pltpu.CompilerParams(vmem_limit_bytes=limit << 20),
        name=name,
        input_output_aliases=aliases,
        cost_estimate=pl.CostEstimate(flops=flops, bytes_accessed=0, transcendentals=0),
    )(*operands)


def body(volume):
    depths, rows, cols = volume.shape
    il, xl = lax.axis_size("il"), lax.axis_size("xl")
    count = depths - 2
    assert xl == 2 and il % 2 == 0 and count == 2 * SLOTS and rows == 128 and cols == 256
    bf16, f32 = jnp.bfloat16, jnp.float32
    half = count // 2
    work = half * 1024 * 2 * 256 * 256
    packed_rows = -(-REACH * (depths + 2) // 16) * 16

    span = EDGE * SLOTS
    lines, diff_i, smooth, pack_h, diff_h, lines_e, diff_e, pick, mask = call(
        "tables_kernel",
        lambda *refs: tables_kernel(depths, *refs),
        [
            ((rows, rows), bf16),
            ((rows, rows), bf16),
            ((cols, cols), bf16),
            ((256, 256), bf16),
            ((128 * TILES, 512), bf16),
            ((2, span, span), bf16),
            ((EDGE, EDGE), bf16),
            ((cols, 256), bf16),
            ((3, 8, 128), f32),
        ],
        [],
        [],
        flops=work,
    )
    halo_tile = ((TILES, rows, 128), bf16)
    vol, send, own = call("pack_kernel", pack_kernel, [(volume.shape, bf16), halo_tile, halo_tile], [], [volume, pick])
    side = lax.ppermute(send, "xl", [(0, 1), (1, 0)])
    chunks = rows // EDGE - 2
    lined = [((count, chunks, 6, EDGE, cols), bf16), ((2, 6, count, EDGE, cols), f32)]
    moment_slots = [pltpu.VMEM((2, 6, rows, cols), bf16)] * 2
    inner, part = call("lines_kernel", lines_kernel, lined, moment_slots, [vol, lines, mask], flops=work // 4)
    packed = ((packed_rows, cols), bf16)
    halo, near, far = call(
        "rows_kernel",
        rows_kernel,
        [((rows, 128 * TILES), bf16), packed, packed],
        [pltpu.VMEM((2, packed_rows, cols), f32)],
        [vol, own, side, part],
        in_specs=[WHOLE] * 3 + [ANYWHERE],
    )
    swap = [(i, i ^ 1) for i in range(il)]
    ring = [(i, i - 2) for i in range(2, il, 2)] + [(0, 1)]
    ring += [(i, i + 2) for i in range(1, il - 2, 2)] + [(il - 1, il - 2)]
    far_in = lax.ppermute(far, "il", ring)
    near_in = lax.ppermute(near, "il", swap)

    outs = [((count, rows, cols), f32)] * 3
    saved = ((3, 2, EDGE * chunks, cols), f32)
    border = ((6 * EDGE * chunks, 256), f32)
    ready = [((3, count // 2 - 2, EDGE * chunks, cols), f32)]
    own_scratch = moment_slots + [pltpu.VMEM((2, 6 * EDGE * chunks, cols), f32), pltpu.VMEM(*ready[0]), pltpu.SemaphoreType.DMA((count // 4 - 1, 3))]
    shared = [vol, lines, diff_i, smooth, halo, diff_h, pack_h, mask]
    inner, part, *outs_in, done, part_h, border = call(
        "first_own_kernel",
        lambda *refs: own_kernel(0, *refs),
        lined + outs + [saved, ((2, 6, EDGE, 256), f32), border],
        own_scratch,
        shared + [inner, part],
        out_specs=(WHOLE,) * 2 + (IN_HBM,) * 3 + (WHOLE,) * 3,
        flops=3 * work,
        aliases={len(shared) + n: n for n in range(2)},
    )
    (relayed,) = call("relay_kernel", relay_kernel, [packed], [], [far_in, done], in_specs=[WHOLE, ANYWHERE])
    relayed_in = lax.ppermute(relayed, "il", swap)
    inner, part, *outs_in, done = call(
        "second_own_kernel",
        lambda *refs: own_kernel(1, *refs),
        lined + outs + [saved],
        own_scratch + [pltpu.SemaphoreType.DMA((3,))],
        shared + [inner, part, border, done] + outs_in,
        in_specs=[WHOLE] * (len(shared) + 4) + [IN_HBM] * 3,
        out_specs=(WHOLE,) * 2 + (IN_HBM,) * 3 + (WHOLE,),
        flops=3 * work,
        aliases={len(shared): 0, len(shared) + 1: 1} | {len(shared) + 4 + n: 2 + n for n in range(3)},
    )

    end_rows = (3, count, EDGE, cols)
    tables = [smooth, pack_h, diff_h, lines_e, diff_e, mask]
    scratch = [
        pltpu.VMEM((8 + packed_rows, cols), f32),
        pltpu.VMEM((depths, EDGE, cols), bf16),
        pltpu.VMEM((EDGE, 128 * TILES), bf16),
        pltpu.VMEM((6 * EDGE, 256), f32),
        pltpu.VMEM((count, 6, EDGE, cols), bf16),
    ]
    sems = pltpu.SemaphoreType.DMA((3,))
    operands = [vol, halo, near_in, part, part_h, *tables, done]
    *outs_in, done = call(
        "near_end_kernel",
        lambda *refs: end_kernel(0, *refs),
        outs + [(end_rows, f32)],
        scratch + [sems],
        operands + outs_in,
        in_specs=[WHOLE] * len(operands) + [IN_HBM] * 3,
        out_specs=(IN_HBM,) * 3 + (WHOLE,),
        flops=work,
        aliases={len(operands) + n: n for n in range(3)},
    )
    operands = [vol, halo, relayed_in, part, part_h, *tables, done]
    return call(
        "far_end_kernel",
        lambda *refs: end_kernel(1, *refs),
        outs,
        scratch + [pltpu.VMEM(end_rows, f32), sems, pltpu.SemaphoreType.DMA((2, 3))],
        operands + outs_in,
        in_specs=[WHOLE] * len(operands) + [IN_HBM] * 3,
        out_specs=(IN_HBM,) * 3,
        flops=work,
        aliases={len(operands) + n: n for n in range(3)},
    )


def solution(mesh):
    spec = P(None, ("parts", "il"), "xl")
    return jax.shard_map(body, mesh=mesh, in_specs=(spec,), out_specs=(spec,) * 3, check_vma=False)
```

```python
import jax
import jax.numpy as jnp
import ml_dtypes
import numpy as np
from jax import lax
from jax.experimental import pallas as pl
from jax.experimental.pallas import tpu as pltpu
from jax.sharding import PartitionSpec as P

RADIUS = 9
REACH = RADIUS + 1
SIDE = 16
SLOTS = 8
TILES = 3
EDGE = 16
OWN = 2
TINY = float(np.finfo(np.float32).tiny)
HEAD = 2
AHEAD = 2
FAR = -1000
WHOLE = pl.BlockSpec(memory_space=pltpu.VMEM)
IN_HBM = pl.BlockSpec(memory_space=pltpu.HBM)
ANYWHERE = pl.BlockSpec(memory_space=pl.ANY)


def filter_taps():
    offsets = np.arange(2 * RADIUS + 1).astype(np.float32)
    sigma = np.float32(RADIUS / 3.0)
    shape = np.exp(np.float32(-0.5) * ((offsets - RADIUS) / sigma) ** 2)
    return (shape / np.sum(shape, dtype=np.float32)).astype(ml_dtypes.bfloat16).astype(np.float32)


def iota(shape, dim):
    return lax.broadcasted_iota(jnp.int32, shape, dim)


def band(source, target, scale=1.0):
    offset = jnp.abs(source - target)
    weights = jnp.zeros(offset.shape, jnp.float32)
    for distance, tap in enumerate(filter_taps()[RADIUS:]):
        weights = jnp.where(offset == distance, jnp.float32(scale * tap), weights)
    return weights


def difference(source, target):
    offset = source - target
    return jnp.where(offset == 1, 1.0, jnp.where(offset == -1, -1.0, 0.0)).astype(jnp.float32)


def dot(left, right):
    return jnp.dot(left, right, preferred_element_type=jnp.float32)


def halo_plane(lane, tile, depths):
    slot = lax.div(lane, SIDE)
    rest = jnp.where(slot == 0, 0, jnp.where(slot == 1, depths - 1, FAR))
    return jnp.where(tile < 2, 1 + SLOTS * tile + slot, rest)


def halo_column(lane, x, cols):
    place = lax.rem(lane, SIDE)
    return jnp.where(x == 0, cols - OWN + place, place - (SIDE - OWN))


def low_end(exchange):
    even = lax.rem(lax.axis_index("il"), 2) == 0
    return jnp.logical_not(even) if exchange == 0 else even


def tables_kernel(depths, lines_ref, diff_i_ref, smooth_ref, pack_h_ref, diff_h_ref, lines_e_ref, diff_e_ref, pick_ref, mask_ref):
    rows, cols = lines_ref.shape[0], smooth_ref.shape[0]
    x, il, last = lax.axis_index("xl"), lax.axis_index("il"), lax.axis_size("il") - 1
    bf16 = jnp.bfloat16

    target, source = iota((rows, rows), 0), iota((rows, rows), 1)
    inner = (source > 0) & (source < rows - 1)
    lines_ref[...] = jnp.where(inner, band(source, target, 0.25), 0.0).astype(bf16)
    diff_i_ref[...] = difference(source, target).astype(bf16)
    span = EDGE * SLOTS
    target, source = iota((span, span), 0), iota((span, span), 1)
    depth = lax.div(source, EDGE) == lax.div(target, EDGE)
    target, source = lax.rem(target, EDGE), lax.rem(source, EDGE)
    diff_e_ref[...] = difference(source, target)[:EDGE, :EDGE].astype(bf16)
    for exchange in range(2):
        low = low_end(exchange)
        source_at = jnp.where(low, source - REACH, rows - (EDGE - REACH) + source)
        target_at = jnp.where(low, target, rows - EDGE + target)
        first = jnp.where(low & (il > 0), -rows, 0)
        final = jnp.where(jnp.logical_not(low) & (il < last), 2 * rows, rows - 1)
        use = depth & (source_at >= first) & (source_at <= final) & ((source_at <= 0) | (source_at >= rows - 1))
        lines_e_ref[exchange] = jnp.where(use, band(source_at, target_at, 0.25), 0.0).astype(bf16)

    source, target = iota((cols, cols), 0), iota((cols, cols), 1)
    moved = source == jnp.where(x == 0, cols - 1, 0)
    column = lax.rem(target + 128 * x, cols)
    smooth_ref[...] = jnp.where(moved, 0.0, band(source, column)).astype(bf16)
    source, target = iota((256, 256), 0), iota((256, 256), 1)
    place = lax.rem(source, SIDE)
    use = (lax.div(source, SIDE) == lax.div(target, SIDE)) & (place != jnp.where(x == 0, 0, SIDE - 1))
    column = jnp.where(x == 0, cols - SIDE, 0) + lax.rem(target, SIDE)
    pack_h_ref[...] = jnp.where(use, band(halo_column(place, x, cols), column), 0.0).astype(bf16)

    source, target = iota((128, 128), 0), iota((128, 128), 1)
    same = lax.rem(source, SIDE) == lax.rem(target, SIDE)
    across = difference(lax.rem(source, SIDE), lax.rem(target, SIDE))
    for group in range(2):
        centre = halo_plane(target, group, depths)
        for tile in range(TILES):
            plane = halo_plane(source, tile, depths)
            part, out = slice(128 * tile, 128 * (tile + 1)), 128 * group
            diff_h_ref[part, out : out + 128] = jnp.where(same, difference(plane, centre), 0.0).astype(bf16)
            diff_h_ref[part, 256 + out : 384 + out] = jnp.where(plane == centre, across, 0.0).astype(bf16)

    source, lane = iota((cols, 256), 0), iota((cols, 256), 1)
    place = lax.rem(lane, SIDE)
    low, high = place < SIDE - OWN, place >= OWN
    sent = jnp.where(x == 0, jnp.where(low, cols - (SIDE - OWN) + place, FAR), jnp.where(high, place - OWN, FAR))
    low, high = place < OWN, place >= SIDE - OWN
    kept = jnp.where(x == 0, jnp.where(low, cols - OWN + place, FAR), jnp.where(high, place - (SIDE - OWN), FAR))
    pick_ref[...] = jnp.where(source == jnp.where(lane < 128, sent, kept), 1.0, 0.0).astype(bf16)
    lane = iota((8, 128), 1)
    border = jnp.where(x == 0, lane - (128 - SIDE), lane)
    mask_ref[0] = jnp.where((border >= 0) & (border < SIDE), 1.0, 0.0)
    mask_ref[1] = jnp.where(lane > 0, 1.0, 0.0)
    mask_ref[2] = jnp.where(lane < 127, 1.0, 0.0)


def pack_kernel(vol_ref, pick_ref, copy_ref, send_ref, own_ref):
    depths, rows, cols = vol_ref.shape
    slot = lax.div(lax.rem(iota((rows, 256), 1), 128), SIDE)
    copy_ref[...] = vol_ref[...]
    picked = dot(vol_ref[...].reshape(depths * rows, cols), pick_ref[...])
    for tile in range(TILES):
        if tile < 2:
            planes = [(1 + SLOTS * tile + index, index) for index in range(SLOTS)]
        else:
            planes = [(0, 0), (depths - 1, 1)]
        packed = jnp.zeros((rows, 256), jnp.float32)
        for plane, index in planes:
            packed = jnp.where(slot == index, picked[rows * plane : rows * (plane + 1)], packed)
        packed = packed.astype(jnp.bfloat16)
        send_ref[tile] = packed[:, :128]
        own_ref[tile] = packed[:, 128:]


def rows_kernel(vol_ref, own_ref, side_ref, after_ref, halo_ref, near_ref, far_ref, packed_ref):
    depths, rows, cols = vol_ref.shape
    even = lax.rem(lax.axis_index("il"), 2) == 0

    def put(row, top, bottom):
        top, bottom = top[:REACH], bottom[EDGE - REACH :]
        lanes = top.shape[1]
        packed_ref[0, row : row + REACH, :lanes] = jnp.where(even, bottom, top)
        packed_ref[1, row : row + REACH, :lanes] = jnp.where(even, top, bottom)

    packed_ref[:, depths * REACH :, :] = jnp.zeros_like(packed_ref[:, depths * REACH :, :])
    for depth in range(depths):
        top = vol_ref[depth, :EDGE, :].astype(jnp.float32)
        bottom = vol_ref[depth, rows - EDGE :, :].astype(jnp.float32)
        put(REACH * depth, top, bottom)
    tiles = []
    for tile in range(TILES):
        merged = own_ref[tile].astype(jnp.float32) + side_ref[tile].astype(jnp.float32)
        halo_ref[:, 128 * tile : 128 * (tile + 1)] = merged.astype(jnp.bfloat16)
        tiles.append((merged[:EDGE], merged[rows - EDGE :]))
    tops = jnp.concatenate([tiles[0][0], tiles[1][0]], axis=1)
    bottoms = jnp.concatenate([tiles[0][1], tiles[1][1]], axis=1)
    put(REACH * depths, tops, bottoms)
    put(REACH * (depths + 1), *tiles[2])
    near_ref[...] = packed_ref[0].astype(jnp.bfloat16)
    far_ref[...] = packed_ref[1].astype(jnp.bfloat16)


def moments(grad_i, grad_x, grad_z):
    terms = (
        grad_i * grad_i,
        grad_x * grad_x,
        grad_z * grad_z,
        grad_i * grad_x,
        grad_i * grad_z,
        grad_x * grad_z,
    )
    return [term.astype(jnp.bfloat16) for term in terms]


def store_chunks(summed, comp, inner_ref, part_ref):
    chunks = summed.shape[0] // EDGE
    for chunk in range(1, chunks - 1):
        inner_ref[chunk - 1, comp] = summed[EDGE * chunk : EDGE * (chunk + 1)].astype(jnp.bfloat16)
    part_ref[0, comp] = summed[:EDGE]
    part_ref[1, comp] = summed[EDGE * (chunks - 1) :]


def gradients(before, centre, after, mask_ref):
    rows, cols = centre.shape
    left, right = pltpu.roll(centre, 1, 1), pltpu.roll(centre, cols - 1, 1)
    left_0 = (left[:, :128].reshape(-1, 8, 128) * mask_ref[1]).reshape(rows, 128)
    right_1 = (right[:, cols - 128 :].reshape(-1, 8, 128) * mask_ref[2]).reshape(rows, 128)
    grad_x = jnp.concatenate([right[:, : cols - 128] - left_0, right_1 - left[:, 128:]], axis=1)
    return pltpu.roll(centre, rows - 1, 0) - pltpu.roll(centre, 1, 0), grad_x, after - before


def make_moments(pair, vol_ref, mask_ref, moments_ref):
    planes = [vol_ref[2 * pair + k].astype(jnp.float32) for k in range(4)]
    for k in range(2):
        for comp, term in enumerate(moments(*gradients(*planes[k : k + 3], mask_ref))):
            moments_ref[k, comp] = term


def make_lines(z, comp, lines_ref, moments_ref, inner_ref, part_ref):
    store_chunks(dot(lines_ref[...], moments_ref[z % 2, comp]), comp, inner_ref.at[z], part_ref.at[:, :, z])


def lines_kernel(vol_ref, lines_ref, mask_ref, inner_ref, part_ref, even_ref, odd_ref):
    slots = (even_ref, odd_ref)
    for pair in range(HEAD):
        make_moments(pair, vol_ref, mask_ref, slots[pair % 2])
        for k in range(2):
            for comp in range(6):
                make_lines(2 * pair + k, comp, lines_ref, slots[pair % 2], inner_ref, part_ref)


def tensor_of(own, smooth_ref, tensor_ref):
    tensor_ref[...] = dot(own.reshape(-1, own.shape[-1]), smooth_ref[...])


def attributes(tensor, border, store):
    x = lax.axis_index("xl")
    halves = (tensor[:, :128], tensor[:, 128:] + border)
    lanes = (pl.multiple_of(128 * x, 128), pl.multiple_of(128 - 128 * x, 128))
    for half, lane in zip(halves, lanes):
        a, b, c, d, e, f = [half[EDGE * comp : EDGE * (comp + 1)] for comp in range(6)]
        low = -1e-6 - c
        inverse = pl.reciprocal(low, approx=True)
        spread = (a - b) * (a - c) + (b - c) * (b - c) + 3.0 * (d * d + e * e + f * f)
        root = spread * lax.rsqrt(jnp.maximum(spread, TINY))
        store(pl.ds(lane, 128), (e * inverse, f * inverse, root * pl.reciprocal(a + b - low, approx=True)))


def border_of(packed, slot, mask_ref):
    base = jnp.where(lax.axis_index("xl") == 0, 128 - SIDE, 0)
    moved = pltpu.roll(packed, lax.rem(base - SIDE * slot + 128, 128), 1)
    return (moved.reshape(-1, 8, 128) * mask_ref[0]).reshape(packed.shape)


def own_kernel(
    vol_ref, lines_ref, diff_i_ref, smooth_ref, halo_ref, diff_h_ref, pack_h_ref, mask_ref, inner_in_ref, part_in_ref,
    part_ref, dip_i_ref, dip_x_ref, plan_ref, later_ref, part_h_ref,
    inner_ref, border_ref, even_ref, odd_ref, tensor_ref, out_ref, sems,
):
    count, chunks = inner_ref.shape[:2]
    inner = EDGE * chunks
    slots = (even_ref, odd_ref)
    targets = (dip_i_ref, dip_x_ref, plan_ref)
    inner_ref[: 2 * HEAD] = inner_in_ref[...]

    both = dot(halo_ref[...], diff_h_ref[...])
    grad_i = dot(diff_i_ref[...], halo_ref[:, :256])
    lined_h = [[] for chunk in range(chunks)]
    for comp, term in enumerate(moments(grad_i, both[:, 256:], both[:, :256])):
        summed = dot(lines_ref[...], term)
        for chunk, parts in enumerate(lined_h):
            parts.append(summed[EDGE * (chunk + 1) : EDGE * (chunk + 2)].astype(jnp.bfloat16))
        part_h_ref[0, comp] = summed[:EDGE]
        part_h_ref[1, comp] = summed[EDGE * (chunks + 1) :]
    border_ref[...] = dot(jnp.concatenate(sum(lined_h, []), axis=0), pack_h_ref[...])

    copies = []
    tensor_of(inner_ref[0], smooth_ref, tensor_ref.at[0])
    for z in range(count):
        later = z + 2 * HEAD if z + 2 * HEAD < count else None
        if later is not None and later % 2 == 0:
            make_moments(later // 2, vol_ref, mask_ref, slots[later // 2 % 2])
        if z < count - 1:
            tensor_of(inner_ref[z + 1], smooth_ref, tensor_ref.at[(z + 1) % 2])
        group = 128 * (z // SLOTS)
        for chunk in range(chunks):
            rows = slice(EDGE * chunk, EDGE * (chunk + 1))
            part = slice(6 * EDGE * chunk, 6 * EDGE * (chunk + 1))

            def store(lanes, values):
                for n, value in enumerate(values):
                    if z >= count - 2:
                        later_ref[n, z % 2, rows, lanes] = value
                    else:
                        out_ref[n, z, rows, lanes] = value

            border = border_of(border_ref[part, group : group + 128], z % SLOTS, mask_ref)
            attributes(tensor_ref[z % 2, part], border, store)
            if later is not None:
                make_lines(later, chunk, lines_ref, slots[later // 2 % 2], inner_ref, part_ref)
        if z % 2 == 1 and z < count - 2:
            depth = pl.ds(z - 1, 2)
            for n, target in enumerate(targets):
                place = target.at[depth, pl.ds(EDGE, inner)]
                copies.append(pltpu.make_async_copy(out_ref.at[n, depth], place, sems.at[z // 2, n]))
                copies[-1].start()
    for copy in copies:
        copy.wait()


def end_kernel(
    exchange, done_ref, vol_ref, halo_ref, rows_ref, part_ref, part_h_ref,
    smooth_ref, pack_h_ref, diff_h_ref, lines_e_ref, diff_e_ref, mask_ref, *refs,
):
    last = exchange == 1
    targets, refs = refs[3:6], refs[6:]
    if last:
        packed_ref, block_ref, block_h_ref, border_ref, edge_ref, out_ref, done_sems, sems = refs
    else:
        out_ref, packed_ref, block_ref, block_h_ref, border_ref, edge_ref, done_sems = refs
    depths, rows, cols = vol_ref.shape
    count, half = depths - 2, (depths - 2) // 2
    bf16, f32 = jnp.bfloat16, jnp.float32
    low = low_end(exchange)
    end = jnp.where(low, 0, 1)
    start = pl.multiple_of(jnp.where(low, 0, rows - EDGE), EDGE)
    other = pl.multiple_of(jnp.where(low, rows - EDGE, 0), EDGE)
    finished = []
    for n, target in enumerate(targets):
        if last:
            place = target.at[:, pl.ds(other, EDGE)]
        else:
            place = target.at[pl.ds(count - 2, 2), pl.ds(EDGE, rows - 2 * EDGE)]
        finished.append(pltpu.make_async_copy(done_ref.at[n], place, done_sems.at[n]))
    for copy in finished:
        copy.start()

    packed_ref[:8] = jnp.zeros_like(packed_ref[:8])
    if last:
        il = lax.axis_index("il")
        outside = (low & (il == 0)) | (jnp.logical_not(low) & (il == lax.axis_size("il") - 1))
        packed_ref[8:] = jnp.where(outside, 0.0, rows_ref[...].astype(f32))
    else:
        packed_ref[8:] = rows_ref[...].astype(f32)

    def joined(row, own):
        lanes = own.shape[1]
        before = packed_ref[8 + row : 8 + row + EDGE, :lanes]
        after = packed_ref[8 + row - (EDGE - REACH) : 8 + row + REACH, :lanes]
        own = own.astype(f32)
        place = iota(own.shape, 0)
        first = jnp.where(place < REACH, before, pltpu.roll(own, REACH, 0))
        second = jnp.where(place < EDGE - REACH, pltpu.roll(own, EDGE - REACH, 0), after)
        return jnp.where(low, first, second).astype(bf16)

    for depth in range(depths):
        block_ref[depth] = joined(REACH * depth, vol_ref[depth, pl.ds(start, EDGE)])
    own_h = halo_ref[pl.ds(start, EDGE)]
    block_h_ref[:, :256] = joined(REACH * depths, own_h[:, :256])
    block_h_ref[:, 256:] = joined(REACH * (depths + 1), own_h[:, 256:])

    both = dot(block_h_ref[...], diff_h_ref[...])
    grad_i = dot(diff_e_ref[...], block_h_ref[:, :256])
    lined_h = []
    for comp, term in enumerate(moments(grad_i, both[:, 256:], both[:, :256])):
        summed = part_h_ref[end, comp] + dot(lines_e_ref[exchange, :EDGE, :EDGE], term)
        lined_h.append(summed.astype(bf16))
    border_ref[...] = dot(jnp.concatenate(lined_h, axis=0), pack_h_ref[...])

    span = EDGE * half
    copies = []
    def make_block_moments(group):
        first = half * group
        planes = [block_ref[first + k : first + half + k].astype(f32).reshape(span, cols) for k in range(3)]
        return moments(*gradients(*planes, mask_ref))

    def make_edge(group, comp, term):
        first = half * group
        outer = dot(lines_e_ref[exchange, :span, :span], term)
        summed = part_ref[end, comp, first : first + half] + outer.reshape(half, EDGE, cols)
        edge_ref[first : first + half, comp] = summed.astype(bf16)

    def finish(group, k, tensor):
        def store(lanes, values):
            for n, value in enumerate(values):
                out_ref[n, half * group + k, :, lanes] = value

        border = border_of(border_ref[:, 128 * group : 128 * (group + 1)], k, mask_ref)
        attributes(tensor, border, store)

    def send(group):
        depth = pl.ds(half * group, half)
        for n, target in enumerate(targets):
            copy = pltpu.make_async_copy(out_ref.at[n, depth], target.at[depth, pl.ds(start, EDGE)], sems.at[group, n])
            copy.start()
            copies.append(copy)

    for group in range(2):
        for comp, term in enumerate(make_block_moments(group)):
            make_edge(group, comp, term)
    for group in range(2):
        tensor = dot(edge_ref[half * group : half * (group + 1)].reshape(6 * span, cols), smooth_ref[...])
        for k in range(half):
            finish(group, k, tensor[6 * EDGE * k : 6 * EDGE * (k + 1)])
        if last:
            send(group)
    for copy in finished + copies:
        copy.wait()


def call(name, kernel, outs, scratch, operands, in_specs=None, out_specs=None, flops=0, limit=16, aliases={}):
    return pl.pallas_call(
        kernel,
        out_shape=tuple(jax.ShapeDtypeStruct(*out) for out in outs),
        in_specs=in_specs or [WHOLE] * len(operands),
        out_specs=out_specs or (WHOLE,) * len(outs),
        scratch_shapes=scratch,
        compiler_params=pltpu.CompilerParams(vmem_limit_bytes=limit << 20),
        name=name,
        input_output_aliases=aliases,
        cost_estimate=pl.CostEstimate(flops=flops, bytes_accessed=0, transcendentals=0),
    )(*operands)


def body(volume):
    depths, rows, cols = volume.shape
    il, xl = lax.axis_size("il"), lax.axis_size("xl")
    count = depths - 2
    assert xl == 2 and il % 2 == 0 and count == 2 * SLOTS and rows == 128 and cols == 256
    bf16, f32 = jnp.bfloat16, jnp.float32
    half = count // 2
    work = half * 1024 * 2 * 256 * 256
    packed_rows = -(-REACH * (depths + 2) // 16) * 16

    span = EDGE * SLOTS
    lines, diff_i, smooth, pack_h, diff_h, lines_e, diff_e, pick, mask = call(
        "tables_kernel",
        lambda *refs: tables_kernel(depths, *refs),
        [
            ((rows, rows), bf16),
            ((rows, rows), bf16),
            ((cols, cols), bf16),
            ((256, 256), bf16),
            ((128 * TILES, 512), bf16),
            ((2, span, span), bf16),
            ((EDGE, EDGE), bf16),
            ((cols, 256), bf16),
            ((3, 8, 128), f32),
        ],
        [],
        [],
        flops=work,
    )
    halo_tile = ((TILES, rows, 128), bf16)
    vol, send, own = call("pack_kernel", pack_kernel, [(volume.shape, bf16), halo_tile, halo_tile], [], [volume, pick])
    side = lax.ppermute(send, "xl", [(0, 1), (1, 0)])
    chunks = rows // EDGE - 2
    moment_slots = [pltpu.VMEM((2, 6, rows, cols), bf16)] * 2
    partial = ((2, 6, count, EDGE, cols), f32)
    inner, part = call(
        "lines_kernel",
        lines_kernel,
        [((2 * HEAD, chunks, 6, EDGE, cols), bf16), partial],
        moment_slots,
        [vol, lines, mask],
        flops=work // 4,
    )
    packed = ((packed_rows, cols), bf16)
    halo, near, far = call(
        "rows_kernel",
        rows_kernel,
        [((rows, 128 * TILES), bf16), packed, packed],
        [pltpu.VMEM((2, packed_rows, cols), f32)],
        [vol, own, side, part],
        in_specs=[WHOLE] * 3 + [ANYWHERE],
    )
    near_in = lax.ppermute(near, "il", [(i, i ^ 1) for i in range(il)])
    pairs = [(i, i + 1) for i in range(1, il - 1, 2)]
    far_in = lax.ppermute(far, "il", pairs + [(j, i) for i, j in pairs] + [(0, 0), (il - 1, il - 1)])

    outs = [((count, rows, cols), f32)] * 3
    operands = [vol, lines, diff_i, smooth, halo, diff_h, pack_h, mask, inner, part]
    part, *outs_in, done, part_h = call(
        "own_kernel",
        own_kernel,
        [partial, *outs, ((3, 2, EDGE * chunks, cols), f32), ((2, 6, EDGE, 256), f32)],
        [
            pltpu.VMEM((count, chunks, 6, EDGE, cols), bf16),
            pltpu.VMEM((6 * EDGE * chunks, 256), f32),
            *moment_slots,
            pltpu.VMEM((2, 6 * EDGE * chunks, cols), f32),
            pltpu.VMEM((3, count - 2, EDGE * chunks, cols), f32),
            pltpu.SemaphoreType.DMA((half - 1, 3)),
        ],
        operands,
        out_specs=(WHOLE,) + (IN_HBM,) * 3 + (WHOLE,) * 2,
        flops=5 * work,
        limit=24,
        aliases={len(operands) - 1: 0},
    )

    end_rows = (3, count, EDGE, cols)
    tables = [smooth, pack_h, diff_h, lines_e, diff_e, mask]
    scratch = [
        pltpu.VMEM((8 + packed_rows, cols), f32),
        pltpu.VMEM((depths, EDGE, cols), bf16),
        pltpu.VMEM((EDGE, 128 * TILES), bf16),
        pltpu.VMEM((6 * EDGE, 256), f32),
        pltpu.VMEM((count, 6, EDGE, cols), bf16),
    ]
    sems = pltpu.SemaphoreType.DMA((3,))
    operands = [done, vol, halo, near_in, part, part_h, *tables]
    *outs_in, done = call(
        "near_end_kernel",
        lambda *refs: end_kernel(0, *refs),
        outs + [(end_rows, f32)],
        scratch + [sems],
        operands + outs_in,
        in_specs=[WHOLE] * len(operands) + [IN_HBM] * 3,
        out_specs=(IN_HBM,) * 3 + (WHOLE,),
        flops=work,
        aliases={len(operands) + n: n for n in range(3)},
    )
    operands = [done, vol, halo, far_in, part, part_h, *tables]
    return call(
        "far_end_kernel",
        lambda *refs: end_kernel(1, *refs),
        outs,
        scratch + [pltpu.VMEM(end_rows, f32), sems, pltpu.SemaphoreType.DMA((2, 3))],
        operands + outs_in,
        in_specs=[WHOLE] * len(operands) + [IN_HBM] * 3,
        out_specs=(IN_HBM,) * 3,
        flops=work,
        aliases={len(operands) + n: n for n in range(3)},
    )


def solution(mesh):
    spec = P(None, ("parts", "il"), "xl")
    return jax.shard_map(body, mesh=mesh, in_specs=(spec,), out_specs=(spec,) * 3, check_vma=False)
```

```python
import jax
import jax.numpy as jnp
import ml_dtypes
import numpy as np
from jax import lax
from jax.experimental import pallas as pl
from jax.experimental.pallas import tpu as pltpu
from jax.sharding import PartitionSpec as P

RADIUS = 9
REACH = RADIUS + 1
SIDE = 16
SLOTS = 8
TILES = 3
EDGE = 16
OWN = 2
TINY = float(np.finfo(np.float32).tiny)
HEAD = 3
AHEAD = 3
FAR = -1000
WHOLE = pl.BlockSpec(memory_space=pltpu.VMEM)
IN_HBM = pl.BlockSpec(memory_space=pltpu.HBM)
ANYWHERE = pl.BlockSpec(memory_space=pl.ANY)


def filter_taps():
    offsets = np.arange(2 * RADIUS + 1).astype(np.float32)
    sigma = np.float32(RADIUS / 3.0)
    shape = np.exp(np.float32(-0.5) * ((offsets - RADIUS) / sigma) ** 2)
    return (shape / np.sum(shape, dtype=np.float32)).astype(ml_dtypes.bfloat16).astype(np.float32)


def iota(shape, dim):
    return lax.broadcasted_iota(jnp.int32, shape, dim)


def band(source, target, scale=1.0):
    offset = jnp.abs(source - target)
    weights = jnp.zeros(offset.shape, jnp.float32)
    for distance, tap in enumerate(filter_taps()[RADIUS:]):
        weights = jnp.where(offset == distance, jnp.float32(scale * tap), weights)
    return weights


def difference(source, target):
    offset = source - target
    return jnp.where(offset == 1, 1.0, jnp.where(offset == -1, -1.0, 0.0)).astype(jnp.float32)


def dot(left, right):
    return jnp.dot(left, right, preferred_element_type=jnp.float32)


def halo_plane(lane, tile, depths):
    slot = lax.div(lane, SIDE)
    rest = jnp.where(slot == 0, 0, jnp.where(slot == 1, depths - 1, FAR))
    return jnp.where(tile < 2, 1 + SLOTS * tile + slot, rest)


def halo_column(lane, x, cols):
    place = lax.rem(lane, SIDE)
    return jnp.where(x == 0, cols - OWN + place, place - (SIDE - OWN))


def low_end(exchange):
    even = lax.rem(lax.axis_index("il"), 2) == 0
    return jnp.logical_not(even) if exchange == 0 else even


def tables_kernel(depths, lines_ref, diff_i_ref, smooth_ref, pack_h_ref, diff_h_ref, lines_e_ref, diff_e_ref, pick_ref, mask_ref):
    rows, cols = lines_ref.shape[0], smooth_ref.shape[0]
    x, il, last = lax.axis_index("xl"), lax.axis_index("il"), lax.axis_size("il") - 1
    bf16 = jnp.bfloat16

    target, source = iota((rows, rows), 0), iota((rows, rows), 1)
    inner = (source > 0) & (source < rows - 1)
    lines_ref[...] = jnp.where(inner, band(source, target, 0.25), 0.0).astype(bf16)
    diff_i_ref[...] = difference(source, target).astype(bf16)
    span = EDGE * SLOTS
    target, source = iota((span, span), 0), iota((span, span), 1)
    depth = lax.div(source, EDGE) == lax.div(target, EDGE)
    target, source = lax.rem(target, EDGE), lax.rem(source, EDGE)
    diff_e_ref[...] = difference(source, target)[:EDGE, :EDGE].astype(bf16)
    for exchange in range(2):
        low = low_end(exchange)
        source_at = jnp.where(low, source - REACH, rows - (EDGE - REACH) + source)
        target_at = jnp.where(low, target, rows - EDGE + target)
        first = jnp.where(low & (il > 0), -rows, 0)
        final = jnp.where(jnp.logical_not(low) & (il < last), 2 * rows, rows - 1)
        use = depth & (source_at >= first) & (source_at <= final) & ((source_at <= 0) | (source_at >= rows - 1))
        lines_e_ref[exchange] = jnp.where(use, band(source_at, target_at, 0.25), 0.0).astype(bf16)

    source, target = iota((cols, cols), 0), iota((cols, cols), 1)
    moved = source == jnp.where(x == 0, cols - 1, 0)
    column = lax.rem(target + 128 * x, cols)
    smooth_ref[...] = jnp.where(moved, 0.0, band(source, column)).astype(bf16)
    source, target = iota((256, 256), 0), iota((256, 256), 1)
    place = lax.rem(source, SIDE)
    use = (lax.div(source, SIDE) == lax.div(target, SIDE)) & (place != jnp.where(x == 0, 0, SIDE - 1))
    column = jnp.where(x == 0, cols - SIDE, 0) + lax.rem(target, SIDE)
    pack_h_ref[...] = jnp.where(use, band(halo_column(place, x, cols), column), 0.0).astype(bf16)

    source, target = iota((128, 128), 0), iota((128, 128), 1)
    same = lax.rem(source, SIDE) == lax.rem(target, SIDE)
    across = difference(lax.rem(source, SIDE), lax.rem(target, SIDE))
    for group in range(2):
        centre = halo_plane(target, group, depths)
        for tile in range(TILES):
            plane = halo_plane(source, tile, depths)
            part, out = slice(128 * tile, 128 * (tile + 1)), 128 * group
            diff_h_ref[part, out : out + 128] = jnp.where(same, difference(plane, centre), 0.0).astype(bf16)
            diff_h_ref[part, 256 + out : 384 + out] = jnp.where(plane == centre, across, 0.0).astype(bf16)

    source, lane = iota((128, 256), 0), iota((128, 256), 1)
    place = lax.rem(lane, SIDE)
    low, high = place < SIDE - OWN, place >= OWN
    sent = jnp.where(x == 0, jnp.where(low, 128 - (SIDE - OWN) + place, FAR), jnp.where(high, place - OWN, FAR))
    low, high = place < OWN, place >= SIDE - OWN
    kept = jnp.where(x == 0, jnp.where(low, 128 - OWN + place, FAR), jnp.where(high, place - (SIDE - OWN), FAR))
    pick = jnp.where(source == jnp.where(lane < 128, sent, kept), 1.0, 0.0)
    slot = lax.div(lax.rem(lane, 128), SIDE)
    for index in range(SLOTS):
        pick_ref[128 * index : 128 * (index + 1)] = jnp.where(slot == index, pick, 0.0).astype(bf16)
    lane = iota((8, 128), 1)
    border = jnp.where(x == 0, lane - (128 - SIDE), lane)
    mask_ref[0] = jnp.where((border >= 0) & (border < SIDE), 1.0, 0.0)
    mask_ref[1] = jnp.where(lane > 0, 1.0, 0.0)
    mask_ref[2] = jnp.where(lane < 127, 1.0, 0.0)


def pack_kernel(vol_ref, pick_ref, copy_ref, send_ref, own_ref):
    depths, rows, cols = vol_ref.shape
    edge = pl.ds(pl.multiple_of((cols - 128) * (1 - lax.axis_index("xl")), 128), 128)
    copy_ref[...] = vol_ref[...]
    for tile in range(TILES):
        planes = (0, depths - 1) if tile == 2 else range(1 + SLOTS * tile, 1 + SLOTS * (tile + 1))
        beside = jnp.concatenate([vol_ref[plane, :, edge] for plane in planes], axis=1)
        packed = dot(beside, pick_ref[: beside.shape[1]]).astype(jnp.bfloat16)
        send_ref[tile] = packed[:, :128]
        own_ref[tile] = packed[:, 128:]


def rows_kernel(vol_ref, own_ref, side_ref, after_ref, halo_ref, near_ref, far_ref, packed_ref):
    depths, rows, cols = vol_ref.shape
    even = lax.rem(lax.axis_index("il"), 2) == 0

    def put(row, top, bottom):
        top, bottom = top[:REACH], bottom[EDGE - REACH :]
        lanes = top.shape[1]
        packed_ref[0, row : row + REACH, :lanes] = jnp.where(even, bottom, top)
        packed_ref[1, row : row + REACH, :lanes] = jnp.where(even, top, bottom)

    packed_ref[:, depths * REACH :, :] = jnp.zeros_like(packed_ref[:, depths * REACH :, :])
    for depth in range(depths):
        top = vol_ref[depth, :EDGE, :].astype(jnp.float32)
        bottom = vol_ref[depth, rows - EDGE :, :].astype(jnp.float32)
        put(REACH * depth, top, bottom)
    tiles = []
    for tile in range(TILES):
        merged = own_ref[tile].astype(jnp.float32) + side_ref[tile].astype(jnp.float32)
        halo_ref[:, 128 * tile : 128 * (tile + 1)] = merged.astype(jnp.bfloat16)
        tiles.append((merged[:EDGE], merged[rows - EDGE :]))
    tops = jnp.concatenate([tiles[0][0], tiles[1][0]], axis=1)
    bottoms = jnp.concatenate([tiles[0][1], tiles[1][1]], axis=1)
    put(REACH * depths, tops, bottoms)
    put(REACH * (depths + 1), *tiles[2])
    near_ref[...] = packed_ref[0].astype(jnp.bfloat16)
    far_ref[...] = packed_ref[1].astype(jnp.bfloat16)


def moments(grad_i, grad_x, grad_z):
    terms = (
        grad_i * grad_i,
        grad_x * grad_x,
        grad_z * grad_z,
        grad_i * grad_x,
        grad_i * grad_z,
        grad_x * grad_z,
    )
    return [term.astype(jnp.bfloat16) for term in terms]


def store_chunks(summed, comp, inner_ref, part_ref):
    chunks = summed.shape[0] // EDGE
    for chunk in range(1, chunks - 1):
        inner_ref[chunk - 1, comp] = summed[EDGE * chunk : EDGE * (chunk + 1)].astype(jnp.bfloat16)
    part_ref[0, comp] = summed[:EDGE]
    part_ref[1, comp] = summed[EDGE * (chunks - 1) :]


def gradients(before, centre, after, mask_ref):
    rows, cols = centre.shape
    left, right = pltpu.roll(centre, 1, 1), pltpu.roll(centre, cols - 1, 1)
    left_0 = (left[:, :128].reshape(-1, 8, 128) * mask_ref[1]).reshape(rows, 128)
    right_1 = (right[:, cols - 128 :].reshape(-1, 8, 128) * mask_ref[2]).reshape(rows, 128)
    grad_x = jnp.concatenate([right[:, : cols - 128] - left_0, right_1 - left[:, 128:]], axis=1)
    return pltpu.roll(centre, rows - 1, 0) - pltpu.roll(centre, 1, 0), grad_x, after - before


def make_moments(pair, vol_ref, mask_ref, moments_ref):
    planes = [vol_ref[2 * pair + k].astype(jnp.float32) for k in range(4)]
    for k in range(2):
        for comp, term in enumerate(moments(*gradients(*planes[k : k + 3], mask_ref))):
            moments_ref[k, comp] = term


def make_lines(z, comp, lines_ref, moments_ref, inner_ref, part_ref):
    store_chunks(dot(lines_ref[...], moments_ref[z % 2, comp]), comp, inner_ref.at[z], part_ref.at[:, :, z])


def lines_kernel(vol_ref, lines_ref, mask_ref, inner_ref, part_ref, even_ref, odd_ref):
    slots = (even_ref, odd_ref)
    for pair in range(HEAD):
        make_moments(pair, vol_ref, mask_ref, slots[pair % 2])
        for k in range(2):
            for comp in range(6):
                make_lines(2 * pair + k, comp, lines_ref, slots[pair % 2], inner_ref, part_ref)


def tensor_of(own, smooth_ref, tensor_ref):
    tensor_ref[...] = dot(own.reshape(-1, own.shape[-1]), smooth_ref[...])


def attributes(tensor, border, store):
    x = lax.axis_index("xl")
    halves = (tensor[:, :128], tensor[:, 128:] + border)
    lanes = (pl.multiple_of(128 * x, 128), pl.multiple_of(128 - 128 * x, 128))
    for half, lane in zip(halves, lanes):
        a, b, c, d, e, f = [half[EDGE * comp : EDGE * (comp + 1)] for comp in range(6)]
        low = -1e-6 - c
        inverse = pl.reciprocal(low, approx=True)
        spread = (a - b) * (a - c) + (b - c) * (b - c) + 3.0 * (d * d + e * e + f * f)
        root = spread * lax.rsqrt(jnp.maximum(spread, TINY))
        store(pl.ds(lane, 128), (e * inverse, f * inverse, root * pl.reciprocal(a + b - low, approx=True)))


def border_of(packed, slot, mask_ref):
    base = jnp.where(lax.axis_index("xl") == 0, 128 - SIDE, 0)
    moved = pltpu.roll(packed, lax.rem(base - SIDE * slot + 128, 128), 1)
    return (moved.reshape(-1, 8, 128) * mask_ref[0]).reshape(packed.shape)


def own_kernel(
    vol_ref, lines_ref, diff_i_ref, smooth_ref, halo_ref, diff_h_ref, pack_h_ref, mask_ref, inner_in_ref, part_in_ref,
    part_ref, dip_i_ref, dip_x_ref, plan_ref, later_ref, part_h_ref,
    inner_ref, border_ref, even_ref, odd_ref, tensor_ref, out_ref, sems,
):
    count, chunks = inner_ref.shape[:2]
    inner = EDGE * chunks
    slots = (even_ref, odd_ref)
    targets = (dip_i_ref, dip_x_ref, plan_ref)
    inner_ref[: 2 * HEAD] = inner_in_ref[...]

    both = dot(halo_ref[...], diff_h_ref[...])
    grad_i = dot(diff_i_ref[...], halo_ref[:, :256])
    lined_h = [[] for chunk in range(chunks)]
    for comp, term in enumerate(moments(grad_i, both[:, 256:], both[:, :256])):
        summed = dot(lines_ref[...], term)
        for chunk, parts in enumerate(lined_h):
            parts.append(summed[EDGE * (chunk + 1) : EDGE * (chunk + 2)].astype(jnp.bfloat16))
        part_h_ref[0, comp] = summed[:EDGE]
        part_h_ref[1, comp] = summed[EDGE * (chunks + 1) :]
    border_ref[...] = dot(jnp.concatenate(sum(lined_h, []), axis=0), pack_h_ref[...])

    copies = []
    tensor_of(inner_ref[0], smooth_ref, tensor_ref.at[0])
    for z in range(count):
        later = z + 2 * HEAD if z + 2 * HEAD < count else None
        if later is not None and later % 2 == 0:
            make_moments(later // 2, vol_ref, mask_ref, slots[later // 2 % 2])
        if z < count - 1:
            tensor_of(inner_ref[z + 1], smooth_ref, tensor_ref.at[(z + 1) % 2])
        group = 128 * (z // SLOTS)
        for chunk in range(chunks):
            rows = slice(EDGE * chunk, EDGE * (chunk + 1))
            part = slice(6 * EDGE * chunk, 6 * EDGE * (chunk + 1))

            def store(lanes, values):
                for n, value in enumerate(values):
                    if z >= count - 2:
                        later_ref[n, z % 2, rows, lanes] = value
                    else:
                        out_ref[n, z, rows, lanes] = value

            border = border_of(border_ref[part, group : group + 128], z % SLOTS, mask_ref)
            attributes(tensor_ref[z % 2, part], border, store)
            if later is not None:
                make_lines(later, chunk, lines_ref, slots[later // 2 % 2], inner_ref, part_ref)
        if z % 2 == 1 and z < count - 2:
            depth = pl.ds(z - 1, 2)
            for n, target in enumerate(targets):
                place = target.at[depth, pl.ds(EDGE, inner)]
                copies.append(pltpu.make_async_copy(out_ref.at[n, depth], place, sems.at[z // 2, n]))
                copies[-1].start()
    for copy in copies:
        copy.wait()


def end_kernel(
    exchange, done_ref, vol_ref, halo_ref, rows_ref, part_ref, part_h_ref,
    smooth_ref, pack_h_ref, diff_h_ref, lines_e_ref, diff_e_ref, mask_ref, *refs,
):
    last = exchange == 1
    targets, refs = refs[3:6], refs[6:]
    if last:
        packed_ref, block_ref, block_h_ref, border_ref, edge_ref, out_ref, done_sems, sems = refs
    else:
        out_ref, packed_ref, block_ref, block_h_ref, border_ref, edge_ref, done_sems = refs
    depths, rows, cols = vol_ref.shape
    count, half = depths - 2, (depths - 2) // 2
    bf16, f32 = jnp.bfloat16, jnp.float32
    low = low_end(exchange)
    end = jnp.where(low, 0, 1)
    start = pl.multiple_of(jnp.where(low, 0, rows - EDGE), EDGE)
    other = pl.multiple_of(jnp.where(low, rows - EDGE, 0), EDGE)
    finished = []
    for n, target in enumerate(targets):
        if last:
            place = target.at[:, pl.ds(other, EDGE)]
        else:
            place = target.at[pl.ds(count - 2, 2), pl.ds(EDGE, rows - 2 * EDGE)]
        finished.append(pltpu.make_async_copy(done_ref.at[n], place, done_sems.at[n]))
    for copy in finished:
        copy.start()

    rows_in = rows_ref[...].astype(f32)
    if last:
        il = lax.axis_index("il")
        outside = (low & (il == 0)) | (jnp.logical_not(low) & (il == lax.axis_size("il") - 1))
        rows_in = jnp.where(outside, 0.0, rows_in)
    packed_ref[...] = pltpu.roll(rows_in, jnp.where(low, 0, EDGE - REACH), 0)
    place = iota((EDGE, cols), 0)
    received = jnp.where(low, place, EDGE - 1 - place) < REACH

    def joined(row, own):
        lanes = own.shape[1]
        rows_in = packed_ref[row : row + EDGE, :lanes]
        own = pltpu.roll(own.astype(f32), jnp.where(low, REACH, EDGE - REACH), 0)
        return jnp.where(received[:, :lanes], rows_in, own).astype(bf16)

    for depth in range(depths):
        block_ref[depth] = joined(REACH * depth, vol_ref[depth, pl.ds(start, EDGE)])
    own_h = halo_ref[pl.ds(start, EDGE)]
    block_h_ref[:, :256] = joined(REACH * depths, own_h[:, :256])
    block_h_ref[:, 256:] = joined(REACH * (depths + 1), own_h[:, 256:])

    both = dot(block_h_ref[...], diff_h_ref[...])
    grad_i = dot(diff_e_ref[...], block_h_ref[:, :256])
    lined_h = []
    for comp, term in enumerate(moments(grad_i, both[:, 256:], both[:, :256])):
        summed = part_h_ref[end, comp] + dot(lines_e_ref[exchange, :EDGE, :EDGE], term)
        lined_h.append(summed.astype(bf16))
    border_ref[...] = dot(jnp.concatenate(lined_h, axis=0), pack_h_ref[...])

    span = EDGE * half
    copies = []
    def make_block_moments(group):
        first = half * group
        planes = [block_ref[first + k : first + half + k].astype(f32).reshape(span, cols) for k in range(3)]
        return moments(*gradients(*planes, mask_ref))

    def make_edge(group, comp, term):
        first = half * group
        outer = dot(lines_e_ref[exchange, :span, :span], term)
        summed = part_ref[end, comp, first : first + half] + outer.reshape(half, EDGE, cols)
        edge_ref[first : first + half, comp] = summed.astype(bf16)

    def finish(group, k, tensor):
        def store(lanes, values):
            for n, value in enumerate(values):
                out_ref[n, half * group + k, :, lanes] = value

        border = border_of(border_ref[:, 128 * group : 128 * (group + 1)], k, mask_ref)
        attributes(tensor, border, store)

    def send(group):
        depth = pl.ds(half * group, half)
        for n, target in enumerate(targets):
            copy = pltpu.make_async_copy(out_ref.at[n, depth], target.at[depth, pl.ds(start, EDGE)], sems.at[group, n])
            copy.start()
            copies.append(copy)

    for group in range(2):
        for comp, term in enumerate(make_block_moments(group)):
            make_edge(group, comp, term)
    for group in range(2):
        tensor = dot(edge_ref[half * group : half * (group + 1)].reshape(6 * span, cols), smooth_ref[...])
        for k in range(half):
            finish(group, k, tensor[6 * EDGE * k : 6 * EDGE * (k + 1)])
        if last:
            send(group)
    for copy in finished + copies:
        copy.wait()


def call(name, kernel, outs, scratch, operands, in_specs=None, out_specs=None, flops=0, limit=16, aliases={}):
    return pl.pallas_call(
        kernel,
        out_shape=tuple(jax.ShapeDtypeStruct(*out) for out in outs),
        in_specs=in_specs or [WHOLE] * len(operands),
        out_specs=out_specs or (WHOLE,) * len(outs),
        scratch_shapes=scratch,
        compiler_params=pltpu.CompilerParams(vmem_limit_bytes=limit << 20),
        name=name,
        input_output_aliases=aliases,
        cost_estimate=pl.CostEstimate(flops=flops, bytes_accessed=0, transcendentals=0),
    )(*operands)


def body(volume):
    depths, rows, cols = volume.shape
    il, xl = lax.axis_size("il"), lax.axis_size("xl")
    count = depths - 2
    assert xl == 2 and il % 2 == 0 and count == 2 * SLOTS and rows == 128 and cols == 256
    bf16, f32 = jnp.bfloat16, jnp.float32
    half = count // 2
    work = half * 1024 * 2 * 256 * 256
    packed_rows = -(-REACH * (depths + 2) // 16) * 16

    span = EDGE * SLOTS
    lines, diff_i, smooth, pack_h, diff_h, lines_e, diff_e, pick, mask = call(
        "tables_kernel",
        lambda *refs: tables_kernel(depths, *refs),
        [
            ((rows, rows), bf16),
            ((rows, rows), bf16),
            ((cols, cols), bf16),
            ((256, 256), bf16),
            ((128 * TILES, 512), bf16),
            ((2, span, span), bf16),
            ((EDGE, EDGE), bf16),
            ((128 * SLOTS, 256), bf16),
            ((3, 8, 128), f32),
        ],
        [],
        [],
        flops=work,
    )
    halo_tile = ((TILES, rows, 128), bf16)
    vol, send, own = call("pack_kernel", pack_kernel, [(volume.shape, bf16), halo_tile, halo_tile], [], [volume, pick])
    side = lax.ppermute(send, "xl", [(0, 1), (1, 0)])
    chunks = rows // EDGE - 2
    moment_slots = [pltpu.VMEM((2, 6, rows, cols), bf16)] * 2
    partial = ((2, 6, count, EDGE, cols), f32)
    inner, part = call(
        "lines_kernel",
        lines_kernel,
        [((2 * HEAD, chunks, 6, EDGE, cols), bf16), partial],
        moment_slots,
        [vol, lines, mask],
        flops=work // 4,
    )
    packed = ((packed_rows, cols), bf16)
    halo, near, far = call(
        "rows_kernel",
        rows_kernel,
        [((rows, 128 * TILES), bf16), packed, packed],
        [pltpu.VMEM((2, packed_rows, cols), f32)],
        [vol, own, side, part],
        in_specs=[WHOLE] * 3 + [ANYWHERE],
    )
    near_in = lax.ppermute(near, "il", [(i, i ^ 1) for i in range(il)])
    pairs = [(i, i + 1) for i in range(1, il - 1, 2)]
    far_in = lax.ppermute(far, "il", pairs + [(j, i) for i, j in pairs] + [(0, 0), (il - 1, il - 1)])

    outs = [((count, rows, cols), f32)] * 3
    operands = [vol, lines, diff_i, smooth, halo, diff_h, pack_h, mask, inner, part]
    part, *outs_in, done, part_h = call(
        "own_kernel",
        own_kernel,
        [partial, *outs, ((3, 2, EDGE * chunks, cols), f32), ((2, 6, EDGE, 256), f32)],
        [
            pltpu.VMEM((count, chunks, 6, EDGE, cols), bf16),
            pltpu.VMEM((6 * EDGE * chunks, 256), f32),
            *moment_slots,
            pltpu.VMEM((2, 6 * EDGE * chunks, cols), f32),
            pltpu.VMEM((3, count - 2, EDGE * chunks, cols), f32),
            pltpu.SemaphoreType.DMA((half - 1, 3)),
        ],
        operands,
        out_specs=(WHOLE,) + (IN_HBM,) * 3 + (WHOLE,) * 2,
        flops=5 * work,
        limit=24,
        aliases={len(operands) - 1: 0},
    )

    end_rows = (3, count, EDGE, cols)
    tables = [smooth, pack_h, diff_h, lines_e, diff_e, mask]
    scratch = [
        pltpu.VMEM((packed_rows, cols), f32),
        pltpu.VMEM((depths, EDGE, cols), bf16),
        pltpu.VMEM((EDGE, 128 * TILES), bf16),
        pltpu.VMEM((6 * EDGE, 256), f32),
        pltpu.VMEM((count, 6, EDGE, cols), bf16),
    ]
    sems = pltpu.SemaphoreType.DMA((3,))
    operands = [done, vol, halo, near_in, part, part_h, *tables]
    *outs_in, done = call(
        "near_end_kernel",
        lambda *refs: end_kernel(0, *refs),
        outs + [(end_rows, f32)],
        scratch + [sems],
        operands + outs_in,
        in_specs=[WHOLE] * len(operands) + [IN_HBM] * 3,
        out_specs=(IN_HBM,) * 3 + (WHOLE,),
        flops=work,
        aliases={len(operands) + n: n for n in range(3)},
    )
    operands = [done, vol, halo, far_in, part, part_h, *tables]
    return call(
        "far_end_kernel",
        lambda *refs: end_kernel(1, *refs),
        outs,
        scratch + [pltpu.VMEM(end_rows, f32), sems, pltpu.SemaphoreType.DMA((2, 3))],
        operands + outs_in,
        in_specs=[WHOLE] * len(operands) + [IN_HBM] * 3,
        out_specs=(IN_HBM,) * 3,
        flops=work,
        aliases={len(operands) + n: n for n in range(3)},
    )


def solution(mesh):
    spec = P(None, ("parts", "il"), "xl")
    return jax.shard_map(body, mesh=mesh, in_specs=(spec,), out_specs=(spec,) * 3, check_vma=False)
```

```python
import jax
import jax.numpy as jnp
import ml_dtypes
import numpy as np
from jax import lax
from jax.experimental import pallas as pl
from jax.experimental.pallas import tpu as pltpu
from jax.sharding import PartitionSpec as P

RADIUS = 9
REACH = RADIUS + 1
SIDE = 16
SLOTS = 8
TILES = 3
EDGE = 16
OWN = 2
TINY = float(np.finfo(np.float32).tiny)
HEAD = 3
AHEAD = 3
FAR = -1000
WHOLE = pl.BlockSpec(memory_space=pltpu.VMEM)
IN_HBM = pl.BlockSpec(memory_space=pltpu.HBM)
ANYWHERE = pl.BlockSpec(memory_space=pl.ANY)


def filter_taps():
    offsets = np.arange(2 * RADIUS + 1).astype(np.float32)
    sigma = np.float32(RADIUS / 3.0)
    shape = np.exp(np.float32(-0.5) * ((offsets - RADIUS) / sigma) ** 2)
    return (shape / np.sum(shape, dtype=np.float32)).astype(ml_dtypes.bfloat16).astype(np.float32)


def iota(shape, dim):
    return lax.broadcasted_iota(jnp.int32, shape, dim)


def band(source, target, scale=1.0):
    offset = jnp.abs(source - target)
    weights = jnp.zeros(offset.shape, jnp.float32)
    for distance, tap in enumerate(filter_taps()[RADIUS:]):
        weights = jnp.where(offset == distance, jnp.float32(scale * tap), weights)
    return weights


def difference(source, target):
    offset = source - target
    return jnp.where(offset == 1, 1.0, jnp.where(offset == -1, -1.0, 0.0)).astype(jnp.float32)


def dot(left, right):
    return jnp.dot(left, right, preferred_element_type=jnp.float32)


def halo_plane(lane, tile, depths):
    slot = lax.div(lane, SIDE)
    rest = jnp.where(slot == 0, 0, jnp.where(slot == 1, depths - 1, FAR))
    return jnp.where(tile < 2, 1 + SLOTS * tile + slot, rest)


def halo_column(lane, x, cols):
    place = lax.rem(lane, SIDE)
    return jnp.where(x == 0, cols - OWN + place, place - (SIDE - OWN))


def low_end(exchange):
    even = lax.rem(lax.axis_index("il"), 2) == 0
    return jnp.logical_not(even) if exchange == 0 else even


def tables_kernel(depths, lines_ref, diff_i_ref, smooth_ref, pack_h_ref, diff_h_ref, lines_e_ref, diff_e_ref, pick_ref, mask_ref):
    rows, cols = lines_ref.shape[0], smooth_ref.shape[0]
    x, il, last = lax.axis_index("xl"), lax.axis_index("il"), lax.axis_size("il") - 1
    bf16 = jnp.bfloat16

    target, source = iota((rows, rows), 0), iota((rows, rows), 1)
    inner = (source > 0) & (source < rows - 1)
    lines_ref[...] = jnp.where(inner, band(source, target, 0.25), 0.0).astype(bf16)
    diff_i_ref[...] = difference(source, target).astype(bf16)
    span = EDGE * SLOTS
    target, source = iota((span, span), 0), iota((span, span), 1)
    depth = lax.div(source, EDGE) == lax.div(target, EDGE)
    target, source = lax.rem(target, EDGE), lax.rem(source, EDGE)
    diff_e_ref[...] = difference(source, target)[:EDGE, :EDGE].astype(bf16)
    for exchange in range(2):
        low = low_end(exchange)
        source_at = jnp.where(low, source - REACH, rows - (EDGE - REACH) + source)
        target_at = jnp.where(low, target, rows - EDGE + target)
        first = jnp.where(low & (il > 0), -rows, 0)
        final = jnp.where(jnp.logical_not(low) & (il < last), 2 * rows, rows - 1)
        use = depth & (source_at >= first) & (source_at <= final) & ((source_at <= 0) | (source_at >= rows - 1))
        lines_e_ref[exchange] = jnp.where(use, band(source_at, target_at, 0.25), 0.0).astype(bf16)

    source, target = iota((cols, cols), 0), iota((cols, cols), 1)
    moved = source == jnp.where(x == 0, cols - 1, 0)
    column = lax.rem(target + 128 * x, cols)
    smooth_ref[...] = jnp.where(moved, 0.0, band(source, column)).astype(bf16)
    source, target = iota((256, 256), 0), iota((256, 256), 1)
    place = lax.rem(source, SIDE)
    use = (lax.div(source, SIDE) == lax.div(target, SIDE)) & (place != jnp.where(x == 0, 0, SIDE - 1))
    column = jnp.where(x == 0, cols - SIDE, 0) + lax.rem(target, SIDE)
    pack_h_ref[...] = jnp.where(use, band(halo_column(place, x, cols), column), 0.0).astype(bf16)

    source, target = iota((128, 128), 0), iota((128, 128), 1)
    same = lax.rem(source, SIDE) == lax.rem(target, SIDE)
    across = difference(lax.rem(source, SIDE), lax.rem(target, SIDE))
    for group in range(2):
        centre = halo_plane(target, group, depths)
        for tile in range(TILES):
            plane = halo_plane(source, tile, depths)
            part, out = slice(128 * tile, 128 * (tile + 1)), 128 * group
            diff_h_ref[part, out : out + 128] = jnp.where(same, difference(plane, centre), 0.0).astype(bf16)
            diff_h_ref[part, 256 + out : 384 + out] = jnp.where(plane == centre, across, 0.0).astype(bf16)

    source, lane = iota((128, 256), 0), iota((128, 256), 1)
    place = lax.rem(lane, SIDE)
    low, high = place < SIDE - OWN, place >= OWN
    sent = jnp.where(x == 0, jnp.where(low, 128 - (SIDE - OWN) + place, FAR), jnp.where(high, place - OWN, FAR))
    low, high = place < OWN, place >= SIDE - OWN
    kept = jnp.where(x == 0, jnp.where(low, 128 - OWN + place, FAR), jnp.where(high, place - (SIDE - OWN), FAR))
    pick = jnp.where(source == jnp.where(lane < 128, sent, kept), 1.0, 0.0)
    slot = lax.div(lax.rem(lane, 128), SIDE)
    for index in range(SLOTS):
        pick_ref[128 * index : 128 * (index + 1)] = jnp.where(slot == index, pick, 0.0).astype(bf16)
    lane = iota((8, 128), 1)
    border = jnp.where(x == 0, lane - (128 - SIDE), lane)
    mask_ref[0] = jnp.where((border >= 0) & (border < SIDE), 1.0, 0.0)
    mask_ref[1] = jnp.where(lane > 0, 1.0, 0.0)
    mask_ref[2] = jnp.where(lane < 127, 1.0, 0.0)


def pack_kernel(vol_ref, pick_ref, copy_ref, send_ref, own_ref):
    depths, rows, cols = vol_ref.shape
    edge = pl.ds(pl.multiple_of((cols - 128) * (1 - lax.axis_index("xl")), 128), 128)
    copy_ref[...] = vol_ref[...]
    for tile in range(TILES):
        planes = (0, depths - 1) if tile == 2 else range(1 + SLOTS * tile, 1 + SLOTS * (tile + 1))
        beside = jnp.concatenate([vol_ref[plane, :, edge] for plane in planes], axis=1)
        packed = dot(beside, pick_ref[: beside.shape[1]]).astype(jnp.bfloat16)
        send_ref[tile] = packed[:, :128]
        own_ref[tile] = packed[:, 128:]


def rows_kernel(vol_ref, own_ref, side_ref, after_ref, halo_ref, near_ref, far_ref, packed_ref):
    depths, rows, cols = vol_ref.shape
    even = lax.rem(lax.axis_index("il"), 2) == 0

    def put(row, top, bottom):
        top, bottom = top[:REACH], bottom[EDGE - REACH :]
        lanes = top.shape[1]
        packed_ref[0, row : row + REACH, :lanes] = jnp.where(even, bottom, top)
        packed_ref[1, row : row + REACH, :lanes] = jnp.where(even, top, bottom)

    packed_ref[:, depths * REACH :, :] = jnp.zeros_like(packed_ref[:, depths * REACH :, :])
    for depth in range(depths):
        top = vol_ref[depth, :EDGE, :].astype(jnp.float32)
        bottom = vol_ref[depth, rows - EDGE :, :].astype(jnp.float32)
        put(REACH * depth, top, bottom)
    tiles = []
    for tile in range(TILES):
        merged = own_ref[tile].astype(jnp.float32) + side_ref[tile].astype(jnp.float32)
        halo_ref[:, 128 * tile : 128 * (tile + 1)] = merged.astype(jnp.bfloat16)
        tiles.append((merged[:EDGE], merged[rows - EDGE :]))
    tops = jnp.concatenate([tiles[0][0], tiles[1][0]], axis=1)
    bottoms = jnp.concatenate([tiles[0][1], tiles[1][1]], axis=1)
    put(REACH * depths, tops, bottoms)
    put(REACH * (depths + 1), *tiles[2])
    near_ref[...] = packed_ref[0].astype(jnp.bfloat16)
    far_ref[...] = packed_ref[1].astype(jnp.bfloat16)


def moments(grad_i, grad_x, grad_z):
    terms = (
        grad_i * grad_i,
        grad_x * grad_x,
        grad_z * grad_z,
        grad_i * grad_x,
        grad_i * grad_z,
        grad_x * grad_z,
    )
    return [term.astype(jnp.bfloat16) for term in terms]


def store_chunks(summed, comp, inner_ref, part_ref):
    chunks = summed.shape[0] // EDGE
    for chunk in range(1, chunks - 1):
        inner_ref[chunk - 1, comp] = summed[EDGE * chunk : EDGE * (chunk + 1)].astype(jnp.bfloat16)
    part_ref[0, comp] = summed[:EDGE]
    part_ref[1, comp] = summed[EDGE * (chunks - 1) :]


def gradients(before, centre, after, mask_ref):
    rows, cols = centre.shape
    left, right = pltpu.roll(centre, 1, 1), pltpu.roll(centre, cols - 1, 1)
    left_0 = (left[:, :128].reshape(-1, 8, 128) * mask_ref[1]).reshape(rows, 128)
    right_1 = (right[:, cols - 128 :].reshape(-1, 8, 128) * mask_ref[2]).reshape(rows, 128)
    grad_x = jnp.concatenate([right[:, : cols - 128] - left_0, right_1 - left[:, 128:]], axis=1)
    return pltpu.roll(centre, rows - 1, 0) - pltpu.roll(centre, 1, 0), grad_x, after - before


def make_moments(pair, vol_ref, mask_ref, moments_ref):
    planes = [vol_ref[2 * pair + k].astype(jnp.float32) for k in range(4)]
    for k in range(2):
        for comp, term in enumerate(moments(*gradients(*planes[k : k + 3], mask_ref))):
            moments_ref[k, comp] = term


def make_lines(z, comp, lines_ref, moments_ref, inner_ref, part_ref):
    store_chunks(dot(lines_ref[...], moments_ref[z % 2, comp]), comp, inner_ref.at[z], part_ref.at[:, :, z])


def lines_kernel(vol_ref, lines_ref, mask_ref, inner_ref, part_ref, even_ref, odd_ref):
    slots = (even_ref, odd_ref)
    for pair in range(HEAD):
        make_moments(pair, vol_ref, mask_ref, slots[pair % 2])
        for k in range(2):
            for comp in range(6):
                make_lines(2 * pair + k, comp, lines_ref, slots[pair % 2], inner_ref, part_ref)


def tensor_of(own, smooth_ref, tensor_ref):
    tensor_ref[...] = dot(own.reshape(-1, own.shape[-1]), smooth_ref[...])


def attributes(tensor, border, store):
    x = lax.axis_index("xl")
    halves = (tensor[:, :128], tensor[:, 128:] + border)
    lanes = (pl.multiple_of(128 * x, 128), pl.multiple_of(128 - 128 * x, 128))
    for half, lane in zip(halves, lanes):
        a, b, c, d, e, f = [half[EDGE * comp : EDGE * (comp + 1)] for comp in range(6)]
        low = -1e-6 - c
        inverse = pl.reciprocal(low, approx=True)
        spread = (a - b) * (a - c) + (b - c) * (b - c) + 3.0 * (d * d + e * e + f * f)
        root = spread * lax.rsqrt(jnp.maximum(spread, TINY))
        store(pl.ds(lane, 128), (e * inverse, f * inverse, root * pl.reciprocal(a + b - low, approx=True)))


def border_of(packed, slot, mask_ref):
    base = jnp.where(lax.axis_index("xl") == 0, 128 - SIDE, 0)
    moved = pltpu.roll(packed, lax.rem(base - SIDE * slot + 128, 128), 1)
    return (moved.reshape(-1, 8, 128) * mask_ref[0]).reshape(packed.shape)


def own_kernel(
    vol_ref, lines_ref, diff_i_ref, smooth_ref, halo_ref, diff_h_ref, pack_h_ref, mask_ref, inner_in_ref, part_in_ref,
    part_ref, dip_i_ref, dip_x_ref, plan_ref, later_ref, part_h_ref,
    inner_ref, border_ref, even_ref, odd_ref, tensor_ref, out_ref, sems,
):
    count, chunks = inner_ref.shape[:2]
    inner = EDGE * chunks
    slots = (even_ref, odd_ref)
    targets = (dip_i_ref, dip_x_ref, plan_ref)
    inner_ref[: 2 * HEAD] = inner_in_ref[...]

    both = dot(halo_ref[...], diff_h_ref[...])
    grad_i = dot(diff_i_ref[...], halo_ref[:, :256])
    lined_h = [[] for chunk in range(chunks)]
    for comp, term in enumerate(moments(grad_i, both[:, 256:], both[:, :256])):
        summed = dot(lines_ref[...], term)
        for chunk, parts in enumerate(lined_h):
            parts.append(summed[EDGE * (chunk + 1) : EDGE * (chunk + 2)].astype(jnp.bfloat16))
        part_h_ref[0, comp] = summed[:EDGE]
        part_h_ref[1, comp] = summed[EDGE * (chunks + 1) :]
    border_ref[...] = dot(jnp.concatenate(sum(lined_h, []), axis=0), pack_h_ref[...])

    copies = []
    tensor_of(inner_ref[0], smooth_ref, tensor_ref.at[0])
    for z in range(count):
        later = z + 2 * HEAD if z + 2 * HEAD < count else None
        if later is not None and later % 2 == 0:
            make_moments(later // 2, vol_ref, mask_ref, slots[later // 2 % 2])
        if z < count - 1:
            tensor_of(inner_ref[z + 1], smooth_ref, tensor_ref.at[(z + 1) % 2])
        group = 128 * (z // SLOTS)
        for chunk in range(chunks):
            rows = slice(EDGE * chunk, EDGE * (chunk + 1))
            part = slice(6 * EDGE * chunk, 6 * EDGE * (chunk + 1))

            def store(lanes, values):
                for n, value in enumerate(values):
                    if z >= count - 2:
                        later_ref[n, z % 2, rows, lanes] = value
                    else:
                        out_ref[n, z, rows, lanes] = value

            border = border_of(border_ref[part, group : group + 128], z % SLOTS, mask_ref)
            attributes(tensor_ref[z % 2, part], border, store)
            if later is not None:
                make_lines(later, chunk, lines_ref, slots[later // 2 % 2], inner_ref, part_ref)
        if z % 2 == 1 and z < count - 2:
            depth = pl.ds(z - 1, 2)
            for n, target in enumerate(targets):
                place = target.at[depth, pl.ds(EDGE, inner)]
                copies.append(pltpu.make_async_copy(out_ref.at[n, depth], place, sems.at[z // 2, n]))
                copies[-1].start()
    for copy in copies:
        copy.wait()


def ends_kernel(
    done_ref, vol_ref, halo_ref, near_ref, far_ref, part_ref, part_h_ref,
    smooth_ref, pack_h_ref, diff_h_ref, lines_e_ref, diff_e_ref, mask_ref, in_i_ref, in_x_ref, in_p_ref,
    dip_i_ref, dip_x_ref, plan_ref,
    packed_ref, block_ref, block_h_ref, border_ref, edge_ref, out_ref, done_sems, sems,
):
    depths, rows, cols = vol_ref.shape
    count, half = depths - 2, (depths - 2) // 2
    bf16, f32 = jnp.bfloat16, jnp.float32
    span = EDGE * half
    targets = (dip_i_ref, dip_x_ref, plan_ref)
    copies = []
    for n, target in enumerate(targets):
        place = target.at[pl.ds(count - 2, 2), pl.ds(EDGE, rows - 2 * EDGE)]
        copies.append(pltpu.make_async_copy(done_ref.at[n], place, done_sems.at[n]))
        copies[-1].start()
    lows = [low_end(exchange) for exchange in range(2)]
    ends = [jnp.where(low, 0, 1) for low in lows]
    starts = [pl.multiple_of(jnp.where(low, 0, rows - EDGE), EDGE) for low in lows]

    def prepare(exchange, rows_ref):
        low, start, end = lows[exchange], starts[exchange], ends[exchange]
        rows_in = rows_ref[...].astype(f32)
        if exchange == 1:
            il = lax.axis_index("il")
            outside = (low & (il == 0)) | (jnp.logical_not(low) & (il == lax.axis_size("il") - 1))
            rows_in = jnp.where(outside, 0.0, rows_in)
        packed_ref[exchange] = pltpu.roll(rows_in, jnp.where(low, 0, EDGE - REACH), 0)
        place = iota((EDGE, cols), 0)
        received = jnp.where(low, place, EDGE - 1 - place) < REACH

        def joined(row, own):
            lanes = own.shape[1]
            own = pltpu.roll(own.astype(f32), jnp.where(low, REACH, EDGE - REACH), 0)
            return jnp.where(received[:, :lanes], packed_ref[exchange, row : row + EDGE, :lanes], own).astype(bf16)

        for depth in range(depths):
            block_ref[exchange, depth] = joined(REACH * depth, vol_ref[depth, pl.ds(start, EDGE)])
        own_h = halo_ref[pl.ds(start, EDGE)]
        block_h_ref[exchange, :, :256] = joined(REACH * depths, own_h[:, :256])
        block_h_ref[exchange, :, 256:] = joined(REACH * (depths + 1), own_h[:, 256:])

        both = dot(block_h_ref[exchange], diff_h_ref[...])
        grad_i = dot(diff_e_ref[...], block_h_ref[exchange, :, :256])
        lined_h = []
        for comp, term in enumerate(moments(grad_i, both[:, 256:], both[:, :256])):
            summed = part_h_ref[end, comp] + dot(lines_e_ref[exchange, :EDGE, :EDGE], term)
            lined_h.append(summed.astype(bf16))
        border_ref[exchange] = dot(jnp.concatenate(lined_h, axis=0), pack_h_ref[...])

    def make_edges(exchange, group):
        first = half * group
        planes = [block_ref[exchange, first + k : first + half + k].astype(f32).reshape(span, cols) for k in range(3)]
        for comp, term in enumerate(moments(*gradients(*planes, mask_ref))):
            outer = dot(lines_e_ref[exchange], term)
            summed = part_ref[ends[exchange], comp, first : first + half] + outer.reshape(half, EDGE, cols)
            edge_ref[exchange, first : first + half, comp] = summed.astype(bf16)

    def finish(exchange, group):
        first = half * group
        own = edge_ref[exchange, first : first + half].reshape(6 * span, cols)
        tensor = dot(own, smooth_ref[...])
        for k in range(half):

            def store(lanes, values):
                for n, value in enumerate(values):
                    out_ref[exchange, n, first + k, :, lanes] = value

            border = border_of(border_ref[exchange, :, 128 * group : 128 * (group + 1)], k, mask_ref)
            attributes(tensor[6 * EDGE * k : 6 * EDGE * (k + 1)], border, store)
        depth = pl.ds(first, half)
        for n, target in enumerate(targets):
            place = target.at[depth, pl.ds(starts[exchange], EDGE)]
            copies.append(pltpu.make_async_copy(out_ref.at[exchange, n, depth], place, sems.at[exchange, group, n]))
            copies[-1].start()

    for exchange, rows_ref in enumerate((near_ref, far_ref)):
        prepare(exchange, rows_ref)
    for exchange in range(2):
        for group in range(2):
            make_edges(exchange, group)
    for exchange in range(2):
        for group in range(2):
            finish(exchange, group)
    for copy in copies:
        copy.wait()


def call(name, kernel, outs, scratch, operands, in_specs=None, out_specs=None, flops=0, limit=16, aliases={}):
    return pl.pallas_call(
        kernel,
        out_shape=tuple(jax.ShapeDtypeStruct(*out) for out in outs),
        in_specs=in_specs or [WHOLE] * len(operands),
        out_specs=out_specs or (WHOLE,) * len(outs),
        scratch_shapes=scratch,
        compiler_params=pltpu.CompilerParams(vmem_limit_bytes=limit << 20),
        name=name,
        input_output_aliases=aliases,
        cost_estimate=pl.CostEstimate(flops=flops, bytes_accessed=0, transcendentals=0),
    )(*operands)


def body(volume):
    depths, rows, cols = volume.shape
    il, xl = lax.axis_size("il"), lax.axis_size("xl")
    count = depths - 2
    assert xl == 2 and il % 2 == 0 and count == 2 * SLOTS and rows == 128 and cols == 256
    bf16, f32 = jnp.bfloat16, jnp.float32
    half = count // 2
    work = half * 1024 * 2 * 256 * 256
    packed_rows = -(-REACH * (depths + 2) // 16) * 16

    span = EDGE * SLOTS
    lines, diff_i, smooth, pack_h, diff_h, lines_e, diff_e, pick, mask = call(
        "tables_kernel",
        lambda *refs: tables_kernel(depths, *refs),
        [
            ((rows, rows), bf16),
            ((rows, rows), bf16),
            ((cols, cols), bf16),
            ((256, 256), bf16),
            ((128 * TILES, 512), bf16),
            ((2, span, span), bf16),
            ((EDGE, EDGE), bf16),
            ((128 * SLOTS, 256), bf16),
            ((3, 8, 128), f32),
        ],
        [],
        [],
        flops=work,
    )
    halo_tile = ((TILES, rows, 128), bf16)
    vol, send, own = call("pack_kernel", pack_kernel, [(volume.shape, bf16), halo_tile, halo_tile], [], [volume, pick])
    side = lax.ppermute(send, "xl", [(0, 1), (1, 0)])
    chunks = rows // EDGE - 2
    moment_slots = [pltpu.VMEM((2, 6, rows, cols), bf16)] * 2
    partial = ((2, 6, count, EDGE, cols), f32)
    inner, part = call(
        "lines_kernel",
        lines_kernel,
        [((2 * HEAD, chunks, 6, EDGE, cols), bf16), partial],
        moment_slots,
        [vol, lines, mask],
        flops=work // 4,
    )
    packed = ((packed_rows, cols), bf16)
    halo, near, far = call(
        "rows_kernel",
        rows_kernel,
        [((rows, 128 * TILES), bf16), packed, packed],
        [pltpu.VMEM((2, packed_rows, cols), f32)],
        [vol, own, side, part],
        in_specs=[WHOLE] * 3 + [ANYWHERE],
    )
    near_in = lax.ppermute(near, "il", [(i, i ^ 1) for i in range(il)])
    pairs = [(i, i + 1) for i in range(1, il - 1, 2)]
    far_in = lax.ppermute(far, "il", pairs + [(j, i) for i, j in pairs] + [(0, 0), (il - 1, il - 1)])

    outs = [((count, rows, cols), f32)] * 3
    operands = [vol, lines, diff_i, smooth, halo, diff_h, pack_h, mask, inner, part]
    part, *outs_in, done, part_h = call(
        "own_kernel",
        own_kernel,
        [partial, *outs, ((3, 2, EDGE * chunks, cols), f32), ((2, 6, EDGE, 256), f32)],
        [
            pltpu.VMEM((count, chunks, 6, EDGE, cols), bf16),
            pltpu.VMEM((6 * EDGE * chunks, 256), f32),
            *moment_slots,
            pltpu.VMEM((2, 6 * EDGE * chunks, cols), f32),
            pltpu.VMEM((3, count - 2, EDGE * chunks, cols), f32),
            pltpu.SemaphoreType.DMA((half - 1, 3)),
        ],
        operands,
        out_specs=(WHOLE,) + (IN_HBM,) * 3 + (WHOLE,) * 2,
        flops=5 * work,
        limit=24,
        aliases={len(operands) - 1: 0},
    )

    operands = [done, vol, halo, near_in, far_in, part, part_h, smooth, pack_h, diff_h, lines_e, diff_e, mask]
    return call(
        "ends_kernel",
        ends_kernel,
        outs,
        [
            pltpu.VMEM((2, packed_rows, cols), f32),
            pltpu.VMEM((2, depths, EDGE, cols), bf16),
            pltpu.VMEM((2, EDGE, 128 * TILES), bf16),
            pltpu.VMEM((2, 6 * EDGE, 256), f32),
            pltpu.VMEM((2, count, 6, EDGE, cols), bf16),
            pltpu.VMEM((2, 3, count, EDGE, cols), f32),
            pltpu.SemaphoreType.DMA((3,)),
            pltpu.SemaphoreType.DMA((2, 2, 3)),
        ],
        operands + outs_in,
        in_specs=[WHOLE] * len(operands) + [IN_HBM] * 3,
        out_specs=(IN_HBM,) * 3,
        flops=2 * work,
        limit=24,
        aliases={len(operands) + n: n for n in range(3)},
    )


def solution(mesh):
    spec = P(None, ("parts", "il"), "xl")
    return jax.shard_map(body, mesh=mesh, in_specs=(spec,), out_specs=(spec,) * 3, check_vma=False)
```

```python
import jax
import jax.numpy as jnp
import ml_dtypes
import numpy as np
from jax import lax
from jax.experimental import pallas as pl
from jax.experimental.pallas import tpu as pltpu
from jax.sharding import PartitionSpec as P

RADIUS = 9
REACH = RADIUS + 1
SIDE = 16
SLOTS = 8
TILES = 3
EDGE = 16
OWN = 2
TINY = float(np.finfo(np.float32).tiny)
HEAD = 3
AHEAD = 3
LATER = 6
FAR = -1000
WHOLE = pl.BlockSpec(memory_space=pltpu.VMEM)
IN_HBM = pl.BlockSpec(memory_space=pltpu.HBM)
ANYWHERE = pl.BlockSpec(memory_space=pl.ANY)


def filter_taps():
    offsets = np.arange(2 * RADIUS + 1).astype(np.float32)
    sigma = np.float32(RADIUS / 3.0)
    shape = np.exp(np.float32(-0.5) * ((offsets - RADIUS) / sigma) ** 2)
    return (shape / np.sum(shape, dtype=np.float32)).astype(ml_dtypes.bfloat16).astype(np.float32)


def iota(shape, dim):
    return lax.broadcasted_iota(jnp.int32, shape, dim)


def band(source, target, scale=1.0):
    offset = jnp.abs(source - target)
    weights = jnp.zeros(offset.shape, jnp.float32)
    for distance, tap in enumerate(filter_taps()[RADIUS:]):
        weights = jnp.where(offset == distance, jnp.float32(scale * tap), weights)
    return weights


def difference(source, target):
    offset = source - target
    return jnp.where(offset == 1, 1.0, jnp.where(offset == -1, -1.0, 0.0)).astype(jnp.float32)


def dot(left, right):
    return jnp.dot(left, right, preferred_element_type=jnp.float32)


def halo_plane(lane, tile, depths):
    slot = lax.div(lane, SIDE)
    rest = jnp.where(slot == 0, 0, jnp.where(slot == 1, depths - 1, FAR))
    return jnp.where(tile < 2, 1 + SLOTS * tile + slot, rest)


def halo_column(lane, x, cols):
    place = lax.rem(lane, SIDE)
    return jnp.where(x == 0, cols - OWN + place, place - (SIDE - OWN))


def low_end(exchange):
    even = lax.rem(lax.axis_index("il"), 2) == 0
    return jnp.logical_not(even) if exchange == 0 else even


def tables_kernel(depths, lines_ref, diff_i_ref, smooth_ref, pack_h_ref, diff_h_ref, lines_e_ref, diff_e_ref, pick_ref, mask_ref):
    rows, cols = lines_ref.shape[0], smooth_ref.shape[0]
    x, il, last = lax.axis_index("xl"), lax.axis_index("il"), lax.axis_size("il") - 1
    bf16 = jnp.bfloat16

    target, source = iota((rows, rows), 0), iota((rows, rows), 1)
    inner = (source > 0) & (source < rows - 1)
    lines_ref[...] = jnp.where(inner, band(source, target, 0.25), 0.0).astype(bf16)
    diff_i_ref[...] = difference(source, target).astype(bf16)
    span = EDGE * SLOTS
    target, source = iota((span, span), 0), iota((span, span), 1)
    depth = lax.div(source, EDGE) == lax.div(target, EDGE)
    target, source = lax.rem(target, EDGE), lax.rem(source, EDGE)
    diff_e_ref[...] = difference(source, target)[:EDGE, :EDGE].astype(bf16)
    for exchange in range(2):
        low = low_end(exchange)
        source_at = jnp.where(low, source - REACH, rows - (EDGE - REACH) + source)
        target_at = jnp.where(low, target, rows - EDGE + target)
        first = jnp.where(low & (il > 0), -rows, 0)
        final = jnp.where(jnp.logical_not(low) & (il < last), 2 * rows, rows - 1)
        use = depth & (source_at >= first) & (source_at <= final) & ((source_at <= 0) | (source_at >= rows - 1))
        lines_e_ref[exchange] = jnp.where(use, band(source_at, target_at, 0.25), 0.0).astype(bf16)

    source, target = iota((cols, cols), 0), iota((cols, cols), 1)
    moved = source == jnp.where(x == 0, cols - 1, 0)
    column = lax.rem(target + 128 * x, cols)
    smooth_ref[...] = jnp.where(moved, 0.0, band(source, column)).astype(bf16)
    source, target = iota((256, 256), 0), iota((256, 256), 1)
    place = lax.rem(source, SIDE)
    use = (lax.div(source, SIDE) == lax.div(target, SIDE)) & (place != jnp.where(x == 0, 0, SIDE - 1))
    column = jnp.where(x == 0, cols - SIDE, 0) + lax.rem(target, SIDE)
    pack_h_ref[...] = jnp.where(use, band(halo_column(place, x, cols), column), 0.0).astype(bf16)

    source, target = iota((128, 128), 0), iota((128, 128), 1)
    same = lax.rem(source, SIDE) == lax.rem(target, SIDE)
    across = difference(lax.rem(source, SIDE), lax.rem(target, SIDE))
    for group in range(2):
        centre = halo_plane(target, group, depths)
        for tile in range(TILES):
            plane = halo_plane(source, tile, depths)
            part, out = slice(128 * tile, 128 * (tile + 1)), 128 * group
            diff_h_ref[part, out : out + 128] = jnp.where(same, difference(plane, centre), 0.0).astype(bf16)
            diff_h_ref[part, 256 + out : 384 + out] = jnp.where(plane == centre, across, 0.0).astype(bf16)

    source, lane = iota((128, 256), 0), iota((128, 256), 1)
    place = lax.rem(lane, SIDE)
    low, high = place < SIDE - OWN, place >= OWN
    sent = jnp.where(x == 0, jnp.where(low, 128 - (SIDE - OWN) + place, FAR), jnp.where(high, place - OWN, FAR))
    low, high = place < OWN, place >= SIDE - OWN
    kept = jnp.where(x == 0, jnp.where(low, 128 - OWN + place, FAR), jnp.where(high, place - (SIDE - OWN), FAR))
    pick = jnp.where(source == jnp.where(lane < 128, sent, kept), 1.0, 0.0)
    slot = lax.div(lax.rem(lane, 128), SIDE)
    for index in range(SLOTS):
        pick_ref[128 * index : 128 * (index + 1)] = jnp.where(slot == index, pick, 0.0).astype(bf16)
    lane = iota((8, 128), 1)
    border = jnp.where(x == 0, lane - (128 - SIDE), lane)
    mask_ref[0] = jnp.where((border >= 0) & (border < SIDE), 1.0, 0.0)
    mask_ref[1] = jnp.where(lane > 0, 1.0, 0.0)
    mask_ref[2] = jnp.where(lane < 127, 1.0, 0.0)


def pack_kernel(vol_ref, pick_ref, copy_ref, send_ref, own_ref):
    depths, rows, cols = vol_ref.shape
    edge = pl.ds(pl.multiple_of((cols - 128) * (1 - lax.axis_index("xl")), 128), 128)
    copy_ref[...] = vol_ref[...]
    for tile in range(TILES):
        planes = (0, depths - 1) if tile == 2 else range(1 + SLOTS * tile, 1 + SLOTS * (tile + 1))
        beside = jnp.concatenate([vol_ref[plane, :, edge] for plane in planes], axis=1)
        packed = dot(beside, pick_ref[: beside.shape[1]]).astype(jnp.bfloat16)
        send_ref[tile] = packed[:, :128]
        own_ref[tile] = packed[:, 128:]


def rows_kernel(vol_ref, own_ref, side_ref, after_ref, halo_ref, near_ref, far_ref, packed_ref):
    depths, rows, cols = vol_ref.shape
    even = lax.rem(lax.axis_index("il"), 2) == 0

    def put(row, top, bottom):
        top, bottom = top[:REACH], bottom[EDGE - REACH :]
        lanes = top.shape[1]
        packed_ref[0, row : row + REACH, :lanes] = jnp.where(even, bottom, top)
        packed_ref[1, row : row + REACH, :lanes] = jnp.where(even, top, bottom)

    packed_ref[:, depths * REACH :, :] = jnp.zeros_like(packed_ref[:, depths * REACH :, :])
    for depth in range(depths):
        top = vol_ref[depth, :EDGE, :].astype(jnp.float32)
        bottom = vol_ref[depth, rows - EDGE :, :].astype(jnp.float32)
        put(REACH * depth, top, bottom)
    tiles = []
    for tile in range(TILES):
        merged = own_ref[tile].astype(jnp.float32) + side_ref[tile].astype(jnp.float32)
        halo_ref[:, 128 * tile : 128 * (tile + 1)] = merged.astype(jnp.bfloat16)
        tiles.append((merged[:EDGE], merged[rows - EDGE :]))
    tops = jnp.concatenate([tiles[0][0], tiles[1][0]], axis=1)
    bottoms = jnp.concatenate([tiles[0][1], tiles[1][1]], axis=1)
    put(REACH * depths, tops, bottoms)
    put(REACH * (depths + 1), *tiles[2])
    near_ref[...] = packed_ref[0].astype(jnp.bfloat16)
    far_ref[...] = packed_ref[1].astype(jnp.bfloat16)


def moments(grad_i, grad_x, grad_z):
    terms = (
        grad_i * grad_i,
        grad_x * grad_x,
        grad_z * grad_z,
        grad_i * grad_x,
        grad_i * grad_z,
        grad_x * grad_z,
    )
    return [term.astype(jnp.bfloat16) for term in terms]


def store_chunks(summed, comp, inner_ref, part_ref):
    chunks = summed.shape[0] // EDGE
    for chunk in range(1, chunks - 1):
        inner_ref[chunk - 1, comp] = summed[EDGE * chunk : EDGE * (chunk + 1)].astype(jnp.bfloat16)
    part_ref[0, comp] = summed[:EDGE]
    part_ref[1, comp] = summed[EDGE * (chunks - 1) :]


def gradients(before, centre, after, mask_ref):
    rows, cols = centre.shape
    left, right = pltpu.roll(centre, 1, 1), pltpu.roll(centre, cols - 1, 1)
    left_0 = (left[:, :128].reshape(-1, 8, 128) * mask_ref[1]).reshape(rows, 128)
    right_1 = (right[:, cols - 128 :].reshape(-1, 8, 128) * mask_ref[2]).reshape(rows, 128)
    grad_x = jnp.concatenate([right[:, : cols - 128] - left_0, right_1 - left[:, 128:]], axis=1)
    return pltpu.roll(centre, rows - 1, 0) - pltpu.roll(centre, 1, 0), grad_x, after - before


def make_moments(pair, vol_ref, mask_ref, moments_ref):
    planes = [vol_ref[2 * pair + k].astype(jnp.float32) for k in range(4)]
    for k in range(2):
        for comp, term in enumerate(moments(*gradients(*planes[k : k + 3], mask_ref))):
            moments_ref[k, comp] = term


def make_lines(z, comp, lines_ref, moments_ref, inner_ref, part_ref):
    store_chunks(dot(lines_ref[...], moments_ref[z % 2, comp]), comp, inner_ref.at[z], part_ref.at[:, :, z])


def lines_kernel(vol_ref, lines_ref, mask_ref, inner_ref, part_ref, even_ref, odd_ref):
    slots = (even_ref, odd_ref)
    for pair in range(HEAD):
        make_moments(pair, vol_ref, mask_ref, slots[pair % 2])
        for k in range(2):
            for comp in range(6):
                make_lines(2 * pair + k, comp, lines_ref, slots[pair % 2], inner_ref, part_ref)


def tensor_of(own, smooth_ref, tensor_ref):
    tensor_ref[...] = dot(own.reshape(-1, own.shape[-1]), smooth_ref[...])


def attributes(tensor, border, store):
    x = lax.axis_index("xl")
    halves = (tensor[:, :128], tensor[:, 128:] + border)
    lanes = (pl.multiple_of(128 * x, 128), pl.multiple_of(128 - 128 * x, 128))
    for half, lane in zip(halves, lanes):
        a, b, c, d, e, f = [half[EDGE * comp : EDGE * (comp + 1)] for comp in range(6)]
        low = -1e-6 - c
        inverse = pl.reciprocal(low, approx=True)
        spread = (a - b) * (a - c) + (b - c) * (b - c) + 3.0 * (d * d + e * e + f * f)
        root = spread * lax.rsqrt(jnp.maximum(spread, TINY))
        store(pl.ds(lane, 128), (e * inverse, f * inverse, root * pl.reciprocal(a + b - low, approx=True)))


def border_of(packed, slot, mask_ref):
    base = jnp.where(lax.axis_index("xl") == 0, 128 - SIDE, 0)
    moved = pltpu.roll(packed, lax.rem(base - SIDE * slot + 128, 128), 1)
    return (moved.reshape(-1, 8, 128) * mask_ref[0]).reshape(packed.shape)


def own_kernel(
    vol_ref, lines_ref, diff_i_ref, smooth_ref, halo_ref, diff_h_ref, pack_h_ref, mask_ref, inner_in_ref, part_in_ref,
    part_ref, dip_i_ref, dip_x_ref, plan_ref, later_ref, part_h_ref,
    inner_ref, border_ref, even_ref, odd_ref, tensor_ref, out_ref, sems,
):
    count, chunks = inner_ref.shape[:2]
    inner = EDGE * chunks
    slots = (even_ref, odd_ref)
    targets = (dip_i_ref, dip_x_ref, plan_ref)
    inner_ref[: 2 * HEAD] = inner_in_ref[...]

    both = dot(halo_ref[...], diff_h_ref[...])
    grad_i = dot(diff_i_ref[...], halo_ref[:, :256])
    lined_h = [[] for chunk in range(chunks)]
    for comp, term in enumerate(moments(grad_i, both[:, 256:], both[:, :256])):
        summed = dot(lines_ref[...], term)
        for chunk, parts in enumerate(lined_h):
            parts.append(summed[EDGE * (chunk + 1) : EDGE * (chunk + 2)].astype(jnp.bfloat16))
        part_h_ref[0, comp] = summed[:EDGE]
        part_h_ref[1, comp] = summed[EDGE * (chunks + 1) :]
    border_ref[...] = dot(jnp.concatenate(sum(lined_h, []), axis=0), pack_h_ref[...])

    copies = []
    tensor_of(inner_ref[0], smooth_ref, tensor_ref.at[0])
    for z in range(count):
        later = z + 2 * HEAD if z + 2 * HEAD < count else None
        if later is not None and later % 2 == 0:
            make_moments(later // 2, vol_ref, mask_ref, slots[later // 2 % 2])
        if z < count - 1:
            tensor_of(inner_ref[z + 1], smooth_ref, tensor_ref.at[(z + 1) % 2])
        group = 128 * (z // SLOTS)
        for chunk in range(chunks):
            rows = slice(EDGE * chunk, EDGE * (chunk + 1))
            part = slice(6 * EDGE * chunk, 6 * EDGE * (chunk + 1))

            def store(lanes, values):
                for n, value in enumerate(values):
                    if z >= count - LATER:
                        later_ref[n, z - (count - LATER), rows, lanes] = value
                    else:
                        out_ref[n, z, rows, lanes] = value

            border = border_of(border_ref[part, group : group + 128], z % SLOTS, mask_ref)
            attributes(tensor_ref[z % 2, part], border, store)
            if later is not None:
                make_lines(later, chunk, lines_ref, slots[later // 2 % 2], inner_ref, part_ref)
        if z % 2 == 1 and z < count - LATER:
            depth = pl.ds(z - 1, 2)
            for n, target in enumerate(targets):
                place = target.at[depth, pl.ds(EDGE, inner)]
                copies.append(pltpu.make_async_copy(out_ref.at[n, depth], place, sems.at[z // 2, n]))
                copies[-1].start()
    for copy in copies:
        copy.wait()


def ends_kernel(
    done_ref, vol_ref, halo_ref, near_ref, far_ref, part_ref, part_h_ref,
    smooth_ref, pack_h_ref, diff_h_ref, lines_e_ref, diff_e_ref, mask_ref, in_i_ref, in_x_ref, in_p_ref,
    dip_i_ref, dip_x_ref, plan_ref,
    packed_ref, block_ref, block_h_ref, border_ref, edge_ref, out_ref, done_sems, sems,
):
    depths, rows, cols = vol_ref.shape
    count, half = depths - 2, (depths - 2) // 2
    bf16, f32 = jnp.bfloat16, jnp.float32
    span = EDGE * half
    targets = (dip_i_ref, dip_x_ref, plan_ref)
    copies = []
    for n, target in enumerate(targets):
        place = target.at[pl.ds(count - LATER, LATER), pl.ds(EDGE, rows - 2 * EDGE)]
        copies.append(pltpu.make_async_copy(done_ref.at[n], place, done_sems.at[n]))
        copies[-1].start()
    lows = [low_end(exchange) for exchange in range(2)]
    ends = [jnp.where(low, 0, 1) for low in lows]
    starts = [pl.multiple_of(jnp.where(low, 0, rows - EDGE), EDGE) for low in lows]

    def prepare(exchange, rows_ref):
        low, start, end = lows[exchange], starts[exchange], ends[exchange]
        rows_in = rows_ref[...].astype(f32)
        if exchange == 1:
            il = lax.axis_index("il")
            outside = (low & (il == 0)) | (jnp.logical_not(low) & (il == lax.axis_size("il") - 1))
            rows_in = jnp.where(outside, 0.0, rows_in)
        packed_ref[exchange] = pltpu.roll(rows_in, jnp.where(low, 0, EDGE - REACH), 0)
        place = iota((EDGE, cols), 0)
        received = jnp.where(low, place, EDGE - 1 - place) < REACH

        def joined(row, own):
            lanes = own.shape[1]
            own = pltpu.roll(own.astype(f32), jnp.where(low, REACH, EDGE - REACH), 0)
            return jnp.where(received[:, :lanes], packed_ref[exchange, row : row + EDGE, :lanes], own).astype(bf16)

        for depth in range(depths):
            block_ref[exchange, depth] = joined(REACH * depth, vol_ref[depth, pl.ds(start, EDGE)])
        own_h = halo_ref[pl.ds(start, EDGE)]
        block_h_ref[exchange, :, :256] = joined(REACH * depths, own_h[:, :256])
        block_h_ref[exchange, :, 256:] = joined(REACH * (depths + 1), own_h[:, 256:])

        both = dot(block_h_ref[exchange], diff_h_ref[...])
        grad_i = dot(diff_e_ref[...], block_h_ref[exchange, :, :256])
        lined_h = []
        for comp, term in enumerate(moments(grad_i, both[:, 256:], both[:, :256])):
            summed = part_h_ref[end, comp] + dot(lines_e_ref[exchange, :EDGE, :EDGE], term)
            lined_h.append(summed.astype(bf16))
        border_ref[exchange] = dot(jnp.concatenate(lined_h, axis=0), pack_h_ref[...])

    def make_edges(exchange, group):
        first = half * group
        planes = [block_ref[exchange, first + k : first + half + k].astype(f32).reshape(span, cols) for k in range(3)]
        for comp, term in enumerate(moments(*gradients(*planes, mask_ref))):
            outer = dot(lines_e_ref[exchange], term)
            summed = part_ref[ends[exchange], comp, first : first + half] + outer.reshape(half, EDGE, cols)
            edge_ref[exchange, first : first + half, comp] = summed.astype(bf16)

    def finish(exchange, group):
        first = half * group
        own = edge_ref[exchange, first : first + half].reshape(6 * span, cols)
        tensor = dot(own, smooth_ref[...])
        for k in range(half):

            def store(lanes, values):
                for n, value in enumerate(values):
                    out_ref[exchange, n, first + k, :, lanes] = value

            border = border_of(border_ref[exchange, :, 128 * group : 128 * (group + 1)], k, mask_ref)
            attributes(tensor[6 * EDGE * k : 6 * EDGE * (k + 1)], border, store)
        depth = pl.ds(first, half)
        for n, target in enumerate(targets):
            place = target.at[depth, pl.ds(starts[exchange], EDGE)]
            copies.append(pltpu.make_async_copy(out_ref.at[exchange, n, depth], place, sems.at[exchange, group, n]))
            copies[-1].start()

    for exchange, rows_ref in enumerate((near_ref, far_ref)):
        prepare(exchange, rows_ref)
    for exchange in range(2):
        for group in range(2):
            make_edges(exchange, group)
    for exchange in range(2):
        for group in range(2):
            finish(exchange, group)
    for copy in copies:
        copy.wait()


def call(name, kernel, outs, scratch, operands, in_specs=None, out_specs=None, flops=0, limit=16, aliases={}):
    return pl.pallas_call(
        kernel,
        out_shape=tuple(jax.ShapeDtypeStruct(*out) for out in outs),
        in_specs=in_specs or [WHOLE] * len(operands),
        out_specs=out_specs or (WHOLE,) * len(outs),
        scratch_shapes=scratch,
        compiler_params=pltpu.CompilerParams(vmem_limit_bytes=limit << 20),
        name=name,
        input_output_aliases=aliases,
        cost_estimate=pl.CostEstimate(flops=flops, bytes_accessed=0, transcendentals=0),
    )(*operands)


def body(volume):
    depths, rows, cols = volume.shape
    il, xl = lax.axis_size("il"), lax.axis_size("xl")
    count = depths - 2
    assert xl == 2 and il % 2 == 0 and count == 2 * SLOTS and rows == 128 and cols == 256
    bf16, f32 = jnp.bfloat16, jnp.float32
    half = count // 2
    work = half * 1024 * 2 * 256 * 256
    packed_rows = -(-REACH * (depths + 2) // 16) * 16

    span = EDGE * SLOTS
    lines, diff_i, smooth, pack_h, diff_h, lines_e, diff_e, pick, mask = call(
        "tables_kernel",
        lambda *refs: tables_kernel(depths, *refs),
        [
            ((rows, rows), bf16),
            ((rows, rows), bf16),
            ((cols, cols), bf16),
            ((256, 256), bf16),
            ((128 * TILES, 512), bf16),
            ((2, span, span), bf16),
            ((EDGE, EDGE), bf16),
            ((128 * SLOTS, 256), bf16),
            ((3, 8, 128), f32),
        ],
        [],
        [],
        flops=work,
    )
    halo_tile = ((TILES, rows, 128), bf16)
    vol, send, own = call("pack_kernel", pack_kernel, [(volume.shape, bf16), halo_tile, halo_tile], [], [volume, pick])
    side = lax.ppermute(send, "xl", [(0, 1), (1, 0)])
    chunks = rows // EDGE - 2
    moment_slots = [pltpu.VMEM((2, 6, rows, cols), bf16)] * 2
    partial = ((2, 6, count, EDGE, cols), f32)
    inner, part = call(
        "lines_kernel",
        lines_kernel,
        [((2 * HEAD, chunks, 6, EDGE, cols), bf16), partial],
        moment_slots,
        [vol, lines, mask],
        flops=work // 4,
    )
    packed = ((packed_rows, cols), bf16)
    halo, near, far = call(
        "rows_kernel",
        rows_kernel,
        [((rows, 128 * TILES), bf16), packed, packed],
        [pltpu.VMEM((2, packed_rows, cols), f32)],
        [vol, own, side, part],
        in_specs=[WHOLE] * 3 + [ANYWHERE],
    )
    near_in = lax.ppermute(near, "il", [(i, i ^ 1) for i in range(il)])
    pairs = [(i, i + 1) for i in range(1, il - 1, 2)]
    far_in = lax.ppermute(far, "il", pairs + [(j, i) for i, j in pairs] + [(0, 0), (il - 1, il - 1)])

    outs = [((count, rows, cols), f32)] * 3
    operands = [vol, lines, diff_i, smooth, halo, diff_h, pack_h, mask, inner, part]
    part, *outs_in, done, part_h = call(
        "own_kernel",
        own_kernel,
        [partial, *outs, ((3, LATER, EDGE * chunks, cols), f32), ((2, 6, EDGE, 256), f32)],
        [
            pltpu.VMEM((count, chunks, 6, EDGE, cols), bf16),
            pltpu.VMEM((6 * EDGE * chunks, 256), f32),
            *moment_slots,
            pltpu.VMEM((2, 6 * EDGE * chunks, cols), f32),
            pltpu.VMEM((3, count - LATER, EDGE * chunks, cols), f32),
            pltpu.SemaphoreType.DMA(((count - LATER) // 2, 3)),
        ],
        operands,
        out_specs=(WHOLE,) + (IN_HBM,) * 3 + (WHOLE,) * 2,
        flops=5 * work,
        limit=24,
        aliases={len(operands) - 1: 0},
    )

    operands = [done, vol, halo, near_in, far_in, part, part_h, smooth, pack_h, diff_h, lines_e, diff_e, mask]
    return call(
        "ends_kernel",
        ends_kernel,
        outs,
        [
            pltpu.VMEM((2, packed_rows, cols), f32),
            pltpu.VMEM((2, depths, EDGE, cols), bf16),
            pltpu.VMEM((2, EDGE, 128 * TILES), bf16),
            pltpu.VMEM((2, 6 * EDGE, 256), f32),
            pltpu.VMEM((2, count, 6, EDGE, cols), bf16),
            pltpu.VMEM((2, 3, count, EDGE, cols), f32),
            pltpu.SemaphoreType.DMA((3,)),
            pltpu.SemaphoreType.DMA((2, 2, 3)),
        ],
        operands + outs_in,
        in_specs=[WHOLE] * len(operands) + [IN_HBM] * 3,
        out_specs=(IN_HBM,) * 3,
        flops=2 * work,
        limit=24,
        aliases={len(operands) + n: n for n in range(3)},
    )


def solution(mesh):
    spec = P(None, ("parts", "il"), "xl")
    return jax.shard_map(body, mesh=mesh, in_specs=(spec,), out_specs=(spec,) * 3, check_vma=False)
```

```python
import jax
import jax.numpy as jnp
import ml_dtypes
import numpy as np
from jax import lax
from jax.experimental import pallas as pl
from jax.experimental.pallas import tpu as pltpu
from jax.sharding import PartitionSpec as P

RADIUS = 9
REACH = RADIUS + 1
SIDE = 16
SLOTS = 8
TILES = 3
EDGE = 16
OWN = 2
TINY = float(np.finfo(np.float32).tiny)
HEAD = 3
AHEAD = 3
LATER = 8
FAR = -1000
WHOLE = pl.BlockSpec(memory_space=pltpu.VMEM)
IN_HBM = pl.BlockSpec(memory_space=pltpu.HBM)
ANYWHERE = pl.BlockSpec(memory_space=pl.ANY)


def filter_taps():
    offsets = np.arange(2 * RADIUS + 1).astype(np.float32)
    sigma = np.float32(RADIUS / 3.0)
    shape = np.exp(np.float32(-0.5) * ((offsets - RADIUS) / sigma) ** 2)
    return (shape / np.sum(shape, dtype=np.float32)).astype(ml_dtypes.bfloat16).astype(np.float32)


def iota(shape, dim):
    return lax.broadcasted_iota(jnp.int32, shape, dim)


def band(source, target, scale=1.0):
    offset = jnp.abs(source - target)
    weights = jnp.zeros(offset.shape, jnp.float32)
    for distance, tap in enumerate(filter_taps()[RADIUS:]):
        weights = jnp.where(offset == distance, jnp.float32(scale * tap), weights)
    return weights


def difference(source, target):
    offset = source - target
    return jnp.where(offset == 1, 1.0, jnp.where(offset == -1, -1.0, 0.0)).astype(jnp.float32)


def dot(left, right):
    return jnp.dot(left, right, preferred_element_type=jnp.float32)


def halo_plane(lane, tile, depths):
    slot = lax.div(lane, SIDE)
    rest = jnp.where(slot == 0, 0, jnp.where(slot == 1, depths - 1, FAR))
    return jnp.where(tile < 2, 1 + SLOTS * tile + slot, rest)


def halo_column(lane, x, cols):
    place = lax.rem(lane, SIDE)
    return jnp.where(x == 0, cols - OWN + place, place - (SIDE - OWN))


def low_end(exchange):
    even = lax.rem(lax.axis_index("il"), 2) == 0
    return jnp.logical_not(even) if exchange == 0 else even


def tables_kernel(depths, lines_ref, diff_i_ref, smooth_ref, pack_h_ref, diff_h_ref, lines_e_ref, diff_e_ref, pick_ref, mask_ref):
    rows, cols = lines_ref.shape[0], smooth_ref.shape[0]
    x, il, last = lax.axis_index("xl"), lax.axis_index("il"), lax.axis_size("il") - 1
    bf16 = jnp.bfloat16

    target, source = iota((rows, rows), 0), iota((rows, rows), 1)
    inner = (source > 0) & (source < rows - 1)
    lines_ref[...] = jnp.where(inner, band(source, target, 0.25), 0.0).astype(bf16)
    diff_i_ref[...] = difference(source, target).astype(bf16)
    span = EDGE * SLOTS
    target, source = iota((span, span), 0), iota((span, span), 1)
    depth = lax.div(source, EDGE) == lax.div(target, EDGE)
    target, source = lax.rem(target, EDGE), lax.rem(source, EDGE)
    diff_e_ref[...] = difference(source, target)[:EDGE, :EDGE].astype(bf16)
    for exchange in range(2):
        low = low_end(exchange)
        source_at = jnp.where(low, source - REACH, rows - (EDGE - REACH) + source)
        target_at = jnp.where(low, target, rows - EDGE + target)
        first = jnp.where(low & (il > 0), -rows, 0)
        final = jnp.where(jnp.logical_not(low) & (il < last), 2 * rows, rows - 1)
        use = depth & (source_at >= first) & (source_at <= final) & ((source_at <= 0) | (source_at >= rows - 1))
        lines_e_ref[exchange] = jnp.where(use, band(source_at, target_at, 0.25), 0.0).astype(bf16)

    source, target = iota((cols, cols), 0), iota((cols, cols), 1)
    moved = source == jnp.where(x == 0, cols - 1, 0)
    column = lax.rem(target + 128 * x, cols)
    smooth_ref[...] = jnp.where(moved, 0.0, band(source, column)).astype(bf16)
    source, target = iota((256, 256), 0), iota((256, 256), 1)
    place = lax.rem(source, SIDE)
    use = (lax.div(source, SIDE) == lax.div(target, SIDE)) & (place != jnp.where(x == 0, 0, SIDE - 1))
    column = jnp.where(x == 0, cols - SIDE, 0) + lax.rem(target, SIDE)
    pack_h_ref[...] = jnp.where(use, band(halo_column(place, x, cols), column), 0.0).astype(bf16)

    source, target = iota((128, 128), 0), iota((128, 128), 1)
    same = lax.rem(source, SIDE) == lax.rem(target, SIDE)
    across = difference(lax.rem(source, SIDE), lax.rem(target, SIDE))
    for group in range(2):
        centre = halo_plane(target, group, depths)
        for tile in range(TILES):
            plane = halo_plane(source, tile, depths)
            part, out = slice(128 * tile, 128 * (tile + 1)), 128 * group
            diff_h_ref[part, out : out + 128] = jnp.where(same, difference(plane, centre), 0.0).astype(bf16)
            diff_h_ref[part, 256 + out : 384 + out] = jnp.where(plane == centre, across, 0.0).astype(bf16)

    source, lane = iota((128, 256), 0), iota((128, 256), 1)
    place = lax.rem(lane, SIDE)
    low, high = place < SIDE - OWN, place >= OWN
    sent = jnp.where(x == 0, jnp.where(low, 128 - (SIDE - OWN) + place, FAR), jnp.where(high, place - OWN, FAR))
    low, high = place < OWN, place >= SIDE - OWN
    kept = jnp.where(x == 0, jnp.where(low, 128 - OWN + place, FAR), jnp.where(high, place - (SIDE - OWN), FAR))
    pick = jnp.where(source == jnp.where(lane < 128, sent, kept), 1.0, 0.0)
    slot = lax.div(lax.rem(lane, 128), SIDE)
    for index in range(SLOTS):
        pick_ref[128 * index : 128 * (index + 1)] = jnp.where(slot == index, pick, 0.0).astype(bf16)
    lane = iota((8, 128), 1)
    border = jnp.where(x == 0, lane - (128 - SIDE), lane)
    mask_ref[0] = jnp.where((border >= 0) & (border < SIDE), 1.0, 0.0)
    mask_ref[1] = jnp.where(lane > 0, 1.0, 0.0)
    mask_ref[2] = jnp.where(lane < 127, 1.0, 0.0)


def pack_kernel(vol_ref, pick_ref, copy_ref, send_ref, own_ref):
    depths, rows, cols = vol_ref.shape
    edge = pl.ds(pl.multiple_of((cols - 128) * (1 - lax.axis_index("xl")), 128), 128)
    copy_ref[...] = vol_ref[...]
    for tile in range(TILES):
        planes = (0, depths - 1) if tile == 2 else range(1 + SLOTS * tile, 1 + SLOTS * (tile + 1))
        beside = jnp.concatenate([vol_ref[plane, :, edge] for plane in planes], axis=1)
        packed = dot(beside, pick_ref[: beside.shape[1]]).astype(jnp.bfloat16)
        send_ref[tile] = packed[:, :128]
        own_ref[tile] = packed[:, 128:]


def rows_kernel(vol_ref, own_ref, side_ref, after_ref, halo_ref, near_ref, far_ref, packed_ref):
    depths, rows, cols = vol_ref.shape
    even = lax.rem(lax.axis_index("il"), 2) == 0

    def put(row, top, bottom):
        top, bottom = top[:REACH], bottom[EDGE - REACH :]
        lanes = top.shape[1]
        packed_ref[0, row : row + REACH, :lanes] = jnp.where(even, bottom, top)
        packed_ref[1, row : row + REACH, :lanes] = jnp.where(even, top, bottom)

    packed_ref[:, depths * REACH :, :] = jnp.zeros_like(packed_ref[:, depths * REACH :, :])
    for depth in range(depths):
        top = vol_ref[depth, :EDGE, :].astype(jnp.float32)
        bottom = vol_ref[depth, rows - EDGE :, :].astype(jnp.float32)
        put(REACH * depth, top, bottom)
    tiles = []
    for tile in range(TILES):
        merged = own_ref[tile].astype(jnp.float32) + side_ref[tile].astype(jnp.float32)
        halo_ref[:, 128 * tile : 128 * (tile + 1)] = merged.astype(jnp.bfloat16)
        tiles.append((merged[:EDGE], merged[rows - EDGE :]))
    tops = jnp.concatenate([tiles[0][0], tiles[1][0]], axis=1)
    bottoms = jnp.concatenate([tiles[0][1], tiles[1][1]], axis=1)
    put(REACH * depths, tops, bottoms)
    put(REACH * (depths + 1), *tiles[2])
    near_ref[...] = packed_ref[0].astype(jnp.bfloat16)
    far_ref[...] = packed_ref[1].astype(jnp.bfloat16)


def moments(grad_i, grad_x, grad_z):
    terms = (
        grad_i * grad_i,
        grad_x * grad_x,
        grad_z * grad_z,
        grad_i * grad_x,
        grad_i * grad_z,
        grad_x * grad_z,
    )
    return [term.astype(jnp.bfloat16) for term in terms]


def store_chunks(summed, comp, inner_ref, part_ref):
    chunks = summed.shape[0] // EDGE
    for chunk in range(1, chunks - 1):
        inner_ref[chunk - 1, comp] = summed[EDGE * chunk : EDGE * (chunk + 1)].astype(jnp.bfloat16)
    part_ref[0, comp] = summed[:EDGE]
    part_ref[1, comp] = summed[EDGE * (chunks - 1) :]


def gradients(before, centre, after, mask_ref):
    rows, cols = centre.shape
    left, right = pltpu.roll(centre, 1, 1), pltpu.roll(centre, cols - 1, 1)
    left_0 = (left[:, :128].reshape(-1, 8, 128) * mask_ref[1]).reshape(rows, 128)
    right_1 = (right[:, cols - 128 :].reshape(-1, 8, 128) * mask_ref[2]).reshape(rows, 128)
    grad_x = jnp.concatenate([right[:, : cols - 128] - left_0, right_1 - left[:, 128:]], axis=1)
    return pltpu.roll(centre, rows - 1, 0) - pltpu.roll(centre, 1, 0), grad_x, after - before


def make_moments(pair, vol_ref, mask_ref, moments_ref):
    planes = [vol_ref[2 * pair + k].astype(jnp.float32) for k in range(4)]
    for k in range(2):
        for comp, term in enumerate(moments(*gradients(*planes[k : k + 3], mask_ref))):
            moments_ref[k, comp] = term


def make_lines(z, comp, lines_ref, moments_ref, inner_ref, part_ref):
    store_chunks(dot(lines_ref[...], moments_ref[z % 2, comp]), comp, inner_ref.at[z], part_ref.at[:, :, z])


def lines_kernel(vol_ref, lines_ref, mask_ref, inner_ref, part_ref, even_ref, odd_ref):
    slots = (even_ref, odd_ref)
    for pair in range(HEAD):
        make_moments(pair, vol_ref, mask_ref, slots[pair % 2])
        for k in range(2):
            for comp in range(6):
                make_lines(2 * pair + k, comp, lines_ref, slots[pair % 2], inner_ref, part_ref)


def tensor_of(own, smooth_ref, tensor_ref):
    tensor_ref[...] = dot(own.reshape(-1, own.shape[-1]), smooth_ref[...])


def attributes(tensor, border, store):
    x = lax.axis_index("xl")
    halves = (tensor[:, :128], tensor[:, 128:] + border)
    lanes = (pl.multiple_of(128 * x, 128), pl.multiple_of(128 - 128 * x, 128))
    for half, lane in zip(halves, lanes):
        a, b, c, d, e, f = [half[EDGE * comp : EDGE * (comp + 1)] for comp in range(6)]
        low = -1e-6 - c
        inverse = pl.reciprocal(low, approx=True)
        spread = (a - b) * (a - c) + (b - c) * (b - c) + 3.0 * (d * d + e * e + f * f)
        root = spread * lax.rsqrt(jnp.maximum(spread, TINY))
        store(pl.ds(lane, 128), (e * inverse, f * inverse, root * pl.reciprocal(a + b - low, approx=True)))


def border_of(packed, slot, mask_ref):
    base = jnp.where(lax.axis_index("xl") == 0, 128 - SIDE, 0)
    moved = pltpu.roll(packed, lax.rem(base - SIDE * slot + 128, 128), 1)
    return (moved.reshape(-1, 8, 128) * mask_ref[0]).reshape(packed.shape)


def own_kernel(
    vol_ref, lines_ref, diff_i_ref, smooth_ref, halo_ref, diff_h_ref, pack_h_ref, mask_ref, inner_in_ref, part_in_ref,
    part_ref, dip_i_ref, dip_x_ref, plan_ref, later_ref, part_h_ref,
    inner_ref, border_ref, even_ref, odd_ref, tensor_ref, out_ref, sems,
):
    count, chunks = inner_ref.shape[:2]
    inner = EDGE * chunks
    slots = (even_ref, odd_ref)
    targets = (dip_i_ref, dip_x_ref, plan_ref)
    inner_ref[: 2 * HEAD] = inner_in_ref[...]

    both = dot(halo_ref[...], diff_h_ref[...])
    grad_i = dot(diff_i_ref[...], halo_ref[:, :256])
    lined_h = [[] for chunk in range(chunks)]
    for comp, term in enumerate(moments(grad_i, both[:, 256:], both[:, :256])):
        summed = dot(lines_ref[...], term)
        for chunk, parts in enumerate(lined_h):
            parts.append(summed[EDGE * (chunk + 1) : EDGE * (chunk + 2)].astype(jnp.bfloat16))
        part_h_ref[0, comp] = summed[:EDGE]
        part_h_ref[1, comp] = summed[EDGE * (chunks + 1) :]
    border_ref[...] = dot(jnp.concatenate(sum(lined_h, []), axis=0), pack_h_ref[...])

    copies = []
    tensor_of(inner_ref[0], smooth_ref, tensor_ref.at[0])
    for z in range(count):
        later = z + 2 * HEAD if z + 2 * HEAD < count else None
        if later is not None and later % 2 == 0:
            make_moments(later // 2, vol_ref, mask_ref, slots[later // 2 % 2])
        if z < count - 1:
            tensor_of(inner_ref[z + 1], smooth_ref, tensor_ref.at[(z + 1) % 2])
        group = 128 * (z // SLOTS)
        for chunk in range(chunks):
            rows = slice(EDGE * chunk, EDGE * (chunk + 1))
            part = slice(6 * EDGE * chunk, 6 * EDGE * (chunk + 1))

            def store(lanes, values):
                for n, value in enumerate(values):
                    if z >= count - LATER:
                        later_ref[n, z - (count - LATER), rows, lanes] = value
                    else:
                        out_ref[n, z, rows, lanes] = value

            border = border_of(border_ref[part, group : group + 128], z % SLOTS, mask_ref)
            attributes(tensor_ref[z % 2, part], border, store)
            if later is not None:
                make_lines(later, chunk, lines_ref, slots[later // 2 % 2], inner_ref, part_ref)
        if z == count - LATER - 1:
            depth = pl.ds(0, count - LATER)
            for n, target in enumerate(targets):
                place = target.at[depth, pl.ds(EDGE, inner)]
                copies.append(pltpu.make_async_copy(out_ref.at[n], place, sems.at[n]))
                copies[-1].start()
    for copy in copies:
        copy.wait()


def ends_kernel(
    done_ref, vol_ref, halo_ref, near_ref, far_ref, part_ref, part_h_ref,
    smooth_ref, pack_h_ref, diff_h_ref, lines_e_ref, diff_e_ref, mask_ref, in_i_ref, in_x_ref, in_p_ref,
    dip_i_ref, dip_x_ref, plan_ref,
    packed_ref, block_ref, block_h_ref, border_ref, edge_ref, out_ref, done_sems, sems,
):
    depths, rows, cols = vol_ref.shape
    count, half = depths - 2, (depths - 2) // 2
    bf16, f32 = jnp.bfloat16, jnp.float32
    span = EDGE * half
    targets = (dip_i_ref, dip_x_ref, plan_ref)
    copies = []
    for n, target in enumerate(targets):
        place = target.at[pl.ds(count - LATER, LATER), pl.ds(EDGE, rows - 2 * EDGE)]
        copies.append(pltpu.make_async_copy(done_ref.at[n], place, done_sems.at[n]))
        copies[-1].start()
    lows = [low_end(exchange) for exchange in range(2)]
    ends = [jnp.where(low, 0, 1) for low in lows]
    starts = [pl.multiple_of(jnp.where(low, 0, rows - EDGE), EDGE) for low in lows]

    def prepare(exchange, rows_ref):
        low, start, end = lows[exchange], starts[exchange], ends[exchange]
        rows_in = rows_ref[...].astype(f32)
        if exchange == 1:
            il = lax.axis_index("il")
            outside = (low & (il == 0)) | (jnp.logical_not(low) & (il == lax.axis_size("il") - 1))
            rows_in = jnp.where(outside, 0.0, rows_in)
        packed_ref[exchange] = pltpu.roll(rows_in, jnp.where(low, 0, EDGE - REACH), 0)
        place = iota((EDGE, cols), 0)
        received = jnp.where(low, place, EDGE - 1 - place) < REACH

        def joined(row, own):
            lanes = own.shape[1]
            own = pltpu.roll(own.astype(f32), jnp.where(low, REACH, EDGE - REACH), 0)
            return jnp.where(received[:, :lanes], packed_ref[exchange, row : row + EDGE, :lanes], own).astype(bf16)

        for depth in range(depths):
            block_ref[exchange, depth] = joined(REACH * depth, vol_ref[depth, pl.ds(start, EDGE)])
        own_h = halo_ref[pl.ds(start, EDGE)]
        block_h_ref[exchange, :, :256] = joined(REACH * depths, own_h[:, :256])
        block_h_ref[exchange, :, 256:] = joined(REACH * (depths + 1), own_h[:, 256:])

        both = dot(block_h_ref[exchange], diff_h_ref[...])
        grad_i = dot(diff_e_ref[...], block_h_ref[exchange, :, :256])
        lined_h = []
        for comp, term in enumerate(moments(grad_i, both[:, 256:], both[:, :256])):
            summed = part_h_ref[end, comp] + dot(lines_e_ref[exchange, :EDGE, :EDGE], term)
            lined_h.append(summed.astype(bf16))
        border_ref[exchange] = dot(jnp.concatenate(lined_h, axis=0), pack_h_ref[...])

    def make_edges(exchange, group):
        first = half * group
        planes = [block_ref[exchange, first + k : first + half + k].astype(f32).reshape(span, cols) for k in range(3)]
        for comp, term in enumerate(moments(*gradients(*planes, mask_ref))):
            outer = dot(lines_e_ref[exchange], term)
            summed = part_ref[ends[exchange], comp, first : first + half] + outer.reshape(half, EDGE, cols)
            edge_ref[exchange, first : first + half, comp] = summed.astype(bf16)

    def finish(exchange, group):
        first = half * group
        own = edge_ref[exchange, first : first + half].reshape(6 * span, cols)
        tensor = dot(own, smooth_ref[...])
        for k in range(half):

            def store(lanes, values):
                for n, value in enumerate(values):
                    out_ref[exchange, n, first + k, :, lanes] = value

            border = border_of(border_ref[exchange, :, 128 * group : 128 * (group + 1)], k, mask_ref)
            attributes(tensor[6 * EDGE * k : 6 * EDGE * (k + 1)], border, store)
        depth = pl.ds(first, half)
        for n, target in enumerate(targets):
            place = target.at[depth, pl.ds(starts[exchange], EDGE)]
            copies.append(pltpu.make_async_copy(out_ref.at[exchange, n, depth], place, sems.at[exchange, group, n]))
            copies[-1].start()

    for exchange, rows_ref in enumerate((near_ref, far_ref)):
        prepare(exchange, rows_ref)
    for exchange in range(2):
        for group in range(2):
            make_edges(exchange, group)
    for exchange in range(2):
        for group in range(2):
            finish(exchange, group)
    for copy in copies:
        copy.wait()


def call(name, kernel, outs, scratch, operands, in_specs=None, out_specs=None, flops=0, limit=16, aliases={}):
    return pl.pallas_call(
        kernel,
        out_shape=tuple(jax.ShapeDtypeStruct(*out) for out in outs),
        in_specs=in_specs or [WHOLE] * len(operands),
        out_specs=out_specs or (WHOLE,) * len(outs),
        scratch_shapes=scratch,
        compiler_params=pltpu.CompilerParams(vmem_limit_bytes=limit << 20),
        name=name,
        input_output_aliases=aliases,
        cost_estimate=pl.CostEstimate(flops=flops, bytes_accessed=0, transcendentals=0),
    )(*operands)


def body(volume):
    depths, rows, cols = volume.shape
    il, xl = lax.axis_size("il"), lax.axis_size("xl")
    count = depths - 2
    assert xl == 2 and il % 2 == 0 and count == 2 * SLOTS and rows == 128 and cols == 256
    bf16, f32 = jnp.bfloat16, jnp.float32
    half = count // 2
    work = half * 1024 * 2 * 256 * 256
    packed_rows = -(-REACH * (depths + 2) // 16) * 16

    span = EDGE * SLOTS
    lines, diff_i, smooth, pack_h, diff_h, lines_e, diff_e, pick, mask = call(
        "tables_kernel",
        lambda *refs: tables_kernel(depths, *refs),
        [
            ((rows, rows), bf16),
            ((rows, rows), bf16),
            ((cols, cols), bf16),
            ((256, 256), bf16),
            ((128 * TILES, 512), bf16),
            ((2, span, span), bf16),
            ((EDGE, EDGE), bf16),
            ((128 * SLOTS, 256), bf16),
            ((3, 8, 128), f32),
        ],
        [],
        [],
        flops=work,
    )
    halo_tile = ((TILES, rows, 128), bf16)
    vol, send, own = call("pack_kernel", pack_kernel, [(volume.shape, bf16), halo_tile, halo_tile], [], [volume, pick])
    side = lax.ppermute(send, "xl", [(0, 1), (1, 0)])
    chunks = rows // EDGE - 2
    moment_slots = [pltpu.VMEM((2, 6, rows, cols), bf16)] * 2
    partial = ((2, 6, count, EDGE, cols), f32)
    inner, part = call(
        "lines_kernel",
        lines_kernel,
        [((2 * HEAD, chunks, 6, EDGE, cols), bf16), partial],
        moment_slots,
        [vol, lines, mask],
        flops=work // 4,
    )
    packed = ((packed_rows, cols), bf16)
    halo, near, far = call(
        "rows_kernel",
        rows_kernel,
        [((rows, 128 * TILES), bf16), packed, packed],
        [pltpu.VMEM((2, packed_rows, cols), f32)],
        [vol, own, side, part],
        in_specs=[WHOLE] * 3 + [ANYWHERE],
    )
    near_in = lax.ppermute(near, "il", [(i, i ^ 1) for i in range(il)])
    pairs = [(i, i + 1) for i in range(1, il - 1, 2)]
    far_in = lax.ppermute(far, "il", pairs + [(j, i) for i, j in pairs] + [(0, 0), (il - 1, il - 1)])

    outs = [((count, rows, cols), f32)] * 3
    operands = [vol, lines, diff_i, smooth, halo, diff_h, pack_h, mask, inner, part]
    part, *outs_in, done, part_h = call(
        "own_kernel",
        own_kernel,
        [partial, *outs, ((3, LATER, EDGE * chunks, cols), f32), ((2, 6, EDGE, 256), f32)],
        [
            pltpu.VMEM((count, chunks, 6, EDGE, cols), bf16),
            pltpu.VMEM((6 * EDGE * chunks, 256), f32),
            *moment_slots,
            pltpu.VMEM((2, 6 * EDGE * chunks, cols), f32),
            pltpu.VMEM((3, count - LATER, EDGE * chunks, cols), f32),
            pltpu.SemaphoreType.DMA((3,)),
        ],
        operands,
        out_specs=(WHOLE,) + (IN_HBM,) * 3 + (WHOLE,) * 2,
        flops=5 * work,
        limit=24,
        aliases={len(operands) - 1: 0},
    )

    operands = [done, vol, halo, near_in, far_in, part, part_h, smooth, pack_h, diff_h, lines_e, diff_e, mask]
    return call(
        "ends_kernel",
        ends_kernel,
        outs,
        [
            pltpu.VMEM((2, packed_rows, cols), f32),
            pltpu.VMEM((2, depths, EDGE, cols), bf16),
            pltpu.VMEM((2, EDGE, 128 * TILES), bf16),
            pltpu.VMEM((2, 6 * EDGE, 256), f32),
            pltpu.VMEM((2, count, 6, EDGE, cols), bf16),
            pltpu.VMEM((2, 3, count, EDGE, cols), f32),
            pltpu.SemaphoreType.DMA((3,)),
            pltpu.SemaphoreType.DMA((2, 2, 3)),
        ],
        operands + outs_in,
        in_specs=[WHOLE] * len(operands) + [IN_HBM] * 3,
        out_specs=(IN_HBM,) * 3,
        flops=2 * work,
        limit=24,
        aliases={len(operands) + n: n for n in range(3)},
    )


def solution(mesh):
    spec = P(None, ("parts", "il"), "xl")
    return jax.shard_map(body, mesh=mesh, in_specs=(spec,), out_specs=(spec,) * 3, check_vma=False)
```

```python
import jax
import jax.numpy as jnp
import ml_dtypes
import numpy as np
from jax import lax
from jax.experimental import pallas as pl
from jax.experimental.pallas import tpu as pltpu
from jax.sharding import PartitionSpec as P

RADIUS = 9
REACH = RADIUS + 1
SIDE = 16
SLOTS = 8
TILES = 3
EDGE = 16
OWN = 2
TINY = float(np.finfo(np.float32).tiny)
HEAD = 3
AHEAD = 3
LATER = 6
SHARED = 2
FAR = -1000
WHOLE = pl.BlockSpec(memory_space=pltpu.VMEM)
IN_HBM = pl.BlockSpec(memory_space=pltpu.HBM)
ANYWHERE = pl.BlockSpec(memory_space=pl.ANY)


def filter_taps():
    offsets = np.arange(2 * RADIUS + 1).astype(np.float32)
    sigma = np.float32(RADIUS / 3.0)
    shape = np.exp(np.float32(-0.5) * ((offsets - RADIUS) / sigma) ** 2)
    return (shape / np.sum(shape, dtype=np.float32)).astype(ml_dtypes.bfloat16).astype(np.float32)


def iota(shape, dim):
    return lax.broadcasted_iota(jnp.int32, shape, dim)


def band(source, target, scale=1.0):
    offset = jnp.abs(source - target)
    weights = jnp.zeros(offset.shape, jnp.float32)
    for distance, tap in enumerate(filter_taps()[RADIUS:]):
        weights = jnp.where(offset == distance, jnp.float32(scale * tap), weights)
    return weights


def difference(source, target):
    offset = source - target
    return jnp.where(offset == 1, 1.0, jnp.where(offset == -1, -1.0, 0.0)).astype(jnp.float32)


def dot(left, right):
    return jnp.dot(left, right, preferred_element_type=jnp.float32)


def halo_plane(lane, tile, depths):
    slot = lax.div(lane, SIDE)
    rest = jnp.where(slot == 0, 0, jnp.where(slot == 1, depths - 1, FAR))
    return jnp.where(tile < 2, 1 + SLOTS * tile + slot, rest)


def halo_column(lane, x, cols):
    place = lax.rem(lane, SIDE)
    return jnp.where(x == 0, cols - OWN + place, place - (SIDE - OWN))


def low_end(exchange):
    even = lax.rem(lax.axis_index("il"), 2) == 0
    return jnp.logical_not(even) if exchange == 0 else even


def tables_kernel(depths, lines_ref, diff_i_ref, smooth_ref, pack_h_ref, diff_h_ref, lines_e_ref, diff_e_ref, pick_ref, mask_ref):
    rows, cols = lines_ref.shape[0], smooth_ref.shape[0]
    x, il, last = lax.axis_index("xl"), lax.axis_index("il"), lax.axis_size("il") - 1
    bf16 = jnp.bfloat16

    target, source = iota((rows, rows), 0), iota((rows, rows), 1)
    inner = (source > 0) & (source < rows - 1)
    lines_ref[...] = jnp.where(inner, band(source, target, 0.25), 0.0).astype(bf16)
    diff_i_ref[...] = difference(source, target).astype(bf16)
    span = EDGE * SLOTS
    target, source = iota((span, span), 0), iota((span, span), 1)
    depth = lax.div(source, EDGE) == lax.div(target, EDGE)
    target, source = lax.rem(target, EDGE), lax.rem(source, EDGE)
    diff_e_ref[...] = difference(source, target)[:EDGE, :EDGE].astype(bf16)
    for exchange in range(2):
        low = low_end(exchange)
        source_at = jnp.where(low, source - REACH, rows - (EDGE - REACH) + source)
        target_at = jnp.where(low, target, rows - EDGE + target)
        first = jnp.where(low & (il > 0), -rows, 0)
        final = jnp.where(jnp.logical_not(low) & (il < last), 2 * rows, rows - 1)
        use = depth & (source_at >= first) & (source_at <= final) & ((source_at <= 0) | (source_at >= rows - 1))
        lines_e_ref[exchange] = jnp.where(use, band(source_at, target_at, 0.25), 0.0).astype(bf16)

    source, target = iota((cols, cols), 0), iota((cols, cols), 1)
    moved = source == jnp.where(x == 0, cols - 1, 0)
    column = lax.rem(target + 128 * x, cols)
    smooth_ref[...] = jnp.where(moved, 0.0, band(source, column)).astype(bf16)
    source, target = iota((256, 256), 0), iota((256, 256), 1)
    place = lax.rem(source, SIDE)
    use = (lax.div(source, SIDE) == lax.div(target, SIDE)) & (place != jnp.where(x == 0, 0, SIDE - 1))
    column = jnp.where(x == 0, cols - SIDE, 0) + lax.rem(target, SIDE)
    pack_h_ref[...] = jnp.where(use, band(halo_column(place, x, cols), column), 0.0).astype(bf16)

    source, target = iota((128, 128), 0), iota((128, 128), 1)
    same = lax.rem(source, SIDE) == lax.rem(target, SIDE)
    across = difference(lax.rem(source, SIDE), lax.rem(target, SIDE))
    for group in range(2):
        centre = halo_plane(target, group, depths)
        for tile in range(TILES):
            plane = halo_plane(source, tile, depths)
            part, out = slice(128 * tile, 128 * (tile + 1)), 128 * group
            diff_h_ref[part, out : out + 128] = jnp.where(same, difference(plane, centre), 0.0).astype(bf16)
            diff_h_ref[part, 256 + out : 384 + out] = jnp.where(plane == centre, across, 0.0).astype(bf16)

    source, lane = iota((128, 256), 0), iota((128, 256), 1)
    place = lax.rem(lane, SIDE)
    low, high = place < SIDE - OWN, place >= OWN
    sent = jnp.where(x == 0, jnp.where(low, 128 - (SIDE - OWN) + place, FAR), jnp.where(high, place - OWN, FAR))
    low, high = place < OWN, place >= SIDE - OWN
    kept = jnp.where(x == 0, jnp.where(low, 128 - OWN + place, FAR), jnp.where(high, place - (SIDE - OWN), FAR))
    pick = jnp.where(source == jnp.where(lane < 128, sent, kept), 1.0, 0.0)
    slot = lax.div(lax.rem(lane, 128), SIDE)
    for index in range(SLOTS):
        pick_ref[128 * index : 128 * (index + 1)] = jnp.where(slot == index, pick, 0.0).astype(bf16)
    lane = iota((8, 128), 1)
    border = jnp.where(x == 0, lane - (128 - SIDE), lane)
    mask_ref[0] = jnp.where((border >= 0) & (border < SIDE), 1.0, 0.0)
    mask_ref[1] = jnp.where(lane > 0, 1.0, 0.0)
    mask_ref[2] = jnp.where(lane < 127, 1.0, 0.0)


def pack_kernel(vol_ref, pick_ref, copy_ref, send_ref, own_ref):
    depths, rows, cols = vol_ref.shape
    edge = pl.ds(pl.multiple_of((cols - 128) * (1 - lax.axis_index("xl")), 128), 128)
    copy_ref[...] = vol_ref[...]
    for tile in range(TILES):
        planes = (0, depths - 1) if tile == 2 else range(1 + SLOTS * tile, 1 + SLOTS * (tile + 1))
        beside = jnp.concatenate([vol_ref[plane, :, edge] for plane in planes], axis=1)
        packed = dot(beside, pick_ref[: beside.shape[1]]).astype(jnp.bfloat16)
        send_ref[tile] = packed[:, :128]
        own_ref[tile] = packed[:, 128:]


def rows_kernel(vol_ref, own_ref, side_ref, after_ref, halo_ref, near_ref, far_ref, packed_ref):
    depths, rows, cols = vol_ref.shape
    even = lax.rem(lax.axis_index("il"), 2) == 0

    def put(row, top, bottom):
        top, bottom = top[:REACH], bottom[EDGE - REACH :]
        lanes = top.shape[1]
        packed_ref[0, row : row + REACH, :lanes] = jnp.where(even, bottom, top)
        packed_ref[1, row : row + REACH, :lanes] = jnp.where(even, top, bottom)

    packed_ref[:, depths * REACH :, :] = jnp.zeros_like(packed_ref[:, depths * REACH :, :])
    for depth in range(depths):
        top = vol_ref[depth, :EDGE, :].astype(jnp.float32)
        bottom = vol_ref[depth, rows - EDGE :, :].astype(jnp.float32)
        put(REACH * depth, top, bottom)
    tiles = []
    for tile in range(TILES):
        merged = own_ref[tile].astype(jnp.float32) + side_ref[tile].astype(jnp.float32)
        halo_ref[:, 128 * tile : 128 * (tile + 1)] = merged.astype(jnp.bfloat16)
        tiles.append((merged[:EDGE], merged[rows - EDGE :]))
    tops = jnp.concatenate([tiles[0][0], tiles[1][0]], axis=1)
    bottoms = jnp.concatenate([tiles[0][1], tiles[1][1]], axis=1)
    put(REACH * depths, tops, bottoms)
    put(REACH * (depths + 1), *tiles[2])
    near_ref[...] = packed_ref[0].astype(jnp.bfloat16)
    far_ref[...] = packed_ref[1].astype(jnp.bfloat16)


def moments(grad_i, grad_x, grad_z):
    terms = (
        grad_i * grad_i,
        grad_x * grad_x,
        grad_z * grad_z,
        grad_i * grad_x,
        grad_i * grad_z,
        grad_x * grad_z,
    )
    return [term.astype(jnp.bfloat16) for term in terms]


def store_chunks(summed, comp, inner_ref, part_ref):
    chunks = summed.shape[0] // EDGE
    for chunk in range(1, chunks - 1):
        inner_ref[chunk - 1, comp] = summed[EDGE * chunk : EDGE * (chunk + 1)].astype(jnp.bfloat16)
    part_ref[0, comp] = summed[:EDGE]
    part_ref[1, comp] = summed[EDGE * (chunks - 1) :]


def gradients(before, centre, after, mask_ref):
    rows, cols = centre.shape
    left, right = pltpu.roll(centre, 1, 1), pltpu.roll(centre, cols - 1, 1)
    left_0 = (left[:, :128].reshape(-1, 8, 128) * mask_ref[1]).reshape(rows, 128)
    right_1 = (right[:, cols - 128 :].reshape(-1, 8, 128) * mask_ref[2]).reshape(rows, 128)
    grad_x = jnp.concatenate([right[:, : cols - 128] - left_0, right_1 - left[:, 128:]], axis=1)
    return pltpu.roll(centre, rows - 1, 0) - pltpu.roll(centre, 1, 0), grad_x, after - before


def make_moments(pair, vol_ref, mask_ref, moments_ref):
    planes = [vol_ref[2 * pair + k].astype(jnp.float32) for k in range(4)]
    for k in range(2):
        for comp, term in enumerate(moments(*gradients(*planes[k : k + 3], mask_ref))):
            moments_ref[k, comp] = term


def make_lines(z, comp, lines_ref, moments_ref, inner_ref, part_ref):
    store_chunks(dot(lines_ref[...], moments_ref[z % 2, comp]), comp, inner_ref.at[z], part_ref.at[:, :, z])


def lines_kernel(vol_ref, lines_ref, mask_ref, inner_ref, part_ref, even_ref, odd_ref):
    slots = (even_ref, odd_ref)
    for pair in range(HEAD):
        make_moments(pair, vol_ref, mask_ref, slots[pair % 2])
        for k in range(2):
            for comp in range(6):
                make_lines(2 * pair + k, comp, lines_ref, slots[pair % 2], inner_ref, part_ref)


def shared_lines_kernel(
    parity, vol_ref, lines_ref, mask_ref, rows_ref, part_in_ref, *refs,
):
    inner_ref, part_ref, rows_out_ref, even_ref, odd_ref = refs[-5:]
    rows_out_ref[...] = rows_ref[...]

    @pl.when(lax.rem(lax.axis_index("il"), 2) == parity)
    def _():
        for index in range(SHARED):
            pair, slot = HEAD + index, (even_ref, odd_ref)[index % 2]
            make_moments(pair, vol_ref, mask_ref, slot)
            for k in range(2):
                z = 2 * pair + k
                for comp in range(6):
                    summed = dot(lines_ref[...], slot[k, comp])
                    store_chunks(summed, comp, inner_ref.at[2 * index + k], part_ref.at[:, :, z])


def tensor_of(own, smooth_ref, tensor_ref):
    tensor_ref[...] = dot(own.reshape(-1, own.shape[-1]), smooth_ref[...])


def attributes(tensor, border, store):
    x = lax.axis_index("xl")
    halves = (tensor[:, :128], tensor[:, 128:] + border)
    lanes = (pl.multiple_of(128 * x, 128), pl.multiple_of(128 - 128 * x, 128))
    for half, lane in zip(halves, lanes):
        a, b, c, d, e, f = [half[EDGE * comp : EDGE * (comp + 1)] for comp in range(6)]
        low = -1e-6 - c
        inverse = pl.reciprocal(low, approx=True)
        spread = (a - b) * (a - c) + (b - c) * (b - c) + 3.0 * (d * d + e * e + f * f)
        root = spread * lax.rsqrt(jnp.maximum(spread, TINY))
        store(pl.ds(lane, 128), (e * inverse, f * inverse, root * pl.reciprocal(a + b - low, approx=True)))


def border_of(packed, slot, mask_ref):
    base = jnp.where(lax.axis_index("xl") == 0, 128 - SIDE, 0)
    moved = pltpu.roll(packed, lax.rem(base - SIDE * slot + 128, 128), 1)
    return (moved.reshape(-1, 8, 128) * mask_ref[0]).reshape(packed.shape)


def own_kernel(
    vol_ref, lines_ref, diff_i_ref, smooth_ref, halo_ref, diff_h_ref, pack_h_ref, mask_ref, inner_in_ref, shared_ref, part_in_ref,
    part_ref, dip_i_ref, dip_x_ref, plan_ref, later_ref, part_h_ref,
    inner_ref, border_ref, even_ref, odd_ref, tensor_ref, out_ref, sems,
):
    count, chunks = vol_ref.shape[0] - 2, inner_ref.shape[1]
    inner = EDGE * chunks
    slots = (even_ref, odd_ref)
    targets = (dip_i_ref, dip_x_ref, plan_ref)
    ready, known = 2 * HEAD, 2 * (HEAD + SHARED)

    def inner_of(z):
        return inner_in_ref[z] if z < ready else shared_ref[z - ready] if z < known else inner_ref[z - known]


    both = dot(halo_ref[...], diff_h_ref[...])
    grad_i = dot(diff_i_ref[...], halo_ref[:, :256])
    lined_h = [[] for chunk in range(chunks)]
    for comp, term in enumerate(moments(grad_i, both[:, 256:], both[:, :256])):
        summed = dot(lines_ref[...], term)
        for chunk, parts in enumerate(lined_h):
            parts.append(summed[EDGE * (chunk + 1) : EDGE * (chunk + 2)].astype(jnp.bfloat16))
        part_h_ref[0, comp] = summed[:EDGE]
        part_h_ref[1, comp] = summed[EDGE * (chunks + 1) :]
    border_ref[...] = dot(jnp.concatenate(sum(lined_h, []), axis=0), pack_h_ref[...])

    copies = []
    tensor_of(inner_of(0), smooth_ref, tensor_ref.at[0])
    for z in range(count):
        later = z + known if z + known < count else None
        if later is not None and later % 2 == 0:
            make_moments(later // 2, vol_ref, mask_ref, slots[later // 2 % 2])
        if z < count - 1:
            tensor_of(inner_of(z + 1), smooth_ref, tensor_ref.at[(z + 1) % 2])
        group = 128 * (z // SLOTS)
        for chunk in range(chunks):
            rows = slice(EDGE * chunk, EDGE * (chunk + 1))
            part = slice(6 * EDGE * chunk, 6 * EDGE * (chunk + 1))

            def store(lanes, values):
                for n, value in enumerate(values):
                    if z >= count - LATER:
                        later_ref[n, z - (count - LATER), rows, lanes] = value
                    else:
                        out_ref[n, z, rows, lanes] = value

            border = border_of(border_ref[part, group : group + 128], z % SLOTS, mask_ref)
            attributes(tensor_ref[z % 2, part], border, store)
            if later is not None:
                summed = dot(lines_ref[...], slots[later // 2 % 2][later % 2, chunk])
                store_chunks(summed, chunk, inner_ref.at[later - known], part_ref.at[:, :, later])
        if z % 2 == 1 and z < count - LATER:
            depth = pl.ds(z - 1, 2)
            for n, target in enumerate(targets):
                place = target.at[depth, pl.ds(EDGE, inner)]
                copies.append(pltpu.make_async_copy(out_ref.at[n, depth], place, sems.at[z // 2, n]))
                copies[-1].start()
    for copy in copies:
        copy.wait()


def ends_kernel(
    done_ref, vol_ref, halo_ref, near_ref, far_ref, part_ref, part_h_ref,
    smooth_ref, pack_h_ref, diff_h_ref, lines_e_ref, diff_e_ref, mask_ref, in_i_ref, in_x_ref, in_p_ref,
    dip_i_ref, dip_x_ref, plan_ref,
    packed_ref, block_ref, block_h_ref, border_ref, edge_ref, out_ref, done_sems, sems,
):
    depths, rows, cols = vol_ref.shape
    count, half = depths - 2, (depths - 2) // 2
    bf16, f32 = jnp.bfloat16, jnp.float32
    span = EDGE * half
    targets = (dip_i_ref, dip_x_ref, plan_ref)
    copies = []
    for n, target in enumerate(targets):
        place = target.at[pl.ds(count - LATER, LATER), pl.ds(EDGE, rows - 2 * EDGE)]
        copies.append(pltpu.make_async_copy(done_ref.at[n], place, done_sems.at[n]))
        copies[-1].start()
    lows = [low_end(exchange) for exchange in range(2)]
    ends = [jnp.where(low, 0, 1) for low in lows]
    starts = [pl.multiple_of(jnp.where(low, 0, rows - EDGE), EDGE) for low in lows]

    def prepare(exchange, rows_ref):
        low, start, end = lows[exchange], starts[exchange], ends[exchange]
        rows_in = rows_ref[...].astype(f32)
        if exchange == 1:
            il = lax.axis_index("il")
            outside = (low & (il == 0)) | (jnp.logical_not(low) & (il == lax.axis_size("il") - 1))
            rows_in = jnp.where(outside, 0.0, rows_in)
        packed_ref[exchange] = pltpu.roll(rows_in, jnp.where(low, 0, EDGE - REACH), 0)
        place = iota((EDGE, cols), 0)
        received = jnp.where(low, place, EDGE - 1 - place) < REACH

        def joined(row, own):
            lanes = own.shape[1]
            own = pltpu.roll(own.astype(f32), jnp.where(low, REACH, EDGE - REACH), 0)
            return jnp.where(received[:, :lanes], packed_ref[exchange, row : row + EDGE, :lanes], own).astype(bf16)

        for depth in range(depths):
            block_ref[exchange, depth] = joined(REACH * depth, vol_ref[depth, pl.ds(start, EDGE)])
        own_h = halo_ref[pl.ds(start, EDGE)]
        block_h_ref[exchange, :, :256] = joined(REACH * depths, own_h[:, :256])
        block_h_ref[exchange, :, 256:] = joined(REACH * (depths + 1), own_h[:, 256:])

        both = dot(block_h_ref[exchange], diff_h_ref[...])
        grad_i = dot(diff_e_ref[...], block_h_ref[exchange, :, :256])
        lined_h = []
        for comp, term in enumerate(moments(grad_i, both[:, 256:], both[:, :256])):
            summed = part_h_ref[end, comp] + dot(lines_e_ref[exchange, :EDGE, :EDGE], term)
            lined_h.append(summed.astype(bf16))
        border_ref[exchange] = dot(jnp.concatenate(lined_h, axis=0), pack_h_ref[...])

    def make_edges(exchange, group):
        first = half * group
        planes = [block_ref[exchange, first + k : first + half + k].astype(f32).reshape(span, cols) for k in range(3)]
        for comp, term in enumerate(moments(*gradients(*planes, mask_ref))):
            outer = dot(lines_e_ref[exchange], term)
            summed = part_ref[ends[exchange], comp, first : first + half] + outer.reshape(half, EDGE, cols)
            edge_ref[exchange, first : first + half, comp] = summed.astype(bf16)

    def finish(exchange, group):
        first = half * group
        own = edge_ref[exchange, first : first + half].reshape(6 * span, cols)
        tensor = dot(own, smooth_ref[...])
        for k in range(half):

            def store(lanes, values):
                for n, value in enumerate(values):
                    out_ref[exchange, n, first + k, :, lanes] = value

            border = border_of(border_ref[exchange, :, 128 * group : 128 * (group + 1)], k, mask_ref)
            attributes(tensor[6 * EDGE * k : 6 * EDGE * (k + 1)], border, store)
        depth = pl.ds(first, half)
        for n, target in enumerate(targets):
            place = target.at[depth, pl.ds(starts[exchange], EDGE)]
            copies.append(pltpu.make_async_copy(out_ref.at[exchange, n, depth], place, sems.at[exchange, group, n]))
            copies[-1].start()

    for exchange, rows_ref in enumerate((near_ref, far_ref)):
        prepare(exchange, rows_ref)
    for exchange in range(2):
        for group in range(2):
            make_edges(exchange, group)
    for exchange in range(2):
        for group in range(2):
            finish(exchange, group)
    for copy in copies:
        copy.wait()


def call(name, kernel, outs, scratch, operands, in_specs=None, out_specs=None, flops=0, limit=16, aliases={}):
    return pl.pallas_call(
        kernel,
        out_shape=tuple(jax.ShapeDtypeStruct(*out) for out in outs),
        in_specs=in_specs or [WHOLE] * len(operands),
        out_specs=out_specs or (WHOLE,) * len(outs),
        scratch_shapes=scratch,
        compiler_params=pltpu.CompilerParams(vmem_limit_bytes=limit << 20),
        name=name,
        input_output_aliases=aliases,
        cost_estimate=pl.CostEstimate(flops=flops, bytes_accessed=0, transcendentals=0),
    )(*operands)


def body(volume):
    depths, rows, cols = volume.shape
    il, xl = lax.axis_size("il"), lax.axis_size("xl")
    count = depths - 2
    assert xl == 2 and il % 2 == 0 and count == 2 * SLOTS and rows == 128 and cols == 256
    bf16, f32 = jnp.bfloat16, jnp.float32
    half = count // 2
    work = half * 1024 * 2 * 256 * 256
    packed_rows = -(-REACH * (depths + 2) // 16) * 16

    span = EDGE * SLOTS
    lines, diff_i, smooth, pack_h, diff_h, lines_e, diff_e, pick, mask = call(
        "tables_kernel",
        lambda *refs: tables_kernel(depths, *refs),
        [
            ((rows, rows), bf16),
            ((rows, rows), bf16),
            ((cols, cols), bf16),
            ((256, 256), bf16),
            ((128 * TILES, 512), bf16),
            ((2, span, span), bf16),
            ((EDGE, EDGE), bf16),
            ((128 * SLOTS, 256), bf16),
            ((3, 8, 128), f32),
        ],
        [],
        [],
        flops=work,
    )
    halo_tile = ((TILES, rows, 128), bf16)
    vol, send, own = call("pack_kernel", pack_kernel, [(volume.shape, bf16), halo_tile, halo_tile], [], [volume, pick])
    side = lax.ppermute(send, "xl", [(0, 1), (1, 0)])
    chunks = rows // EDGE - 2
    moment_slots = [pltpu.VMEM((2, 6, rows, cols), bf16)] * 2
    partial = ((2, 6, count, EDGE, cols), f32)
    inner, part = call(
        "lines_kernel",
        lines_kernel,
        [((2 * HEAD, chunks, 6, EDGE, cols), bf16), partial],
        moment_slots,
        [vol, lines, mask],
        flops=work // 4,
    )
    packed = ((packed_rows, cols), bf16)
    halo, near, far = call(
        "rows_kernel",
        rows_kernel,
        [((rows, 128 * TILES), bf16), packed, packed],
        [pltpu.VMEM((2, packed_rows, cols), f32)],
        [vol, own, side, part],
        in_specs=[WHOLE] * 3 + [ANYWHERE],
    )
    near_in = lax.ppermute(near, "il", [(i, i ^ 1) for i in range(il)])
    pairs = [(i, i + 1) for i in range(1, il - 1, 2)]
    shared_shape = ((2 * SHARED, chunks, 6, EDGE, cols), bf16)
    operands = [vol, lines, mask, far, part]
    shared, part, far = call(
        "odd_lines_kernel",
        lambda *refs: shared_lines_kernel(1, *refs),
        [shared_shape, partial, packed],
        moment_slots,
        operands,
        flops=work // 4,
        aliases={4: 1},
    )
    far_in = lax.ppermute(far, "il", pairs + [(j, i) for i, j in pairs] + [(0, 0), (il - 1, il - 1)])
    operands = [vol, lines, mask, far, part, shared]
    shared, part, _ = call(
        "even_lines_kernel",
        lambda *refs: shared_lines_kernel(0, *refs),
        [shared_shape, partial, packed],
        moment_slots,
        operands,
        flops=work // 4,
        aliases={4: 1, 5: 0},
    )

    outs = [((count, rows, cols), f32)] * 3
    operands = [vol, lines, diff_i, smooth, halo, diff_h, pack_h, mask, inner, shared, part]
    part, *outs_in, done, part_h = call(
        "own_kernel",
        own_kernel,
        [partial, *outs, ((3, LATER, EDGE * chunks, cols), f32), ((2, 6, EDGE, 256), f32)],
        [
            pltpu.VMEM((count - 2 * (HEAD + SHARED), chunks, 6, EDGE, cols), bf16),
            pltpu.VMEM((6 * EDGE * chunks, 256), f32),
            *moment_slots,
            pltpu.VMEM((2, 6 * EDGE * chunks, cols), f32),
            pltpu.VMEM((3, count - LATER, EDGE * chunks, cols), f32),
            pltpu.SemaphoreType.DMA(((count - LATER) // 2, 3)),
        ],
        operands,
        out_specs=(WHOLE,) + (IN_HBM,) * 3 + (WHOLE,) * 2,
        flops=5 * work,
        limit=24,
        aliases={len(operands) - 1: 0},
    )

    operands = [done, vol, halo, near_in, far_in, part, part_h, smooth, pack_h, diff_h, lines_e, diff_e, mask]
    return call(
        "ends_kernel",
        ends_kernel,
        outs,
        [
            pltpu.VMEM((2, packed_rows, cols), f32),
            pltpu.VMEM((2, depths, EDGE, cols), bf16),
            pltpu.VMEM((2, EDGE, 128 * TILES), bf16),
            pltpu.VMEM((2, 6 * EDGE, 256), f32),
            pltpu.VMEM((2, count, 6, EDGE, cols), bf16),
            pltpu.VMEM((2, 3, count, EDGE, cols), f32),
            pltpu.SemaphoreType.DMA((3,)),
            pltpu.SemaphoreType.DMA((2, 2, 3)),
        ],
        operands + outs_in,
        in_specs=[WHOLE] * len(operands) + [IN_HBM] * 3,
        out_specs=(IN_HBM,) * 3,
        flops=2 * work,
        limit=24,
        aliases={len(operands) + n: n for n in range(3)},
    )


def solution(mesh):
    spec = P(None, ("parts", "il"), "xl")
    return jax.shard_map(body, mesh=mesh, in_specs=(spec,), out_specs=(spec,) * 3, check_vma=False)
```

```python
import jax
import jax.numpy as jnp
import ml_dtypes
import numpy as np
from jax import lax
from jax.experimental import pallas as pl
from jax.experimental.pallas import tpu as pltpu
from jax.sharding import PartitionSpec as P

RADIUS = 9
REACH = RADIUS + 1
SIDE = 16
SLOTS = 8
TILES = 3
EDGE = 16
OWN = 2
TINY = float(np.finfo(np.float32).tiny)
HEAD = 3
AHEAD = 3
LATER = 6
SHARED = 2
FAR = -1000
WHOLE = pl.BlockSpec(memory_space=pltpu.VMEM)
IN_HBM = pl.BlockSpec(memory_space=pltpu.HBM)
ANYWHERE = pl.BlockSpec(memory_space=pl.ANY)


def filter_taps():
    offsets = np.arange(2 * RADIUS + 1).astype(np.float32)
    sigma = np.float32(RADIUS / 3.0)
    shape = np.exp(np.float32(-0.5) * ((offsets - RADIUS) / sigma) ** 2)
    return (shape / np.sum(shape, dtype=np.float32)).astype(ml_dtypes.bfloat16).astype(np.float32)


def iota(shape, dim):
    return lax.broadcasted_iota(jnp.int32, shape, dim)


def band(source, target, scale=1.0):
    offset = jnp.abs(source - target)
    weights = jnp.zeros(offset.shape, jnp.float32)
    for distance, tap in enumerate(filter_taps()[RADIUS:]):
        weights = jnp.where(offset == distance, jnp.float32(scale * tap), weights)
    return weights


def difference(source, target):
    offset = source - target
    return jnp.where(offset == 1, 1.0, jnp.where(offset == -1, -1.0, 0.0)).astype(jnp.float32)


def dot(left, right):
    return jnp.dot(left, right, preferred_element_type=jnp.float32)


def halo_plane(lane, tile, depths):
    slot = lax.div(lane, SIDE)
    rest = jnp.where(slot == 0, 0, jnp.where(slot == 1, depths - 1, FAR))
    return jnp.where(tile < 2, 1 + SLOTS * tile + slot, rest)


def halo_column(lane, x, cols):
    place = lax.rem(lane, SIDE)
    return jnp.where(x == 0, cols - OWN + place, place - (SIDE - OWN))


def low_end(exchange):
    even = lax.rem(lax.axis_index("il"), 2) == 0
    return jnp.logical_not(even) if exchange == 0 else even


def tables_kernel(depths, lines_ref, diff_i_ref, smooth_ref, pack_h_ref, diff_h_ref, lines_e_ref, diff_e_ref, pick_ref, mask_ref):
    rows, cols = lines_ref.shape[0], smooth_ref.shape[0]
    x, il, last = lax.axis_index("xl"), lax.axis_index("il"), lax.axis_size("il") - 1
    bf16 = jnp.bfloat16

    target, source = iota((rows, rows), 0), iota((rows, rows), 1)
    inner = (source > 0) & (source < rows - 1)
    lines_ref[...] = jnp.where(inner, band(source, target, 0.25), 0.0).astype(bf16)
    diff_i_ref[...] = difference(source, target).astype(bf16)
    span = EDGE * SLOTS
    target, source = iota((span, span), 0), iota((span, span), 1)
    depth = lax.div(source, EDGE) == lax.div(target, EDGE)
    target, source = lax.rem(target, EDGE), lax.rem(source, EDGE)
    diff_e_ref[...] = difference(source, target)[:EDGE, :EDGE].astype(bf16)
    for exchange in range(2):
        low = low_end(exchange)
        source_at = jnp.where(low, source - REACH, rows - (EDGE - REACH) + source)
        target_at = jnp.where(low, target, rows - EDGE + target)
        first = jnp.where(low & (il > 0), -rows, 0)
        final = jnp.where(jnp.logical_not(low) & (il < last), 2 * rows, rows - 1)
        use = depth & (source_at >= first) & (source_at <= final) & ((source_at <= 0) | (source_at >= rows - 1))
        lines_e_ref[exchange] = jnp.where(use, band(source_at, target_at, 0.25), 0.0).astype(bf16)

    source, target = iota((cols, cols), 0), iota((cols, cols), 1)
    moved = source == jnp.where(x == 0, cols - 1, 0)
    column = lax.rem(target + 128 * x, cols)
    smooth_ref[...] = jnp.where(moved, 0.0, band(source, column)).astype(bf16)
    source, target = iota((256, 256), 0), iota((256, 256), 1)
    place = lax.rem(source, SIDE)
    use = (lax.div(source, SIDE) == lax.div(target, SIDE)) & (place != jnp.where(x == 0, 0, SIDE - 1))
    column = jnp.where(x == 0, cols - SIDE, 0) + lax.rem(target, SIDE)
    pack_h_ref[...] = jnp.where(use, band(halo_column(place, x, cols), column), 0.0).astype(bf16)

    source, target = iota((128, 128), 0), iota((128, 128), 1)
    same = lax.rem(source, SIDE) == lax.rem(target, SIDE)
    across = difference(lax.rem(source, SIDE), lax.rem(target, SIDE))
    for group in range(2):
        centre = halo_plane(target, group, depths)
        for tile in range(TILES):
            plane = halo_plane(source, tile, depths)
            part, out = slice(128 * tile, 128 * (tile + 1)), 128 * group
            diff_h_ref[part, out : out + 128] = jnp.where(same, difference(plane, centre), 0.0).astype(bf16)
            diff_h_ref[part, 256 + out : 384 + out] = jnp.where(plane == centre, across, 0.0).astype(bf16)

    source, lane = iota((128, 256), 0), iota((128, 256), 1)
    place = lax.rem(lane, SIDE)
    low, high = place < SIDE - OWN, place >= OWN
    sent = jnp.where(x == 0, jnp.where(low, 128 - (SIDE - OWN) + place, FAR), jnp.where(high, place - OWN, FAR))
    low, high = place < OWN, place >= SIDE - OWN
    kept = jnp.where(x == 0, jnp.where(low, 128 - OWN + place, FAR), jnp.where(high, place - (SIDE - OWN), FAR))
    pick = jnp.where(source == jnp.where(lane < 128, sent, kept), 1.0, 0.0)
    slot = lax.div(lax.rem(lane, 128), SIDE)
    for index in range(SLOTS):
        pick_ref[128 * index : 128 * (index + 1)] = jnp.where(slot == index, pick, 0.0).astype(bf16)
    lane = iota((8, 128), 1)
    border = jnp.where(x == 0, lane - (128 - SIDE), lane)
    mask_ref[0] = jnp.where((border >= 0) & (border < SIDE), 1.0, 0.0)
    mask_ref[1] = jnp.where(lane > 0, 1.0, 0.0)
    mask_ref[2] = jnp.where(lane < 127, 1.0, 0.0)


def pack_kernel(vol_ref, pick_ref, copy_ref, send_ref, own_ref):
    depths, rows, cols = vol_ref.shape
    edge = pl.ds(pl.multiple_of((cols - 128) * (1 - lax.axis_index("xl")), 128), 128)
    copy_ref[...] = vol_ref[...]
    for tile in range(TILES):
        planes = (0, depths - 1) if tile == 2 else range(1 + SLOTS * tile, 1 + SLOTS * (tile + 1))
        beside = jnp.concatenate([vol_ref[plane, :, edge] for plane in planes], axis=1)
        packed = dot(beside, pick_ref[: beside.shape[1]]).astype(jnp.bfloat16)
        send_ref[tile] = packed[:, :128]
        own_ref[tile] = packed[:, 128:]


def rows_kernel(vol_ref, own_ref, side_ref, after_ref, halo_ref, near_ref, far_ref, packed_ref):
    depths, rows, cols = vol_ref.shape
    even = lax.rem(lax.axis_index("il"), 2) == 0

    def put(row, top, bottom):
        top, bottom = top[:REACH], bottom[EDGE - REACH :]
        lanes = top.shape[1]
        packed_ref[0, row : row + REACH, :lanes] = jnp.where(even, bottom, top)
        packed_ref[1, row : row + REACH, :lanes] = jnp.where(even, top, bottom)

    packed_ref[:, depths * REACH :, :] = jnp.zeros_like(packed_ref[:, depths * REACH :, :])
    for depth in range(depths):
        top = vol_ref[depth, :EDGE, :].astype(jnp.float32)
        bottom = vol_ref[depth, rows - EDGE :, :].astype(jnp.float32)
        put(REACH * depth, top, bottom)
    tiles = []
    for tile in range(TILES):
        merged = own_ref[tile].astype(jnp.float32) + side_ref[tile].astype(jnp.float32)
        halo_ref[:, 128 * tile : 128 * (tile + 1)] = merged.astype(jnp.bfloat16)
        tiles.append((merged[:EDGE], merged[rows - EDGE :]))
    tops = jnp.concatenate([tiles[0][0], tiles[1][0]], axis=1)
    bottoms = jnp.concatenate([tiles[0][1], tiles[1][1]], axis=1)
    put(REACH * depths, tops, bottoms)
    put(REACH * (depths + 1), *tiles[2])
    near_ref[...] = packed_ref[0].astype(jnp.bfloat16)
    far_ref[...] = packed_ref[1].astype(jnp.bfloat16)


def moments(grad_i, grad_x, grad_z):
    terms = (
        grad_i * grad_i,
        grad_x * grad_x,
        grad_z * grad_z,
        grad_i * grad_x,
        grad_i * grad_z,
        grad_x * grad_z,
    )
    return [term.astype(jnp.bfloat16) for term in terms]


def store_chunks(summed, comp, inner_ref, part_ref):
    chunks = summed.shape[0] // EDGE
    for chunk in range(1, chunks - 1):
        inner_ref[chunk - 1, comp] = summed[EDGE * chunk : EDGE * (chunk + 1)].astype(jnp.bfloat16)
    part_ref[0, comp] = summed[:EDGE]
    part_ref[1, comp] = summed[EDGE * (chunks - 1) :]


def gradients(before, centre, after, mask_ref):
    rows, cols = centre.shape
    left, right = pltpu.roll(centre, 1, 1), pltpu.roll(centre, cols - 1, 1)
    left_0 = (left[:, :128].reshape(-1, 8, 128) * mask_ref[1]).reshape(rows, 128)
    right_1 = (right[:, cols - 128 :].reshape(-1, 8, 128) * mask_ref[2]).reshape(rows, 128)
    grad_x = jnp.concatenate([right[:, : cols - 128] - left_0, right_1 - left[:, 128:]], axis=1)
    return pltpu.roll(centre, rows - 1, 0) - pltpu.roll(centre, 1, 0), grad_x, after - before


def make_moments(pair, vol_ref, mask_ref, moments_ref):
    planes = [vol_ref[2 * pair + k].astype(jnp.float32) for k in range(4)]
    for k in range(2):
        for comp, term in enumerate(moments(*gradients(*planes[k : k + 3], mask_ref))):
            moments_ref[k, comp] = term


def make_lines(z, comp, lines_ref, moments_ref, inner_ref, part_ref):
    store_chunks(dot(lines_ref[...], moments_ref[z % 2, comp]), comp, inner_ref.at[z], part_ref.at[:, :, z])


def lines_kernel(vol_ref, lines_ref, mask_ref, inner_ref, part_ref, even_ref, odd_ref):
    slots = (even_ref, odd_ref)
    for pair in range(HEAD):
        make_moments(pair, vol_ref, mask_ref, slots[pair % 2])
        for k in range(2):
            for comp in range(6):
                make_lines(2 * pair + k, comp, lines_ref, slots[pair % 2], inner_ref, part_ref)


def shared_lines_kernel(
    parity, vol_ref, lines_ref, mask_ref, part_in_ref, *refs,
):
    if parity == 1:
        rows_ref, inner_ref, part_ref, rows_out_ref, even_ref, odd_ref = refs
        rows_out_ref[...] = rows_ref[...]
    else:
        shared_in_ref, inner_ref, part_ref, even_ref, odd_ref = refs

    @pl.when(lax.rem(lax.axis_index("il"), 2) == parity)
    def _():
        for index in range(SHARED):
            pair, slot = HEAD + index, (even_ref, odd_ref)[index % 2]
            make_moments(pair, vol_ref, mask_ref, slot)
            for k in range(2):
                z = 2 * pair + k
                for comp in range(6):
                    summed = dot(lines_ref[...], slot[k, comp])
                    store_chunks(summed, comp, inner_ref.at[2 * index + k], part_ref.at[:, :, z])


def tensor_of(own, smooth_ref, tensor_ref):
    tensor_ref[...] = dot(own.reshape(-1, own.shape[-1]), smooth_ref[...])


def attributes(tensor, border, store):
    x = lax.axis_index("xl")
    halves = (tensor[:, :128], tensor[:, 128:] + border)
    lanes = (pl.multiple_of(128 * x, 128), pl.multiple_of(128 - 128 * x, 128))
    for half, lane in zip(halves, lanes):
        a, b, c, d, e, f = [half[EDGE * comp : EDGE * (comp + 1)] for comp in range(6)]
        low = -1e-6 - c
        inverse = pl.reciprocal(low, approx=True)
        spread = (a - b) * (a - c) + (b - c) * (b - c) + 3.0 * (d * d + e * e + f * f)
        root = spread * lax.rsqrt(jnp.maximum(spread, TINY))
        store(pl.ds(lane, 128), (e * inverse, f * inverse, root * pl.reciprocal(a + b - low, approx=True)))


def border_of(packed, slot, mask_ref):
    base = jnp.where(lax.axis_index("xl") == 0, 128 - SIDE, 0)
    moved = pltpu.roll(packed, lax.rem(base - SIDE * slot + 128, 128), 1)
    return (moved.reshape(-1, 8, 128) * mask_ref[0]).reshape(packed.shape)


def own_kernel(
    vol_ref, lines_ref, diff_i_ref, smooth_ref, halo_ref, diff_h_ref, pack_h_ref, mask_ref, inner_in_ref, shared_ref, part_in_ref,
    part_ref, dip_i_ref, dip_x_ref, plan_ref, later_ref, part_h_ref,
    inner_ref, border_ref, even_ref, odd_ref, tensor_ref, out_ref, sems,
):
    count, chunks = vol_ref.shape[0] - 2, inner_ref.shape[1]
    inner = EDGE * chunks
    slots = (even_ref, odd_ref)
    targets = (dip_i_ref, dip_x_ref, plan_ref)
    ready, known = 2 * HEAD, 2 * (HEAD + SHARED)

    def inner_of(z):
        return inner_in_ref[z] if z < ready else shared_ref[z - ready] if z < known else inner_ref[z - known]


    both = dot(halo_ref[...], diff_h_ref[...])
    grad_i = dot(diff_i_ref[...], halo_ref[:, :256])
    lined_h = [[] for chunk in range(chunks)]
    for comp, term in enumerate(moments(grad_i, both[:, 256:], both[:, :256])):
        summed = dot(lines_ref[...], term)
        for chunk, parts in enumerate(lined_h):
            parts.append(summed[EDGE * (chunk + 1) : EDGE * (chunk + 2)].astype(jnp.bfloat16))
        part_h_ref[0, comp] = summed[:EDGE]
        part_h_ref[1, comp] = summed[EDGE * (chunks + 1) :]
    border_ref[...] = dot(jnp.concatenate(sum(lined_h, []), axis=0), pack_h_ref[...])

    copies = []
    tensor_of(inner_of(0), smooth_ref, tensor_ref.at[0])
    for z in range(count):
        later = z + known if z + known < count else None
        if later is not None and later % 2 == 0:
            make_moments(later // 2, vol_ref, mask_ref, slots[later // 2 % 2])
        if z < count - 1:
            tensor_of(inner_of(z + 1), smooth_ref, tensor_ref.at[(z + 1) % 2])
        group = 128 * (z // SLOTS)
        for chunk in range(chunks):
            rows = slice(EDGE * chunk, EDGE * (chunk + 1))
            part = slice(6 * EDGE * chunk, 6 * EDGE * (chunk + 1))

            def store(lanes, values):
                for n, value in enumerate(values):
                    if z >= count - LATER:
                        later_ref[n, z - (count - LATER), rows, lanes] = value
                    else:
                        out_ref[n, z, rows, lanes] = value

            border = border_of(border_ref[part, group : group + 128], z % SLOTS, mask_ref)
            attributes(tensor_ref[z % 2, part], border, store)
            if later is not None:
                summed = dot(lines_ref[...], slots[later // 2 % 2][later % 2, chunk])
                store_chunks(summed, chunk, inner_ref.at[later - known], part_ref.at[:, :, later])
        if z % 2 == 1 and z < count - LATER:
            depth = pl.ds(z - 1, 2)
            for n, target in enumerate(targets):
                place = target.at[depth, pl.ds(EDGE, inner)]
                copies.append(pltpu.make_async_copy(out_ref.at[n, depth], place, sems.at[z // 2, n]))
                copies[-1].start()
    for copy in copies:
        copy.wait()


def ends_kernel(
    done_ref, vol_ref, halo_ref, near_ref, far_ref, part_ref, part_h_ref,
    smooth_ref, pack_h_ref, diff_h_ref, lines_e_ref, diff_e_ref, mask_ref, in_i_ref, in_x_ref, in_p_ref,
    dip_i_ref, dip_x_ref, plan_ref,
    packed_ref, block_ref, block_h_ref, border_ref, edge_ref, out_ref, done_sems, sems,
):
    depths, rows, cols = vol_ref.shape
    count, half = depths - 2, (depths - 2) // 2
    bf16, f32 = jnp.bfloat16, jnp.float32
    span = EDGE * half
    targets = (dip_i_ref, dip_x_ref, plan_ref)
    copies = []
    for n, target in enumerate(targets):
        place = target.at[pl.ds(count - LATER, LATER), pl.ds(EDGE, rows - 2 * EDGE)]
        copies.append(pltpu.make_async_copy(done_ref.at[n], place, done_sems.at[n]))
        copies[-1].start()
    lows = [low_end(exchange) for exchange in range(2)]
    ends = [jnp.where(low, 0, 1) for low in lows]
    starts = [pl.multiple_of(jnp.where(low, 0, rows - EDGE), EDGE) for low in lows]

    def prepare(exchange, rows_ref):
        low, start, end = lows[exchange], starts[exchange], ends[exchange]
        rows_in = rows_ref[...].astype(f32)
        if exchange == 1:
            il = lax.axis_index("il")
            outside = (low & (il == 0)) | (jnp.logical_not(low) & (il == lax.axis_size("il") - 1))
            rows_in = jnp.where(outside, 0.0, rows_in)
        packed_ref[exchange] = pltpu.roll(rows_in, jnp.where(low, 0, EDGE - REACH), 0)
        place = iota((EDGE, cols), 0)
        received = jnp.where(low, place, EDGE - 1 - place) < REACH

        def joined(row, own):
            lanes = own.shape[1]
            own = pltpu.roll(own.astype(f32), jnp.where(low, REACH, EDGE - REACH), 0)
            return jnp.where(received[:, :lanes], packed_ref[exchange, row : row + EDGE, :lanes], own).astype(bf16)

        for depth in range(depths):
            block_ref[exchange, depth] = joined(REACH * depth, vol_ref[depth, pl.ds(start, EDGE)])
        own_h = halo_ref[pl.ds(start, EDGE)]
        block_h_ref[exchange, :, :256] = joined(REACH * depths, own_h[:, :256])
        block_h_ref[exchange, :, 256:] = joined(REACH * (depths + 1), own_h[:, 256:])

        both = dot(block_h_ref[exchange], diff_h_ref[...])
        grad_i = dot(diff_e_ref[...], block_h_ref[exchange, :, :256])
        lined_h = []
        for comp, term in enumerate(moments(grad_i, both[:, 256:], both[:, :256])):
            summed = part_h_ref[end, comp] + dot(lines_e_ref[exchange, :EDGE, :EDGE], term)
            lined_h.append(summed.astype(bf16))
        border_ref[exchange] = dot(jnp.concatenate(lined_h, axis=0), pack_h_ref[...])

    def make_edges(exchange, group):
        first = half * group
        planes = [block_ref[exchange, first + k : first + half + k].astype(f32).reshape(span, cols) for k in range(3)]
        for comp, term in enumerate(moments(*gradients(*planes, mask_ref))):
            outer = dot(lines_e_ref[exchange], term)
            summed = part_ref[ends[exchange], comp, first : first + half] + outer.reshape(half, EDGE, cols)
            edge_ref[exchange, first : first + half, comp] = summed.astype(bf16)

    def finish(exchange, group):
        first = half * group
        own = edge_ref[exchange, first : first + half].reshape(6 * span, cols)
        tensor = dot(own, smooth_ref[...])
        for k in range(half):

            def store(lanes, values):
                for n, value in enumerate(values):
                    out_ref[exchange, n, first + k, :, lanes] = value

            border = border_of(border_ref[exchange, :, 128 * group : 128 * (group + 1)], k, mask_ref)
            attributes(tensor[6 * EDGE * k : 6 * EDGE * (k + 1)], border, store)
        depth = pl.ds(first, half)
        for n, target in enumerate(targets):
            place = target.at[depth, pl.ds(starts[exchange], EDGE)]
            copies.append(pltpu.make_async_copy(out_ref.at[exchange, n, depth], place, sems.at[exchange, group, n]))
            copies[-1].start()

    for exchange, rows_ref in enumerate((near_ref, far_ref)):
        prepare(exchange, rows_ref)
    for exchange in range(2):
        for group in range(2):
            make_edges(exchange, group)
    for exchange in range(2):
        for group in range(2):
            finish(exchange, group)
    for copy in copies:
        copy.wait()


def call(name, kernel, outs, scratch, operands, in_specs=None, out_specs=None, flops=0, limit=16, aliases={}):
    return pl.pallas_call(
        kernel,
        out_shape=tuple(jax.ShapeDtypeStruct(*out) for out in outs),
        in_specs=in_specs or [WHOLE] * len(operands),
        out_specs=out_specs or (WHOLE,) * len(outs),
        scratch_shapes=scratch,
        compiler_params=pltpu.CompilerParams(vmem_limit_bytes=limit << 20),
        name=name,
        input_output_aliases=aliases,
        cost_estimate=pl.CostEstimate(flops=flops, bytes_accessed=0, transcendentals=0),
    )(*operands)


def body(volume):
    depths, rows, cols = volume.shape
    il, xl = lax.axis_size("il"), lax.axis_size("xl")
    count = depths - 2
    assert xl == 2 and il % 2 == 0 and count == 2 * SLOTS and rows == 128 and cols == 256
    bf16, f32 = jnp.bfloat16, jnp.float32
    half = count // 2
    work = half * 1024 * 2 * 256 * 256
    packed_rows = -(-REACH * (depths + 2) // 16) * 16

    span = EDGE * SLOTS
    lines, diff_i, smooth, pack_h, diff_h, lines_e, diff_e, pick, mask = call(
        "tables_kernel",
        lambda *refs: tables_kernel(depths, *refs),
        [
            ((rows, rows), bf16),
            ((rows, rows), bf16),
            ((cols, cols), bf16),
            ((256, 256), bf16),
            ((128 * TILES, 512), bf16),
            ((2, span, span), bf16),
            ((EDGE, EDGE), bf16),
            ((128 * SLOTS, 256), bf16),
            ((3, 8, 128), f32),
        ],
        [],
        [],
        flops=work,
    )
    halo_tile = ((TILES, rows, 128), bf16)
    vol, send, own = call("pack_kernel", pack_kernel, [(volume.shape, bf16), halo_tile, halo_tile], [], [volume, pick])
    side = lax.ppermute(send, "xl", [(0, 1), (1, 0)])
    chunks = rows // EDGE - 2
    moment_slots = [pltpu.VMEM((2, 6, rows, cols), bf16)] * 2
    partial = ((2, 6, count, EDGE, cols), f32)
    inner, part = call(
        "lines_kernel",
        lines_kernel,
        [((2 * HEAD, chunks, 6, EDGE, cols), bf16), partial],
        moment_slots,
        [vol, lines, mask],
        flops=work // 4,
    )
    packed = ((packed_rows, cols), bf16)
    halo, near, far = call(
        "rows_kernel",
        rows_kernel,
        [((rows, 128 * TILES), bf16), packed, packed],
        [pltpu.VMEM((2, packed_rows, cols), f32)],
        [vol, own, side, part],
        in_specs=[WHOLE] * 3 + [ANYWHERE],
    )
    near_in = lax.ppermute(near, "il", [(i, i ^ 1) for i in range(il)])
    pairs = [(i, i + 1) for i in range(1, il - 1, 2)]
    shared_shape = ((2 * SHARED, chunks, 6, EDGE, cols), bf16)
    operands = [vol, lines, mask, part, far]
    shared, part, far = call(
        "odd_lines_kernel",
        lambda *refs: shared_lines_kernel(1, *refs),
        [shared_shape, partial, packed],
        moment_slots,
        operands,
        flops=work // 4,
        aliases={3: 1},
    )
    far_in = lax.ppermute(far, "il", pairs + [(j, i) for i, j in pairs] + [(0, 0), (il - 1, il - 1)])
    operands = [vol, lines, mask, part, shared]
    shared, part = call(
        "even_lines_kernel",
        lambda *refs: shared_lines_kernel(0, *refs),
        [shared_shape, partial],
        moment_slots,
        operands,
        flops=work // 4,
        aliases={3: 1, 4: 0},
    )

    outs = [((count, rows, cols), f32)] * 3
    operands = [vol, lines, diff_i, smooth, halo, diff_h, pack_h, mask, inner, shared, part]
    part, *outs_in, done, part_h = call(
        "own_kernel",
        own_kernel,
        [partial, *outs, ((3, LATER, EDGE * chunks, cols), f32), ((2, 6, EDGE, 256), f32)],
        [
            pltpu.VMEM((count - 2 * (HEAD + SHARED), chunks, 6, EDGE, cols), bf16),
            pltpu.VMEM((6 * EDGE * chunks, 256), f32),
            *moment_slots,
            pltpu.VMEM((2, 6 * EDGE * chunks, cols), f32),
            pltpu.VMEM((3, count - LATER, EDGE * chunks, cols), f32),
            pltpu.SemaphoreType.DMA(((count - LATER) // 2, 3)),
        ],
        operands,
        out_specs=(WHOLE,) + (IN_HBM,) * 3 + (WHOLE,) * 2,
        flops=5 * work,
        limit=24,
        aliases={len(operands) - 1: 0},
    )

    operands = [done, vol, halo, near_in, far_in, part, part_h, smooth, pack_h, diff_h, lines_e, diff_e, mask]
    return call(
        "ends_kernel",
        ends_kernel,
        outs,
        [
            pltpu.VMEM((2, packed_rows, cols), f32),
            pltpu.VMEM((2, depths, EDGE, cols), bf16),
            pltpu.VMEM((2, EDGE, 128 * TILES), bf16),
            pltpu.VMEM((2, 6 * EDGE, 256), f32),
            pltpu.VMEM((2, count, 6, EDGE, cols), bf16),
            pltpu.VMEM((2, 3, count, EDGE, cols), f32),
            pltpu.SemaphoreType.DMA((3,)),
            pltpu.SemaphoreType.DMA((2, 2, 3)),
        ],
        operands + outs_in,
        in_specs=[WHOLE] * len(operands) + [IN_HBM] * 3,
        out_specs=(IN_HBM,) * 3,
        flops=2 * work,
        limit=24,
        aliases={len(operands) + n: n for n in range(3)},
    )


def solution(mesh):
    spec = P(None, ("parts", "il"), "xl")
    return jax.shard_map(body, mesh=mesh, in_specs=(spec,), out_specs=(spec,) * 3, check_vma=False)
```

```python
import jax
import jax.numpy as jnp
import ml_dtypes
import numpy as np
from jax import lax
from jax.experimental import pallas as pl
from jax.experimental.pallas import tpu as pltpu
from jax.sharding import PartitionSpec as P

RADIUS = 9
REACH = RADIUS + 1
SIDE = 16
SLOTS = 8
TILES = 3
EDGE = 16
OWN = 2
TINY = float(np.finfo(np.float32).tiny)
HEAD = 4
AHEAD = 3
LATER = 6
SHARED = 2
FAR = -1000
WHOLE = pl.BlockSpec(memory_space=pltpu.VMEM)
IN_HBM = pl.BlockSpec(memory_space=pltpu.HBM)
ANYWHERE = pl.BlockSpec(memory_space=pl.ANY)


def filter_taps():
    offsets = np.arange(2 * RADIUS + 1).astype(np.float32)
    sigma = np.float32(RADIUS / 3.0)
    shape = np.exp(np.float32(-0.5) * ((offsets - RADIUS) / sigma) ** 2)
    return (shape / np.sum(shape, dtype=np.float32)).astype(ml_dtypes.bfloat16).astype(np.float32)


def iota(shape, dim):
    return lax.broadcasted_iota(jnp.int32, shape, dim)


def band(source, target, scale=1.0):
    offset = jnp.abs(source - target)
    weights = jnp.zeros(offset.shape, jnp.float32)
    for distance, tap in enumerate(filter_taps()[RADIUS:]):
        weights = jnp.where(offset == distance, jnp.float32(scale * tap), weights)
    return weights


def difference(source, target):
    offset = source - target
    return jnp.where(offset == 1, 1.0, jnp.where(offset == -1, -1.0, 0.0)).astype(jnp.float32)


def dot(left, right):
    return jnp.dot(left, right, preferred_element_type=jnp.float32)


def halo_plane(lane, tile, depths):
    slot = lax.div(lane, SIDE)
    rest = jnp.where(slot == 0, 0, jnp.where(slot == 1, depths - 1, FAR))
    return jnp.where(tile < 2, 1 + SLOTS * tile + slot, rest)


def halo_column(lane, x, cols):
    place = lax.rem(lane, SIDE)
    return jnp.where(x == 0, cols - OWN + place, place - (SIDE - OWN))


def low_end(exchange):
    even = lax.rem(lax.axis_index("il"), 2) == 0
    return jnp.logical_not(even) if exchange == 0 else even


def tables_kernel(depths, lines_ref, diff_i_ref, smooth_ref, pack_h_ref, diff_h_ref, lines_e_ref, diff_e_ref, pick_ref, mask_ref):
    rows, cols = lines_ref.shape[0], smooth_ref.shape[0]
    x, il, last = lax.axis_index("xl"), lax.axis_index("il"), lax.axis_size("il") - 1
    bf16 = jnp.bfloat16

    target, source = iota((rows, rows), 0), iota((rows, rows), 1)
    inner = (source > 0) & (source < rows - 1)
    lines_ref[...] = jnp.where(inner, band(source, target, 0.25), 0.0).astype(bf16)
    diff_i_ref[...] = difference(source, target).astype(bf16)
    span = EDGE * SLOTS
    target, source = iota((span, span), 0), iota((span, span), 1)
    depth = lax.div(source, EDGE) == lax.div(target, EDGE)
    target, source = lax.rem(target, EDGE), lax.rem(source, EDGE)
    diff_e_ref[...] = difference(source, target)[:EDGE, :EDGE].astype(bf16)
    for exchange in range(2):
        low = low_end(exchange)
        source_at = jnp.where(low, source - REACH, rows - (EDGE - REACH) + source)
        target_at = jnp.where(low, target, rows - EDGE + target)
        first = jnp.where(low & (il > 0), -rows, 0)
        final = jnp.where(jnp.logical_not(low) & (il < last), 2 * rows, rows - 1)
        use = depth & (source_at >= first) & (source_at <= final) & ((source_at <= 0) | (source_at >= rows - 1))
        lines_e_ref[exchange] = jnp.where(use, band(source_at, target_at, 0.25), 0.0).astype(bf16)

    source, target = iota((cols, cols), 0), iota((cols, cols), 1)
    moved = source == jnp.where(x == 0, cols - 1, 0)
    column = lax.rem(target + 128 * x, cols)
    smooth_ref[...] = jnp.where(moved, 0.0, band(source, column)).astype(bf16)
    source, target = iota((256, 256), 0), iota((256, 256), 1)
    place = lax.rem(source, SIDE)
    use = (lax.div(source, SIDE) == lax.div(target, SIDE)) & (place != jnp.where(x == 0, 0, SIDE - 1))
    column = jnp.where(x == 0, cols - SIDE, 0) + lax.rem(target, SIDE)
    pack_h_ref[...] = jnp.where(use, band(halo_column(place, x, cols), column), 0.0).astype(bf16)

    source, target = iota((128, 128), 0), iota((128, 128), 1)
    same = lax.rem(source, SIDE) == lax.rem(target, SIDE)
    across = difference(lax.rem(source, SIDE), lax.rem(target, SIDE))
    for group in range(2):
        centre = halo_plane(target, group, depths)
        for tile in range(TILES):
            plane = halo_plane(source, tile, depths)
            part, out = slice(128 * tile, 128 * (tile + 1)), 128 * group
            diff_h_ref[part, out : out + 128] = jnp.where(same, difference(plane, centre), 0.0).astype(bf16)
            diff_h_ref[part, 256 + out : 384 + out] = jnp.where(plane == centre, across, 0.0).astype(bf16)

    source, lane = iota((128, 256), 0), iota((128, 256), 1)
    place = lax.rem(lane, SIDE)
    low, high = place < SIDE - OWN, place >= OWN
    sent = jnp.where(x == 0, jnp.where(low, 128 - (SIDE - OWN) + place, FAR), jnp.where(high, place - OWN, FAR))
    low, high = place < OWN, place >= SIDE - OWN
    kept = jnp.where(x == 0, jnp.where(low, 128 - OWN + place, FAR), jnp.where(high, place - (SIDE - OWN), FAR))
    pick = jnp.where(source == jnp.where(lane < 128, sent, kept), 1.0, 0.0)
    slot = lax.div(lax.rem(lane, 128), SIDE)
    for index in range(SLOTS):
        pick_ref[128 * index : 128 * (index + 1)] = jnp.where(slot == index, pick, 0.0).astype(bf16)
    lane = iota((8, 128), 1)
    border = jnp.where(x == 0, lane - (128 - SIDE), lane)
    mask_ref[0] = jnp.where((border >= 0) & (border < SIDE), 1.0, 0.0)
    mask_ref[1] = jnp.where(lane > 0, 1.0, 0.0)
    mask_ref[2] = jnp.where(lane < 127, 1.0, 0.0)


def pack_kernel(vol_ref, pick_ref, copy_ref, send_ref, own_ref):
    depths, rows, cols = vol_ref.shape
    edge = pl.ds(pl.multiple_of((cols - 128) * (1 - lax.axis_index("xl")), 128), 128)
    copy_ref[...] = vol_ref[...]
    for tile in range(TILES):
        planes = (0, depths - 1) if tile == 2 else range(1 + SLOTS * tile, 1 + SLOTS * (tile + 1))
        beside = jnp.concatenate([vol_ref[plane, :, edge] for plane in planes], axis=1)
        packed = dot(beside, pick_ref[: beside.shape[1]]).astype(jnp.bfloat16)
        send_ref[tile] = packed[:, :128]
        own_ref[tile] = packed[:, 128:]


def rows_kernel(vol_ref, own_ref, side_ref, after_ref, halo_ref, near_ref, far_ref, packed_ref):
    depths, rows, cols = vol_ref.shape
    even = lax.rem(lax.axis_index("il"), 2) == 0

    def put(row, top, bottom):
        top, bottom = top[:REACH], bottom[EDGE - REACH :]
        lanes = top.shape[1]
        packed_ref[0, row : row + REACH, :lanes] = jnp.where(even, bottom, top)
        packed_ref[1, row : row + REACH, :lanes] = jnp.where(even, top, bottom)

    packed_ref[:, depths * REACH :, :] = jnp.zeros_like(packed_ref[:, depths * REACH :, :])
    for depth in range(depths):
        top = vol_ref[depth, :EDGE, :].astype(jnp.float32)
        bottom = vol_ref[depth, rows - EDGE :, :].astype(jnp.float32)
        put(REACH * depth, top, bottom)
    tiles = []
    for tile in range(TILES):
        merged = own_ref[tile].astype(jnp.float32) + side_ref[tile].astype(jnp.float32)
        halo_ref[:, 128 * tile : 128 * (tile + 1)] = merged.astype(jnp.bfloat16)
        tiles.append((merged[:EDGE], merged[rows - EDGE :]))
    tops = jnp.concatenate([tiles[0][0], tiles[1][0]], axis=1)
    bottoms = jnp.concatenate([tiles[0][1], tiles[1][1]], axis=1)
    put(REACH * depths, tops, bottoms)
    put(REACH * (depths + 1), *tiles[2])
    near_ref[...] = packed_ref[0].astype(jnp.bfloat16)
    far_ref[...] = packed_ref[1].astype(jnp.bfloat16)


def moments(grad_i, grad_x, grad_z):
    terms = (
        grad_i * grad_i,
        grad_x * grad_x,
        grad_z * grad_z,
        grad_i * grad_x,
        grad_i * grad_z,
        grad_x * grad_z,
    )
    return [term.astype(jnp.bfloat16) for term in terms]


def store_chunks(summed, comp, inner_ref, part_ref):
    chunks = summed.shape[0] // EDGE
    for chunk in range(1, chunks - 1):
        inner_ref[chunk - 1, comp] = summed[EDGE * chunk : EDGE * (chunk + 1)].astype(jnp.bfloat16)
    part_ref[0, comp] = summed[:EDGE]
    part_ref[1, comp] = summed[EDGE * (chunks - 1) :]


def gradients(before, centre, after, mask_ref):
    rows, cols = centre.shape
    left, right = pltpu.roll(centre, 1, 1), pltpu.roll(centre, cols - 1, 1)
    left_0 = (left[:, :128].reshape(-1, 8, 128) * mask_ref[1]).reshape(rows, 128)
    right_1 = (right[:, cols - 128 :].reshape(-1, 8, 128) * mask_ref[2]).reshape(rows, 128)
    grad_x = jnp.concatenate([right[:, : cols - 128] - left_0, right_1 - left[:, 128:]], axis=1)
    return pltpu.roll(centre, rows - 1, 0) - pltpu.roll(centre, 1, 0), grad_x, after - before


def make_moments(pair, vol_ref, mask_ref, moments_ref):
    planes = [vol_ref[2 * pair + k].astype(jnp.float32) for k in range(4)]
    for k in range(2):
        for comp, term in enumerate(moments(*gradients(*planes[k : k + 3], mask_ref))):
            moments_ref[k, comp] = term


def make_lines(z, comp, lines_ref, moments_ref, inner_ref, part_ref):
    store_chunks(dot(lines_ref[...], moments_ref[z % 2, comp]), comp, inner_ref.at[z], part_ref.at[:, :, z])


def lines_kernel(vol_ref, lines_ref, mask_ref, inner_ref, part_ref, even_ref, odd_ref):
    slots = (even_ref, odd_ref)
    for pair in range(HEAD):
        make_moments(pair, vol_ref, mask_ref, slots[pair % 2])
        for k in range(2):
            for comp in range(6):
                make_lines(2 * pair + k, comp, lines_ref, slots[pair % 2], inner_ref, part_ref)


def shared_lines_kernel(
    parity, vol_ref, lines_ref, mask_ref, part_in_ref, *refs,
):
    if parity == 1:
        rows_ref, inner_ref, part_ref, rows_out_ref, even_ref, odd_ref = refs
        rows_out_ref[...] = rows_ref[...]
    else:
        shared_in_ref, inner_ref, part_ref, even_ref, odd_ref = refs

    @pl.when(lax.rem(lax.axis_index("il"), 2) == parity)
    def _():
        for index in range(SHARED):
            pair, slot = HEAD + index, (even_ref, odd_ref)[index % 2]
            make_moments(pair, vol_ref, mask_ref, slot)
            for k in range(2):
                z = 2 * pair + k
                for comp in range(6):
                    summed = dot(lines_ref[...], slot[k, comp])
                    store_chunks(summed, comp, inner_ref.at[2 * index + k], part_ref.at[:, :, z])


def tensor_of(own, smooth_ref, tensor_ref):
    tensor_ref[...] = dot(own.reshape(-1, own.shape[-1]), smooth_ref[...])


def attributes(tensor, border, store):
    x = lax.axis_index("xl")
    halves = (tensor[:, :128], tensor[:, 128:] + border)
    lanes = (pl.multiple_of(128 * x, 128), pl.multiple_of(128 - 128 * x, 128))
    for half, lane in zip(halves, lanes):
        a, b, c, d, e, f = [half[EDGE * comp : EDGE * (comp + 1)] for comp in range(6)]
        low = -1e-6 - c
        inverse = pl.reciprocal(low, approx=True)
        spread = (a - b) * (a - c) + (b - c) * (b - c) + 3.0 * (d * d + e * e + f * f)
        root = spread * lax.rsqrt(jnp.maximum(spread, TINY))
        store(pl.ds(lane, 128), (e * inverse, f * inverse, root * pl.reciprocal(a + b - low, approx=True)))


def border_of(packed, slot, mask_ref):
    base = jnp.where(lax.axis_index("xl") == 0, 128 - SIDE, 0)
    moved = pltpu.roll(packed, lax.rem(base - SIDE * slot + 128, 128), 1)
    return (moved.reshape(-1, 8, 128) * mask_ref[0]).reshape(packed.shape)


def own_kernel(
    vol_ref, lines_ref, diff_i_ref, smooth_ref, halo_ref, diff_h_ref, pack_h_ref, mask_ref, inner_in_ref, shared_ref, part_in_ref,
    part_ref, dip_i_ref, dip_x_ref, plan_ref, later_ref, part_h_ref,
    inner_ref, border_ref, even_ref, odd_ref, tensor_ref, out_ref, sems,
):
    count, chunks = vol_ref.shape[0] - 2, inner_ref.shape[1]
    inner = EDGE * chunks
    slots = (even_ref, odd_ref)
    targets = (dip_i_ref, dip_x_ref, plan_ref)
    ready, known = 2 * HEAD, 2 * (HEAD + SHARED)

    def inner_of(z):
        return inner_in_ref[z] if z < ready else shared_ref[z - ready] if z < known else inner_ref[z - known]


    both = dot(halo_ref[...], diff_h_ref[...])
    grad_i = dot(diff_i_ref[...], halo_ref[:, :256])
    lined_h = [[] for chunk in range(chunks)]
    for comp, term in enumerate(moments(grad_i, both[:, 256:], both[:, :256])):
        summed = dot(lines_ref[...], term)
        for chunk, parts in enumerate(lined_h):
            parts.append(summed[EDGE * (chunk + 1) : EDGE * (chunk + 2)].astype(jnp.bfloat16))
        part_h_ref[0, comp] = summed[:EDGE]
        part_h_ref[1, comp] = summed[EDGE * (chunks + 1) :]
    border_ref[...] = dot(jnp.concatenate(sum(lined_h, []), axis=0), pack_h_ref[...])

    copies = []
    tensor_of(inner_of(0), smooth_ref, tensor_ref.at[0])
    for z in range(count):
        later = z + known if z + known < count else None
        if later is not None and later % 2 == 0:
            make_moments(later // 2, vol_ref, mask_ref, slots[later // 2 % 2])
        if z < count - 1:
            tensor_of(inner_of(z + 1), smooth_ref, tensor_ref.at[(z + 1) % 2])
        group = 128 * (z // SLOTS)
        for chunk in range(chunks):
            rows = slice(EDGE * chunk, EDGE * (chunk + 1))
            part = slice(6 * EDGE * chunk, 6 * EDGE * (chunk + 1))

            def store(lanes, values):
                for n, value in enumerate(values):
                    if z >= count - LATER:
                        later_ref[n, z - (count - LATER), rows, lanes] = value
                    else:
                        out_ref[n, z, rows, lanes] = value

            border = border_of(border_ref[part, group : group + 128], z % SLOTS, mask_ref)
            attributes(tensor_ref[z % 2, part], border, store)
            if later is not None:
                summed = dot(lines_ref[...], slots[later // 2 % 2][later % 2, chunk])
                store_chunks(summed, chunk, inner_ref.at[later - known], part_ref.at[:, :, later])
        if z % 2 == 1 and z < count - LATER:
            depth = pl.ds(z - 1, 2)
            for n, target in enumerate(targets):
                place = target.at[depth, pl.ds(EDGE, inner)]
                copies.append(pltpu.make_async_copy(out_ref.at[n, depth], place, sems.at[z // 2, n]))
                copies[-1].start()
    for copy in copies:
        copy.wait()


def ends_kernel(
    done_ref, vol_ref, halo_ref, near_ref, far_ref, part_ref, part_h_ref,
    smooth_ref, pack_h_ref, diff_h_ref, lines_e_ref, diff_e_ref, mask_ref, in_i_ref, in_x_ref, in_p_ref,
    dip_i_ref, dip_x_ref, plan_ref,
    packed_ref, block_ref, block_h_ref, border_ref, edge_ref, out_ref, done_sems, sems,
):
    depths, rows, cols = vol_ref.shape
    count, half = depths - 2, (depths - 2) // 2
    bf16, f32 = jnp.bfloat16, jnp.float32
    span = EDGE * half
    targets = (dip_i_ref, dip_x_ref, plan_ref)
    copies = []
    for n, target in enumerate(targets):
        place = target.at[pl.ds(count - LATER, LATER), pl.ds(EDGE, rows - 2 * EDGE)]
        copies.append(pltpu.make_async_copy(done_ref.at[n], place, done_sems.at[n]))
        copies[-1].start()
    lows = [low_end(exchange) for exchange in range(2)]
    ends = [jnp.where(low, 0, 1) for low in lows]
    starts = [pl.multiple_of(jnp.where(low, 0, rows - EDGE), EDGE) for low in lows]

    def prepare(exchange, rows_ref):
        low, start, end = lows[exchange], starts[exchange], ends[exchange]
        rows_in = rows_ref[...].astype(f32)
        if exchange == 1:
            il = lax.axis_index("il")
            outside = (low & (il == 0)) | (jnp.logical_not(low) & (il == lax.axis_size("il") - 1))
            rows_in = jnp.where(outside, 0.0, rows_in)
        packed_ref[exchange] = pltpu.roll(rows_in, jnp.where(low, 0, EDGE - REACH), 0)
        place = iota((EDGE, cols), 0)
        received = jnp.where(low, place, EDGE - 1 - place) < REACH

        def joined(row, own):
            lanes = own.shape[1]
            own = pltpu.roll(own.astype(f32), jnp.where(low, REACH, EDGE - REACH), 0)
            return jnp.where(received[:, :lanes], packed_ref[exchange, row : row + EDGE, :lanes], own).astype(bf16)

        for depth in range(depths):
            block_ref[exchange, depth] = joined(REACH * depth, vol_ref[depth, pl.ds(start, EDGE)])
        own_h = halo_ref[pl.ds(start, EDGE)]
        block_h_ref[exchange, :, :256] = joined(REACH * depths, own_h[:, :256])
        block_h_ref[exchange, :, 256:] = joined(REACH * (depths + 1), own_h[:, 256:])

        both = dot(block_h_ref[exchange], diff_h_ref[...])
        grad_i = dot(diff_e_ref[...], block_h_ref[exchange, :, :256])
        lined_h = []
        for comp, term in enumerate(moments(grad_i, both[:, 256:], both[:, :256])):
            summed = part_h_ref[end, comp] + dot(lines_e_ref[exchange, :EDGE, :EDGE], term)
            lined_h.append(summed.astype(bf16))
        border_ref[exchange] = dot(jnp.concatenate(lined_h, axis=0), pack_h_ref[...])

    def make_edges(exchange, group):
        first = half * group
        planes = [block_ref[exchange, first + k : first + half + k].astype(f32).reshape(span, cols) for k in range(3)]
        for comp, term in enumerate(moments(*gradients(*planes, mask_ref))):
            outer = dot(lines_e_ref[exchange], term)
            summed = part_ref[ends[exchange], comp, first : first + half] + outer.reshape(half, EDGE, cols)
            edge_ref[exchange, first : first + half, comp] = summed.astype(bf16)

    def finish(exchange, group):
        first = half * group
        own = edge_ref[exchange, first : first + half].reshape(6 * span, cols)
        tensor = dot(own, smooth_ref[...])
        for k in range(half):

            def store(lanes, values):
                for n, value in enumerate(values):
                    out_ref[exchange, n, first + k, :, lanes] = value

            border = border_of(border_ref[exchange, :, 128 * group : 128 * (group + 1)], k, mask_ref)
            attributes(tensor[6 * EDGE * k : 6 * EDGE * (k + 1)], border, store)
        depth = pl.ds(first, half)
        for n, target in enumerate(targets):
            place = target.at[depth, pl.ds(starts[exchange], EDGE)]
            copies.append(pltpu.make_async_copy(out_ref.at[exchange, n, depth], place, sems.at[exchange, group, n]))
            copies[-1].start()

    for exchange, rows_ref in enumerate((near_ref, far_ref)):
        prepare(exchange, rows_ref)
    for exchange in range(2):
        for group in range(2):
            make_edges(exchange, group)
    for exchange in range(2):
        for group in range(2):
            finish(exchange, group)
    for copy in copies:
        copy.wait()


def call(name, kernel, outs, scratch, operands, in_specs=None, out_specs=None, flops=0, limit=16, aliases={}):
    return pl.pallas_call(
        kernel,
        out_shape=tuple(jax.ShapeDtypeStruct(*out) for out in outs),
        in_specs=in_specs or [WHOLE] * len(operands),
        out_specs=out_specs or (WHOLE,) * len(outs),
        scratch_shapes=scratch,
        compiler_params=pltpu.CompilerParams(vmem_limit_bytes=limit << 20),
        name=name,
        input_output_aliases=aliases,
        cost_estimate=pl.CostEstimate(flops=flops, bytes_accessed=0, transcendentals=0),
    )(*operands)


def body(volume):
    depths, rows, cols = volume.shape
    il, xl = lax.axis_size("il"), lax.axis_size("xl")
    count = depths - 2
    assert xl == 2 and il % 2 == 0 and count == 2 * SLOTS and rows == 128 and cols == 256
    bf16, f32 = jnp.bfloat16, jnp.float32
    half = count // 2
    work = half * 1024 * 2 * 256 * 256
    packed_rows = -(-REACH * (depths + 2) // 16) * 16

    span = EDGE * SLOTS
    lines, diff_i, smooth, pack_h, diff_h, lines_e, diff_e, pick, mask = call(
        "tables_kernel",
        lambda *refs: tables_kernel(depths, *refs),
        [
            ((rows, rows), bf16),
            ((rows, rows), bf16),
            ((cols, cols), bf16),
            ((256, 256), bf16),
            ((128 * TILES, 512), bf16),
            ((2, span, span), bf16),
            ((EDGE, EDGE), bf16),
            ((128 * SLOTS, 256), bf16),
            ((3, 8, 128), f32),
        ],
        [],
        [],
        flops=work,
    )
    halo_tile = ((TILES, rows, 128), bf16)
    vol, send, own = call("pack_kernel", pack_kernel, [(volume.shape, bf16), halo_tile, halo_tile], [], [volume, pick])
    side = lax.ppermute(send, "xl", [(0, 1), (1, 0)])
    chunks = rows // EDGE - 2
    moment_slots = [pltpu.VMEM((2, 6, rows, cols), bf16)] * 2
    partial = ((2, 6, count, EDGE, cols), f32)
    inner, part = call(
        "lines_kernel",
        lines_kernel,
        [((2 * HEAD, chunks, 6, EDGE, cols), bf16), partial],
        moment_slots,
        [vol, lines, mask],
        flops=work // 4,
    )
    packed = ((packed_rows, cols), bf16)
    halo, near, far = call(
        "rows_kernel",
        rows_kernel,
        [((rows, 128 * TILES), bf16), packed, packed],
        [pltpu.VMEM((2, packed_rows, cols), f32)],
        [vol, own, side, part],
        in_specs=[WHOLE] * 3 + [ANYWHERE],
    )
    near_in = lax.ppermute(near, "il", [(i, i ^ 1) for i in range(il)])
    pairs = [(i, i + 1) for i in range(1, il - 1, 2)]
    shared_shape = ((2 * SHARED, chunks, 6, EDGE, cols), bf16)
    operands = [vol, lines, mask, part, far]
    shared, part, far = call(
        "odd_lines_kernel",
        lambda *refs: shared_lines_kernel(1, *refs),
        [shared_shape, partial, packed],
        moment_slots,
        operands,
        flops=work // 4,
        aliases={3: 1},
    )
    far_in = lax.ppermute(far, "il", pairs + [(j, i) for i, j in pairs] + [(0, 0), (il - 1, il - 1)])
    operands = [vol, lines, mask, part, shared]
    shared, part = call(
        "even_lines_kernel",
        lambda *refs: shared_lines_kernel(0, *refs),
        [shared_shape, partial],
        moment_slots,
        operands,
        flops=work // 4,
        aliases={3: 1, 4: 0},
    )

    outs = [((count, rows, cols), f32)] * 3
    operands = [vol, lines, diff_i, smooth, halo, diff_h, pack_h, mask, inner, shared, part]
    part, *outs_in, done, part_h = call(
        "own_kernel",
        own_kernel,
        [partial, *outs, ((3, LATER, EDGE * chunks, cols), f32), ((2, 6, EDGE, 256), f32)],
        [
            pltpu.VMEM((count - 2 * (HEAD + SHARED), chunks, 6, EDGE, cols), bf16),
            pltpu.VMEM((6 * EDGE * chunks, 256), f32),
            *moment_slots,
            pltpu.VMEM((2, 6 * EDGE * chunks, cols), f32),
            pltpu.VMEM((3, count - LATER, EDGE * chunks, cols), f32),
            pltpu.SemaphoreType.DMA(((count - LATER) // 2, 3)),
        ],
        operands,
        out_specs=(WHOLE,) + (IN_HBM,) * 3 + (WHOLE,) * 2,
        flops=5 * work,
        limit=24,
        aliases={len(operands) - 1: 0},
    )

    operands = [done, vol, halo, near_in, far_in, part, part_h, smooth, pack_h, diff_h, lines_e, diff_e, mask]
    return call(
        "ends_kernel",
        ends_kernel,
        outs,
        [
            pltpu.VMEM((2, packed_rows, cols), f32),
            pltpu.VMEM((2, depths, EDGE, cols), bf16),
            pltpu.VMEM((2, EDGE, 128 * TILES), bf16),
            pltpu.VMEM((2, 6 * EDGE, 256), f32),
            pltpu.VMEM((2, count, 6, EDGE, cols), bf16),
            pltpu.VMEM((2, 3, count, EDGE, cols), f32),
            pltpu.SemaphoreType.DMA((3,)),
            pltpu.SemaphoreType.DMA((2, 2, 3)),
        ],
        operands + outs_in,
        in_specs=[WHOLE] * len(operands) + [IN_HBM] * 3,
        out_specs=(IN_HBM,) * 3,
        flops=2 * work,
        limit=24,
        aliases={len(operands) + n: n for n in range(3)},
    )


def solution(mesh):
    spec = P(None, ("parts", "il"), "xl")
    return jax.shard_map(body, mesh=mesh, in_specs=(spec,), out_specs=(spec,) * 3, check_vma=False)
```
